32 devices in a mesh: section: 2 (over core), dp: 4 (over y, x), tensor: 4 (over z).
Axes of the slice: x: 2, y: 2, z: 4, core: 2. Of those that a mesh axis runs over, the one named last changes fastest.
Arguments:
- inputs: bfloat16 [8, 1024, 1536], P('dp', 'tensor'), may hold values from -6 to 6
- lengths: int32 [8], P('dp'), may hold values from 256 to 1024, as said below
- adapter_ids: int32 [8], P('dp'), may hold values from 0 to 7, as said below
- cotangent: bfloat16 [8, 1024, 1536], P('dp', 'tensor'), may hold values from -6 to 6
- norm_gain: bfloat16 [2, 2, 1536], P('section'), may hold values from 0.25 to 1.75
- query_weight: bfloat16 [2, 1536, 1536], P('section', 'dp', 'tensor'), may hold values from -0.15625 to 0.15625
- query_bias: bfloat16 [2, 1536], P('section', 'tensor'), may hold values from -3 to 3
- keyvalue_weight: bfloat16 [2, 2, 1536, 256], P('section', None, 'dp'), may hold values from -0.15625 to 0.15625
- keyvalue_bias: bfloat16 [2, 2, 256], P('section'), may hold values from -3 to 3
- output_weight: bfloat16 [2, 1536, 1536], P('section', 'tensor', 'dp'), may hold values from -1.25 to 1.25
- expand_weight: bfloat16 [2, 2, 1536, 8960], P('section', None, 'dp', 'tensor'), may hold values from -0.15625 to 0.15625
- shrink_weight: bfloat16 [2, 8960, 1536], P('section', 'tensor', 'dp'), may hold values from -0.0625 to 0.0625
- adapter_input: bfloat16 [2, 8, 1536, 80], P('section'), may hold values from -0.15625 to 0.15625
- adapter_query: bfloat16 [2, 8, 16, 1536], P('section', None, None, 'tensor'), may hold values from -0.75 to 0.75
- adapter_keyvalue: bfloat16 [2, 8, 2, 16, 256], P('section'), may hold values from -0.75 to 0.75
- adapter_expand: bfloat16 [2, 8, 2, 16, 8960], P('section', None, None, None, 'tensor'), may hold values from -0.75 to 0.75
- adapter_attend: bfloat16 [2, 8, 1536, 16], P('section', None, 'tensor'), may hold values from -1.25 to 1.25
- adapter_shrink: bfloat16 [2, 8, 8960, 16], P('section', None, 'tensor'), may hold values from -0.0625 to 0.0625
- adapter_residual: bfloat16 [2, 8, 2, 16, 1536], P('section'), may hold values from -0.75 to 0.75
Outputs:
- layer_output: bfloat16 [2, 8, 1024, 1536], P('section', 'dp', 'tensor')
- input_grad: float32 [2, 8, 1024, 1536], P('section', 'dp', 'tensor')
- grad_adapter_input: float32 [2, 8, 1536, 80], P('section')
- grad_adapter_query: float32 [2, 8, 16, 1536], P('section', None, None, 'tensor')
- grad_adapter_keyvalue: float32 [2, 8, 2, 16, 256], P('section')
- grad_adapter_expand: float32 [2, 8, 2, 16, 8960], P('section', None, None, None, 'tensor')
- grad_adapter_attend: float32 [2, 8, 1536, 16], P('section', None, 'tensor')
- grad_adapter_shrink: float32 [2, 8, 8960, 16], P('section', None, 'tensor')
- grad_adapter_residual: float32 [2, 8, 2, 16, 1536], P('section')
The draws below stay inside these ranges and needn't reach their ends.
Inputs may be any that keep to these rules, and one draw needn't show every extreme that they name: `lengths`: slots 0 to len - 1 of a sequence are valid; some sequence is full, some holds 256. `adapter_ids`: the first and the last adapter are named by some sequence.
All inputs are finite; a program needn't handle non-finite values.
Results may differ from the reference program's by a relative error of at most 0.03.
Values may be sent and summed in bfloat16 or wider, within the bound.
A program may use at most 248 MiB of HBM per device.

```python
import math
import jax
import jax.numpy as jnp
from jax import lax

D = 1536
HEADS = 12
KV_HEADS = 2
HEAD_DIM = 128
FF = 8960
RANK = 16
ADAPTERS = 8
SLOTS = 1024
SEQS = 8
TOKENS = 8192


def draw_lengths(key, part):
    base_key = jax.random.fold_in(key, 11)
    drawn = jax.random.randint(jax.random.fold_in(base_key, 1), (SEQS,), SLOTS // 4, SLOTS + 1, dtype=jnp.int32)
    shuffled = jax.random.permutation(jax.random.fold_in(base_key, 2), SEQS)
    drawn = drawn.at[shuffled[0]].set(SLOTS)
    return drawn.at[shuffled[1]].set(SLOTS // 4)


def draw_adapter_ids(key, part):
    base_key = jax.random.fold_in(key, 23)
    drawn = jax.random.randint(jax.random.fold_in(base_key, 1), (SEQS,), 0, ADAPTERS, dtype=jnp.int32)
    shuffled = jax.random.permutation(jax.random.fold_in(base_key, 2), SEQS)
    drawn = drawn.at[shuffled[0]].set(ADAPTERS - 1)
    return drawn.at[shuffled[1]].set(0)


def block_scale(key, extent, cuts, smallest, high):
    def one(dim, parts):
        steps = jax.random.uniform(jax.random.fold_in(jax.random.fold_in(key, 6), dim), (parts,), jnp.float32, smallest / len(cuts), high / len(cuts))
        return jnp.repeat(jnp.exp(steps), extent[dim] // parts).reshape((-1,) + (1,) * (len(extent) - dim - 1))

    gain = one(*cuts[0])
    for cut in cuts[1:]:
        gain = gain * one(*cut)
    return gain


def centred(own_key, dims, scale, most, cuts=(), kind=jnp.bfloat16):
    result = scale * jax.random.normal(own_key, dims, jnp.float32)
    if cuts:
        result = result * block_scale(own_key, dims, cuts, -0.22, 0.18)
    return jnp.clip(result, -most, most).astype(kind)


def setup_inputs(seed: int = 0) -> dict:
    keys = jax.random.split(jax.random.key(seed), 20)
    inputs = centred(keys[0], (SEQS, SLOTS, D), 1.0, 6.0, ((0, 4), (1, 4)))
    lengths = draw_lengths(jax.random.fold_in(keys[19], 71), 0)
    adapter_ids = draw_adapter_ids(jax.random.fold_in(keys[19], 71), 0)
    cotangent = centred(keys[3], (SEQS, SLOTS, D), 1.0, 6.0, ((0, 4), (1, 4)))
    norm_gain = jnp.clip(1.0 + 0.15 * jax.random.normal(keys[4], (2, 2, D), jnp.float32), 0.25, 1.75).astype(jnp.bfloat16)
    query_weight = centred(keys[5], (2, D, HEADS * HEAD_DIM), D ** -0.5, 0.15625, ((0, 2), (1, 4), (2, 4)))
    query_bias = centred(keys[6], (2, HEADS * HEAD_DIM), 0.5, 3.0, ((0, 2), (1, 4)))
    keyvalue_weight = centred(keys[7], (2, 2, D, KV_HEADS * HEAD_DIM), D ** -0.5, 0.15625, ((0, 2), (2, 4)))
    keyvalue_bias = centred(keys[8], (2, 2, KV_HEADS * HEAD_DIM), 0.5, 3.0, ((0, 2),))
    output_weight = centred(keys[9], (2, HEADS * HEAD_DIM, D), (HEADS * HEAD_DIM // 64) ** -0.5, 1.25, ((0, 2), (1, 4), (2, 4)))
    expand_weight = centred(keys[10], (2, 2, D, FF), D ** -0.5, 0.15625, ((0, 2), (2, 4), (3, 4)))
    shrink_weight = centred(keys[11], (2, FF, D), FF ** -0.5, 0.0625, ((0, 2), (1, 4), (2, 4)))
    adapter_input = centred(keys[12], (2, ADAPTERS, D, 5 * RANK), D ** -0.5, 0.15625, ((0, 2),))
    adapter_query = centred(keys[13], (2, ADAPTERS, RANK, HEADS * HEAD_DIM), (4 * RANK) ** -0.5, 0.75, ((0, 2), (3, 4)))
    adapter_keyvalue = centred(keys[14], (2, ADAPTERS, 2, RANK, KV_HEADS * HEAD_DIM), (4 * RANK) ** -0.5, 0.75, ((0, 2),))
    adapter_expand = centred(keys[15], (2, ADAPTERS, 2, RANK, FF), (4 * RANK) ** -0.5, 0.75, ((0, 2), (4, 4)))
    adapter_attend = centred(keys[16], (2, ADAPTERS, HEADS * HEAD_DIM, RANK), (HEADS * HEAD_DIM // 64) ** -0.5, 1.25, ((0, 2), (2, 4)))
    adapter_shrink = centred(keys[17], (2, ADAPTERS, FF, RANK), FF ** -0.5, 0.0625, ((0, 2), (2, 4)))
    adapter_residual = centred(keys[18], (2, ADAPTERS, 2, RANK, D), (4 * RANK) ** -0.5, 0.75, ((0, 2),))
    return dict(inputs=inputs, lengths=lengths, adapter_ids=adapter_ids, cotangent=cotangent, norm_gain=norm_gain, query_weight=query_weight, query_bias=query_bias, keyvalue_weight=keyvalue_weight, keyvalue_bias=keyvalue_bias, output_weight=output_weight, expand_weight=expand_weight, shrink_weight=shrink_weight, adapter_input=adapter_input, adapter_query=adapter_query, adapter_keyvalue=adapter_keyvalue, adapter_expand=adapter_expand, adapter_attend=adapter_attend, adapter_shrink=adapter_shrink, adapter_residual=adapter_residual)


HIGHEST = lax.Precision.HIGHEST
EPSILON = 1e-06
ROPE_BASE = 1000000.0
MASKED_SCORE = -1e+30

@jax.custom_vjp
def low(v):
    return lax.optimization_barrier(v.astype(jnp.bfloat16)).astype(jnp.float32)

@jax.custom_vjp
def low_back(v):
    return v

def low_keep(v):
    return (low(v), None)

def low_pass(kept, grad):
    return (grad,)

def back_keep(v):
    return (v, None)

def back_low(kept, grad):
    return (low(grad),)
low.defvjp(low_keep, low_pass)
low_back.defvjp(back_keep, back_low)

def exact_dot(left_side, right_side):
    return jnp.dot(left_side, right_side, precision=HIGHEST)

def rms_scale(values, gain_row):
    return values * lax.rsqrt(lax.optimization_barrier(jnp.mean(values * values, axis=-1, keepdims=True)) + EPSILON) * gain_row

def rotary_tables(seq_len, head_width):
    half_width = head_width // 2
    frequency = jnp.exp(-math.log(ROPE_BASE) * (2.0 * jnp.arange(half_width, dtype=jnp.float32) / head_width))
    angles = jnp.arange(seq_len, dtype=jnp.float32)[:, None] * frequency[None, :]
    return (jnp.cos(angles), jnp.sin(angles))

def rotate(tensor, cosine_table, sine_table):
    half_width = tensor.shape[-1] // 2
    front_half = tensor[..., :half_width]
    back_half = tensor[..., half_width:]
    cos_part = cosine_table[:, None, :]
    sin_part = sine_table[:, None, :]
    return jnp.concatenate([front_half * cos_part - back_half * sin_part, back_half * cos_part + front_half * sin_part], axis=-1)

def layer(inputs_f, frozen, adapter, length):
    norm_gains, query_weight, query_bias, keyvalue_weight, keyvalue_bias, output_weight, expand_weight, shrink_weight = frozen
    adapter_input, adapter_query, adapter_keyvalue, adapter_expand, adapter_attend, adapter_shrink, adapter_residual = adapter
    seq_len = inputs_f.shape[0]
    normed = low(rms_scale(inputs_f, norm_gains[0]))
    low_rank = exact_dot(normed, adapter_input[:, :3 * RANK])
    queries = low_back(exact_dot(normed, query_weight) + query_bias + exact_dot(low_rank[:, :RANK], adapter_query))
    key_proj = low_back(exact_dot(normed, keyvalue_weight[0]) + keyvalue_bias[0] + exact_dot(low_rank[:, RANK:2 * RANK], adapter_keyvalue[0]))
    value_proj = low_back(exact_dot(normed, keyvalue_weight[1]) + keyvalue_bias[1] + exact_dot(low_rank[:, 2 * RANK:], adapter_keyvalue[1]))
    cosine_table, sine_table = rotary_tables(seq_len, HEAD_DIM)
    query_rot = low(rotate(queries.reshape(seq_len, HEADS, HEAD_DIM), cosine_table, sine_table))
    key_rot = low(rotate(key_proj.reshape(seq_len, KV_HEADS, HEAD_DIM), cosine_table, sine_table))
    value_rot = low(value_proj.reshape(seq_len, KV_HEADS, HEAD_DIM))
    group_size = HEADS // KV_HEADS
    key_repeat = jnp.repeat(key_rot, group_size, axis=1)
    value_repeat = jnp.repeat(value_rot, group_size, axis=1)
    scores = low_back(jnp.einsum('qhd,khd->hqk', query_rot, key_repeat, precision=HIGHEST) * HEAD_DIM ** (-0.5))
    slot_ids = jnp.arange(seq_len)
    allowed = (slot_ids[None, :] <= slot_ids[:, None]) & (slot_ids[None, :] < length)
    soft_rounded = low(jax.nn.softmax(jnp.where(allowed[None], scores, MASKED_SCORE), axis=-1))
    attended = jnp.einsum('hqk,khd->qhd', soft_rounded, value_repeat, precision=HIGHEST).reshape(seq_len, HEADS * HEAD_DIM)
    attended = low(low_back(attended))
    branch = low_back(exact_dot(attended, output_weight) + exact_dot(exact_dot(attended, adapter_attend), adapter_residual[0]))
    middle = inputs_f + branch
    normed_two = low(rms_scale(middle, norm_gains[1]))
    expand_rank = exact_dot(normed_two, adapter_input[:, 3 * RANK:])
    gate_value = low_back(exact_dot(normed_two, expand_weight[0]) + exact_dot(expand_rank[:, :RANK], adapter_expand[0]))
    upward = low_back(exact_dot(normed_two, expand_weight[1]) + exact_dot(expand_rank[:, RANK:], adapter_expand[1]))
    activated = low(jax.nn.silu(gate_value) * upward)
    shrunk = low_back(exact_dot(activated, shrink_weight) + exact_dot(exact_dot(activated, adapter_shrink), adapter_residual[1]))
    return middle + shrunk

def reference(inputs, lengths, adapter_ids, cotangent, norm_gain, query_weight, query_bias, keyvalue_weight, keyvalue_bias, output_weight, expand_weight, shrink_weight, adapter_input, adapter_query, adapter_keyvalue, adapter_expand, adapter_attend, adapter_shrink, adapter_residual):
    frozen_all = (norm_gain, query_weight, query_bias, keyvalue_weight, keyvalue_bias, output_weight, expand_weight, shrink_weight)
    adapter_all = (adapter_input, adapter_query, adapter_keyvalue, adapter_expand, adapter_attend, adapter_shrink, adapter_residual)
    frozen_section = [tuple((stack[section_id].astype(jnp.float32) for stack in frozen_all)) for section_id in range(2)]
    adapter_section = [tuple((stack[section_id].astype(jnp.float32) for stack in adapter_all)) for section_id in range(2)]
    grad_scale = 1.0 / math.sqrt(TOKENS)

    def one_sequence(carry, item):
        rows_in, rows_cot, length, adapter_index = item

        def run_zero(rows, stacks):
            chosen = tuple((lax.dynamic_index_in_dim(stack, adapter_index, 0, keepdims=False) for stack in stacks))
            return layer(rows, frozen_section[0], chosen, length)

        def run_one(rows, stacks):
            chosen = tuple((lax.dynamic_index_in_dim(stack, adapter_index, 0, keepdims=False) for stack in stacks))
            return layer(rows, frozen_section[1], chosen, length)
        out_zero, back_zero = jax.vjp(run_zero, rows_in.astype(jnp.float32), adapter_section[0])
        rows_one = low(out_zero)
        out_one, back_one = jax.vjp(run_one, rows_one, adapter_section[1])
        valid = (jnp.arange(SLOTS) < length).astype(jnp.float32)[:, None]
        grad_one, adapters_one = back_one(rows_cot.astype(jnp.float32) * valid)
        grad_zero, adapters_zero = back_zero(grad_one)
        carry = (jax.tree.map(jnp.add, carry[0], adapters_zero), jax.tree.map(jnp.add, carry[1], adapters_one))
        return (carry, (out_zero.astype(jnp.bfloat16), out_one.astype(jnp.bfloat16), grad_zero, grad_one))
    start_sums = (tuple((jnp.zeros_like(stack) for stack in adapter_section[0])), tuple((jnp.zeros_like(stack) for stack in adapter_section[1])))
    sums, (outs_zero, outs_one, grads_zero, grads_one) = lax.scan(one_sequence, start_sums, (inputs, cotangent, lengths, adapter_ids))
    layer_output = jnp.stack([outs_zero, outs_one])
    input_grad = jnp.stack([grads_zero, grads_one])
    adapter_grads = tuple((jnp.stack([sums[0][slot], sums[1][slot]]) * grad_scale for slot in range(7)))
    return (layer_output, input_grad, adapter_grads[0], adapter_grads[1], adapter_grads[2], adapter_grads[3], adapter_grads[4], adapter_grads[5], adapter_grads[6])
```

```python
from functools import partial
import math

import jax
import jax.numpy as jnp
from jax import lax
from jax.experimental import pallas as pl
from jax.experimental.pallas import tpu as pltpu
from jax.sharding import PartitionSpec as P

KV_HEADS = 2
HEAD_DIM = 128
RANK = 16
EPSILON = 1e-06
ROPE_BASE = 1000000.0
MASKED_SCORE = -1e30
CHUNKS = 2
BF = jnp.bfloat16
F32 = jnp.float32


def dot(a, b):
    return jnp.dot(a, b, preferred_element_type=F32)


def dot_t(a, b):
    return lax.dot_general(a, b, (((1,), (1,)), ((), ())), preferred_element_type=F32)


def t_dot(a, b):
    return lax.dot_general(a, b, (((0,), (0,)), ((), ())), preferred_element_type=F32)


def rotary_tables(first_slot, rows):
    half = HEAD_DIM // 2
    frequency = jnp.exp(-math.log(ROPE_BASE) * (2.0 * jnp.arange(half, dtype=F32) / HEAD_DIM))
    slots = (first_slot + jnp.arange(rows, dtype=jnp.int32)).astype(F32)
    angles = slots[:, None] * frequency[None, :]
    return jnp.cos(angles)[:, None, :], jnp.sin(angles)[:, None, :]


def rotate(flat, tables, sign):
    cos, sin = tables
    x = flat.reshape(flat.shape[0], -1, HEAD_DIM)
    u, w = x[..., : HEAD_DIM // 2], x[..., HEAD_DIM // 2 :]
    sin = sin * sign
    return jnp.concatenate([u * cos - w * sin, w * cos + u * sin], axis=-1).reshape(flat.shape)


def norm_back(values, inverse, gain_row, grad_out):
    weighted = gain_row * grad_out
    return inverse * weighted - inverse * inverse * inverse * values * jnp.mean(
        weighted * values, axis=-1, keepdims=True
    )


def attend_kernel(scale, info_ref, q_ref, k_ref, v_ref, out_ref, log_ref):
    keys, rows = k_ref.shape[0], q_ref.shape[0]
    scores = dot_t(k_ref[...], q_ref[...]) * scale
    row = info_ref[0] + lax.broadcasted_iota(jnp.int32, (1, rows), 1)
    last = jnp.minimum(row, info_ref[1] - 1)
    key = lax.broadcasted_iota(jnp.int32, (keys, rows), 0)
    scores = jnp.where(key <= last, scores, MASKED_SCORE)
    peak = jnp.max(scores, axis=0, keepdims=True)
    soft = jnp.exp(scores - peak)
    total = jnp.sum(soft, axis=0, keepdims=True)
    soft = (soft * (1.0 / total)).astype(BF)
    out_ref[...] = t_dot(v_ref[...], soft).T.astype(BF)
    log_ref[0] = peak + jnp.log(total)


def attend(queries, keyvalue, info):
    rows, width = queries.shape
    keys = keyvalue.shape[0]
    heads = width // HEAD_DIM
    group = heads // KV_HEADS
    return pl.pallas_call(
        partial(attend_kernel, HEAD_DIM**-0.5),
        grid=(heads,),
        in_specs=[
            pl.BlockSpec(memory_space=pltpu.SMEM),
            pl.BlockSpec((rows, HEAD_DIM), lambda h: (0, h)),
            pl.BlockSpec((keys, HEAD_DIM), lambda h: (0, h // group)),
            pl.BlockSpec((keys, HEAD_DIM), lambda h: (0, KV_HEADS + h // group)),
        ],
        out_specs=[
            pl.BlockSpec((rows, HEAD_DIM), lambda h: (0, h)),
            pl.BlockSpec((1, 1, rows), lambda h: (h, 0, 0)),
        ],
        out_shape=[
            jax.ShapeDtypeStruct((rows, width), BF),
            jax.ShapeDtypeStruct((heads, 1, rows), F32),
        ],
        compiler_params=pltpu.CompilerParams(vmem_limit_bytes=32 * 2**20),
    )(info, queries, keyvalue, keyvalue)


def attend_back_kernel(scale, group, info_ref, q_ref, k_ref, v_ref, do_ref, log_ref, dq_ref, dk_ref, dv_ref):
    keys, rows = k_ref.shape[0], q_ref.shape[0]
    first = pl.program_id(0) % group == 0
    q, k, v, do = q_ref[...], k_ref[...], v_ref[...], do_ref[...]
    scores = dot_t(k, q) * scale - log_ref[0]
    row = info_ref[0] + lax.broadcasted_iota(jnp.int32, (1, rows), 1)
    last = jnp.minimum(row, info_ref[1] - 1)
    key = lax.broadcasted_iota(jnp.int32, (keys, rows), 0)
    soft = jnp.exp(jnp.where(key <= last, scores, MASKED_SCORE))
    soft_grad = dot_t(v, do)
    delta = jnp.sum(soft_grad * soft, axis=0, keepdims=True)
    score_grad = (soft * (soft_grad - delta)).astype(BF)
    dq_ref[...] = t_dot(k, score_grad).T * scale
    dk = dot(score_grad, q) * scale
    dv = dot(soft.astype(BF), do)

    @pl.when(first)
    def _():
        dk_ref[...] = dk
        dv_ref[...] = dv

    @pl.when(jnp.logical_not(first))
    def _():
        dk_ref[...] += dk
        dv_ref[...] += dv


def attend_back(queries, keyvalue, grad_out, logs, info):
    rows, width = queries.shape
    keys = keyvalue.shape[0]
    heads = width // HEAD_DIM
    group = heads // KV_HEADS
    return pl.pallas_call(
        partial(attend_back_kernel, HEAD_DIM**-0.5, group),
        grid=(heads,),
        in_specs=[
            pl.BlockSpec(memory_space=pltpu.SMEM),
            pl.BlockSpec((rows, HEAD_DIM), lambda h: (0, h)),
            pl.BlockSpec((keys, HEAD_DIM), lambda h: (0, h // group)),
            pl.BlockSpec((keys, HEAD_DIM), lambda h: (0, KV_HEADS + h // group)),
            pl.BlockSpec((rows, HEAD_DIM), lambda h: (0, h)),
            pl.BlockSpec((1, 1, rows), lambda h: (h, 0, 0)),
        ],
        out_specs=[
            pl.BlockSpec((rows, HEAD_DIM), lambda h: (0, h)),
            pl.BlockSpec((keys, HEAD_DIM), lambda h: (0, h // group)),
            pl.BlockSpec((keys, HEAD_DIM), lambda h: (0, h // group)),
        ],
        out_shape=[
            jax.ShapeDtypeStruct((rows, width), F32),
            jax.ShapeDtypeStruct((keys, KV_HEADS * HEAD_DIM), F32),
            jax.ShapeDtypeStruct((keys, KV_HEADS * HEAD_DIM), F32),
        ],
        compiler_params=pltpu.CompilerParams(vmem_limit_bytes=40 * 2**20),
    )(info, queries, keyvalue, keyvalue, grad_out, logs)


def spread(rows):
    return lax.all_gather(rows, "tensor", axis=0, tiled=True)


def fold(partial_rows):
    return lax.psum_scatter(
        partial_rows.astype(BF), "tensor", scatter_dimension=0, tiled=True
    ).astype(F32)


def row_chunks(x):
    step = x.shape[0] // CHUNKS
    return [x[i * step : (i + 1) * step] for i in range(CHUNKS)]


def forward(x, w, ad, info, tables):
    inverse_one = lax.rsqrt(jnp.mean(x * x, axis=-1, keepdims=True) + EPSILON)
    normed = (x * inverse_one * w["gain"][0]).astype(BF)
    low = dot(normed, ad["input"][:, : 3 * RANK]).astype(BF)
    kv_width = KV_HEADS * HEAD_DIM
    kv = dot(normed, w["kv"]) + w["kv_bias"]
    kv = kv + jnp.concatenate(
        [
            dot(low[:, RANK : 2 * RANK], ad["kv"][0]),
            dot(low[:, 2 * RANK :], ad["kv"][1]),
        ],
        axis=1,
    )
    kv = jnp.concatenate(
        [rotate(kv[:, :kv_width], tables, 1.0), kv[:, kv_width:]], axis=1
    ).astype(BF)
    kv_all = spread(kv)
    q = dot(normed, w["q"]) + w["q_bias"] + dot(low[:, :RANK], ad["q"])
    q = rotate(q, tables, 1.0).astype(BF)
    attended, logs = attend(q, kv_all, info)
    attend_rank = dot(attended, ad["attend"]).astype(BF)
    middle = x + dot_t(attended, w["out_t"]) + dot(attend_rank, ad["residual"][0])
    inverse_two = lax.rsqrt(jnp.mean(middle * middle, axis=-1, keepdims=True) + EPSILON)
    normed_two = (middle * inverse_two * w["gain"][1]).astype(BF)
    shrunk, saved = [], []
    for part in row_chunks(normed_two):
        n2 = spread(part)
        expand_rank = dot(n2, ad["input"][:, 3 * RANK :]).astype(BF)
        gate = dot(n2, w["gate"]) + dot(expand_rank[:, :RANK], ad["expand"][0])
        up = dot(n2, w["up"]) + dot(expand_rank[:, RANK:], ad["expand"][1])
        act = (jax.nn.silu(gate) * up).astype(BF)
        shrink_rank = dot(act, ad["shrink"]).astype(BF)
        shrunk.append(fold(dot_t(act, w["shrink_t"]) + dot(shrink_rank, ad["residual"][1])))
        saved.append((n2, expand_rank, gate.astype(BF), up.astype(BF), act, shrink_rank))
    y = middle + jnp.concatenate(shrunk, axis=0)
    kept = (x, inverse_one, normed, low, q, kv_all, attended, logs, attend_rank, middle, inverse_two, saved)
    return y, kept


def backward(dy, w, ad, kept, info, tables):
    (x, inverse_one, normed, low, q, kv_all, attended, logs, attend_rank, middle, inverse_two, saved) = kept
    width = x.shape[1]
    high = ad["input"][:, 3 * RANK :]
    folded, g_high, g_expand, g_shrink, g_res_two = [], 0, 0, 0, 0
    for part, (n2, expand_rank, gate, up, act, shrink_rank) in zip(row_chunks(dy.astype(BF)), saved):
        ds = spread(part)
        shrink_rank_grad = dot_t(ds, ad["residual"][1]).astype(BF)
        act_grad = dot(ds, w["shrink_t"]) + dot_t(shrink_rank_grad, ad["shrink"])
        gate, up = gate.astype(F32), up.astype(F32)
        sig = jax.nn.sigmoid(gate)
        gate_grad = (act_grad * up * sig * (1.0 + gate * (1.0 - sig))).astype(BF)
        up_grad = (act_grad * gate * sig).astype(BF)
        rank_grad = jnp.concatenate(
            [dot_t(gate_grad, ad["expand"][0]), dot_t(up_grad, ad["expand"][1])], axis=1
        ).astype(BF)
        folded.append(
            fold(dot_t(gate_grad, w["gate"]) + dot_t(up_grad, w["up"]) + dot_t(rank_grad, high))
        )
        g_high = g_high + t_dot(rank_grad, n2)
        g_expand = g_expand + jnp.concatenate(
            [t_dot(expand_rank[:, :RANK], gate_grad), t_dot(expand_rank[:, RANK:], up_grad)], axis=0
        )
        g_shrink = g_shrink + t_dot(shrink_rank_grad, act)
        g_res_two = g_res_two + t_dot(shrink_rank, ds)
    middle_grad = dy + norm_back(middle, inverse_two, w["gain"][1], jnp.concatenate(folded, axis=0))
    branch_grad = middle_grad.astype(BF)
    attend_rank_grad = dot_t(branch_grad, ad["residual"][0]).astype(BF)
    attended_grad = (dot(branch_grad, w["out_t"]) + dot_t(attend_rank_grad, ad["attend"])).astype(BF)
    g_attend = t_dot(attend_rank_grad, attended)
    g_res_one = t_dot(attend_rank, branch_grad)
    dq, dk, dv = attend_back(q, kv_all, attended_grad, logs, info)
    kv_width = KV_HEADS * HEAD_DIM
    dkv = fold(jnp.concatenate([dk, dv], axis=1))
    dq = rotate(dq, tables, -1.0).astype(BF)
    dkv = jnp.concatenate([rotate(dkv[:, :kv_width], tables, -1.0), dkv[:, kv_width:]], axis=1).astype(BF)
    low_grad = jnp.concatenate(
        [
            dot_t(dq, ad["q"]),
            dot_t(dkv[:, :kv_width], ad["kv"][0]),
            dot_t(dkv[:, kv_width:], ad["kv"][1]),
        ],
        axis=1,
    ).astype(BF)
    normed_grad = dot_t(dq, w["q"]) + dot_t(dkv, w["kv"]) + dot_t(low_grad, ad["input"][:, : 3 * RANK])
    dx = middle_grad + norm_back(x, inverse_one, w["gain"][0], normed_grad)
    g_q = t_dot(low[:, :RANK], dq)
    g_kv = jnp.concatenate(
        [
            t_dot(low[:, RANK : 2 * RANK], dkv[:, :kv_width]),
            t_dot(low[:, 2 * RANK :], dkv[:, kv_width:]),
        ],
        axis=1,
    )
    g_low = t_dot(low_grad, normed)
    pad = jnp.zeros((RANK, width - 2 * kv_width), F32)
    whole = jnp.concatenate(
        [g_low, g_high, g_res_one, g_res_two, g_q, g_attend, jnp.concatenate([g_kv, pad], axis=1)], axis=0
    ).astype(BF)
    parts = jnp.concatenate([g_expand, g_shrink], axis=0).astype(BF)
    return dx, whole, parts


def swap(pair):
    return lax.all_to_all(pair, "section", split_axis=0, concat_axis=0, tiled=True)


def local(
    inputs,
    lengths,
    adapter_ids,
    cotangent,
    norm_gain,
    query_weight,
    query_bias,
    keyvalue_weight,
    keyvalue_bias,
    output_weight,
    expand_weight,
    shrink_weight,
    adapter_input,
    adapter_query,
    adapter_keyvalue,
    adapter_expand,
    adapter_attend,
    adapter_shrink,
    adapter_residual,
):
    layers = lax.axis_size("section")
    tensor = lax.axis_size("tensor")
    core = lax.axis_index("section")
    place = lax.axis_index("tensor")
    rows, width = inputs.shape[1:]
    tokens = layers * rows * tensor * lax.axis_size("dp")

    kv = jnp.concatenate([keyvalue_weight[0, 0], keyvalue_weight[0, 1]], axis=1)
    kv_cols = kv.shape[1] // tensor
    kv = lax.dynamic_slice_in_dim(kv, place * kv_cols, kv_cols, 1)
    attn = jnp.concatenate([query_weight[0], output_weight[0].T, kv], axis=1)
    q_cols = query_weight.shape[2]
    halves = [
        swap(m.reshape(layers, m.shape[0] // layers, m.shape[1]))
        for m in (attn, expand_weight[0, 0], expand_weight[0, 1], shrink_weight[0].T)
    ]
    every = ("dp", "section")
    small = jnp.concatenate(
        [norm_gain[0, 0], norm_gain[0, 1], keyvalue_bias[0].reshape(-1)], axis=0
    )
    small = lax.all_gather(small, "section", axis=0)
    q_bias = lax.all_gather(query_bias[0], ("section", "tensor"), axis=0, tiled=True).reshape(layers, -1)

    def weights(layer):
        g = lax.all_gather(halves[0][layer], every + ("tensor",), axis=0)
        g = g.reshape(-1, tensor, g.shape[1], g.shape[2])
        g = jnp.swapaxes(g, 1, 2)

        def cut(start, size):
            return g[..., start : start + size].reshape(width, tensor * size)

        gain = small[layer, : 2 * width].reshape(2, width).astype(F32)
        return dict(
            gain=gain,
            q=cut(0, q_cols),
            out_t=cut(q_cols, q_cols),
            kv=cut(2 * q_cols, kv_cols),
            gate=lax.all_gather(halves[1][layer], every, axis=0, tiled=True),
            up=lax.all_gather(halves[2][layer], every, axis=0, tiled=True),
            shrink_t=lax.all_gather(halves[3][layer], every, axis=0, tiled=True),
            q_bias=q_bias[layer].astype(F32),
            kv_bias=small[layer, 2 * width :].astype(F32),
        )

    def pick(stack):
        chosen = jnp.stack(
            [lax.dynamic_index_in_dim(stack[0], adapter_ids[i], 0, keepdims=False) for i in range(layers)]
        )
        return swap(chosen)

    picked = [
        pick(stack)
        for stack in (
            adapter_input,
            adapter_query,
            adapter_keyvalue,
            adapter_expand,
            adapter_attend,
            adapter_shrink,
            adapter_residual,
        )
    ]
    query_all = lax.all_gather(picked[1], "tensor", axis=2, tiled=True)
    attend_all = lax.all_gather(picked[4], "tensor", axis=1, tiled=True)

    def adapters(layer):
        return dict(
            input=picked[0][layer],
            q=query_all[layer],
            kv=picked[2][layer],
            expand=picked[3][layer],
            attend=attend_all[layer],
            shrink=picked[5][layer],
            residual=picked[6][layer],
        )

    x = lax.dynamic_index_in_dim(inputs, core, 0, keepdims=False).astype(F32)
    cot = lax.dynamic_index_in_dim(cotangent, core, 0, keepdims=False).astype(F32)
    length = lax.dynamic_index_in_dim(lengths, core, 0, keepdims=False)
    first_slot = place * rows
    info = jnp.stack([first_slot, length]).astype(jnp.int32)
    tables = rotary_tables(first_slot, rows)
    slot_ids = first_slot + jnp.arange(rows, dtype=jnp.int32)

    w = [weights(layer) for layer in range(layers)]
    ad = [adapters(layer) for layer in range(layers)]
    outs, kept = [], []
    for layer in range(layers):
        y, saved = forward(x, w[layer], ad[layer], info, tables)
        outs.append(y.astype(BF))
        kept.append(saved)
        x = outs[-1].astype(F32)
    grad = cot * (slot_ids < length).astype(F32)[:, None]
    grads, wholes, parts = [None] * layers, [None] * layers, [None] * layers
    for layer in reversed(range(layers)):
        grad, wholes[layer], parts[layer] = backward(grad, w[layer], ad[layer], kept[layer], info, tables)
        grads[layer] = grad
    layer_output = swap(jnp.stack(outs))
    input_grad = swap(jnp.stack(grads))

    whole = lax.psum(swap(jnp.stack(wholes)), "tensor")
    part = swap(jnp.stack(parts))
    own = 7 * RANK
    q_rows = lax.dynamic_slice_in_dim(whole[:, own : own + 2 * RANK], place * q_cols, q_cols, 2)
    rest = jnp.concatenate([whole[:, :own], whole[:, own + 2 * RANK :]], axis=1)
    rest, q_rows, part, ids = (
        lax.all_gather(a, "dp", axis=0, tiled=True) for a in (rest, q_rows, part, adapter_ids)
    )
    count = adapter_input.shape[1]
    pick_matrix = (jnp.arange(count, dtype=jnp.int32)[:, None] == ids[None, :]).astype(BF)
    scale = 1.0 / math.sqrt(tokens)

    def by_adapter(a):
        return jnp.einsum("as,srw->arw", pick_matrix, a, preferred_element_type=F32) * scale

    rest, q_rows, part = by_adapter(rest), by_adapter(q_rows), by_adapter(part)
    r = RANK
    kv_width = KV_HEADS * HEAD_DIM
    return (
        layer_output[None],
        input_grad[None],
        jnp.swapaxes(rest[:, : 5 * r], 1, 2)[None],
        q_rows[:, :r][None],
        jnp.stack([rest[:, 7 * r :, :kv_width], rest[:, 7 * r :, kv_width : 2 * kv_width]], axis=1)[None],
        jnp.stack([part[:, :r], part[:, r : 2 * r]], axis=1)[None],
        jnp.swapaxes(q_rows[:, r:], 1, 2)[None],
        jnp.swapaxes(part[:, 2 * r :], 1, 2)[None],
        jnp.stack([rest[:, 5 * r : 6 * r], rest[:, 6 * r : 7 * r]], axis=1)[None],
    )


def solution(mesh):
    placed = (
        P("dp", "tensor", None),
        P("dp"),
        P("dp"),
        P("dp", "tensor", None),
        P("section", None, None),
        P("section", "dp", "tensor"),
        P("section", "tensor"),
        P("section", None, "dp", None),
        P("section", None, None),
        P("section", "tensor", "dp"),
        P("section", None, "dp", "tensor"),
        P("section", "tensor", "dp"),
        P("section", None, None, None),
        P("section", None, None, "tensor"),
        P("section", None, None, None, None),
        P("section", None, None, None, "tensor"),
        P("section", None, "tensor", None),
        P("section", None, "tensor", None),
        P("section", None, None, None, None),
    )
    return jax.shard_map(
        local,
        mesh=mesh,
        in_specs=placed,
        out_specs=(
            P("section", "dp", "tensor", None),
            P("section", "dp", "tensor", None),
            P("section", None, None, None),
            P("section", None, None, "tensor"),
            P("section", None, None, None, None),
            P("section", None, None, None, "tensor"),
            P("section", None, "tensor", None),
            P("section", None, "tensor", None),
            P("section", None, None, None, None),
        ),
        check_vma=False,
    )
```

```python
from functools import partial
import math

import jax
import jax.numpy as jnp
from jax import lax
from jax.experimental import pallas as pl
from jax.experimental.pallas import tpu as pltpu
from jax.sharding import PartitionSpec as P

KV_HEADS = 2
HEAD_DIM = 128
RANK = 16
EPSILON = 1e-06
ROPE_BASE = 1000000.0
MASKED_SCORE = -1e30
CHUNKS = 4
LANES = 128
VMEM_LIMIT = 60 * 2**20
MESH = pl.DeviceIdType.MESH
BF = jnp.bfloat16
F32 = jnp.float32


def dot(a, b):
    return jnp.dot(a, b, preferred_element_type=F32)


def dot_t(a, b):
    return lax.dot_general(a, b, (((1,), (1,)), ((), ())), preferred_element_type=F32)


def t_dot(a, b):
    return lax.dot_general(a, b, (((0,), (0,)), ((), ())), preferred_element_type=F32)


def rotary_tables(first_slot, rows):
    half = HEAD_DIM // 2
    frequency = jnp.exp(-math.log(ROPE_BASE) * (2.0 * jnp.arange(half, dtype=F32) / HEAD_DIM))
    slots = (first_slot + jnp.arange(rows, dtype=jnp.int32)).astype(F32)
    angles = slots[:, None] * frequency[None, :]
    return jnp.cos(angles)[:, None, :], jnp.sin(angles)[:, None, :]


def rotate(flat, tables, sign):
    cos, sin = tables
    x = flat.reshape(flat.shape[0], -1, HEAD_DIM)
    u, w = x[..., : HEAD_DIM // 2], x[..., HEAD_DIM // 2 :]
    sin = sin * sign
    return jnp.concatenate([u * cos - w * sin, w * cos + u * sin], axis=-1).reshape(flat.shape)


def norm_back(values, inverse, gain_row, grad_out):
    weighted = gain_row * grad_out
    return inverse * weighted - inverse * inverse * inverse * values * jnp.mean(
        weighted * values, axis=-1, keepdims=True
    )


def attend_kernel(scale, info_ref, q_ref, k_ref, v_ref, out_ref, log_ref):
    keys, rows = k_ref.shape[0], q_ref.shape[0]
    scores = dot_t(k_ref[...], q_ref[...]) * scale
    row = info_ref[0] + lax.broadcasted_iota(jnp.int32, (1, rows), 1)
    last = jnp.minimum(row, info_ref[1] - 1)
    key = lax.broadcasted_iota(jnp.int32, (keys, rows), 0)
    scores = jnp.where(key <= last, scores, MASKED_SCORE)
    peak = jnp.max(scores, axis=0, keepdims=True)
    soft = jnp.exp(scores - peak)
    total = jnp.sum(soft, axis=0, keepdims=True)
    soft = (soft * (1.0 / total)).astype(BF)
    out_ref[...] = t_dot(v_ref[...], soft).T.astype(BF)
    log_ref[0] = peak + jnp.log(total)


def attend(queries, keyvalue, info):
    rows, width = queries.shape
    keys = keyvalue.shape[0]
    heads = width // HEAD_DIM
    group = heads // KV_HEADS
    return pl.pallas_call(
        partial(attend_kernel, HEAD_DIM**-0.5),
        grid=(heads,),
        in_specs=[
            pl.BlockSpec(memory_space=pltpu.SMEM),
            pl.BlockSpec((rows, HEAD_DIM), lambda h: (0, h)),
            pl.BlockSpec((keys, HEAD_DIM), lambda h: (0, h // group)),
            pl.BlockSpec((keys, HEAD_DIM), lambda h: (0, KV_HEADS + h // group)),
        ],
        out_specs=[
            pl.BlockSpec((rows, HEAD_DIM), lambda h: (0, h)),
            pl.BlockSpec((1, 1, rows), lambda h: (h, 0, 0)),
        ],
        out_shape=[
            jax.ShapeDtypeStruct((rows, width), BF),
            jax.ShapeDtypeStruct((heads, 1, rows), F32),
        ],
        compiler_params=pltpu.CompilerParams(vmem_limit_bytes=32 * 2**20),
    )(info, queries, keyvalue, keyvalue)


def attend_back_kernel(scale, group, info_ref, q_ref, k_ref, v_ref, do_ref, log_ref, dq_ref, dk_ref, dv_ref):
    keys, rows = k_ref.shape[0], q_ref.shape[0]
    first = pl.program_id(0) % group == 0
    q, k, v, do = q_ref[...], k_ref[...], v_ref[...], do_ref[...]
    scores = dot_t(k, q) * scale - log_ref[0]
    row = info_ref[0] + lax.broadcasted_iota(jnp.int32, (1, rows), 1)
    last = jnp.minimum(row, info_ref[1] - 1)
    key = lax.broadcasted_iota(jnp.int32, (keys, rows), 0)
    soft = jnp.exp(jnp.where(key <= last, scores, MASKED_SCORE))
    soft_grad = dot_t(v, do)
    delta = jnp.sum(soft_grad * soft, axis=0, keepdims=True)
    score_grad = (soft * (soft_grad - delta)).astype(BF)
    dq_ref[...] = t_dot(k, score_grad).T * scale
    dk = dot(score_grad, q) * scale
    dv = dot(soft.astype(BF), do)

    @pl.when(first)
    def _():
        dk_ref[...] = dk
        dv_ref[...] = dv

    @pl.when(jnp.logical_not(first))
    def _():
        dk_ref[...] += dk
        dv_ref[...] += dv


def attend_back(queries, keyvalue, grad_out, logs, info):
    rows, width = queries.shape
    keys = keyvalue.shape[0]
    heads = width // HEAD_DIM
    group = heads // KV_HEADS
    return pl.pallas_call(
        partial(attend_back_kernel, HEAD_DIM**-0.5, group),
        grid=(heads,),
        in_specs=[
            pl.BlockSpec(memory_space=pltpu.SMEM),
            pl.BlockSpec((rows, HEAD_DIM), lambda h: (0, h)),
            pl.BlockSpec((keys, HEAD_DIM), lambda h: (0, h // group)),
            pl.BlockSpec((keys, HEAD_DIM), lambda h: (0, KV_HEADS + h // group)),
            pl.BlockSpec((rows, HEAD_DIM), lambda h: (0, h)),
            pl.BlockSpec((1, 1, rows), lambda h: (h, 0, 0)),
        ],
        out_specs=[
            pl.BlockSpec((rows, HEAD_DIM), lambda h: (0, h)),
            pl.BlockSpec((keys, HEAD_DIM), lambda h: (0, h // group)),
            pl.BlockSpec((keys, HEAD_DIM), lambda h: (0, h // group)),
        ],
        out_shape=[
            jax.ShapeDtypeStruct((rows, width), F32),
            jax.ShapeDtypeStruct((keys, KV_HEADS * HEAD_DIM), F32),
            jax.ShapeDtypeStruct((keys, KV_HEADS * HEAD_DIM), F32),
        ],
        compiler_params=pltpu.CompilerParams(vmem_limit_bytes=40 * 2**20),
    )(info, queries, keyvalue, keyvalue, grad_out, logs)


def vspec():
    return pl.BlockSpec(memory_space=pltpu.VMEM)


def hspec():
    return pl.BlockSpec(memory_space=pl.ANY)


def line_barrier(me, line):
    barrier = pltpu.get_barrier_semaphore()

    @pl.when(me > 0)
    def _():
        pl.semaphore_signal(barrier, inc=1, device_id={"tensor": me - 1}, device_id_type=MESH)

    @pl.when(me < line - 1)
    def _():
        pl.semaphore_signal(barrier, inc=1, device_id={"tensor": me + 1}, device_id_type=MESH)

    pl.semaphore_wait(barrier, jnp.where(me > 0, 1, 0) + jnp.where(me < line - 1, 1, 0))


def within(c, chunks):
    return jnp.logical_and(c >= 0, c < chunks)


def line_exchange(line, chunks, gathered, partial_ref, from_left, from_right, own_out, sems, begin, work):
    ag_recv, ag_right, ag_left, r_recv, r_send, l_recv, l_send = sems
    me = lax.axis_index("tensor")

    def copy(ref, src, c, o, send, recv, side):
        return pltpu.make_async_remote_copy(
            src_ref=src.at[c, o],
            dst_ref=ref.at[c, o],
            send_sem=send.at[c, o],
            recv_sem=recv.at[c, o],
            device_id={"tensor": me + side},
            device_id_type=MESH,
        )

    def ag(c, o, side):
        return copy(gathered, gathered, c, o, ag_right if side > 0 else ag_left, ag_recv, side)

    def rs(c, o, side):
        if side > 0:
            return copy(from_left, partial_ref, c, o, r_send, r_recv, 1)
        return copy(from_right, partial_ref, c, o, l_send, l_recv, -1)

    has_left, has_right = me > 0, me < line - 1

    def step(s, carry):
        first = s + line - 1

        @pl.when(jnp.logical_and(within(first, chunks), has_right))
        def _():
            ag(first, me, 1).start()

        @pl.when(jnp.logical_and(within(first, chunks), has_left))
        def _():
            ag(first, me, -1).start()

        for d in range(1, line):
            c = s + line - 1 - d

            @pl.when(jnp.logical_and(within(c, chunks), me - d >= 0))
            def _():
                ag(c, me - d, 1).wait_recv()

                @pl.when(has_right)
                def _():
                    ag(c, me - d, 1).start()

            @pl.when(jnp.logical_and(within(c, chunks), me + d < line))
            def _():
                ag(c, me + d, -1).wait_recv()

                @pl.when(has_left)
                def _():
                    ag(c, me + d, -1).start()

        @pl.when(within(s, chunks))
        def _():
            work(s)

        for h in range(line):
            c = s - h

            @pl.when(jnp.logical_and(within(c, chunks), me == h))
            def _():
                for j in range(h + 1, line):
                    if h > 0:
                        rs(c, j, 1).wait_recv()
                        partial_ref[c, j] = (
                            partial_ref[c, j].astype(F32) + from_left[c, j].astype(F32)
                        ).astype(BF)
                    if h < line - 1:
                        rs(c, j, 1).start()

            @pl.when(jnp.logical_and(within(c, chunks), me == line - 1 - h))
            def _():
                for j in range(line - 1 - h):
                    if h > 0:
                        rs(c, j, -1).wait_recv()
                        partial_ref[c, j] = (
                            partial_ref[c, j].astype(F32) + from_right[c, j].astype(F32)
                        ).astype(BF)
                    if h < line - 1:
                        rs(c, j, -1).start()

        last = s - (line - 1)

        @pl.when(within(last, chunks))
        def _():
            own_out[last] = partial_ref[last, me].astype(F32)

            @pl.when(has_left)
            def _():
                rs(last, me, 1).wait_recv()
                own_out[last] += from_left[last, me].astype(F32)

            @pl.when(has_right)
            def _():
                rs(last, me, -1).wait_recv()
                own_out[last] += from_right[last, me].astype(F32)

        return carry

    line_barrier(me, line)
    begin()
    lax.fori_loop(-(line - 1), chunks + line - 1, step, 0)

    def drain(c, carry):
        for o in range(line):

            @pl.when(jnp.logical_and(has_right, me >= o))
            def _():
                ag(c, o, 1).wait_send()

            @pl.when(jnp.logical_and(has_left, me <= o))
            def _():
                ag(c, o, -1).wait_send()

            @pl.when(me < o)
            def _():
                rs(c, o, 1).wait_send()

            @pl.when(me > o)
            def _():
                rs(c, o, -1).wait_send()

        return carry

    lax.fori_loop(0, chunks, drain, 0)


def exchange_scratch(line, chunks, rows, width):
    slots = (chunks, line, rows, width)
    return [pltpu.VMEM(slots, BF)] * 4 + [pltpu.SemaphoreType.DMA((chunks, line))] * 7


def mlp_kernel(
    line, chunks, tile,
    n2_ref, gate_hbm, up_hbm, shrink_hbm, high_ref, expand_ref, ash_ref, res_ref,
    out_ref, n2_out, gate_out, up_out,
    gathered, partial_ref, from_left, from_right, s0, s1, s2, s3, s4, s5, s6,
    wg, wu, ws, gate_st, up_st, acc, wsem, osem, nsem,
):
    rows, width = n2_ref.shape[1:]
    every = line * rows
    tiles = wg.shape[1] // tile
    me = lax.axis_index("tensor")
    loads = [
        pltpu.make_async_copy(a, b, wsem.at[i])
        for i, (a, b) in enumerate(((gate_hbm, wg), (up_hbm, wu), (shrink_hbm, ws)))
    ]

    def begin():
        for load in loads:
            load.start()
        for c in range(chunks):
            gathered[c, me] = n2_ref[c]

    def saves(c, slot):
        return (
            pltpu.make_async_copy(gate_st.at[slot], gate_out.at[c], osem.at[0, slot]),
            pltpu.make_async_copy(up_st.at[slot], up_out.at[c], osem.at[1, slot]),
        )

    def keep(c):
        return pltpu.make_async_copy(gathered.at[c], n2_out.at[c], nsem.at[c])

    def work(c):
        slot = c % 2

        @pl.when(c == 0)
        def _():
            for load in loads:
                load.wait()

        @pl.when(c >= 2)
        def _():
            for save in saves(c - 2, slot):
                save.wait()

        keep(c).start()
        x = gathered[c].reshape(every, width)
        er = dot(x, high_ref[...]).astype(BF)

        def one(f, rank):
            cols = pl.ds(pl.multiple_of(f * tile, tile), tile)
            gate = dot(x, wg[:, cols]) + dot(er, expand_ref[0, :, cols])
            up = dot(x, wu[:, cols]) + dot(er, expand_ref[1, :, cols])
            gate_st[slot, :, cols] = gate.astype(BF)
            up_st[slot, :, cols] = up.astype(BF)
            act = (gate * (1.0 / (1.0 + jnp.exp(-gate))) * up).astype(BF)
            now = dot_t(act, ws[:, cols])

            @pl.when(f == 0)
            def _():
                acc[...] = now

            @pl.when(f > 0)
            def _():
                acc[...] += now

            return rank + dot_t(act, ash_ref[:, cols])

        rank = lax.fori_loop(0, tiles, one, jnp.zeros((every, ash_ref.shape[0]), F32))
        total = acc[...] + dot(rank.astype(BF), res_ref[...])
        partial_ref[c] = total.astype(BF).reshape(line, rows, width)
        for save in saves(c, slot):
            save.start()

    line_exchange(
        line, chunks, gathered, partial_ref, from_left, from_right, out_ref,
        (s0, s1, s2, s3, s4, s5, s6), begin, work,
    )
    for c in range(chunks):
        keep(c).wait()
    for c in range(max(chunks - 2, 0), chunks):
        for save in saves(c, c % 2):
            save.wait()


def ff_tile(hidden):
    return hidden // 3 if hidden % (3 * LANES) == 0 else LANES


def mlp_forward(n2, w, ad):
    line = lax.axis_size("tensor")
    rows, width = n2.shape
    hidden = w["gate"].shape[1]
    part = rows // CHUNKS
    every = line * part
    out, n2_all, gate, up = pl.pallas_call(
        partial(mlp_kernel, line, CHUNKS, ff_tile(hidden)),
        in_specs=[vspec()] + [hspec()] * 3 + [vspec()] * 4,
        out_specs=[vspec()] + [hspec()] * 3,
        out_shape=[
            jax.ShapeDtypeStruct((CHUNKS, part, width), F32),
            jax.ShapeDtypeStruct((CHUNKS, line, part, width), BF),
            jax.ShapeDtypeStruct((CHUNKS, every, hidden), BF),
            jax.ShapeDtypeStruct((CHUNKS, every, hidden), BF),
        ],
        scratch_shapes=exchange_scratch(line, CHUNKS, part, width)
        + [pltpu.VMEM((width, hidden), BF)] * 3
        + [pltpu.VMEM((2, every, hidden), BF)] * 2
        + [
            pltpu.VMEM((every, width), F32),
            pltpu.SemaphoreType.DMA((3,)),
            pltpu.SemaphoreType.DMA((2, 2)),
            pltpu.SemaphoreType.DMA((CHUNKS,)),
        ],
        compiler_params=pltpu.CompilerParams(
            collective_id=0, has_side_effects=True, vmem_limit_bytes=VMEM_LIMIT
        ),
        cost_estimate=pl.CostEstimate(
            flops=6 * line * rows * width * hidden,
            bytes_accessed=6 * width * hidden + 4 * line * rows * hidden,
            transcendentals=line * rows * hidden,
        ),
    )(
        n2.reshape(CHUNKS, part, width), w["gate"], w["up"], w["shrink_t"],
        ad["high"], ad["expand"], ad["shrink"], ad["residual"][1],
    )
    return out.reshape(rows, width), (n2_all.reshape(CHUNKS, every, width), gate, up)


def mlp_back_kernel(
    line, chunks, tile,
    ds_ref, gate_hbm, up_hbm, shrink_hbm, n2_hbm, gate_in, up_in, high_ref, expand_ref, ash_ref, res_ref,
    out_ref, ghigh_ref, gexp_ref, gsh_ref, gres_ref,
    gathered, partial_ref, from_left, from_right, s0, s1, s2, s3, s4, s5, s6,
    wg, wu, ws, gate_st, up_st, n2_st, acc, wsem, isem,
):
    rows, width = ds_ref.shape[1:]
    every = line * rows
    tiles = wg.shape[1] // tile
    me = lax.axis_index("tensor")
    loads = [
        pltpu.make_async_copy(a, b, wsem.at[i])
        for i, (a, b) in enumerate(((shrink_hbm, ws), (gate_hbm, wg), (up_hbm, wu)))
    ]

    def fetch(c):
        slot = c % 2
        return (
            pltpu.make_async_copy(gate_in.at[c], gate_st.at[slot], isem.at[0, slot]),
            pltpu.make_async_copy(up_in.at[c], up_st.at[slot], isem.at[1, slot]),
            pltpu.make_async_copy(n2_hbm.at[c], n2_st.at[slot], isem.at[2, slot]),
        )

    def begin():
        for load in loads:
            load.start()
        for one in fetch(0):
            one.start()
        for c in range(chunks):
            gathered[c, me] = ds_ref[c]
        for ref in (ghigh_ref, gexp_ref, gsh_ref, gres_ref):
            ref[...] = jnp.zeros_like(ref)

    def work(c):
        slot = c % 2

        @pl.when(c == 0)
        def _():
            for load in loads:
                load.wait()

        for one in fetch(c):
            one.wait()

        @pl.when(c + 1 < chunks)
        def _():
            for one in fetch(c + 1):
                one.start()

        ds = gathered[c].reshape(every, width)
        n2 = n2_st[slot]
        er = dot(n2, high_ref[...]).astype(BF)
        rank_in = dot_t(ds, res_ref[...]).astype(BF)

        def one(f, carry):
            rank_out, srank = carry
            cols = pl.ds(pl.multiple_of(f * tile, tile), tile)
            act_grad = dot(ds, ws[:, cols]) + dot(rank_in, ash_ref[:, cols])
            gate = gate_st[slot, :, cols].astype(F32)
            up = up_st[slot, :, cols].astype(F32)
            sig = 1.0 / (1.0 + jnp.exp(-gate))
            silu = gate * sig
            act = (silu * up).astype(BF)
            gate_grad = (act_grad * up * (sig + silu * (1.0 - sig))).astype(BF)
            up_grad = (act_grad * silu).astype(BF)
            now = dot_t(gate_grad, wg[:, cols]) + dot_t(up_grad, wu[:, cols])

            @pl.when(f == 0)
            def _():
                acc[...] = now

            @pl.when(f > 0)
            def _():
                acc[...] += now

            gexp_ref[0, :, cols] += t_dot(er, gate_grad)
            gexp_ref[1, :, cols] += t_dot(er, up_grad)
            gsh_ref[:, cols] += t_dot(rank_in, act)
            rank_out = rank_out + dot_t(gate_grad, expand_ref[0, :, cols])
            rank_out = rank_out + dot_t(up_grad, expand_ref[1, :, cols])
            return rank_out, srank + dot_t(act, ash_ref[:, cols])

        rank_out, srank = lax.fori_loop(
            0,
            tiles,
            one,
            (
                jnp.zeros((every, expand_ref.shape[1]), F32),
                jnp.zeros((every, ash_ref.shape[0]), F32),
            ),
        )
        rank_out = rank_out.astype(BF)
        total = acc[...] + dot_t(rank_out, high_ref[...])
        partial_ref[c] = total.astype(BF).reshape(line, rows, width)
        ghigh_ref[...] += t_dot(rank_out, n2)
        gres_ref[...] += t_dot(srank.astype(BF), ds)

    line_exchange(
        line, chunks, gathered, partial_ref, from_left, from_right, out_ref,
        (s0, s1, s2, s3, s4, s5, s6), begin, work,
    )


def mlp_backward(ds, w, ad, saved):
    n2_all, gate, up = saved
    line = lax.axis_size("tensor")
    rows, width = ds.shape
    hidden = w["gate"].shape[1]
    part = rows // CHUNKS
    every = line * part
    out, g_high, g_expand, g_shrink, g_res = pl.pallas_call(
        partial(mlp_back_kernel, line, CHUNKS, ff_tile(hidden)),
        in_specs=[vspec()] + [hspec()] * 6 + [vspec()] * 4,
        out_specs=[vspec()] * 5,
        out_shape=[
            jax.ShapeDtypeStruct((CHUNKS, part, width), F32),
            jax.ShapeDtypeStruct((2 * RANK, width), F32),
            jax.ShapeDtypeStruct((2, 2 * RANK, hidden), F32),
            jax.ShapeDtypeStruct((RANK, hidden), F32),
            jax.ShapeDtypeStruct((RANK, width), F32),
        ],
        scratch_shapes=exchange_scratch(line, CHUNKS, part, width)
        + [pltpu.VMEM((width, hidden), BF)] * 3
        + [pltpu.VMEM((2, every, hidden), BF)] * 2
        + [
            pltpu.VMEM((2, every, width), BF),
            pltpu.VMEM((every, width), F32),
            pltpu.SemaphoreType.DMA((3,)),
            pltpu.SemaphoreType.DMA((3, 2)),
        ],
        compiler_params=pltpu.CompilerParams(
            collective_id=1, has_side_effects=True, vmem_limit_bytes=VMEM_LIMIT
        ),
        cost_estimate=pl.CostEstimate(
            flops=6 * line * rows * width * hidden,
            bytes_accessed=6 * width * hidden + 4 * line * rows * hidden,
            transcendentals=line * rows * hidden,
        ),
    )(
        ds.reshape(CHUNKS, part, width), w["gate"], w["up"], w["shrink_t"], n2_all, gate, up,
        ad["high"], ad["expand"], ad["shrink"], ad["residual"][1],
    )
    g_expand = jnp.concatenate([g_expand[0, :RANK], g_expand[1, RANK:]], axis=0)
    return out.reshape(rows, width), g_high, g_expand, g_shrink, g_res


def spread(rows):
    return lax.all_gather(rows, "tensor", axis=0, tiled=True)


def fold(partial_rows):
    return lax.psum_scatter(
        partial_rows.astype(BF), "tensor", scatter_dimension=0, tiled=True
    ).astype(F32)


def forward(x, w, ad, info, tables):
    inverse_one = lax.rsqrt(jnp.mean(x * x, axis=-1, keepdims=True) + EPSILON)
    normed = (x * inverse_one * w["gain"][0]).astype(BF)
    low = dot(normed, ad["input"][:, : 3 * RANK]).astype(BF)
    kv_width = KV_HEADS * HEAD_DIM
    kv = dot(normed, w["kv"]) + w["kv_bias"]
    kv = kv + jnp.concatenate(
        [
            dot(low[:, RANK : 2 * RANK], ad["kv"][0]),
            dot(low[:, 2 * RANK :], ad["kv"][1]),
        ],
        axis=1,
    )
    kv = jnp.concatenate(
        [rotate(kv[:, :kv_width], tables, 1.0), kv[:, kv_width:]], axis=1
    ).astype(BF)
    kv_all = spread(kv)
    q = dot(normed, w["q"]) + w["q_bias"] + dot(low[:, :RANK], ad["q"])
    q = rotate(q, tables, 1.0).astype(BF)
    attended, logs = attend(q, kv_all, info)
    attend_rank = dot(attended, ad["attend"]).astype(BF)
    middle = x + dot_t(attended, w["out_t"]) + dot(attend_rank, ad["residual"][0])
    inverse_two = lax.rsqrt(jnp.mean(middle * middle, axis=-1, keepdims=True) + EPSILON)
    normed_two = (middle * inverse_two * w["gain"][1]).astype(BF)
    shrunk, saved = mlp_forward(normed_two, w, ad)
    y = middle + shrunk
    kept = (x, inverse_one, normed, low, q, kv_all, attended, logs, attend_rank, middle, inverse_two, saved)
    return y, kept


def backward(dy, w, ad, kept, info, tables):
    (x, inverse_one, normed, low, q, kv_all, attended, logs, attend_rank, middle, inverse_two, saved) = kept
    width = x.shape[1]
    normed_two_grad, g_high, g_expand, g_shrink, g_res_two = mlp_backward(dy.astype(BF), w, ad, saved)
    middle_grad = dy + norm_back(middle, inverse_two, w["gain"][1], normed_two_grad)
    branch_grad = middle_grad.astype(BF)
    attend_rank_grad = dot_t(branch_grad, ad["residual"][0]).astype(BF)
    attended_grad = (dot(branch_grad, w["out_t"]) + dot_t(attend_rank_grad, ad["attend"])).astype(BF)
    g_attend = t_dot(attend_rank_grad, attended)
    g_res_one = t_dot(attend_rank, branch_grad)
    dq, dk, dv = attend_back(q, kv_all, attended_grad, logs, info)
    kv_width = KV_HEADS * HEAD_DIM
    dkv = fold(jnp.concatenate([dk, dv], axis=1))
    dq = rotate(dq, tables, -1.0).astype(BF)
    dkv = jnp.concatenate([rotate(dkv[:, :kv_width], tables, -1.0), dkv[:, kv_width:]], axis=1).astype(BF)
    low_grad = jnp.concatenate(
        [
            dot_t(dq, ad["q"]),
            dot_t(dkv[:, :kv_width], ad["kv"][0]),
            dot_t(dkv[:, kv_width:], ad["kv"][1]),
        ],
        axis=1,
    ).astype(BF)
    normed_grad = dot_t(dq, w["q"]) + dot_t(dkv, w["kv"]) + dot_t(low_grad, ad["input"][:, : 3 * RANK])
    dx = middle_grad + norm_back(x, inverse_one, w["gain"][0], normed_grad)
    g_q = t_dot(low[:, :RANK], dq)
    g_kv = jnp.concatenate(
        [
            t_dot(low[:, RANK : 2 * RANK], dkv[:, :kv_width]),
            t_dot(low[:, 2 * RANK :], dkv[:, kv_width:]),
        ],
        axis=1,
    )
    g_low = t_dot(low_grad, normed)
    pad = jnp.zeros((RANK, width - 2 * kv_width), F32)
    whole = jnp.concatenate(
        [g_low, g_high, g_res_one, g_res_two, g_q, g_attend, jnp.concatenate([g_kv, pad], axis=1)], axis=0
    ).astype(BF)
    parts = jnp.concatenate([g_expand, g_shrink], axis=0).astype(BF)
    return dx, whole, parts


def swap(pair):
    return lax.all_to_all(pair, "section", split_axis=0, concat_axis=0, tiled=True)


def local(
    inputs,
    lengths,
    adapter_ids,
    cotangent,
    norm_gain,
    query_weight,
    query_bias,
    keyvalue_weight,
    keyvalue_bias,
    output_weight,
    expand_weight,
    shrink_weight,
    adapter_input,
    adapter_query,
    adapter_keyvalue,
    adapter_expand,
    adapter_attend,
    adapter_shrink,
    adapter_residual,
):
    layers = lax.axis_size("section")
    tensor = lax.axis_size("tensor")
    core = lax.axis_index("section")
    place = lax.axis_index("tensor")
    rows, width = inputs.shape[1:]
    tokens = layers * rows * tensor * lax.axis_size("dp")

    kv = jnp.concatenate([keyvalue_weight[0, 0], keyvalue_weight[0, 1]], axis=1)
    kv_cols = kv.shape[1] // tensor
    kv = lax.dynamic_slice_in_dim(kv, place * kv_cols, kv_cols, 1)
    attn = jnp.concatenate([query_weight[0], output_weight[0].T, kv], axis=1)
    q_cols = query_weight.shape[2]
    hidden = expand_weight.shape[3]
    padding = -hidden % (2 * LANES)

    def padded(m):
        return jnp.pad(m, [(0, 0)] * (m.ndim - 1) + [(0, padding)])

    halves = [
        swap(m.reshape(layers, m.shape[0] // layers, m.shape[1]))
        for m in (attn, *(padded(m) for m in (expand_weight[0, 0], expand_weight[0, 1], shrink_weight[0].T)))
    ]
    every = ("dp", "section")
    small = jnp.concatenate(
        [norm_gain[0, 0], norm_gain[0, 1], keyvalue_bias[0].reshape(-1)], axis=0
    )
    small = lax.all_gather(small, "section", axis=0)
    q_bias = lax.all_gather(query_bias[0], ("section", "tensor"), axis=0, tiled=True).reshape(layers, -1)

    def weights(layer):
        g = lax.all_gather(halves[0][layer], every + ("tensor",), axis=0)
        g = g.reshape(-1, tensor, g.shape[1], g.shape[2])
        g = jnp.swapaxes(g, 1, 2)

        def cut(start, size):
            return g[..., start : start + size].reshape(width, tensor * size)

        gain = small[layer, : 2 * width].reshape(2, width).astype(F32)
        return dict(
            gain=gain,
            q=cut(0, q_cols),
            out_t=cut(q_cols, q_cols),
            kv=cut(2 * q_cols, kv_cols),
            gate=lax.all_gather(halves[1][layer], every, axis=0, tiled=True),
            up=lax.all_gather(halves[2][layer], every, axis=0, tiled=True),
            shrink_t=lax.all_gather(halves[3][layer], every, axis=0, tiled=True),
            q_bias=q_bias[layer].astype(F32),
            kv_bias=small[layer, 2 * width :].astype(F32),
        )

    def pick(stack):
        chosen = jnp.stack(
            [lax.dynamic_index_in_dim(stack[0], adapter_ids[i], 0, keepdims=False) for i in range(layers)]
        )
        return swap(chosen)

    picked = [
        pick(stack)
        for stack in (
            adapter_input,
            adapter_query,
            adapter_keyvalue,
            adapter_expand,
            adapter_attend,
            adapter_shrink,
            adapter_residual,
        )
    ]
    query_all = lax.all_gather(picked[1], "tensor", axis=2, tiled=True)
    attend_all = lax.all_gather(picked[4], "tensor", axis=1, tiled=True)

    def adapters(layer):
        return dict(
            input=picked[0][layer],
            q=query_all[layer],
            kv=picked[2][layer],
            high=picked[0][layer][:, 3 * RANK :],
            expand=jnp.pad(
                jnp.stack(
                    [jnp.pad(picked[3][layer][i], [(i * RANK, (1 - i) * RANK), (0, 0)]) for i in range(2)]
                ),
                [(0, 0), (0, 0), (0, padding)],
            ),
            attend=attend_all[layer],
            shrink=padded(picked[5][layer].T),
            residual=picked[6][layer],
        )

    x = lax.dynamic_index_in_dim(inputs, core, 0, keepdims=False).astype(F32)
    cot = lax.dynamic_index_in_dim(cotangent, core, 0, keepdims=False).astype(F32)
    length = lax.dynamic_index_in_dim(lengths, core, 0, keepdims=False)
    first_slot = place * rows
    info = jnp.stack([first_slot, length]).astype(jnp.int32)
    tables = rotary_tables(first_slot, rows)
    slot_ids = first_slot + jnp.arange(rows, dtype=jnp.int32)

    w = [weights(layer) for layer in range(layers)]
    ad = [adapters(layer) for layer in range(layers)]
    outs, kept = [], []
    for layer in range(layers):
        y, saved = forward(x, w[layer], ad[layer], info, tables)
        outs.append(y.astype(BF))
        kept.append(saved)
        x = outs[-1].astype(F32)
    grad = cot * (slot_ids < length).astype(F32)[:, None]
    grads, wholes, parts = [None] * layers, [None] * layers, [None] * layers
    for layer in reversed(range(layers)):
        grad, wholes[layer], parts[layer] = backward(grad, w[layer], ad[layer], kept[layer], info, tables)
        grads[layer] = grad
    layer_output = swap(jnp.stack(outs))
    input_grad = swap(jnp.stack(grads))

    whole = lax.psum(swap(jnp.stack(wholes)), "tensor")
    part = swap(jnp.stack(parts)[..., :hidden])
    own = 7 * RANK
    q_rows = lax.dynamic_slice_in_dim(whole[:, own : own + 2 * RANK], place * q_cols, q_cols, 2)
    rest = jnp.concatenate([whole[:, :own], whole[:, own + 2 * RANK :]], axis=1)
    rest, q_rows, part, ids = (
        lax.all_gather(a, "dp", axis=0, tiled=True) for a in (rest, q_rows, part, adapter_ids)
    )
    count = adapter_input.shape[1]
    pick_matrix = (jnp.arange(count, dtype=jnp.int32)[:, None] == ids[None, :]).astype(BF)
    scale = 1.0 / math.sqrt(tokens)

    def by_adapter(a):
        return jnp.einsum("as,srw->arw", pick_matrix, a, preferred_element_type=F32) * scale

    rest, q_rows, part = by_adapter(rest), by_adapter(q_rows), by_adapter(part)
    r = RANK
    kv_width = KV_HEADS * HEAD_DIM
    return (
        layer_output[None],
        input_grad[None],
        jnp.swapaxes(rest[:, : 5 * r], 1, 2)[None],
        q_rows[:, :r][None],
        jnp.stack([rest[:, 7 * r :, :kv_width], rest[:, 7 * r :, kv_width : 2 * kv_width]], axis=1)[None],
        jnp.stack([part[:, :r], part[:, r : 2 * r]], axis=1)[None],
        jnp.swapaxes(q_rows[:, r:], 1, 2)[None],
        jnp.swapaxes(part[:, 2 * r :], 1, 2)[None],
        jnp.stack([rest[:, 5 * r : 6 * r], rest[:, 6 * r : 7 * r]], axis=1)[None],
    )


def solution(mesh):
    placed = (
        P("dp", "tensor", None),
        P("dp"),
        P("dp"),
        P("dp", "tensor", None),
        P("section", None, None),
        P("section", "dp", "tensor"),
        P("section", "tensor"),
        P("section", None, "dp", None),
        P("section", None, None),
        P("section", "tensor", "dp"),
        P("section", None, "dp", "tensor"),
        P("section", "tensor", "dp"),
        P("section", None, None, None),
        P("section", None, None, "tensor"),
        P("section", None, None, None, None),
        P("section", None, None, None, "tensor"),
        P("section", None, "tensor", None),
        P("section", None, "tensor", None),
        P("section", None, None, None, None),
    )
    return jax.shard_map(
        local,
        mesh=mesh,
        in_specs=placed,
        out_specs=(
            P("section", "dp", "tensor", None),
            P("section", "dp", "tensor", None),
            P("section", None, None, None),
            P("section", None, None, "tensor"),
            P("section", None, None, None, None),
            P("section", None, None, None, "tensor"),
            P("section", None, "tensor", None),
            P("section", None, "tensor", None),
            P("section", None, None, None, None),
        ),
        check_vma=False,
    )
```

```python
from functools import partial
import math

import jax
import jax.numpy as jnp
from jax import lax
from jax.experimental import pallas as pl
from jax.experimental.pallas import tpu as pltpu
from jax.sharding import PartitionSpec as P

KV_HEADS = 2
HEAD_DIM = 128
RANK = 16
EPSILON = 1e-06
ROPE_BASE = 1000000.0
MASKED_SCORE = -1e30
CHUNKS = 4
LANES = 128
VMEM_LIMIT = 60 * 2**20
MESH = pl.DeviceIdType.MESH
BF = jnp.bfloat16
F32 = jnp.float32


def dot(a, b):
    return jnp.dot(a, b, preferred_element_type=F32)


def dot_t(a, b):
    return lax.dot_general(a, b, (((1,), (1,)), ((), ())), preferred_element_type=F32)


def t_dot(a, b):
    return lax.dot_general(a, b, (((0,), (0,)), ((), ())), preferred_element_type=F32)


def rotary_tables(first_slot, rows):
    half = HEAD_DIM // 2
    frequency = jnp.exp(-math.log(ROPE_BASE) * (2.0 * jnp.arange(half, dtype=F32) / HEAD_DIM))
    slots = (first_slot + jnp.arange(rows, dtype=jnp.int32)).astype(F32)
    angles = slots[:, None] * frequency[None, :]
    cos, sin = jnp.cos(angles), jnp.sin(angles)
    return jnp.concatenate([cos, cos], axis=1), jnp.concatenate([-sin, sin], axis=1)


def vspec():
    return pl.BlockSpec(memory_space=pltpu.VMEM)


def hspec():
    return pl.BlockSpec(memory_space=pl.ANY)


def line_barrier(me, line):
    barrier = pltpu.get_barrier_semaphore()

    @pl.when(me > 0)
    def _():
        pl.semaphore_signal(barrier, inc=1, device_id={"tensor": me - 1}, device_id_type=MESH)

    @pl.when(me < line - 1)
    def _():
        pl.semaphore_signal(barrier, inc=1, device_id={"tensor": me + 1}, device_id_type=MESH)

    pl.semaphore_wait(barrier, jnp.where(me > 0, 1, 0) + jnp.where(me < line - 1, 1, 0))


def within(c, chunks):
    return jnp.logical_and(c >= 0, c < chunks)


def line_exchange(line, chunks, gathered, partial_ref, from_left, from_right, own_out, sems, begin, work):
    ag_recv, ag_right, ag_left, r_recv, r_send, l_recv, l_send = sems
    me = lax.axis_index("tensor")

    def copy(ref, src, c, o, send, recv, side):
        return pltpu.make_async_remote_copy(
            src_ref=src.at[c, o],
            dst_ref=ref.at[c, o],
            send_sem=send.at[c, o],
            recv_sem=recv.at[c, o],
            device_id={"tensor": me + side},
            device_id_type=MESH,
        )

    def ag(c, o, side):
        return copy(gathered, gathered, c, o, ag_right if side > 0 else ag_left, ag_recv, side)

    def rs(c, o, side):
        if side > 0:
            return copy(from_left, partial_ref, c, o, r_send, r_recv, 1)
        return copy(from_right, partial_ref, c, o, l_send, l_recv, -1)

    has_left, has_right = me > 0, me < line - 1

    def step(s, carry):
        first = s + line - 1

        @pl.when(jnp.logical_and(within(first, chunks), has_right))
        def _():
            ag(first, me, 1).start()

        @pl.when(jnp.logical_and(within(first, chunks), has_left))
        def _():
            ag(first, me, -1).start()

        for d in range(1, line):
            c = s + line - 1 - d

            @pl.when(jnp.logical_and(within(c, chunks), me - d >= 0))
            def _():
                ag(c, me - d, 1).wait_recv()

                @pl.when(has_right)
                def _():
                    ag(c, me - d, 1).start()

            @pl.when(jnp.logical_and(within(c, chunks), me + d < line))
            def _():
                ag(c, me + d, -1).wait_recv()

                @pl.when(has_left)
                def _():
                    ag(c, me + d, -1).start()

        @pl.when(within(s, chunks))
        def _():
            work(s)

        for h in range(line):
            c = s - h

            @pl.when(jnp.logical_and(within(c, chunks), me == h))
            def _():
                for j in range(h + 1, line):
                    if h > 0:
                        rs(c, j, 1).wait_recv()
                        partial_ref[c, j] = (
                            partial_ref[c, j].astype(F32) + from_left[c, j].astype(F32)
                        ).astype(BF)
                    if h < line - 1:
                        rs(c, j, 1).start()

            @pl.when(jnp.logical_and(within(c, chunks), me == line - 1 - h))
            def _():
                for j in range(line - 1 - h):
                    if h > 0:
                        rs(c, j, -1).wait_recv()
                        partial_ref[c, j] = (
                            partial_ref[c, j].astype(F32) + from_right[c, j].astype(F32)
                        ).astype(BF)
                    if h < line - 1:
                        rs(c, j, -1).start()

        last = s - (line - 1)

        @pl.when(within(last, chunks))
        def _():
            own_out[last] = partial_ref[last, me].astype(F32)

            @pl.when(has_left)
            def _():
                rs(last, me, 1).wait_recv()
                own_out[last] += from_left[last, me].astype(F32)

            @pl.when(has_right)
            def _():
                rs(last, me, -1).wait_recv()
                own_out[last] += from_right[last, me].astype(F32)

        return carry

    line_barrier(me, line)
    begin()
    lax.fori_loop(-(line - 1), chunks + line - 1, step, 0)

    def drain(c, carry):
        for o in range(line):

            @pl.when(jnp.logical_and(has_right, me >= o))
            def _():
                ag(c, o, 1).wait_send()

            @pl.when(jnp.logical_and(has_left, me <= o))
            def _():
                ag(c, o, -1).wait_send()

            @pl.when(me < o)
            def _():
                rs(c, o, 1).wait_send()

            @pl.when(me > o)
            def _():
                rs(c, o, -1).wait_send()

        return carry

    lax.fori_loop(0, chunks, drain, 0)


def exchange_scratch(line, chunks, rows, width):
    slots = (chunks, line, rows, width)
    return [pltpu.VMEM(slots, BF)] * 4 + [pltpu.SemaphoreType.DMA((chunks, line))] * 7


def mlp_kernel(
    line, chunks, tile,
    n2_ref, packed, high_ref, expand_ref, ash_ref, res_ref,
    out_ref, n2_out, gate_out, up_out,
    gathered, partial_ref, from_left, from_right, s0, s1, s2, s3, s4, s5, s6,
    wg, wu, ws, gate_st, up_st, acc, wsem, osem, nsem,
):
    rows, width = n2_ref.shape[1:]
    every = line * rows
    tiles = wg.shape[2] // tile
    me = lax.axis_index("tensor")
    loads = [pltpu.make_async_copy(packed.at[:, i], ref, wsem.at[i]) for i, ref in enumerate((wg, wu, ws))]

    def begin():
        for load in loads:
            load.start()
        for c in range(chunks):
            gathered[c, me] = n2_ref[c]

    def saves(c, slot):
        return (
            pltpu.make_async_copy(gate_st.at[slot], gate_out.at[c], osem.at[0, slot]),
            pltpu.make_async_copy(up_st.at[slot], up_out.at[c], osem.at[1, slot]),
        )

    def keep(c):
        return pltpu.make_async_copy(gathered.at[c], n2_out.at[c], nsem.at[c])

    def work(c):
        slot = c % 2

        @pl.when(c == 0)
        def _():
            for load in loads:
                load.wait()

        @pl.when(c >= 2)
        def _():
            for save in saves(c - 2, slot):
                save.wait()

        keep(c).start()
        x = gathered[c].reshape(every, width)
        er = dot(x, high_ref[...]).astype(BF)

        def one(f, rank):
            cols = pl.ds(pl.multiple_of(f * tile, tile), tile)
            gate = dot(x, wg[:, :, cols].reshape(width, tile)) + dot(er, expand_ref[0, :, cols])
            up = dot(x, wu[:, :, cols].reshape(width, tile)) + dot(er, expand_ref[1, :, cols])
            gate_st[slot, :, cols] = gate.astype(BF)
            up_st[slot, :, cols] = up.astype(BF)
            act = (gate * (1.0 / (1.0 + jnp.exp(-gate))) * up).astype(BF)
            now = dot_t(act, ws[:, :, cols].reshape(width, tile))

            @pl.when(f == 0)
            def _():
                acc[...] = now

            @pl.when(f > 0)
            def _():
                acc[...] += now

            return rank + dot_t(act, ash_ref[:, cols])

        rank = lax.fori_loop(0, tiles, one, jnp.zeros((every, ash_ref.shape[0]), F32))
        total = acc[...] + dot(rank.astype(BF), res_ref[...])
        partial_ref[c] = total.astype(BF).reshape(line, rows, width)
        for save in saves(c, slot):
            save.start()

    line_exchange(
        line, chunks, gathered, partial_ref, from_left, from_right, out_ref,
        (s0, s1, s2, s3, s4, s5, s6), begin, work,
    )
    for c in range(chunks):
        keep(c).wait()
    for c in range(max(chunks - 2, 0), chunks):
        for save in saves(c, c % 2):
            save.wait()


def ff_tile(hidden):
    return hidden // 3 if hidden % (3 * LANES) == 0 else LANES


def mlp_forward(n2, w, ad):
    line = lax.axis_size("tensor")
    rows, width = n2.shape
    groups, _, _, hidden = w["mlp"].shape
    part = rows // CHUNKS
    every = line * part
    out, n2_all, gate, up = pl.pallas_call(
        partial(mlp_kernel, line, CHUNKS, ff_tile(hidden)),
        in_specs=[vspec(), hspec()] + [vspec()] * 4,
        out_specs=[vspec()] + [hspec()] * 3,
        out_shape=[
            jax.ShapeDtypeStruct((CHUNKS, part, width), F32),
            jax.ShapeDtypeStruct((CHUNKS, line, part, width), BF),
            jax.ShapeDtypeStruct((CHUNKS, every, hidden), BF),
            jax.ShapeDtypeStruct((CHUNKS, every, hidden), BF),
        ],
        scratch_shapes=exchange_scratch(line, CHUNKS, part, width)
        + [pltpu.VMEM((groups, width // groups, hidden), BF)] * 3
        + [pltpu.VMEM((2, every, hidden), BF)] * 2
        + [
            pltpu.VMEM((every, width), F32),
            pltpu.SemaphoreType.DMA((3,)),
            pltpu.SemaphoreType.DMA((2, 2)),
            pltpu.SemaphoreType.DMA((CHUNKS,)),
        ],
        compiler_params=pltpu.CompilerParams(
            collective_id=0, has_side_effects=True, vmem_limit_bytes=VMEM_LIMIT
        ),
        cost_estimate=pl.CostEstimate(
            flops=6 * line * rows * width * hidden,
            bytes_accessed=6 * width * hidden + 4 * line * rows * hidden,
            transcendentals=line * rows * hidden,
        ),
    )(
        n2.reshape(CHUNKS, part, width), w["mlp"],
        ad["high"], ad["expand"], ad["shrink"], ad["res_two"],
    )
    return out.reshape(rows, width), (n2_all.reshape(CHUNKS, every, width), gate, up)


def mlp_back_kernel(
    line, chunks, tile,
    ds_ref, packed, n2_hbm, gate_in, up_in, high_ref, expand_ref, ash_ref, res_ref,
    out_ref, ghigh_ref, gexp_ref, gsh_ref, gres_ref,
    gathered, partial_ref, from_left, from_right, s0, s1, s2, s3, s4, s5, s6,
    wg, wu, ws, gate_st, up_st, n2_st, acc, wsem, isem,
):
    rows, width = ds_ref.shape[1:]
    every = line * rows
    tiles = wg.shape[2] // tile
    me = lax.axis_index("tensor")
    loads = [pltpu.make_async_copy(packed.at[:, i], ref, wsem.at[i]) for i, ref in enumerate((wg, wu, ws))]

    def fetch(c):
        slot = c % 2
        return (
            pltpu.make_async_copy(gate_in.at[c], gate_st.at[slot], isem.at[0, slot]),
            pltpu.make_async_copy(up_in.at[c], up_st.at[slot], isem.at[1, slot]),
            pltpu.make_async_copy(n2_hbm.at[c], n2_st.at[slot], isem.at[2, slot]),
        )

    def begin():
        for load in loads:
            load.start()
        for one in fetch(0):
            one.start()
        for c in range(chunks):
            gathered[c, me] = ds_ref[c]
        for ref in (ghigh_ref, gexp_ref, gsh_ref, gres_ref):
            ref[...] = jnp.zeros_like(ref)

    def work(c):
        slot = c % 2

        @pl.when(c == 0)
        def _():
            for load in loads:
                load.wait()

        for one in fetch(c):
            one.wait()

        @pl.when(c + 1 < chunks)
        def _():
            for one in fetch(c + 1):
                one.start()

        ds = gathered[c].reshape(every, width)
        n2 = n2_st[slot]
        er = dot(n2, high_ref[...]).astype(BF)
        rank_in = dot_t(ds, res_ref[...]).astype(BF)

        def one(f, carry):
            rank_out, srank = carry
            cols = pl.ds(pl.multiple_of(f * tile, tile), tile)
            act_grad = dot(ds, ws[:, :, cols].reshape(width, tile)) + dot(rank_in, ash_ref[:, cols])
            gate = gate_st[slot, :, cols].astype(F32)
            up = up_st[slot, :, cols].astype(F32)
            sig = 1.0 / (1.0 + jnp.exp(-gate))
            silu = gate * sig
            act = (silu * up).astype(BF)
            gate_grad = (act_grad * up * (sig + silu * (1.0 - sig))).astype(BF)
            up_grad = (act_grad * silu).astype(BF)
            now = dot_t(gate_grad, wg[:, :, cols].reshape(width, tile)) + dot_t(up_grad, wu[:, :, cols].reshape(width, tile))

            @pl.when(f == 0)
            def _():
                acc[...] = now

            @pl.when(f > 0)
            def _():
                acc[...] += now

            gexp_ref[0, :, cols] += t_dot(er, gate_grad)
            gexp_ref[1, :, cols] += t_dot(er, up_grad)
            gsh_ref[:, cols] += t_dot(rank_in, act)
            rank_out = rank_out + dot_t(gate_grad, expand_ref[0, :, cols])
            rank_out = rank_out + dot_t(up_grad, expand_ref[1, :, cols])
            return rank_out, srank + dot_t(act, ash_ref[:, cols])

        rank_out, srank = lax.fori_loop(
            0,
            tiles,
            one,
            (
                jnp.zeros((every, expand_ref.shape[1]), F32),
                jnp.zeros((every, ash_ref.shape[0]), F32),
            ),
        )
        rank_out = rank_out.astype(BF)
        total = acc[...] + dot_t(rank_out, high_ref[...])
        partial_ref[c] = total.astype(BF).reshape(line, rows, width)
        ghigh_ref[...] += t_dot(rank_out, n2)
        gres_ref[...] += t_dot(srank.astype(BF), ds)

    line_exchange(
        line, chunks, gathered, partial_ref, from_left, from_right, out_ref,
        (s0, s1, s2, s3, s4, s5, s6), begin, work,
    )


def mlp_backward(ds, w, ad, saved):
    n2_all, gate, up = saved
    line = lax.axis_size("tensor")
    rows, width = ds.shape
    groups, _, _, hidden = w["mlp"].shape
    part = rows // CHUNKS
    every = line * part
    out, g_high, g_expand, g_shrink, g_res = pl.pallas_call(
        partial(mlp_back_kernel, line, CHUNKS, ff_tile(hidden)),
        in_specs=[vspec()] + [hspec()] * 4 + [vspec()] * 4,
        out_specs=[vspec()] * 5,
        out_shape=[
            jax.ShapeDtypeStruct((CHUNKS, part, width), F32),
            jax.ShapeDtypeStruct((2 * RANK, width), F32),
            jax.ShapeDtypeStruct((2, 2 * RANK, hidden), F32),
            jax.ShapeDtypeStruct((RANK, hidden), F32),
            jax.ShapeDtypeStruct((RANK, width), F32),
        ],
        scratch_shapes=exchange_scratch(line, CHUNKS, part, width)
        + [pltpu.VMEM((groups, width // groups, hidden), BF)] * 3
        + [pltpu.VMEM((2, every, hidden), BF)] * 2
        + [
            pltpu.VMEM((2, every, width), BF),
            pltpu.VMEM((every, width), F32),
            pltpu.SemaphoreType.DMA((3,)),
            pltpu.SemaphoreType.DMA((3, 2)),
        ],
        compiler_params=pltpu.CompilerParams(
            collective_id=1, has_side_effects=True, vmem_limit_bytes=VMEM_LIMIT
        ),
        cost_estimate=pl.CostEstimate(
            flops=6 * line * rows * width * hidden,
            bytes_accessed=6 * width * hidden + 4 * line * rows * hidden,
            transcendentals=line * rows * hidden,
        ),
    )(
        ds.reshape(CHUNKS, part, width), w["mlp"], n2_all, gate, up,
        ad["high"], ad["expand"], ad["shrink"], ad["res_two"],
    )
    g_expand = jnp.concatenate([g_expand[0, :RANK], g_expand[1, RANK:]], axis=0)
    return out.reshape(rows, width), g_high, g_expand, g_shrink, g_res


def gather_kernel(
    line, peers,
    attn, extra,
    first_out, second_out, extra_out,
    own_sem, z_recv, z_right, z_left, dp_recv, dp_send, core_recv, core_send,
):
    me, spot, core = lax.axis_index("tensor"), lax.axis_index("dp"), lax.axis_index("section")
    other = 1 - core
    has_left, has_right = me > 0, me < line - 1
    barrier = pltpu.get_barrier_semaphore()

    def greet(**where):
        pl.semaphore_signal(barrier, inc=1, device_id=where, device_id_type=MESH)

    @pl.when(has_left)
    def _():
        greet(tensor=me - 1)

    @pl.when(has_right)
    def _():
        greet(tensor=me + 1)

    greet(section=other)
    for k in range(1, peers):
        greet(dp=lax.rem(spot + k, peers))
    pl.semaphore_wait(barrier, jnp.where(has_left, 1, 0) + jnp.where(has_right, 1, 0) + peers)

    mine = spot * 2 + core

    def places(o):
        return first_out.at[mine, o], second_out.at[o], extra_out.at[o]

    sources = (attn.at[0], attn.at[1], extra)
    keeps = [
        pltpu.make_async_copy(src, dst, own_sem.at[i]) for i, (src, dst) in enumerate(zip(sources, places(me)))
    ]

    def remote(src, dst, send, recv, **where):
        return pltpu.make_async_remote_copy(
            src_ref=src, dst_ref=dst, send_sem=send, recv_sem=recv, device_id=where, device_id_type=MESH
        )

    def along(i, o, side, own):
        dst = places(o)[i]
        return remote(
            sources[i] if own else dst,
            dst,
            (z_right if side > 0 else z_left).at[i, o],
            z_recv.at[i, o],
            tensor=me + side,
        )

    def to_peer(k, o, own):
        dst = first_out.at[mine, o]
        return remote(
            attn.at[0] if own else dst, dst, dp_send.at[k, o], dp_recv.at[spot, o], dp=lax.rem(spot + k, peers)
        )

    def to_core(p, o, own):
        dst = first_out.at[p * 2 + core, o]
        return remote(attn.at[0] if own else dst, dst, core_send.at[p, o], core_recv.at[p, o], section=other)

    def spread_first(o, own):
        for k in range(1, peers):
            to_peer(k, o, own).start()
        to_core(spot, o, own).start()

    for i in range(3):

        @pl.when(has_right)
        def _():
            along(i, me, 1, True).start()

        @pl.when(has_left)
        def _():
            along(i, me, -1, True).start()

        if i == 0:
            spread_first(me, True)
    for keep in keeps:
        keep.start()
    for d in range(1, line):
        for i in range(3):

            @pl.when(me >= d)
            def _():
                along(i, me - d, 1, False).wait_recv()

                @pl.when(has_right)
                def _():
                    along(i, me - d, 1, False).start()

                if i == 0:
                    spread_first(me - d, False)

            @pl.when(me + d < line)
            def _():
                along(i, me + d, -1, False).wait_recv()

                @pl.when(has_left)
                def _():
                    along(i, me + d, -1, False).start()

                if i == 0:
                    spread_first(me + d, False)

    def pass_on(o, carry):
        for k in range(1, peers):
            p = lax.rem(spot + peers - k, peers)
            remote(
                first_out.at[p * 2 + core, o], first_out.at[p * 2 + core, o], dp_send.at[k, o], dp_recv.at[p, o], dp=p
            ).wait_recv()
            to_core(p, o, False).start()
        return carry

    lax.fori_loop(0, line, pass_on, 0)

    def finish(o, carry):
        for k in range(1, peers):
            to_peer(k, o, False).wait_send()
        for p in range(peers):
            to_core(p, o, False).wait_send()
            remote(
                first_out.at[p * 2 + other, o],
                first_out.at[p * 2 + other, o],
                core_send.at[p, o],
                core_recv.at[p, o],
                section=other,
            ).wait_recv()
        for i in range(3):

            @pl.when(jnp.logical_and(has_right, me >= o))
            def _():
                along(i, o, 1, False).wait_send()

            @pl.when(jnp.logical_and(has_left, me <= o))
            def _():
                along(i, o, -1, False).wait_send()

        return carry

    lax.fori_loop(0, line, finish, 0)
    for keep in keeps:
        keep.wait()


def gather_first(attn, extra):
    line, peers = lax.axis_size("tensor"), lax.axis_size("dp")
    cores, part, cols = attn.shape
    dma = pltpu.SemaphoreType.DMA
    return pl.pallas_call(
        partial(gather_kernel, line, peers),
        in_specs=[hspec()] * 2,
        out_specs=[hspec()] * 3,
        out_shape=[
            jax.ShapeDtypeStruct((peers * cores, line, part, cols), BF),
            jax.ShapeDtypeStruct((line, part, cols), BF),
            jax.ShapeDtypeStruct((line,) + extra.shape, BF),
        ],
        scratch_shapes=[dma((3,)), dma((3, line)), dma((3, line)), dma((3, line))]
        + [dma((peers, line))] * 4,
        compiler_params=pltpu.CompilerParams(
            collective_id=4, has_side_effects=True, vmem_limit_bytes=VMEM_LIMIT
        ),
    )(attn, extra)


def rotated(x, cos, sin):
    return x * cos + pltpu.roll(x, HEAD_DIM // 2, 1) * sin


def head_cols(h):
    return pl.ds(pl.multiple_of(h * HEAD_DIM, HEAD_DIM), HEAD_DIM)


def weight_loads(packed, wq, wo, wkv, wsem):
    cols, kv_cols = wq.shape[-1], wkv.shape[-1]
    loads = []
    for i, (ref, start, size) in enumerate(((wkv, 2 * cols, kv_cols), (wq, 0, cols), (wo, cols, cols))):
        loads.append(
            [
                pltpu.make_async_copy(packed.at[:, t, :, pl.ds(start, size)], ref.at[t], wsem.at[i, t])
                for t in range(ref.shape[0])
            ]
        )
    return loads


def flat(ref, t):
    groups, rows, cols = ref.shape[1:]
    return ref[t].reshape(groups * rows, cols)


def allowed_keys(info_ref, block, keys, rows):
    row = info_ref[0] + lax.broadcasted_iota(jnp.int32, (1, rows), 1)
    last = jnp.minimum(row, info_ref[1] - 1)
    return block * keys + lax.broadcasted_iota(jnp.int32, (keys, rows), 0) <= last


def one_way_barrier(me, line, side):
    barrier = pltpu.get_barrier_semaphore()
    first, last = (0, line - 1) if side > 0 else (line - 1, 0)

    @pl.when(me != first)
    def _():
        pl.semaphore_signal(barrier, inc=1, device_id={"tensor": me - side}, device_id_type=MESH)

    @pl.when(me != last)
    def _():
        pl.semaphore_wait(barrier, 1)


def kv_exchange(me, line, kvbuf, recv, send):
    def move(o):
        return pltpu.make_async_remote_copy(
            src_ref=kvbuf.at[o],
            dst_ref=kvbuf.at[o],
            send_sem=send.at[o],
            recv_sem=recv.at[o],
            device_id={"tensor": me + 1},
            device_id_type=MESH,
        )

    return move


def attend_kernel(
    line, group,
    info_ref, x_ref, gain_ref, qb_ref, kvb_ref, low_ref, bq_ref, bkv_ref, att_ref, res_ref, cos_ref, sin_ref, packed,
    mid_ref, n2_ref, normed_ref, rank_ref, q_ref, kv_out, attended_ref, log_ref,
    wq, wo, wkv, kvbuf, acc, peak, total, wsem, recv, send, ksem,
):
    rows, width = x_ref.shape
    heads = width // HEAD_DIM
    cols = wq.shape[-1]
    kv_cols = wkv.shape[-1]
    scale = HEAD_DIM**-0.5
    me = lax.axis_index("tensor")
    one_way_barrier(me, line, 1)
    kv_loads, q_loads, o_loads = weight_loads(packed, wq, wo, wkv, wsem)
    for load in kv_loads + q_loads + o_loads:
        load.start()
    move = kv_exchange(me, line, kvbuf, recv, send)
    x = x_ref[...]
    inverse = lax.rsqrt(jnp.mean(x * x, axis=-1, keepdims=True) + EPSILON)
    normed_ref[...] = (x * inverse * gain_ref[0:1, :]).astype(BF)
    low = dot(normed_ref[...], low_ref[...]).astype(BF)
    cos, sin = cos_ref[...], sin_ref[...]
    for load in kv_loads:
        load.wait()
    for t in range(line):
        span = slice(t * kv_cols, (t + 1) * kv_cols)
        kv = dot(normed_ref[...], flat(wkv, t)) + kvb_ref[:, span] + dot(low, bkv_ref[:, span])
        for h in range(kv_cols // HEAD_DIM):
            at = t * kv_cols + h * HEAD_DIM
            one = kv[:, h * HEAD_DIM : (h + 1) * HEAD_DIM]
            if at < KV_HEADS * HEAD_DIM:
                one = rotated(one, cos, sin)
            kvbuf[me, :, at : at + HEAD_DIM] = one.astype(BF)

    @pl.when(me < line - 1)
    def _():
        move(me).start()

    for load in q_loads:
        load.wait()
    for t in range(line):
        span = slice(t * cols, (t + 1) * cols)
        q = dot(normed_ref[...], flat(wq, t)) + qb_ref[:, span] + dot(low, bq_ref[:, span])
        for h in range(cols // HEAD_DIM):
            at = t * cols + h * HEAD_DIM
            q_ref[:, at : at + HEAD_DIM] = rotated(
                q[:, h * HEAD_DIM : (h + 1) * HEAD_DIM], cos, sin
            ).astype(BF)
    acc[...] = jnp.zeros_like(acc)
    total[...] = jnp.zeros_like(total)
    peak[...] = jnp.full_like(peak, MASKED_SCORE)

    def block(o):
        allowed = allowed_keys(info_ref, o, rows, rows)

        def one(h, carry):
            kv_head = h // group
            k = kvbuf[o, :, head_cols(kv_head)]
            v = kvbuf[o, :, head_cols(KV_HEADS + kv_head)]
            scores = jnp.where(allowed, dot_t(k, q_ref[:, head_cols(h)]) * scale, MASKED_SCORE)
            top = jnp.maximum(peak[h], jnp.max(scores, axis=0, keepdims=True))
            soft = jnp.exp(scores - top)
            shift = jnp.exp(peak[h] - top)
            total[h] = total[h] * shift + jnp.sum(soft, axis=0, keepdims=True)
            acc[h] = acc[h] * shift + t_dot(v, soft.astype(BF))
            peak[h] = top
            return carry

        lax.fori_loop(0, heads, one, 0)

    for d in range(line):

        @pl.when(me >= d)
        def _():
            if d > 0:
                move(me - d).wait_recv()

                @pl.when(me < line - 1)
                def _():
                    move(me - d).start()

            block(me - d)

    keep = pltpu.make_async_copy(kvbuf, kv_out, ksem)
    keep.start()
    for h in range(heads):
        attended_ref[:, h * HEAD_DIM : (h + 1) * HEAD_DIM] = (acc[h] * (1.0 / total[h])).T.astype(BF)
        log_ref[h] = peak[h] + jnp.log(total[h])
    rank = dot_t(attended_ref[...], att_ref[...]).astype(BF)
    rank_ref[0] = low
    rank_ref[1] = rank
    middle = x_ref[...] + dot(rank, res_ref[...])
    for load in o_loads:
        load.wait()
    for t in range(line):
        middle = middle + dot_t(attended_ref[:, t * cols : (t + 1) * cols], flat(wo, t))
    mid_ref[...] = middle
    inverse = lax.rsqrt(jnp.mean(middle * middle, axis=-1, keepdims=True) + EPSILON)
    n2_ref[...] = (middle * inverse * gain_ref[1:2, :]).astype(BF)
    keep.wait()
    for o in range(line):

        @pl.when(jnp.logical_and(me < line - 1, me >= o))
        def _():
            move(o).wait_send()


def attend_forward(x, w, ad, info, tables):
    line = lax.axis_size("tensor")
    rows, width = x.shape
    heads = width // HEAD_DIM
    kv_width = 2 * KV_HEADS * HEAD_DIM
    groups, low_rows = w["packed"].shape[0], w["packed"].shape[2]
    outs = pl.pallas_call(
        partial(attend_kernel, line, heads // KV_HEADS),
        in_specs=[pl.BlockSpec(memory_space=pltpu.SMEM)] + [vspec()] * 11 + [hspec()],
        out_specs=[vspec()] * 5 + [hspec()] + [vspec()] * 2,
        out_shape=[
            jax.ShapeDtypeStruct((rows, width), F32),
            jax.ShapeDtypeStruct((rows, width), BF),
            jax.ShapeDtypeStruct((rows, width), BF),
            jax.ShapeDtypeStruct((2, rows, 3 * RANK), BF),
            jax.ShapeDtypeStruct((rows, width), BF),
            jax.ShapeDtypeStruct((line, rows, kv_width), BF),
            jax.ShapeDtypeStruct((rows, width), BF),
            jax.ShapeDtypeStruct((heads, 1, rows), F32),
        ],
        scratch_shapes=[
            pltpu.VMEM((line, groups, low_rows, width // line), BF),
            pltpu.VMEM((line, groups, low_rows, width // line), BF),
            pltpu.VMEM((line, groups, low_rows, kv_width // line), BF),
            pltpu.VMEM((line, rows, kv_width), BF),
            pltpu.VMEM((heads, HEAD_DIM, rows), F32),
            pltpu.VMEM((heads, 1, rows), F32),
            pltpu.VMEM((heads, 1, rows), F32),
            pltpu.SemaphoreType.DMA((3, line)),
            pltpu.SemaphoreType.DMA((line,)),
            pltpu.SemaphoreType.DMA((line,)),
            pltpu.SemaphoreType.DMA,
        ],
        compiler_params=pltpu.CompilerParams(
            collective_id=2, has_side_effects=True, vmem_limit_bytes=VMEM_LIMIT
        ),
        cost_estimate=pl.CostEstimate(
            flops=4 * rows * width * width * 2, bytes_accessed=5 * width * width, transcendentals=0
        ),
    )(
        info, x, w["gain"], ad["q_bias"], w["kv_bias"], ad["low"], ad["q"], ad["kv"], ad["attend"],
        ad["res_one"], tables[0], tables[1], w["packed"],
    )
    return outs[0], outs[1], outs[2:]


def attend_back_kernel(
    line, group,
    info_ref, x_ref, mid_ref, dy_ref, dn2_ref, gain_ref, low_ref, bq_ref, bkv_ref, att_ref, res_ref, cos_ref, sin_ref,
    normed_ref, rank_ref, q_ref, kv_ref, attended_ref, log_ref, packed,
    dx_ref, glow_ref, gres_ref, gq_ref, gatt_ref, gkv_ref,
    wq, wo, wkv, do_ref, dq_acc, dq_ref, dkv_acc, partial_ref, from_right, delta, wsem, recv, send,
):
    rows, width = x_ref.shape
    heads = width // HEAD_DIM
    cols = wq.shape[-1]
    kv_cols = wkv.shape[-1]
    kv_half = KV_HEADS * HEAD_DIM
    scale = HEAD_DIM**-0.5
    me = lax.axis_index("tensor")
    one_way_barrier(me, line, -1)
    kv_loads, q_loads, o_loads = weight_loads(packed, wq, wo, wkv, wsem)
    for load in o_loads + q_loads + kv_loads:
        load.start()

    def move(o):
        return pltpu.make_async_remote_copy(
            src_ref=partial_ref.at[o],
            dst_ref=from_right.at[o],
            send_sem=send.at[o],
            recv_sem=recv.at[o],
            device_id={"tensor": me - 1},
            device_id_type=MESH,
        )

    def through_norm(values, gain, grad_out):
        inverse = lax.rsqrt(jnp.mean(values * values, axis=-1, keepdims=True) + EPSILON)
        weighted = gain * grad_out
        return inverse * weighted - inverse * inverse * inverse * values * jnp.mean(
            weighted * values, axis=-1, keepdims=True
        )

    middle_grad = dy_ref[...] + through_norm(mid_ref[...], gain_ref[1:2, :], dn2_ref[...])
    dx_ref[...] = middle_grad
    branch_grad = middle_grad.astype(BF)
    low, rank = rank_ref[0], rank_ref[1]
    rank_grad = dot_t(branch_grad, res_ref[...]).astype(BF)
    gres_ref[...] = t_dot(rank, branch_grad)
    gatt_ref[...] = t_dot(rank_grad, attended_ref[...])
    for load in o_loads:
        load.wait()
    for t in range(line):
        span = slice(t * cols, (t + 1) * cols)
        do_ref[:, span] = (dot(branch_grad, flat(wo, t)) + dot(rank_grad, att_ref[:, span])).astype(BF)
    for h in range(heads):
        span = slice(h * HEAD_DIM, (h + 1) * HEAD_DIM)
        both = do_ref[:, span].astype(F32) * attended_ref[:, span].astype(F32)
        delta[h] = jnp.sum(both.T, axis=0, keepdims=True)
    dq_acc[...] = jnp.zeros_like(dq_acc)

    def block(o):
        allowed = allowed_keys(info_ref, o, rows, rows)
        dkv_acc[...] = jnp.zeros_like(dkv_acc)

        def one(h, carry):
            kv_head = h // group
            k = kv_ref[o, :, head_cols(kv_head)]
            v = kv_ref[o, :, head_cols(KV_HEADS + kv_head)]
            q = q_ref[:, head_cols(h)]
            do = do_ref[:, head_cols(h)]
            scores = dot_t(k, q) * scale - log_ref[h]
            soft = jnp.exp(jnp.where(allowed, scores, MASKED_SCORE))
            grad = (soft * (dot_t(v, do) - delta[h])).astype(BF)
            dq_acc[h] += t_dot(k, grad)
            dkv_acc[:, head_cols(kv_head)] += dot(grad, q) * scale
            dkv_acc[:, head_cols(KV_HEADS + kv_head)] += dot(soft.astype(BF), do)
            return carry

        lax.fori_loop(0, heads, one, 0)
        partial_ref[o] = dkv_acc[...].astype(BF)

    for s in range(2 * line - 1):
        if s < line:

            @pl.when(me >= s)
            def _():
                block(s)

        for h in range(line - 1):
            o = s - h
            if 0 <= o < line - 1 - h:

                @pl.when(me == line - 1 - h)
                def _():
                    if h > 0:
                        move(o).wait_recv()
                        partial_ref[o] = (partial_ref[o].astype(F32) + from_right[o].astype(F32)).astype(BF)
                    move(o).start()

    cos, sin = cos_ref[...], -sin_ref[...]
    for h in range(heads):
        dq_ref[:, h * HEAD_DIM : (h + 1) * HEAD_DIM] = rotated(dq_acc[h].T * scale, cos, sin).astype(BF)
    dq = dq_ref[...]
    gq_ref[...] = t_dot(low, dq)
    low_grad = dot_t(dq, bq_ref[...])
    for load in q_loads:
        load.wait()
    normed_grad = dot_t(dq[:, :cols], flat(wq, 0))
    for t in range(1, line):
        normed_grad = normed_grad + dot_t(dq[:, t * cols : (t + 1) * cols], flat(wq, t))
    dkv_acc[...] = partial_ref[me].astype(F32)

    @pl.when(me < line - 1)
    def _():
        move(me).wait_recv()
        dkv_acc[...] += from_right[me].astype(F32)

    for h in range(KV_HEADS):
        span = slice(h * HEAD_DIM, (h + 1) * HEAD_DIM)
        dkv_acc[:, span] = rotated(dkv_acc[:, span], cos, sin)
    dkv = dkv_acc[...].astype(BF)
    gkv_ref[...] = t_dot(low, dkv)
    low_grad = (low_grad + dot_t(dkv, bkv_ref[...])).astype(BF)
    glow_ref[...] = t_dot(low_grad, normed_ref[...])
    for load in kv_loads:
        load.wait()
    for t in range(line):
        normed_grad = normed_grad + dot_t(dkv[:, t * kv_cols : (t + 1) * kv_cols], flat(wkv, t))
    normed_grad = normed_grad + dot_t(low_grad, low_ref[...])
    dx_ref[...] += through_norm(x_ref[...], gain_ref[0:1, :], normed_grad)
    for o in range(line - 1):

        @pl.when(me > o)
        def _():
            move(o).wait_send()


def attend_backward(x, middle, dy, dn2, w, ad, kept, info, tables):
    line = lax.axis_size("tensor")
    rows, width = x.shape
    heads = width // HEAD_DIM
    kv_width = 2 * KV_HEADS * HEAD_DIM
    groups, low_rows = w["packed"].shape[0], w["packed"].shape[2]
    return pl.pallas_call(
        partial(attend_back_kernel, line, heads // KV_HEADS),
        in_specs=[pl.BlockSpec(memory_space=pltpu.SMEM)] + [vspec()] * 18 + [hspec()],
        out_specs=[vspec()] * 6,
        out_shape=[
            jax.ShapeDtypeStruct((rows, width), F32),
            jax.ShapeDtypeStruct((3 * RANK, width), F32),
            jax.ShapeDtypeStruct((3 * RANK, width), F32),
            jax.ShapeDtypeStruct((3 * RANK, width), F32),
            jax.ShapeDtypeStruct((3 * RANK, width), F32),
            jax.ShapeDtypeStruct((3 * RANK, kv_width), F32),
        ],
        scratch_shapes=[
            pltpu.VMEM((line, groups, low_rows, width // line), BF),
            pltpu.VMEM((line, groups, low_rows, width // line), BF),
            pltpu.VMEM((line, groups, low_rows, kv_width // line), BF),
            pltpu.VMEM((rows, width), BF),
            pltpu.VMEM((heads, HEAD_DIM, rows), F32),
            pltpu.VMEM((rows, width), BF),
            pltpu.VMEM((rows, kv_width), F32),
            pltpu.VMEM((line, rows, kv_width), BF),
            pltpu.VMEM((line, rows, kv_width), BF),
            pltpu.VMEM((heads, 1, rows), F32),
            pltpu.SemaphoreType.DMA((3, line)),
            pltpu.SemaphoreType.DMA((line,)),
            pltpu.SemaphoreType.DMA((line,)),
        ],
        compiler_params=pltpu.CompilerParams(
            collective_id=3, has_side_effects=True, vmem_limit_bytes=VMEM_LIMIT
        ),
        cost_estimate=pl.CostEstimate(
            flops=4 * rows * width * width * 2, bytes_accessed=5 * width * width, transcendentals=0
        ),
    )(
        info, x, middle, dy, dn2, w["gain"], ad["low"], ad["q"], ad["kv"], ad["attend"], ad["res_one"],
        tables[0], tables[1], *kept, w["packed"],
    )


def swap(pair):
    return lax.all_to_all(pair, "section", split_axis=0, concat_axis=0, tiled=True)


def at_rows(a, first, rows):
    return jnp.pad(a, [(first, rows - first - a.shape[0]), (0, 0)])


def local(
    inputs,
    lengths,
    adapter_ids,
    cotangent,
    norm_gain,
    query_weight,
    query_bias,
    keyvalue_weight,
    keyvalue_bias,
    output_weight,
    expand_weight,
    shrink_weight,
    adapter_input,
    adapter_query,
    adapter_keyvalue,
    adapter_expand,
    adapter_attend,
    adapter_shrink,
    adapter_residual,
):
    layers = lax.axis_size("section")
    tensor = lax.axis_size("tensor")
    core = lax.axis_index("section")
    place = lax.axis_index("tensor")
    rows, width = inputs.shape[1:]
    tokens = layers * rows * tensor * lax.axis_size("dp")
    kv_half = KV_HEADS * HEAD_DIM
    hidden = expand_weight.shape[3]
    padding = -hidden % (2 * LANES)
    r = RANK

    def padded(m):
        return jnp.pad(m, [(0, 0)] * (m.ndim - 1) + [(0, padding)])

    kv = jnp.concatenate([keyvalue_weight[0, 0], keyvalue_weight[0, 1]], axis=1)
    kv_cols = kv.shape[1] // tensor
    kv = lax.dynamic_slice_in_dim(kv, place * kv_cols, kv_cols, 1)
    attn = jnp.concatenate([query_weight[0], output_weight[0].T, kv], axis=1)
    q_cols = query_weight.shape[2]
    part = attn.shape[0] // layers
    attn = swap(attn.reshape(layers, part, attn.shape[1]))
    mlp = padded(jnp.concatenate([expand_weight[0], shrink_weight[0].T[None]], axis=0))
    mlp = swap(jnp.swapaxes(mlp.reshape(3, layers, part, mlp.shape[2]), 0, 1))
    every = ("dp", "section")
    small = jnp.concatenate([norm_gain[0, 0], norm_gain[0, 1], keyvalue_bias[0].reshape(-1)], axis=0)
    small = swap(jnp.broadcast_to(small[None], (layers,) + small.shape)).astype(F32)

    def pick(stack):
        chosen = jnp.stack(
            [lax.dynamic_index_in_dim(stack[0], adapter_ids[i], 0, keepdims=False) for i in range(layers)]
        )
        return swap(chosen)

    heads_part = jnp.concatenate(
        [adapter_query[0], jnp.swapaxes(adapter_attend[0], 1, 2)]
        + [jnp.pad(query_bias[0][None, None], [(0, adapter_query.shape[1] - 1), (0, r - 1), (0, 0)], mode="edge")],
        axis=1,
    )
    heads_part = pick(heads_part[None])
    first_attn, line_attn, heads_part = gather_first(attn, heads_part.reshape(-1, q_cols))
    heads_part = jnp.moveaxis(heads_part.reshape(tensor, layers, 3 * r, q_cols), 0, 2)
    heads_part = heads_part.reshape(layers, 3 * r, width)

    def weights(layer):
        packed = first_attn if layer == 0 else lax.all_gather(line_attn, every, axis=0)
        return dict(
            gain=small[layer, : 2 * width].reshape(2, width),
            packed=packed,
            mlp=lax.all_gather(mlp[layer], every, axis=0),
            kv_bias=small[layer, 2 * width :][None],
        )

    low_high, keyvalue, expand, shrink, residual = (
        pick(stack) for stack in (adapter_input, adapter_keyvalue, adapter_expand, adapter_shrink, adapter_residual)
    )
    def adapters(layer):
        return dict(
            low=low_high[layer, :, : 3 * r],
            high=low_high[layer, :, 3 * r :],
            q=at_rows(heads_part[layer, :r], 0, 3 * r),
            attend=at_rows(heads_part[layer, r : 2 * r], 0, 3 * r),
            q_bias=heads_part[layer, 2 * r : 2 * r + 1].astype(F32),
            kv=jnp.concatenate(
                [at_rows(keyvalue[layer, 0], r, 3 * r), at_rows(keyvalue[layer, 1], 2 * r, 3 * r)], axis=1
            ),
            expand=jnp.stack([at_rows(padded(expand[layer, i]), i * r, 2 * r) for i in range(2)]),
            shrink=padded(shrink[layer].T),
            res_one=at_rows(residual[layer, 0], 0, 3 * r),
            res_two=residual[layer, 1],
        )

    x = lax.dynamic_index_in_dim(inputs, core, 0, keepdims=False).astype(F32)
    cot = lax.dynamic_index_in_dim(cotangent, core, 0, keepdims=False).astype(F32)
    length = lax.dynamic_index_in_dim(lengths, core, 0, keepdims=False)
    own_id = lax.dynamic_index_in_dim(adapter_ids, core, 0, keepdims=False)
    first_slot = place * rows
    info = jnp.stack([first_slot, length]).astype(jnp.int32)
    tables = rotary_tables(first_slot, rows)
    slot_ids = first_slot + jnp.arange(rows, dtype=jnp.int32)

    w = [weights(layer) for layer in range(layers)]
    ad = [adapters(layer) for layer in range(layers)]
    outs, kept = [], []
    for layer in range(layers):
        middle, normed_two, attn_kept = attend_forward(x, w[layer], ad[layer], info, tables)
        shrunk, mlp_kept = mlp_forward(normed_two, w[layer], ad[layer])
        outs.append((middle + shrunk).astype(BF))
        kept.append((x, middle, attn_kept, mlp_kept))
        x = outs[-1].astype(F32)
    count = adapter_input.shape[1]
    pad_one = jnp.zeros((r, width - 2 * kv_half), F32)
    chosen_row = at_rows(
        jnp.pad((jnp.arange(count, dtype=jnp.int32) == own_id).astype(BF)[None], [(0, 0), (0, width - count)]), 0, 8
    )
    grad = cot * (slot_ids < length).astype(F32)[:, None]
    grads, gathered = [None] * layers, [None] * layers
    for layer in reversed(range(layers)):
        x, middle, attn_kept, mlp_kept = kept[layer]
        if layer < layers - 1:
            grad, whole_here = lax.optimization_barrier((grad, whole_here))
        dn2, g_high, g_expand, g_shrink, g_res_two = mlp_backward(grad.astype(BF), w[layer], ad[layer], mlp_kept)
        grad, g_low, g_res_one, g_q, g_attend, g_kv = attend_backward(
            x, middle, grad, dn2, w[layer], ad[layer], attn_kept, info, tables
        )
        grads[layer] = grad
        g_kv = jnp.concatenate([g_kv[r : 2 * r, :kv_half], g_kv[2 * r :, kv_half:], pad_one], axis=1)
        whole_here = jnp.concatenate(
            [g_low, g_high, g_res_one[:r], g_res_two, g_kv, g_q[:r], g_attend[:r]], axis=0
        ).astype(BF)
        if layer < layers - 1:
            whole_here, gathered[layer + 1] = lax.optimization_barrier((whole_here, gathered[layer + 1]))
        whole = lax.psum(whole_here, "tensor")
        mine = lax.dynamic_slice_in_dim(whole[8 * r :], place * q_cols, q_cols, 1)
        parts = jnp.concatenate([g_expand, g_shrink], axis=0).astype(BF)
        block = jnp.concatenate(
            [whole[: 8 * r], mine.reshape(-1, width), parts.reshape(-1, width), chosen_row], axis=0
        )
        gathered[layer] = lax.all_gather(block, ("section", "dp"), axis=0)
    layer_output = swap(jnp.stack(outs))
    input_grad = swap(jnp.stack(grads))

    block = jnp.where(core == 0, gathered[0], gathered[1])
    pick_matrix = block[:, -8, :count]
    total = jnp.einsum("sa,srw->arw", pick_matrix, block[:, :-8], preferred_element_type=F32)
    total = total * (1.0 / math.sqrt(tokens))
    q_rows = 2 * r * q_cols // width
    heads_sum = total[:, 8 * r : 8 * r + q_rows].reshape(count, 2 * r, q_cols)
    ff_sum = total[:, 8 * r + q_rows :].reshape(count, 3 * r, hidden + padding)[..., :hidden]
    kv_sum = total[:, 7 * r : 8 * r]
    return (
        layer_output[None],
        input_grad[None],
        jnp.swapaxes(total[:, : 5 * r], 1, 2)[None],
        heads_sum[:, :r][None],
        jnp.stack([kv_sum[..., :kv_half], kv_sum[..., kv_half : 2 * kv_half]], axis=1)[None],
        jnp.stack([ff_sum[:, :r], ff_sum[:, r : 2 * r]], axis=1)[None],
        jnp.swapaxes(heads_sum[:, r:], 1, 2)[None],
        jnp.swapaxes(ff_sum[:, 2 * r :], 1, 2)[None],
        jnp.stack([total[:, 5 * r : 6 * r], total[:, 6 * r : 7 * r]], axis=1)[None],
    )


def solution(mesh):
    placed = (
        P("dp", "tensor", None),
        P("dp"),
        P("dp"),
        P("dp", "tensor", None),
        P("section", None, None),
        P("section", "dp", "tensor"),
        P("section", "tensor"),
        P("section", None, "dp", None),
        P("section", None, None),
        P("section", "tensor", "dp"),
        P("section", None, "dp", "tensor"),
        P("section", "tensor", "dp"),
        P("section", None, None, None),
        P("section", None, None, "tensor"),
        P("section", None, None, None, None),
        P("section", None, None, None, "tensor"),
        P("section", None, "tensor", None),
        P("section", None, "tensor", None),
        P("section", None, None, None, None),
    )
    return jax.shard_map(
        local,
        mesh=mesh,
        in_specs=placed,
        out_specs=(
            P("section", "dp", "tensor", None),
            P("section", "dp", "tensor", None),
            P("section", None, None, None),
            P("section", None, None, "tensor"),
            P("section", None, None, None, None),
            P("section", None, None, None, "tensor"),
            P("section", None, "tensor", None),
            P("section", None, "tensor", None),
            P("section", None, None, None, None),
        ),
        check_vma=False,
    )
```

```python
from functools import partial
import math

import jax
import jax.numpy as jnp
from jax import lax
from jax.experimental import pallas as pl
from jax.experimental.pallas import tpu as pltpu
from jax.sharding import PartitionSpec as P

KV_HEADS = 2
HEAD_DIM = 128
RANK = 16
EPSILON = 1e-06
ROPE_BASE = 1000000.0
MASKED_SCORE = -1e30
CHUNKS = 4
LANES = 128
VMEM_LIMIT = 60 * 2**20
MESH = pl.DeviceIdType.MESH
BF = jnp.bfloat16
F32 = jnp.float32


def dot(a, b):
    return jnp.dot(a, b, preferred_element_type=F32)


def dot_t(a, b):
    return lax.dot_general(a, b, (((1,), (1,)), ((), ())), preferred_element_type=F32)


def t_dot(a, b):
    return lax.dot_general(a, b, (((0,), (0,)), ((), ())), preferred_element_type=F32)


def rotary_tables(first_slot, rows):
    half = HEAD_DIM // 2
    frequency = jnp.exp(-math.log(ROPE_BASE) * (2.0 * jnp.arange(half, dtype=F32) / HEAD_DIM))
    slots = (first_slot + jnp.arange(rows, dtype=jnp.int32)).astype(F32)
    angles = slots[:, None] * frequency[None, :]
    cos, sin = jnp.cos(angles), jnp.sin(angles)
    return jnp.concatenate([cos, cos], axis=1), jnp.concatenate([-sin, sin], axis=1)


B_INPUT, B_RES_ONE, B_RES_TWO, B_KV, B_MISC, B_FF, B_FF_TAIL, B_HEADS, B_ROWS = 0, 5, 6, 7, 8, 9, 12, 15, 18


def rows_of(first, count=1):
    return slice(first * RANK, (first + count) * RANK)


def pick_kernel(
    ids_ref, input_ref, res_ref, kv_ref, expand_ref, shrink_ref, query_ref, attend_ref, gain_ref, kvb_ref, qb_ref,
    out_ref, heads_ref,
):
    width = out_ref.shape[2]
    out_ref[0] = jnp.zeros(out_ref.shape[1:], BF)
    out_ref[0, rows_of(B_INPUT, 5)] = input_ref[0]
    out_ref[0, rows_of(B_RES_ONE, 2)] = res_ref[0]
    kv_half = kv_ref.shape[2]
    for i in range(2):
        out_ref[0, rows_of(B_KV), i * kv_half : (i + 1) * kv_half] = kv_ref[0, rows_of(i)]
    misc = rows_of(B_MISC).start
    out_ref[0, misc : misc + 2] = gain_ref[...]
    out_ref[0, misc + 2 : misc + 3, : 2 * kv_half] = kvb_ref[...]
    tail = expand_ref.shape[2] - width
    for i in range(3):
        part = expand_ref[0, rows_of(i)] if i < 2 else shrink_ref[0]
        out_ref[0, rows_of(B_FF + i)] = part[:, :width]
        out_ref[0, rows_of(B_FF_TAIL + i), :tail] = part[:, width:]
    heads_ref[0] = jnp.zeros(heads_ref.shape[1:], BF)
    heads_ref[0, rows_of(0)] = query_ref[0]
    heads_ref[0, rows_of(1)] = attend_ref[0]
    heads_ref[0, 2 * RANK : 2 * RANK + 1] = qb_ref[...]


def pick_adapters(ids, stacks, shared):
    count = ids.shape[0]
    width = stacks[0].shape[2]
    q_cols = stacks[5].shape[2]
    shapes = [(B_ROWS * RANK, width), (3 * RANK, q_cols)]
    return pl.pallas_call(
        pick_kernel,
        grid_spec=pltpu.PrefetchScalarGridSpec(
            num_scalar_prefetch=1,
            grid=(count,),
            in_specs=[pl.BlockSpec((1,) + a.shape[1:], lambda i, ids: (ids[i], 0, 0)) for a in stacks]
            + [pl.BlockSpec(a.shape, lambda i, ids: (0, 0)) for a in shared],
            out_specs=[pl.BlockSpec((1,) + a, lambda i, ids: (i, 0, 0)) for a in shapes],
        ),
        out_shape=[jax.ShapeDtypeStruct((count,) + a, BF) for a in shapes],
    )(ids, *stacks, *shared)


def spread_factors(bundle_ref, expand_ref, ash_ref):
    width = bundle_ref.shape[1]
    tail = ash_ref.shape[1] - width
    expand_ref[...] = jnp.zeros_like(expand_ref)
    for i in range(2):
        expand_ref[i, rows_of(i), :width] = bundle_ref[rows_of(B_FF + i)]
        expand_ref[i, rows_of(i), width:] = bundle_ref[rows_of(B_FF_TAIL + i), :tail]
    ash_ref[:, :width] = bundle_ref[rows_of(B_FF + 2)]
    ash_ref[:, width:] = bundle_ref[rows_of(B_FF_TAIL + 2), :tail]


def vspec():
    return pl.BlockSpec(memory_space=pltpu.VMEM)


def hspec():
    return pl.BlockSpec(memory_space=pl.ANY)


def line_barrier(me, line):
    barrier = pltpu.get_barrier_semaphore()

    @pl.when(me > 0)
    def _():
        pl.semaphore_signal(barrier, inc=1, device_id={"tensor": me - 1}, device_id_type=MESH)

    @pl.when(me < line - 1)
    def _():
        pl.semaphore_signal(barrier, inc=1, device_id={"tensor": me + 1}, device_id_type=MESH)

    pl.semaphore_wait(barrier, jnp.where(me > 0, 1, 0) + jnp.where(me < line - 1, 1, 0))


def within(c, chunks):
    return jnp.logical_and(c >= 0, c < chunks)


def line_exchange(line, chunks, gathered, partial_ref, from_left, from_right, own_out, sems, begin, work):
    ag_recv, ag_right, ag_left, r_recv, r_send, l_recv, l_send = sems
    me = lax.axis_index("tensor")

    def copy(ref, src, c, o, send, recv, side):
        return pltpu.make_async_remote_copy(
            src_ref=src.at[c, o],
            dst_ref=ref.at[c, o],
            send_sem=send.at[c, o],
            recv_sem=recv.at[c, o],
            device_id={"tensor": me + side},
            device_id_type=MESH,
        )

    def ag(c, o, side):
        return copy(gathered, gathered, c, o, ag_right if side > 0 else ag_left, ag_recv, side)

    def rs(c, o, side):
        if side > 0:
            return copy(from_left, partial_ref, c, o, r_send, r_recv, 1)
        return copy(from_right, partial_ref, c, o, l_send, l_recv, -1)

    has_left, has_right = me > 0, me < line - 1

    def step(s, carry):
        first = s + line - 1

        @pl.when(jnp.logical_and(within(first, chunks), has_right))
        def _():
            ag(first, me, 1).start()

        @pl.when(jnp.logical_and(within(first, chunks), has_left))
        def _():
            ag(first, me, -1).start()

        for d in range(1, line):
            c = s + line - 1 - d

            @pl.when(jnp.logical_and(within(c, chunks), me - d >= 0))
            def _():
                ag(c, me - d, 1).wait_recv()

                @pl.when(has_right)
                def _():
                    ag(c, me - d, 1).start()

            @pl.when(jnp.logical_and(within(c, chunks), me + d < line))
            def _():
                ag(c, me + d, -1).wait_recv()

                @pl.when(has_left)
                def _():
                    ag(c, me + d, -1).start()

        @pl.when(within(s, chunks))
        def _():
            work(s)

        for h in range(line):
            c = s - h

            @pl.when(jnp.logical_and(within(c, chunks), me == h))
            def _():
                for j in range(line - 1, h, -1):
                    if h > 0:
                        rs(c, j, 1).wait_recv()
                        partial_ref[c, j] = (
                            partial_ref[c, j].astype(F32) + from_left[c, j].astype(F32)
                        ).astype(BF)
                    if h < line - 1:
                        rs(c, j, 1).start()

            @pl.when(jnp.logical_and(within(c, chunks), me == line - 1 - h))
            def _():
                for j in range(line - 1 - h):
                    if h > 0:
                        rs(c, j, -1).wait_recv()
                        partial_ref[c, j] = (
                            partial_ref[c, j].astype(F32) + from_right[c, j].astype(F32)
                        ).astype(BF)
                    if h < line - 1:
                        rs(c, j, -1).start()

        last = s - (line - 1)

        @pl.when(within(last, chunks))
        def _():
            own_out[last] = partial_ref[last, me].astype(F32)

            @pl.when(has_left)
            def _():
                rs(last, me, 1).wait_recv()
                own_out[last] += from_left[last, me].astype(F32)

            @pl.when(has_right)
            def _():
                rs(last, me, -1).wait_recv()
                own_out[last] += from_right[last, me].astype(F32)

        return carry

    line_barrier(me, line)
    begin()
    lax.fori_loop(-(line - 1), chunks + line - 1, step, 0)

    def drain(c, carry):
        for o in range(line):

            @pl.when(jnp.logical_and(has_right, me >= o))
            def _():
                ag(c, o, 1).wait_send()

            @pl.when(jnp.logical_and(has_left, me <= o))
            def _():
                ag(c, o, -1).wait_send()

            @pl.when(me < o)
            def _():
                rs(c, o, 1).wait_send()

            @pl.when(me > o)
            def _():
                rs(c, o, -1).wait_send()

        return carry

    lax.fori_loop(0, chunks, drain, 0)


def exchange_scratch(line, chunks, rows, width):
    slots = (chunks, line, rows, width)
    return [pltpu.VMEM(slots, BF)] * 4 + [pltpu.SemaphoreType.DMA((chunks, line))] * 7


def ff_loads(packed, refs, wsem):
    halves, parts, _, rows, cols = packed.shape
    return [
        pltpu.make_async_copy(
            packed.at[h, p, i],
            ref.at[pl.ds(h * rows, rows), pl.ds(p * cols, cols)],
            wsem.at[i, h, p],
        )
        for i, ref in enumerate(refs)
        for h in range(halves)
        for p in range(parts)
    ]


def clear_tail(packed, refs):
    hidden = packed.shape[0] * packed.shape[3]
    for ref in refs:
        if ref.shape[0] > hidden:
            ref[hidden:] = jnp.zeros((ref.shape[0] - hidden, ref.shape[1]), BF)


def mlp_kernel(
    line, chunks, tile,
    n2_ref, packed, bundle_ref,
    out_ref, n2_out, gate_out, up_out,
    gathered, partial_ref, from_left, from_right, s0, s1, s2, s3, s4, s5, s6,
    wg, wu, ws, gate_st, up_st, acc, expand_ref, ash_ref, wsem, osem, nsem,
):
    rows, width = n2_ref.shape[1:]
    every = line * rows
    tiles = wg.shape[0] // tile
    high = bundle_ref[rows_of(B_INPUT + 3, 2)]
    res = bundle_ref[rows_of(B_RES_TWO)]
    me = lax.axis_index("tensor")
    loads = ff_loads(packed, (wg, wu, ws), wsem)

    def begin():
        for load in loads:
            load.start()
        clear_tail(packed, (wg, wu, ws))
        spread_factors(bundle_ref, expand_ref, ash_ref)
        for c in range(chunks):
            gathered[c, me] = n2_ref[c]

    def saves(c, slot):
        return (
            pltpu.make_async_copy(gate_st.at[slot], gate_out.at[c], osem.at[0, slot]),
            pltpu.make_async_copy(up_st.at[slot], up_out.at[c], osem.at[1, slot]),
        )

    def keep(c):
        return pltpu.make_async_copy(gathered.at[c], n2_out.at[c], nsem.at[c])

    def work(c):
        slot = c % 2

        @pl.when(c == 0)
        def _():
            for load in loads:
                load.wait()

        @pl.when(c >= 2)
        def _():
            for save in saves(c - 2, slot):
                save.wait()

        keep(c).start()
        x = gathered[c].reshape(every, width)
        er = dot_t(x, high).astype(BF)

        def one(f, rank):
            cols = pl.ds(pl.multiple_of(f * tile, tile), tile)
            gate = dot_t(x, wg[cols]) + dot(er, expand_ref[0, :, cols])
            up = dot_t(x, wu[cols]) + dot(er, expand_ref[1, :, cols])
            gate_st[slot, :, cols] = gate.astype(BF)
            up_st[slot, :, cols] = up.astype(BF)
            act = (gate * (1.0 / (1.0 + jnp.exp(-gate))) * up).astype(BF)
            now = dot(act, ws[cols])

            @pl.when(f == 0)
            def _():
                acc[...] = now

            @pl.when(f > 0)
            def _():
                acc[...] += now

            return rank + dot_t(act, ash_ref[:, cols])

        rank = lax.fori_loop(0, tiles, one, jnp.zeros((every, ash_ref.shape[0]), F32))
        total = acc[...] + dot(rank.astype(BF), res)
        partial_ref[c] = total.astype(BF).reshape(line, rows, width)
        for save in saves(c, slot):
            save.start()

    line_exchange(
        line, chunks, gathered, partial_ref, from_left, from_right, out_ref,
        (s0, s1, s2, s3, s4, s5, s6), begin, work,
    )
    for c in range(chunks):
        keep(c).wait()
    for c in range(max(chunks - 2, 0), chunks):
        for save in saves(c, c % 2):
            save.wait()


def ff_tile(hidden):
    return hidden // 3 if hidden % (3 * LANES) == 0 else LANES


def mlp_forward(n2, w):
    line = lax.axis_size("tensor")
    rows, width = n2.shape
    halves, groups, _, low_rows, _ = w["mlp"].shape
    hidden = halves * low_rows + -(halves * low_rows) % (2 * LANES)
    part = rows // CHUNKS
    every = line * part
    out, n2_all, gate, up = pl.pallas_call(
        partial(mlp_kernel, line, CHUNKS, ff_tile(hidden)),
        in_specs=[vspec(), hspec(), vspec()],
        out_specs=[vspec()] + [hspec()] * 3,
        out_shape=[
            jax.ShapeDtypeStruct((CHUNKS, part, width), F32),
            jax.ShapeDtypeStruct((CHUNKS, line, part, width), BF),
            jax.ShapeDtypeStruct((CHUNKS, every, hidden), BF),
            jax.ShapeDtypeStruct((CHUNKS, every, hidden), BF),
        ],
        scratch_shapes=exchange_scratch(line, CHUNKS, part, width)
        + [pltpu.VMEM((hidden, width), BF)] * 3
        + [pltpu.VMEM((2, every, hidden), BF)] * 2
        + [
            pltpu.VMEM((every, width), F32),
            pltpu.VMEM((2, 2 * RANK, hidden), BF),
            pltpu.VMEM((RANK, hidden), BF),
            pltpu.SemaphoreType.DMA((3, halves, groups)),
            pltpu.SemaphoreType.DMA((2, 2)),
            pltpu.SemaphoreType.DMA((CHUNKS,)),
        ],
        compiler_params=pltpu.CompilerParams(
            collective_id=0, has_side_effects=True, vmem_limit_bytes=VMEM_LIMIT
        ),
        cost_estimate=pl.CostEstimate(
            flops=6 * line * rows * width * hidden,
            bytes_accessed=6 * width * hidden + 4 * line * rows * hidden,
            transcendentals=line * rows * hidden,
        ),
    )(
        n2.reshape(CHUNKS, part, width), w["mlp"], w["bundle"],
    )
    return out.reshape(rows, width), (n2_all.reshape(CHUNKS, every, width), gate, up)


def mlp_back_kernel(
    line, chunks, tile,
    ds_ref, packed, n2_hbm, gate_in, up_in, bundle_ref,
    out_ref, whole_ref, parts_ref,
    gathered, partial_ref, from_left, from_right, s0, s1, s2, s3, s4, s5, s6,
    wg, wu, ws, gate_st, up_st, n2_st, acc, ghigh_ref, gexp_ref, gsh_ref, gres_ref, expand_ref, ash_ref, wsem, isem,
):
    rows, width = ds_ref.shape[1:]
    every = line * rows
    tiles = wg.shape[0] // tile
    high = bundle_ref[rows_of(B_INPUT + 3, 2)]
    res = bundle_ref[rows_of(B_RES_TWO)]
    me = lax.axis_index("tensor")
    loads = ff_loads(packed, (wg, wu, ws), wsem)

    def fetch(c):
        slot = c % 2
        return (
            pltpu.make_async_copy(gate_in.at[c], gate_st.at[slot], isem.at[0, slot]),
            pltpu.make_async_copy(up_in.at[c], up_st.at[slot], isem.at[1, slot]),
            pltpu.make_async_copy(n2_hbm.at[c], n2_st.at[slot], isem.at[2, slot]),
        )

    def begin():
        for load in loads:
            load.start()
        clear_tail(packed, (wg, wu, ws))
        spread_factors(bundle_ref, expand_ref, ash_ref)
        for one in fetch(0):
            one.start()
        for c in range(chunks):
            gathered[c, me] = ds_ref[c]
        for ref in (ghigh_ref, gexp_ref, gsh_ref, gres_ref):
            ref[...] = jnp.zeros_like(ref)

    def work(c):
        slot = c % 2

        @pl.when(c == 0)
        def _():
            for load in loads:
                load.wait()

        for one in fetch(c):
            one.wait()

        @pl.when(c + 1 < chunks)
        def _():
            for one in fetch(c + 1):
                one.start()

        ds = gathered[c].reshape(every, width)
        n2 = n2_st[slot]
        er = dot_t(n2, high).astype(BF)
        rank_in = dot_t(ds, res).astype(BF)

        def one(f, carry):
            rank_out, srank = carry
            cols = pl.ds(pl.multiple_of(f * tile, tile), tile)
            act_grad = dot_t(ds, ws[cols]) + dot(rank_in, ash_ref[:, cols])
            gate = gate_st[slot, :, cols].astype(F32)
            up = up_st[slot, :, cols].astype(F32)
            sig = 1.0 / (1.0 + jnp.exp(-gate))
            silu = gate * sig
            act = (silu * up).astype(BF)
            gate_grad = (act_grad * up * (sig + silu * (1.0 - sig))).astype(BF)
            up_grad = (act_grad * silu).astype(BF)
            now = dot(gate_grad, wg[cols]) + dot(up_grad, wu[cols])

            @pl.when(f == 0)
            def _():
                acc[...] = now

            @pl.when(f > 0)
            def _():
                acc[...] += now

            gexp_ref[0, :, cols] += t_dot(er, gate_grad)
            gexp_ref[1, :, cols] += t_dot(er, up_grad)
            gsh_ref[:, cols] += t_dot(rank_in, act)
            rank_out = rank_out + dot_t(gate_grad, expand_ref[0, :, cols])
            rank_out = rank_out + dot_t(up_grad, expand_ref[1, :, cols])
            return rank_out, srank + dot_t(act, ash_ref[:, cols])

        rank_out, srank = lax.fori_loop(
            0,
            tiles,
            one,
            (
                jnp.zeros((every, expand_ref.shape[1]), F32),
                jnp.zeros((every, ash_ref.shape[0]), F32),
            ),
        )
        rank_out = rank_out.astype(BF)
        total = acc[...] + dot(rank_out, high)
        partial_ref[c] = total.astype(BF).reshape(line, rows, width)
        ghigh_ref[...] += t_dot(rank_out, n2)
        gres_ref[...] += t_dot(srank.astype(BF), ds)

    line_exchange(
        line, chunks, gathered, partial_ref, from_left, from_right, out_ref,
        (s0, s1, s2, s3, s4, s5, s6), begin, work,
    )
    whole_ref[: 2 * RANK] = ghigh_ref[...].astype(BF)
    whole_ref[2 * RANK :] = gres_ref[...].astype(BF)
    extra = gsh_ref.shape[1] - width
    parts_ref[3 * RANK :, extra:] = jnp.zeros((3 * RANK, width - extra), BF)
    for i, part in enumerate((gexp_ref[0, :RANK], gexp_ref[1, RANK:], gsh_ref[...])):
        part = part.astype(BF)
        parts_ref[i * RANK : (i + 1) * RANK] = part[:, :width]
        parts_ref[(3 + i) * RANK : (4 + i) * RANK, :extra] = part[:, width:]


def mlp_backward(ds, w, saved):
    n2_all, gate, up = saved
    line = lax.axis_size("tensor")
    rows, width = ds.shape
    halves, groups, _, low_rows, _ = w["mlp"].shape
    hidden = halves * low_rows + -(halves * low_rows) % (2 * LANES)
    part = rows // CHUNKS
    every = line * part
    out, whole, parts = pl.pallas_call(
        partial(mlp_back_kernel, line, CHUNKS, ff_tile(hidden)),
        in_specs=[vspec()] + [hspec()] * 4 + [vspec()],
        out_specs=[vspec()] * 3,
        out_shape=[
            jax.ShapeDtypeStruct((CHUNKS, part, width), F32),
            jax.ShapeDtypeStruct((3 * RANK, width), BF),
            jax.ShapeDtypeStruct((6 * RANK, width), BF),
        ],
        scratch_shapes=exchange_scratch(line, CHUNKS, part, width)
        + [pltpu.VMEM((hidden, width), BF)] * 3
        + [pltpu.VMEM((2, every, hidden), BF)] * 2
        + [
            pltpu.VMEM((2, every, width), BF),
            pltpu.VMEM((every, width), F32),
            pltpu.VMEM((2 * RANK, width), F32),
            pltpu.VMEM((2, 2 * RANK, hidden), F32),
            pltpu.VMEM((RANK, hidden), F32),
            pltpu.VMEM((RANK, width), F32),
            pltpu.VMEM((2, 2 * RANK, hidden), BF),
            pltpu.VMEM((RANK, hidden), BF),
            pltpu.SemaphoreType.DMA((3, halves, groups)),
            pltpu.SemaphoreType.DMA((3, 2)),
        ],
        compiler_params=pltpu.CompilerParams(
            collective_id=1, has_side_effects=True, vmem_limit_bytes=VMEM_LIMIT
        ),
        cost_estimate=pl.CostEstimate(
            flops=6 * line * rows * width * hidden,
            bytes_accessed=6 * width * hidden + 4 * line * rows * hidden,
            transcendentals=line * rows * hidden,
        ),
    )(
        ds.reshape(CHUNKS, part, width), w["mlp"], n2_all, gate, up, w["bundle"],
    )
    return out.reshape(rows, width), whole, parts


def gather_kernel(
    line, peers,
    attn, bundles, heads,
    first_out, second_out, bundle_out,
    own_sem, z_recv, z_right, z_left, dp_recv, dp_send, core_recv, core_send, side_recv, side_send, side_own,
):
    me, spot, core = lax.axis_index("tensor"), lax.axis_index("dp"), lax.axis_index("section")
    other = 1 - core
    has_left, has_right = me > 0, me < line - 1
    barrier = pltpu.get_barrier_semaphore()

    def greet(**where):
        pl.semaphore_signal(barrier, inc=1, device_id=where, device_id_type=MESH)

    @pl.when(has_left)
    def _():
        greet(tensor=me - 1)

    @pl.when(has_right)
    def _():
        greet(tensor=me + 1)

    greet(section=other)
    for k in range(1, peers):
        greet(dp=lax.rem(spot + k, peers))
    pl.semaphore_wait(barrier, jnp.where(has_left, 1, 0) + jnp.where(has_right, 1, 0) + peers)

    mine = spot * 2 + core
    plain, part = bundles.shape[1] - heads.shape[1], heads.shape[2]

    def head_place(layer, o):
        return bundle_out.at[layer, pl.ds(plain, heads.shape[1]), pl.ds(o * part, part)]

    def places(o):
        return first_out.at[mine, o], second_out.at[o], head_place(core, o), head_place(other, o)

    sides = [
        pltpu.make_async_remote_copy(
            src_ref=src,
            dst_ref=dst,
            send_sem=side_send.at[i],
            recv_sem=side_recv.at[i],
            device_id={"section": other},
            device_id_type=MESH,
        )
        for i, (src, dst) in enumerate(
            (
                (bundles.at[other, pl.ds(0, plain)], bundle_out.at[core, pl.ds(0, plain)]),
                (heads.at[other], head_place(core, me)),
            )
        )
    ]
    side_keep = pltpu.make_async_copy(
        bundles.at[core, pl.ds(0, plain)], bundle_out.at[core, pl.ds(0, plain)], side_own
    )
    sources = (attn.at[0], attn.at[1], heads.at[core], head_place(other, me))
    keeps = [
        pltpu.make_async_copy(src, dst, own_sem.at[i]) for i, (src, dst) in enumerate(zip(sources[:3], places(me)))
    ]

    def remote(src, dst, send, recv, **where):
        return pltpu.make_async_remote_copy(
            src_ref=src, dst_ref=dst, send_sem=send, recv_sem=recv, device_id=where, device_id_type=MESH
        )

    def along(i, o, side, own):
        dst = places(o)[i]
        return remote(
            sources[i] if own else dst,
            dst,
            (z_right if side > 0 else z_left).at[i, o],
            z_recv.at[i, o],
            tensor=me + side,
        )

    def to_peer(k, o, own):
        dst = first_out.at[mine, o]
        return remote(
            attn.at[0] if own else dst, dst, dp_send.at[k, o], dp_recv.at[spot, o], dp=lax.rem(spot + k, peers)
        )

    def to_core(p, o, own):
        dst = first_out.at[p * 2 + core, o]
        return remote(attn.at[0] if own else dst, dst, core_send.at[p, o], core_recv.at[p, o], section=other)

    def spread_first(o, own):
        for k in range(1, peers):
            to_peer(k, o, own).start()
        to_core(spot, o, own).start()

    for side in sides:
        side.start()
    for i in range(4):
        if i == 3:
            sides[1].wait_recv()

        @pl.when(has_right)
        def _():
            along(i, me, 1, True).start()

        @pl.when(has_left)
        def _():
            along(i, me, -1, True).start()

        if i == 0:
            spread_first(me, True)
    for keep in keeps:
        keep.start()
    side_keep.start()
    for d in range(1, line):
        for i in range(4):

            @pl.when(me >= d)
            def _():
                along(i, me - d, 1, False).wait_recv()

                @pl.when(has_right)
                def _():
                    along(i, me - d, 1, False).start()

                if i == 0:
                    spread_first(me - d, False)

            @pl.when(me + d < line)
            def _():
                along(i, me + d, -1, False).wait_recv()

                @pl.when(has_left)
                def _():
                    along(i, me + d, -1, False).start()

                if i == 0:
                    spread_first(me + d, False)

    def pass_on(o, carry):
        for k in range(1, peers):
            p = lax.rem(spot + peers - k, peers)
            remote(
                first_out.at[p * 2 + core, o], first_out.at[p * 2 + core, o], dp_send.at[k, o], dp_recv.at[p, o], dp=p
            ).wait_recv()
            to_core(p, o, False).start()
        return carry

    lax.fori_loop(0, line, pass_on, 0)

    def finish(o, carry):
        for k in range(1, peers):
            to_peer(k, o, False).wait_send()
        for p in range(peers):
            to_core(p, o, False).wait_send()
            remote(
                first_out.at[p * 2 + other, o],
                first_out.at[p * 2 + other, o],
                core_send.at[p, o],
                core_recv.at[p, o],
                section=other,
            ).wait_recv()
        for i in range(4):

            @pl.when(jnp.logical_and(has_right, me >= o))
            def _():
                along(i, o, 1, False).wait_send()

            @pl.when(jnp.logical_and(has_left, me <= o))
            def _():
                along(i, o, -1, False).wait_send()

        return carry

    lax.fori_loop(0, line, finish, 0)
    for keep in keeps:
        keep.wait()
    side_keep.wait()
    sides[0].wait_recv()
    for side in sides:
        side.wait_send()


def gather_first(attn, bundles, heads):
    line, peers = lax.axis_size("tensor"), lax.axis_size("dp")
    cores, part, cols = attn.shape
    dma = pltpu.SemaphoreType.DMA
    return pl.pallas_call(
        partial(gather_kernel, line, peers),
        in_specs=[hspec()] * 3,
        out_specs=[hspec()] * 3,
        out_shape=[
            jax.ShapeDtypeStruct((peers * cores, line, part, cols), BF),
            jax.ShapeDtypeStruct((line, part, cols), BF),
            jax.ShapeDtypeStruct(bundles.shape, BF),
        ],
        scratch_shapes=[dma((3,)), dma((4, line)), dma((4, line)), dma((4, line))]
        + [dma((peers, line))] * 4
        + [dma((2,)), dma((2,)), dma],
        compiler_params=pltpu.CompilerParams(
            collective_id=4, has_side_effects=True, vmem_limit_bytes=VMEM_LIMIT
        ),
    )(attn, bundles, heads)


def rotated(x, cos, sin):
    return x * cos + pltpu.roll(x, HEAD_DIM // 2, 1) * sin


def head_cols(h):
    return pl.ds(pl.multiple_of(h * HEAD_DIM, HEAD_DIM), HEAD_DIM)


def weight_loads(packed, wq, wo, wkv, wsem):
    cols, kv_cols = wq.shape[-1], wkv.shape[-1]
    loads = []
    for i, (ref, start, size) in enumerate(((wkv, 2 * cols, kv_cols), (wq, 0, cols), (wo, cols, cols))):
        loads.append(
            [
                pltpu.make_async_copy(packed.at[:, t, :, pl.ds(start, size)], ref.at[t], wsem.at[i, t])
                for t in range(ref.shape[0])
            ]
        )
    return loads


def flat(ref, t):
    groups, rows, cols = ref.shape[1:]
    return ref[t].reshape(groups * rows, cols)


def allowed_keys(info_ref, block, keys, rows):
    row = info_ref[0] + lax.broadcasted_iota(jnp.int32, (1, rows), 1)
    last = jnp.minimum(row, info_ref[1] - 1)
    return block * keys + lax.broadcasted_iota(jnp.int32, (keys, rows), 0) <= last


def one_way_barrier(me, line, side):
    barrier = pltpu.get_barrier_semaphore()
    first, last = (0, line - 1) if side > 0 else (line - 1, 0)

    @pl.when(me != first)
    def _():
        pl.semaphore_signal(barrier, inc=1, device_id={"tensor": me - side}, device_id_type=MESH)

    @pl.when(me != last)
    def _():
        pl.semaphore_wait(barrier, 1)


def spread_qkv(bundle_ref, bq_ref, bkv_ref):
    kv_half = bkv_ref.shape[1] // 2
    bq_ref[...] = jnp.zeros_like(bq_ref)
    bkv_ref[...] = jnp.zeros_like(bkv_ref)
    bq_ref[rows_of(0)] = bundle_ref[rows_of(B_HEADS)]
    for i in range(2):
        span = slice(i * kv_half, (i + 1) * kv_half)
        bkv_ref[rows_of(1 + i), span] = bundle_ref[rows_of(B_KV), span]


def kv_exchange(me, line, kvbuf, recv, send):
    def move(o):
        return pltpu.make_async_remote_copy(
            src_ref=kvbuf.at[o],
            dst_ref=kvbuf.at[o],
            send_sem=send.at[o],
            recv_sem=recv.at[o],
            device_id={"tensor": me + 1},
            device_id_type=MESH,
        )

    return move


def attend_kernel(
    line, group,
    info_ref, x_ref, bundle_ref, cos_ref, sin_ref, packed,
    mid_ref, n2_ref, normed_ref, lowr_ref, rank_ref, q_ref, kv_out, attended_ref, log_ref,
    wq, wo, wkv, kvbuf, acc, peak, total, bq_ref, bkv_ref, wsem, recv, send, ksem,
):
    rows, width = x_ref.shape
    heads = width // HEAD_DIM
    cols = wq.shape[-1]
    kv_cols = wkv.shape[-1]
    scale = HEAD_DIM**-0.5
    me = lax.axis_index("tensor")
    one_way_barrier(me, line, 1)
    kv_loads, q_loads, o_loads = weight_loads(packed, wq, wo, wkv, wsem)
    for load in kv_loads + q_loads + o_loads:
        load.start()
    move = kv_exchange(me, line, kvbuf, recv, send)
    spread_qkv(bundle_ref, bq_ref, bkv_ref)
    misc = bundle_ref[rows_of(B_MISC)].astype(F32)
    q_bias = bundle_ref[rows_of(B_HEADS + 2)].astype(F32)[:1]
    low_in = bundle_ref[rows_of(B_INPUT, 3)]
    x = x_ref[...].astype(F32)
    inverse = lax.rsqrt(jnp.mean(x * x, axis=-1, keepdims=True) + EPSILON)
    normed_ref[...] = (x * inverse * misc[0:1]).astype(BF)
    low = dot_t(normed_ref[...], low_in).astype(BF)
    cos, sin = cos_ref[...], sin_ref[...]
    for load in kv_loads:
        load.wait()
    for t in range(line):
        span = slice(t * kv_cols, (t + 1) * kv_cols)
        kv = dot(normed_ref[...], flat(wkv, t)) + misc[2:3, span] + dot(low, bkv_ref[:, span])
        for h in range(kv_cols // HEAD_DIM):
            at = t * kv_cols + h * HEAD_DIM
            one = kv[:, h * HEAD_DIM : (h + 1) * HEAD_DIM]
            if at < KV_HEADS * HEAD_DIM:
                one = rotated(one, cos, sin)
            kvbuf[me, :, at : at + HEAD_DIM] = one.astype(BF)

    @pl.when(me < line - 1)
    def _():
        move(me).start()

    for load in q_loads:
        load.wait()
    for t in range(line):
        span = slice(t * cols, (t + 1) * cols)
        q = dot(normed_ref[...], flat(wq, t)) + q_bias[:, span] + dot(low, bq_ref[:, span])
        for h in range(cols // HEAD_DIM):
            at = t * cols + h * HEAD_DIM
            q_ref[:, at : at + HEAD_DIM] = rotated(
                q[:, h * HEAD_DIM : (h + 1) * HEAD_DIM], cos, sin
            ).astype(BF)
    acc[...] = jnp.zeros_like(acc)
    total[...] = jnp.zeros_like(total)
    peak[...] = jnp.full_like(peak, MASKED_SCORE)

    def block(o):
        allowed = allowed_keys(info_ref, o, rows, rows)

        def one(h, carry):
            kv_head = h // group
            k = kvbuf[o, :, head_cols(kv_head)]
            v = kvbuf[o, :, head_cols(KV_HEADS + kv_head)]
            scores = jnp.where(allowed, dot_t(k, q_ref[:, head_cols(h)]) * scale, MASKED_SCORE)
            top = jnp.maximum(peak[h], jnp.max(scores, axis=0, keepdims=True))
            soft = jnp.exp(scores - top)
            shift = jnp.exp(peak[h] - top)
            total[h] = total[h] * shift + jnp.sum(soft, axis=0, keepdims=True)
            acc[h] = acc[h] * shift + t_dot(v, soft.astype(BF))
            peak[h] = top
            return carry

        lax.fori_loop(0, heads, one, 0)

    for d in range(line):

        @pl.when(me >= d)
        def _():
            if d > 0:
                move(me - d).wait_recv()

                @pl.when(me < line - 1)
                def _():
                    move(me - d).start()

            block(me - d)

    keep = pltpu.make_async_copy(kvbuf, kv_out, ksem)
    keep.start()
    for h in range(heads):
        attended_ref[:, h * HEAD_DIM : (h + 1) * HEAD_DIM] = (acc[h] * (1.0 / total[h])).T.astype(BF)
        log_ref[h] = peak[h] + jnp.log(total[h])
    rank = dot_t(attended_ref[...], bundle_ref[rows_of(B_HEADS + 1)]).astype(BF)
    lowr_ref[...] = low
    rank_ref[...] = rank
    middle = x_ref[...].astype(F32) + dot(rank, bundle_ref[rows_of(B_RES_ONE)])
    for load in o_loads:
        load.wait()
    for t in range(line):
        middle = middle + dot_t(attended_ref[:, t * cols : (t + 1) * cols], flat(wo, t))
    mid_ref[...] = middle
    inverse = lax.rsqrt(jnp.mean(middle * middle, axis=-1, keepdims=True) + EPSILON)
    n2_ref[...] = (middle * inverse * misc[1:2]).astype(BF)
    keep.wait()
    for o in range(line):

        @pl.when(jnp.logical_and(me < line - 1, me >= o))
        def _():
            move(o).wait_send()


def attend_forward(x, w, info, tables):
    line = lax.axis_size("tensor")
    rows, width = x.shape
    heads = width // HEAD_DIM
    kv_width = 2 * KV_HEADS * HEAD_DIM
    groups, low_rows = w["packed"].shape[0], w["packed"].shape[2]
    outs = pl.pallas_call(
        partial(attend_kernel, line, heads // KV_HEADS),
        in_specs=[pl.BlockSpec(memory_space=pltpu.SMEM)] + [vspec()] * 4 + [hspec()],
        out_specs=[vspec()] * 6 + [hspec()] + [vspec()] * 2,
        out_shape=[
            jax.ShapeDtypeStruct((rows, width), F32),
            jax.ShapeDtypeStruct((rows, width), BF),
            jax.ShapeDtypeStruct((rows, width), BF),
            jax.ShapeDtypeStruct((rows, 3 * RANK), BF),
            jax.ShapeDtypeStruct((rows, RANK), BF),
            jax.ShapeDtypeStruct((rows, width), BF),
            jax.ShapeDtypeStruct((line, rows, kv_width), BF),
            jax.ShapeDtypeStruct((rows, width), BF),
            jax.ShapeDtypeStruct((heads, 1, rows), F32),
        ],
        scratch_shapes=[
            pltpu.VMEM((line, groups, low_rows, width // line), BF),
            pltpu.VMEM((line, groups, low_rows, width // line), BF),
            pltpu.VMEM((line, groups, low_rows, kv_width // line), BF),
            pltpu.VMEM((line, rows, kv_width), BF),
            pltpu.VMEM((heads, HEAD_DIM, rows), F32),
            pltpu.VMEM((heads, 1, rows), F32),
            pltpu.VMEM((heads, 1, rows), F32),
            pltpu.VMEM((3 * RANK, width), BF),
            pltpu.VMEM((3 * RANK, kv_width), BF),
            pltpu.SemaphoreType.DMA((3, line)),
            pltpu.SemaphoreType.DMA((line,)),
            pltpu.SemaphoreType.DMA((line,)),
            pltpu.SemaphoreType.DMA,
        ],
        compiler_params=pltpu.CompilerParams(
            collective_id=2, has_side_effects=True, vmem_limit_bytes=VMEM_LIMIT
        ),
        cost_estimate=pl.CostEstimate(
            flops=4 * rows * width * width * 2, bytes_accessed=5 * width * width, transcendentals=0
        ),
    )(
        info, x, w["bundle"], tables[0], tables[1], w["packed"],
    )
    return outs[0], outs[1], outs[2:]


def attend_back_kernel(
    line, group,
    info_ref, x_ref, mid_ref, dy_ref, dn2_ref, bundle_ref, cos_ref, sin_ref,
    normed_ref, lowr_ref, rank_ref, q_ref, kv_ref, attended_ref, log_ref, packed,
    dx_ref, dx_low_ref, grads_ref,
    wq, wo, wkv, do_ref, dq_acc, dq_ref, dkv_acc, partial_ref, from_right, delta, bq_ref, bkv_ref, wsem, recv, send,
):
    rows, width = x_ref.shape
    heads = width // HEAD_DIM
    cols = wq.shape[-1]
    kv_cols = wkv.shape[-1]
    kv_half = KV_HEADS * HEAD_DIM
    scale = HEAD_DIM**-0.5
    me = lax.axis_index("tensor")
    one_way_barrier(me, line, -1)
    kv_loads, q_loads, o_loads = weight_loads(packed, wq, wo, wkv, wsem)
    for load in o_loads + q_loads + kv_loads:
        load.start()

    def move(o):
        return pltpu.make_async_remote_copy(
            src_ref=partial_ref.at[o],
            dst_ref=from_right.at[o],
            send_sem=send.at[o],
            recv_sem=recv.at[o],
            device_id={"tensor": me - 1},
            device_id_type=MESH,
        )

    def through_norm(values, gain, grad_out):
        inverse = lax.rsqrt(jnp.mean(values * values, axis=-1, keepdims=True) + EPSILON)
        weighted = gain * grad_out
        return inverse * weighted - inverse * inverse * inverse * values * jnp.mean(
            weighted * values, axis=-1, keepdims=True
        )

    spread_qkv(bundle_ref, bq_ref, bkv_ref)
    misc = bundle_ref[rows_of(B_MISC)].astype(F32)
    att = bundle_ref[rows_of(B_HEADS + 1)]
    middle_grad = dy_ref[...].astype(F32) + through_norm(mid_ref[...], misc[1:2], dn2_ref[...])
    dx_ref[...] = middle_grad
    branch_grad = middle_grad.astype(BF)
    low, rank = lowr_ref[...], rank_ref[...]
    rank_grad = dot_t(branch_grad, bundle_ref[rows_of(B_RES_ONE)]).astype(BF)
    grads_ref[3 * RANK : 4 * RANK] = t_dot(rank, branch_grad).astype(BF)
    grads_ref[6 * RANK :] = t_dot(rank_grad, attended_ref[...]).astype(BF)
    for load in o_loads:
        load.wait()
    for t in range(line):
        span = slice(t * cols, (t + 1) * cols)
        do_ref[:, span] = (dot(branch_grad, flat(wo, t)) + dot(rank_grad, att[:, span])).astype(BF)
    for h in range(heads):
        span = slice(h * HEAD_DIM, (h + 1) * HEAD_DIM)
        both = do_ref[:, span].astype(F32) * attended_ref[:, span].astype(F32)
        delta[h] = jnp.sum(both.T, axis=0, keepdims=True)
    dq_acc[...] = jnp.zeros_like(dq_acc)

    def block(o):
        allowed = allowed_keys(info_ref, o, rows, rows)
        dkv_acc[...] = jnp.zeros_like(dkv_acc)

        def one(h, carry):
            kv_head = h // group
            k = kv_ref[o, :, head_cols(kv_head)]
            v = kv_ref[o, :, head_cols(KV_HEADS + kv_head)]
            q = q_ref[:, head_cols(h)]
            do = do_ref[:, head_cols(h)]
            scores = dot_t(k, q) * scale - log_ref[h]
            soft = jnp.exp(jnp.where(allowed, scores, MASKED_SCORE))
            grad = (soft * (dot_t(v, do) - delta[h])).astype(BF)
            dq_acc[h] += t_dot(k, grad)
            dkv_acc[:, head_cols(kv_head)] += dot(grad, q) * scale
            dkv_acc[:, head_cols(KV_HEADS + kv_head)] += dot(soft.astype(BF), do)
            return carry

        lax.fori_loop(0, heads, one, 0)
        partial_ref[o] = dkv_acc[...].astype(BF)

    for s in range(2 * line - 1):
        if s < line:

            @pl.when(me >= s)
            def _():
                block(s)

        for h in range(line - 1):
            o = s - h
            if 0 <= o < line - 1 - h:

                @pl.when(me == line - 1 - h)
                def _():
                    if h > 0:
                        move(o).wait_recv()
                        partial_ref[o] = (partial_ref[o].astype(F32) + from_right[o].astype(F32)).astype(BF)
                    move(o).start()

    cos, sin = cos_ref[...], -sin_ref[...]
    for h in range(heads):
        dq_ref[:, h * HEAD_DIM : (h + 1) * HEAD_DIM] = rotated(dq_acc[h].T * scale, cos, sin).astype(BF)
    dq = dq_ref[...]
    grads_ref[5 * RANK : 6 * RANK] = t_dot(low, dq)[:RANK].astype(BF)
    low_grad = dot_t(dq, bq_ref[...])
    for load in q_loads:
        load.wait()
    normed_grad = dot_t(dq[:, :cols], flat(wq, 0))
    for t in range(1, line):
        normed_grad = normed_grad + dot_t(dq[:, t * cols : (t + 1) * cols], flat(wq, t))
    dkv_acc[...] = partial_ref[me].astype(F32)

    @pl.when(me < line - 1)
    def _():
        move(me).wait_recv()
        dkv_acc[...] += from_right[me].astype(F32)

    for h in range(KV_HEADS):
        span = slice(h * HEAD_DIM, (h + 1) * HEAD_DIM)
        dkv_acc[:, span] = rotated(dkv_acc[:, span], cos, sin)
    dkv = dkv_acc[...].astype(BF)
    kv_grad = t_dot(low, dkv).astype(BF)
    grads_ref[4 * RANK : 5 * RANK, :kv_half] = kv_grad[RANK : 2 * RANK, :kv_half]
    grads_ref[4 * RANK : 5 * RANK, kv_half : 2 * kv_half] = kv_grad[2 * RANK :, kv_half:]
    grads_ref[4 * RANK : 5 * RANK, 2 * kv_half :] = jnp.zeros((RANK, width - 2 * kv_half), BF)
    low_grad = (low_grad + dot_t(dkv, bkv_ref[...])).astype(BF)
    grads_ref[: 3 * RANK] = t_dot(low_grad, normed_ref[...]).astype(BF)
    for load in kv_loads:
        load.wait()
    for t in range(line):
        normed_grad = normed_grad + dot_t(dkv[:, t * kv_cols : (t + 1) * kv_cols], flat(wkv, t))
    normed_grad = normed_grad + dot(low_grad, bundle_ref[rows_of(B_INPUT, 3)])
    dx = dx_ref[...] + through_norm(x_ref[...].astype(F32), misc[0:1], normed_grad)
    dx_ref[...] = dx
    dx_low_ref[...] = dx.astype(BF)
    for o in range(line - 1):

        @pl.when(me > o)
        def _():
            move(o).wait_send()


def attend_backward(x, middle, dy, dn2, w, kept, info, tables):
    line = lax.axis_size("tensor")
    rows, width = x.shape
    heads = width // HEAD_DIM
    kv_width = 2 * KV_HEADS * HEAD_DIM
    groups, low_rows = w["packed"].shape[0], w["packed"].shape[2]
    return pl.pallas_call(
        partial(attend_back_kernel, line, heads // KV_HEADS),
        in_specs=[pl.BlockSpec(memory_space=pltpu.SMEM)] + [vspec()] * 14 + [hspec()],
        out_specs=[vspec()] * 3,
        out_shape=[
            jax.ShapeDtypeStruct((rows, width), F32),
            jax.ShapeDtypeStruct((rows, width), BF),
            jax.ShapeDtypeStruct((7 * RANK, width), BF),
        ],
        scratch_shapes=[
            pltpu.VMEM((line, groups, low_rows, width // line), BF),
            pltpu.VMEM((line, groups, low_rows, width // line), BF),
            pltpu.VMEM((line, groups, low_rows, kv_width // line), BF),
            pltpu.VMEM((rows, width), BF),
            pltpu.VMEM((heads, HEAD_DIM, rows), F32),
            pltpu.VMEM((rows, width), BF),
            pltpu.VMEM((rows, kv_width), F32),
            pltpu.VMEM((line, rows, kv_width), BF),
            pltpu.VMEM((line, rows, kv_width), BF),
            pltpu.VMEM((heads, 1, rows), F32),
            pltpu.VMEM((3 * RANK, width), BF),
            pltpu.VMEM((3 * RANK, kv_width), BF),
            pltpu.SemaphoreType.DMA((3, line)),
            pltpu.SemaphoreType.DMA((line,)),
            pltpu.SemaphoreType.DMA((line,)),
        ],
        compiler_params=pltpu.CompilerParams(
            collective_id=3 if dy.dtype == F32 else 5, has_side_effects=True, vmem_limit_bytes=VMEM_LIMIT
        ),
        cost_estimate=pl.CostEstimate(
            flops=4 * rows * width * width * 2, bytes_accessed=5 * width * width, transcendentals=0
        ),
    )(
        info, x, middle, dy, dn2, w["bundle"], tables[0], tables[1], *kept, w["packed"],
    )


def total_kernel(
    scale, hidden, q_cols,
    first, second,
    input_ref, query_ref, kv_ref, expand_ref, attend_ref, shrink_ref, res_ref,
    block, sem,
):
    r = RANK
    a = pl.program_id(0)
    core = lax.axis_index("section")
    width = block.shape[2]
    extra = hidden - width
    pad = extra + -hidden % (2 * LANES)

    @pl.when(jnp.logical_and(a == 0, core == 0))
    def _():
        load = pltpu.make_async_copy(first, block, sem)
        load.start()
        load.wait()

    @pl.when(jnp.logical_and(a == 0, core != 0))
    def _():
        load = pltpu.make_async_copy(second, block, sem)
        load.start()
        load.wait()

    lane = lax.broadcasted_iota(jnp.int32, (1, LANES), 1)
    weights = []
    for i in range(block.shape[0]):
        names = block[i, 13 * r : 14 * r, pad : pad + LANES][:1].astype(F32)
        weights.append(jnp.sum(jnp.where(lane == a, names, 0.0), axis=1, keepdims=True) * scale)

    def summed(row, rows, col, cols):
        result = weights[0] * block[0, row : row + rows, col : col + cols].astype(F32)
        for i in range(1, block.shape[0]):
            result = result + weights[i] * block[i, row : row + rows, col : col + cols].astype(F32)
        return result

    step = 4 * LANES
    for col in range(0, width, step):
        input_ref[0, :, col : col + step] = summed(0, 5 * r, col, step)
    res_ref[0, 0] = summed(5 * r, r, 0, width)
    res_ref[0, 1] = summed(6 * r, r, 0, width)
    kv = summed(7 * r, r, 0, 2 * kv_ref.shape[3])
    kv_ref[0, 0] = kv[:, : kv_ref.shape[3]]
    kv_ref[0, 1] = kv[:, kv_ref.shape[3] :]
    for i in range(2):
        expand_ref[0, i, :, :width] = summed((8 + i) * r, r, 0, width)
        expand_ref[0, i, :, width:] = summed((11 + i) * r, r, 0, pad)[:, :extra]
    shrink_ref[0, :, :width] = summed(10 * r, r, 0, width)
    shrink_ref[0, :, width:] = summed(13 * r, r, 0, pad)[:, :extra]
    query_ref[0] = summed(11 * r, r, pad, q_cols)
    attend_ref[0] = summed(12 * r, r, pad, q_cols)


def total_by_adapter(first, second, count, scale, hidden, q_cols, kv_half):
    width = first.shape[2]
    r = RANK
    shapes = [
        (5 * r, width), (r, q_cols), (2, r, kv_half), (2, r, hidden), (r, q_cols), (r, hidden), (2, r, width),
    ]
    return pl.pallas_call(
        partial(total_kernel, scale, hidden, q_cols),
        grid=(count,),
        in_specs=[hspec()] * 2,
        out_specs=[pl.BlockSpec((1,) + s, lambda a, n=len(s): (a,) + (0,) * n) for s in shapes],
        out_shape=[jax.ShapeDtypeStruct((count,) + s, F32) for s in shapes],
        scratch_shapes=[pltpu.VMEM(first.shape, BF), pltpu.SemaphoreType.DMA],
        compiler_params=pltpu.CompilerParams(vmem_limit_bytes=VMEM_LIMIT),
    )(first, second)


def swap(pair):
    return lax.all_to_all(pair, "section", split_axis=0, concat_axis=0, tiled=True)


def local(
    inputs,
    lengths,
    adapter_ids,
    cotangent,
    norm_gain,
    query_weight,
    query_bias,
    keyvalue_weight,
    keyvalue_bias,
    output_weight,
    expand_weight,
    shrink_weight,
    adapter_input,
    adapter_query,
    adapter_keyvalue,
    adapter_expand,
    adapter_attend,
    adapter_shrink,
    adapter_residual,
):
    layers = lax.axis_size("section")
    tensor = lax.axis_size("tensor")
    core = lax.axis_index("section")
    place = lax.axis_index("tensor")
    rows, width = inputs.shape[1:]
    tokens = layers * rows * tensor * lax.axis_size("dp")
    kv_half = KV_HEADS * HEAD_DIM
    hidden = expand_weight.shape[3]
    r = RANK

    def turned(stack):
        return jnp.swapaxes(stack[0], 1, 2)

    def lined(stack):
        return stack[0].reshape(stack.shape[1], -1, stack.shape[-1])

    bundles, heads = pick_adapters(
        adapter_ids,
        (
            turned(adapter_input), lined(adapter_residual), lined(adapter_keyvalue), lined(adapter_expand),
            turned(adapter_shrink), adapter_query[0], turned(adapter_attend),
        ),
        (norm_gain[0], keyvalue_bias.reshape(1, -1), query_bias),
    )

    ff = jnp.concatenate(
        [m.reshape(layers, 1, hidden // layers, m.shape[1]) for m in (*turned(expand_weight), shrink_weight[0])],
        axis=1,
    )
    ff = swap(ff)
    kv = jnp.concatenate([keyvalue_weight[0, 0], keyvalue_weight[0, 1]], axis=1)
    kv_cols = kv.shape[1] // tensor
    kv = lax.dynamic_slice_in_dim(kv, place * kv_cols, kv_cols, 1)
    attn = jnp.concatenate([query_weight[0], output_weight[0].T, kv], axis=1)
    q_cols = query_weight.shape[2]
    attn = swap(attn.reshape(layers, attn.shape[0] // layers, attn.shape[1]))
    first_attn, line_attn, bundle = gather_first(attn, bundles, heads)

    def weights(layer):
        packed = first_attn if layer == 0 else lax.all_gather(line_attn, ("dp", "section"), axis=0)
        mlp = lax.all_gather(ff[layer], ("section", "dp"), axis=0)
        mlp = mlp.reshape(layers, -1, *mlp.shape[1:])
        if mlp.shape[4] % LANES:
            mlp = jnp.moveaxis(mlp, 1, 3)
            mlp = mlp.reshape(layers, 1, *mlp.shape[1:3], width)
        return dict(packed=packed, mlp=mlp, bundle=bundle[layer])

    x = lax.dynamic_index_in_dim(inputs, core, 0, keepdims=False)
    cot = lax.dynamic_index_in_dim(cotangent, core, 0, keepdims=False)
    length = lax.dynamic_index_in_dim(lengths, core, 0, keepdims=False)
    own_id = lax.dynamic_index_in_dim(adapter_ids, core, 0, keepdims=False)
    first_slot = place * rows
    info = jnp.stack([first_slot, length]).astype(jnp.int32)
    tables = rotary_tables(first_slot, rows)
    slot_ids = first_slot + jnp.arange(rows, dtype=jnp.int32)

    w = [weights(layer) for layer in range(layers)]
    outs, kept = [], []
    for layer in range(layers):
        middle, normed_two, attn_kept = attend_forward(x, w[layer], info, tables)
        shrunk, mlp_kept = mlp_forward(normed_two, w[layer])
        outs.append((middle + shrunk).astype(BF))
        kept.append((x, middle, attn_kept, mlp_kept))
        x = outs[-1]
    count = adapter_input.shape[1]
    extra = hidden + -hidden % (2 * LANES) - width
    names = (jnp.arange(LANES, dtype=jnp.int32) == own_id).astype(BF)[None]

    def gather_block(attn_part, whole, parts):
        mine = lax.dynamic_slice_in_dim(attn_part[5 * r :], place * q_cols, q_cols, 1)
        parts = lax.dynamic_update_slice(parts, mine, (3 * r, extra))
        parts = lax.dynamic_update_slice(parts, names, (5 * r, extra))
        block = jnp.concatenate(
            [attn_part[: 3 * r], whole[: 2 * r], attn_part[3 * r : 4 * r], whole[2 * r :], attn_part[4 * r : 5 * r]]
            + [parts],
            axis=0,
        )
        return lax.all_gather(block, ("section", "dp"), axis=0)

    grad = low_grad = jnp.where((slot_ids < length)[:, None], cot, jnp.zeros_like(cot))
    grads, gathered = [None] * layers, [None] * layers
    for layer in reversed(range(layers)):
        x, middle, attn_kept, mlp_kept = kept[layer]
        if layer < layers - 1:
            low_grad, here = lax.optimization_barrier((low_grad, here))
        dn2, whole, parts = mlp_backward(low_grad, w[layer], mlp_kept)
        if layer < layers - 1:
            total, dn2 = lax.optimization_barrier((total, dn2))
            gathered[layer + 1] = gather_block(*total, last_parts)
        grad, low_grad, attn_part = attend_backward(x, middle, grad, dn2, w[layer], attn_kept, info, tables)
        grads[layer] = grad
        here = (attn_part, whole)
        if layer < layers - 1:
            here, gathered[layer + 1] = lax.optimization_barrier((here, gathered[layer + 1]))
        total = lax.psum(here, "tensor")
        last_parts = parts
    gathered[0] = gather_block(*total, parts)
    layer_output = swap(jnp.stack(outs))
    input_grad = swap(jnp.stack(grads))
    totals = total_by_adapter(
        gathered[0], gathered[1], count, 1.0 / math.sqrt(tokens), hidden, q_cols, kv_half
    )
    turned = (0, 4, 5)
    totals = [jnp.swapaxes(total, 1, 2) if i in turned else total for i, total in enumerate(totals)]
    return (layer_output[None], input_grad[None]) + tuple(total[None] for total in totals)


def solution(mesh):
    placed = (
        P("dp", "tensor", None),
        P("dp"),
        P("dp"),
        P("dp", "tensor", None),
        P("section", None, None),
        P("section", "dp", "tensor"),
        P("section", "tensor"),
        P("section", None, "dp", None),
        P("section", None, None),
        P("section", "tensor", "dp"),
        P("section", None, "dp", "tensor"),
        P("section", "tensor", "dp"),
        P("section", None, None, None),
        P("section", None, None, "tensor"),
        P("section", None, None, None, None),
        P("section", None, None, None, "tensor"),
        P("section", None, "tensor", None),
        P("section", None, "tensor", None),
        P("section", None, None, None, None),
    )
    return jax.shard_map(
        local,
        mesh=mesh,
        in_specs=placed,
        out_specs=(
            P("section", "dp", "tensor", None),
            P("section", "dp", "tensor", None),
            P("section", None, None, None),
            P("section", None, None, "tensor"),
            P("section", None, None, None, None),
            P("section", None, None, None, "tensor"),
            P("section", None, "tensor", None),
            P("section", None, "tensor", None),
            P("section", None, None, None, None),
        ),
        check_vma=False,
    )
```

```python
from functools import partial
import math

import jax
import jax.numpy as jnp
from jax import lax
from jax.experimental import pallas as pl
from jax.experimental.pallas import tpu as pltpu
from jax.sharding import PartitionSpec as P

KV_HEADS = 2
HEAD_DIM = 128
RANK = 16
EPSILON = 1e-06
ROPE_BASE = 1000000.0
MASKED_SCORE = -1e30
CHUNKS = 4
LANES = 128
VMEM_LIMIT = 60 * 2**20
MESH = pl.DeviceIdType.MESH
BF = jnp.bfloat16
F32 = jnp.float32


def dot(a, b):
    return jnp.dot(a, b, preferred_element_type=F32)


def dot_t(a, b):
    return lax.dot_general(a, b, (((1,), (1,)), ((), ())), preferred_element_type=F32)


def t_dot(a, b):
    return lax.dot_general(a, b, (((0,), (0,)), ((), ())), preferred_element_type=F32)


def rotary_tables(first_slot, rows):
    half = HEAD_DIM // 2
    frequency = jnp.exp(-math.log(ROPE_BASE) * (2.0 * jnp.arange(half, dtype=F32) / HEAD_DIM))
    slots = (first_slot + jnp.arange(rows, dtype=jnp.int32)).astype(F32)
    angles = slots[:, None] * frequency[None, :]
    cos, sin = jnp.cos(angles), jnp.sin(angles)
    return jnp.concatenate([cos, cos], axis=1), jnp.concatenate([-sin, sin], axis=1)


B_INPUT, B_RES_ONE, B_RES_TWO, B_KV, B_MISC, B_FF, B_FF_TAIL, B_HEADS, B_ROWS = 0, 5, 6, 7, 8, 9, 12, 15, 18


def rows_of(first, count=1):
    return slice(first * RANK, (first + count) * RANK)


def pick_kernel(
    ids_ref, input_ref, res_ref, kv_ref, expand_ref, shrink_ref, query_ref, attend_ref, gain_ref, kvb_ref, qb_ref,
    out_ref, heads_ref,
):
    width = out_ref.shape[2]
    out_ref[0] = jnp.zeros(out_ref.shape[1:], BF)
    out_ref[0, rows_of(B_INPUT, 5)] = input_ref[0]
    out_ref[0, rows_of(B_RES_ONE, 2)] = res_ref[0]
    kv_half = kv_ref.shape[2]
    for i in range(2):
        out_ref[0, rows_of(B_KV), i * kv_half : (i + 1) * kv_half] = kv_ref[0, rows_of(i)]
    misc = rows_of(B_MISC).start
    out_ref[0, misc : misc + 2] = gain_ref[...]
    out_ref[0, misc + 2 : misc + 3, : 2 * kv_half] = kvb_ref[...]
    tail = expand_ref.shape[2] - width
    for i in range(3):
        part = expand_ref[0, rows_of(i)] if i < 2 else shrink_ref[0]
        out_ref[0, rows_of(B_FF + i)] = part[:, :width]
        out_ref[0, rows_of(B_FF_TAIL + i), :tail] = part[:, width:]
    heads_ref[0] = jnp.zeros(heads_ref.shape[1:], BF)
    heads_ref[0, rows_of(0)] = query_ref[0]
    heads_ref[0, rows_of(1)] = attend_ref[0]
    heads_ref[0, 2 * RANK : 2 * RANK + 1] = qb_ref[...]


def pick_adapters(ids, stacks, shared):
    count = ids.shape[0]
    width = stacks[0].shape[2]
    q_cols = stacks[5].shape[2]
    shapes = [(B_ROWS * RANK, width), (3 * RANK, q_cols)]
    return pl.pallas_call(
        pick_kernel,
        grid_spec=pltpu.PrefetchScalarGridSpec(
            num_scalar_prefetch=1,
            grid=(count,),
            in_specs=[pl.BlockSpec((1,) + a.shape[1:], lambda i, ids: (ids[i], 0, 0)) for a in stacks]
            + [pl.BlockSpec(a.shape, lambda i, ids: (0, 0)) for a in shared],
            out_specs=[pl.BlockSpec((1,) + a, lambda i, ids: (i, 0, 0)) for a in shapes],
        ),
        out_shape=[jax.ShapeDtypeStruct((count,) + a, BF) for a in shapes],
    )(ids, *stacks, *shared)


def spread_factors(bundle_ref, expand_ref, ash_ref):
    width = bundle_ref.shape[1]
    tail = ash_ref.shape[1] - width
    expand_ref[...] = jnp.zeros_like(expand_ref)
    for i in range(2):
        expand_ref[i, rows_of(i), :width] = bundle_ref[rows_of(B_FF + i)]
        expand_ref[i, rows_of(i), width:] = bundle_ref[rows_of(B_FF_TAIL + i), :tail]
    ash_ref[:, :width] = bundle_ref[rows_of(B_FF + 2)]
    ash_ref[:, width:] = bundle_ref[rows_of(B_FF_TAIL + 2), :tail]


def vspec():
    return pl.BlockSpec(memory_space=pltpu.VMEM)


def hspec():
    return pl.BlockSpec(memory_space=pl.ANY)


def line_barrier(me, line):
    barrier = pltpu.get_barrier_semaphore()

    @pl.when(me > 0)
    def _():
        pl.semaphore_signal(barrier, inc=1, device_id={"tensor": me - 1}, device_id_type=MESH)

    @pl.when(me < line - 1)
    def _():
        pl.semaphore_signal(barrier, inc=1, device_id={"tensor": me + 1}, device_id_type=MESH)

    pl.semaphore_wait(barrier, jnp.where(me > 0, 1, 0) + jnp.where(me < line - 1, 1, 0))


def within(c, chunks):
    return jnp.logical_and(c >= 0, c < chunks)


def line_exchange(line, chunks, gathered, partial_ref, from_left, from_right, own_out, sems, begin, work):
    ag_recv, ag_right, ag_left, r_recv, r_send, l_recv, l_send = sems
    me = lax.axis_index("tensor")

    def copy(ref, src, c, o, send, recv, side):
        return pltpu.make_async_remote_copy(
            src_ref=src.at[c, o],
            dst_ref=ref.at[c, o],
            send_sem=send.at[c, o],
            recv_sem=recv.at[c, o],
            device_id={"tensor": me + side},
            device_id_type=MESH,
        )

    def ag(c, o, side):
        return copy(gathered, gathered, c, o, ag_right if side > 0 else ag_left, ag_recv, side)

    def rs(c, o, side):
        if side > 0:
            return copy(from_left, partial_ref, c, o, r_send, r_recv, 1)
        return copy(from_right, partial_ref, c, o, l_send, l_recv, -1)

    has_left, has_right = me > 0, me < line - 1

    def step(s, carry):
        first = s + line - 1

        @pl.when(jnp.logical_and(within(first, chunks), has_right))
        def _():
            ag(first, me, 1).start()

        @pl.when(jnp.logical_and(within(first, chunks), has_left))
        def _():
            ag(first, me, -1).start()

        for d in range(1, line):
            c = s + line - 1 - d

            @pl.when(jnp.logical_and(within(c, chunks), me - d >= 0))
            def _():
                ag(c, me - d, 1).wait_recv()

                @pl.when(has_right)
                def _():
                    ag(c, me - d, 1).start()

            @pl.when(jnp.logical_and(within(c, chunks), me + d < line))
            def _():
                ag(c, me + d, -1).wait_recv()

                @pl.when(has_left)
                def _():
                    ag(c, me + d, -1).start()

        @pl.when(within(s, chunks))
        def _():
            work(s)

        for h in range(line):
            c = s - h

            @pl.when(jnp.logical_and(within(c, chunks), me == h))
            def _():
                for j in range(line - 1, h, -1):
                    if h > 0:
                        rs(c, j, 1).wait_recv()
                        partial_ref[c, j] = (
                            partial_ref[c, j].astype(F32) + from_left[c, j].astype(F32)
                        ).astype(BF)
                    if h < line - 1:
                        rs(c, j, 1).start()

            @pl.when(jnp.logical_and(within(c, chunks), me == line - 1 - h))
            def _():
                for j in range(line - 1 - h):
                    if h > 0:
                        rs(c, j, -1).wait_recv()
                        partial_ref[c, j] = (
                            partial_ref[c, j].astype(F32) + from_right[c, j].astype(F32)
                        ).astype(BF)
                    if h < line - 1:
                        rs(c, j, -1).start()

        last = s - (line - 1)

        @pl.when(within(last, chunks))
        def _():
            own_out[last] = partial_ref[last, me].astype(F32)

            @pl.when(has_left)
            def _():
                rs(last, me, 1).wait_recv()
                own_out[last] += from_left[last, me].astype(F32)

            @pl.when(has_right)
            def _():
                rs(last, me, -1).wait_recv()
                own_out[last] += from_right[last, me].astype(F32)

        return carry

    line_barrier(me, line)
    begin()
    lax.fori_loop(-(line - 1), chunks + line - 1, step, 0)

    def drain(c, carry):
        for o in range(line):

            @pl.when(jnp.logical_and(has_right, me >= o))
            def _():
                ag(c, o, 1).wait_send()

            @pl.when(jnp.logical_and(has_left, me <= o))
            def _():
                ag(c, o, -1).wait_send()

            @pl.when(me < o)
            def _():
                rs(c, o, 1).wait_send()

            @pl.when(me > o)
            def _():
                rs(c, o, -1).wait_send()

        return carry

    lax.fori_loop(0, chunks, drain, 0)


def exchange_scratch(line, chunks, rows, width):
    slots = (chunks, line, rows, width)
    return [pltpu.VMEM(slots, BF)] * 4 + [pltpu.SemaphoreType.DMA((chunks, line))] * 7


def ff_loads(packed, refs, wsem):
    halves, parts, _, rows, cols = packed.shape
    return [
        pltpu.make_async_copy(
            packed.at[h, p, i],
            ref.at[pl.ds(h * rows, rows), pl.ds(p * cols, cols)],
            wsem.at[i, h, p],
        )
        for i, ref in enumerate(refs)
        for h in range(halves)
        for p in range(parts)
    ]


def clear_tail(packed, refs):
    hidden = packed.shape[0] * packed.shape[3]
    for ref in refs:
        if ref.shape[0] > hidden:
            ref[hidden:] = jnp.zeros((ref.shape[0] - hidden, ref.shape[1]), BF)


def mlp_kernel(
    line, chunks, tile,
    n2_ref, packed, bundle_ref,
    out_ref, n2_out, gate_out, up_out,
    gathered, partial_ref, from_left, from_right, s0, s1, s2, s3, s4, s5, s6,
    wg, wu, ws, gate_st, up_st, acc, expand_ref, ash_ref, wsem, osem, nsem,
):
    rows, width = n2_ref.shape[1:]
    every = line * rows
    tiles = wg.shape[0] // tile
    high = bundle_ref[rows_of(B_INPUT + 3, 2)]
    res = bundle_ref[rows_of(B_RES_TWO)]
    me = lax.axis_index("tensor")
    loads = ff_loads(packed, (wg, wu, ws), wsem)

    def begin():
        for load in loads:
            load.start()
        clear_tail(packed, (wg, wu, ws))
        spread_factors(bundle_ref, expand_ref, ash_ref)
        for c in range(chunks):
            gathered[c, me] = n2_ref[c]

    def saves(c, slot):
        return (
            pltpu.make_async_copy(gate_st.at[slot], gate_out.at[c], osem.at[0, slot]),
            pltpu.make_async_copy(up_st.at[slot], up_out.at[c], osem.at[1, slot]),
        )

    def keep(c):
        return pltpu.make_async_copy(gathered.at[c], n2_out.at[c], nsem.at[c])

    def work(c):
        slot = c % 2

        @pl.when(c == 0)
        def _():
            for load in loads:
                load.wait()

        @pl.when(c >= 2)
        def _():
            for save in saves(c - 2, slot):
                save.wait()

        keep(c).start()
        x = gathered[c].reshape(every, width)
        er = dot_t(x, high).astype(BF)

        def one(f, rank):
            cols = pl.ds(pl.multiple_of(f * tile, tile), tile)
            gate = dot_t(x, wg[cols]) + dot(er, expand_ref[0, :, cols])
            up = dot_t(x, wu[cols]) + dot(er, expand_ref[1, :, cols])
            gate_st[slot, :, cols] = gate.astype(BF)
            up_st[slot, :, cols] = up.astype(BF)
            act = (gate * (1.0 / (1.0 + jnp.exp(-gate))) * up).astype(BF)
            now = dot(act, ws[cols])

            @pl.when(f == 0)
            def _():
                acc[...] = now

            @pl.when(f > 0)
            def _():
                acc[...] += now

            return rank + dot_t(act, ash_ref[:, cols])

        rank = lax.fori_loop(0, tiles, one, jnp.zeros((every, ash_ref.shape[0]), F32))
        total = acc[...] + dot(rank.astype(BF), res)
        partial_ref[c] = total.astype(BF).reshape(line, rows, width)
        for save in saves(c, slot):
            save.start()

    line_exchange(
        line, chunks, gathered, partial_ref, from_left, from_right, out_ref,
        (s0, s1, s2, s3, s4, s5, s6), begin, work,
    )
    for c in range(chunks):
        keep(c).wait()
    for c in range(max(chunks - 2, 0), chunks):
        for save in saves(c, c % 2):
            save.wait()


def ff_tile(hidden):
    return hidden // 3 if hidden % (3 * LANES) == 0 else LANES


def mlp_forward(n2, w):
    line = lax.axis_size("tensor")
    rows, width = n2.shape
    halves, groups, _, low_rows, _ = w["mlp"].shape
    hidden = halves * low_rows + -(halves * low_rows) % (2 * LANES)
    part = rows // CHUNKS
    every = line * part
    out, n2_all, gate, up = pl.pallas_call(
        partial(mlp_kernel, line, CHUNKS, ff_tile(hidden)),
        in_specs=[vspec(), hspec(), vspec()],
        out_specs=[vspec()] + [hspec()] * 3,
        out_shape=[
            jax.ShapeDtypeStruct((CHUNKS, part, width), F32),
            jax.ShapeDtypeStruct((CHUNKS, line, part, width), BF),
            jax.ShapeDtypeStruct((CHUNKS, every, hidden), BF),
            jax.ShapeDtypeStruct((CHUNKS, every, hidden), BF),
        ],
        scratch_shapes=exchange_scratch(line, CHUNKS, part, width)
        + [pltpu.VMEM((hidden, width), BF)] * 3
        + [pltpu.VMEM((2, every, hidden), BF)] * 2
        + [
            pltpu.VMEM((every, width), F32),
            pltpu.VMEM((2, 2 * RANK, hidden), BF),
            pltpu.VMEM((RANK, hidden), BF),
            pltpu.SemaphoreType.DMA((3, halves, groups)),
            pltpu.SemaphoreType.DMA((2, 2)),
            pltpu.SemaphoreType.DMA((CHUNKS,)),
        ],
        compiler_params=pltpu.CompilerParams(
            collective_id=0, has_side_effects=True, vmem_limit_bytes=VMEM_LIMIT
        ),
        cost_estimate=pl.CostEstimate(
            flops=6 * line * rows * width * hidden,
            bytes_accessed=6 * width * hidden + 4 * line * rows * hidden,
            transcendentals=line * rows * hidden,
        ),
    )(
        n2.reshape(CHUNKS, part, width), w["mlp"], w["bundle"],
    )
    return out.reshape(rows, width), (n2_all.reshape(CHUNKS, every, width), gate, up)


def mlp_back_kernel(
    line, chunks, tile,
    ds_ref, packed, n2_hbm, gate_in, up_in, bundle_ref,
    out_ref, whole_ref, parts_ref,
    gathered, partial_ref, from_left, from_right, s0, s1, s2, s3, s4, s5, s6,
    wg, wu, ws, gate_st, up_st, n2_st, acc, ghigh_ref, gexp_ref, gsh_ref, gres_ref, expand_ref, ash_ref, wsem, isem,
):
    rows, width = ds_ref.shape[1:]
    every = line * rows
    tiles = wg.shape[0] // tile
    high = bundle_ref[rows_of(B_INPUT + 3, 2)]
    res = bundle_ref[rows_of(B_RES_TWO)]
    me = lax.axis_index("tensor")
    loads = ff_loads(packed, (wg, wu, ws), wsem)

    def fetch(c):
        slot = c % 2
        return (
            pltpu.make_async_copy(gate_in.at[c], gate_st.at[slot], isem.at[0, slot]),
            pltpu.make_async_copy(up_in.at[c], up_st.at[slot], isem.at[1, slot]),
            pltpu.make_async_copy(n2_hbm.at[c], n2_st.at[slot], isem.at[2, slot]),
        )

    def begin():
        for load in loads:
            load.start()
        clear_tail(packed, (wg, wu, ws))
        spread_factors(bundle_ref, expand_ref, ash_ref)
        for one in fetch(0):
            one.start()
        for c in range(chunks):
            gathered[c, me] = ds_ref[c]
        for ref in (ghigh_ref, gexp_ref, gsh_ref, gres_ref):
            ref[...] = jnp.zeros_like(ref)

    def work(c):
        slot = c % 2

        @pl.when(c == 0)
        def _():
            for load in loads:
                load.wait()

        for one in fetch(c):
            one.wait()

        @pl.when(c + 1 < chunks)
        def _():
            for one in fetch(c + 1):
                one.start()

        ds = gathered[c].reshape(every, width)
        n2 = n2_st[slot]
        er = dot_t(n2, high).astype(BF)
        rank_in = dot_t(ds, res).astype(BF)

        def one(f, carry):
            rank_out, srank = carry
            cols = pl.ds(pl.multiple_of(f * tile, tile), tile)
            act_grad = dot_t(ds, ws[cols]) + dot(rank_in, ash_ref[:, cols])
            gate = gate_st[slot, :, cols].astype(F32)
            up = up_st[slot, :, cols].astype(F32)
            sig = 1.0 / (1.0 + jnp.exp(-gate))
            silu = gate * sig
            act = (silu * up).astype(BF)
            gate_grad = (act_grad * up * (sig + silu * (1.0 - sig))).astype(BF)
            up_grad = (act_grad * silu).astype(BF)
            now = dot(gate_grad, wg[cols]) + dot(up_grad, wu[cols])

            @pl.when(f == 0)
            def _():
                acc[...] = now

            @pl.when(f > 0)
            def _():
                acc[...] += now

            gexp_ref[0, :, cols] += t_dot(er, gate_grad)
            gexp_ref[1, :, cols] += t_dot(er, up_grad)
            gsh_ref[:, cols] += t_dot(rank_in, act)
            rank_out = rank_out + dot_t(gate_grad, expand_ref[0, :, cols])
            rank_out = rank_out + dot_t(up_grad, expand_ref[1, :, cols])
            return rank_out, srank + dot_t(act, ash_ref[:, cols])

        rank_out, srank = lax.fori_loop(
            0,
            tiles,
            one,
            (
                jnp.zeros((every, expand_ref.shape[1]), F32),
                jnp.zeros((every, ash_ref.shape[0]), F32),
            ),
        )
        rank_out = rank_out.astype(BF)
        total = acc[...] + dot(rank_out, high)
        partial_ref[c] = total.astype(BF).reshape(line, rows, width)
        ghigh_ref[...] += t_dot(rank_out, n2)
        gres_ref[...] += t_dot(srank.astype(BF), ds)

    line_exchange(
        line, chunks, gathered, partial_ref, from_left, from_right, out_ref,
        (s0, s1, s2, s3, s4, s5, s6), begin, work,
    )
    whole_ref[: 2 * RANK] = ghigh_ref[...].astype(BF)
    whole_ref[2 * RANK :] = gres_ref[...].astype(BF)
    extra = gsh_ref.shape[1] - width
    parts_ref[3 * RANK :, extra:] = jnp.zeros((3 * RANK, width - extra), BF)
    for i, part in enumerate((gexp_ref[0, :RANK], gexp_ref[1, RANK:], gsh_ref[...])):
        part = part.astype(BF)
        parts_ref[i * RANK : (i + 1) * RANK] = part[:, :width]
        parts_ref[(3 + i) * RANK : (4 + i) * RANK, :extra] = part[:, width:]


def mlp_backward(ds, w, saved):
    n2_all, gate, up = saved
    line = lax.axis_size("tensor")
    rows, width = ds.shape
    halves, groups, _, low_rows, _ = w["mlp"].shape
    hidden = halves * low_rows + -(halves * low_rows) % (2 * LANES)
    part = rows // CHUNKS
    every = line * part
    out, whole, parts = pl.pallas_call(
        partial(mlp_back_kernel, line, CHUNKS, ff_tile(hidden)),
        in_specs=[vspec()] + [hspec()] * 4 + [vspec()],
        out_specs=[vspec()] * 3,
        out_shape=[
            jax.ShapeDtypeStruct((CHUNKS, part, width), F32),
            jax.ShapeDtypeStruct((3 * RANK, width), BF),
            jax.ShapeDtypeStruct((6 * RANK, width), BF),
        ],
        scratch_shapes=exchange_scratch(line, CHUNKS, part, width)
        + [pltpu.VMEM((hidden, width), BF)] * 3
        + [pltpu.VMEM((2, every, hidden), BF)] * 2
        + [
            pltpu.VMEM((2, every, width), BF),
            pltpu.VMEM((every, width), F32),
            pltpu.VMEM((2 * RANK, width), F32),
            pltpu.VMEM((2, 2 * RANK, hidden), F32),
            pltpu.VMEM((RANK, hidden), F32),
            pltpu.VMEM((RANK, width), F32),
            pltpu.VMEM((2, 2 * RANK, hidden), BF),
            pltpu.VMEM((RANK, hidden), BF),
            pltpu.SemaphoreType.DMA((3, halves, groups)),
            pltpu.SemaphoreType.DMA((3, 2)),
        ],
        compiler_params=pltpu.CompilerParams(
            collective_id=1, has_side_effects=True, vmem_limit_bytes=VMEM_LIMIT
        ),
        cost_estimate=pl.CostEstimate(
            flops=6 * line * rows * width * hidden,
            bytes_accessed=6 * width * hidden + 4 * line * rows * hidden,
            transcendentals=line * rows * hidden,
        ),
    )(
        ds.reshape(CHUNKS, part, width), w["mlp"], n2_all, gate, up, w["bundle"],
    )
    return out.reshape(rows, width), whole, parts


def gather_kernel(
    line, peers,
    attn, bundles, heads,
    first_out, second_out, bundle_out,
    own_sem, z_recv, z_right, z_left, dp_recv, dp_send, core_recv, core_send, side_recv, side_send, side_own,
):
    me, spot, core = lax.axis_index("tensor"), lax.axis_index("dp"), lax.axis_index("section")
    other = 1 - core
    has_left, has_right = me > 0, me < line - 1
    barrier = pltpu.get_barrier_semaphore()

    def greet(**where):
        pl.semaphore_signal(barrier, inc=1, device_id=where, device_id_type=MESH)

    @pl.when(has_left)
    def _():
        greet(tensor=me - 1)

    @pl.when(has_right)
    def _():
        greet(tensor=me + 1)

    greet(section=other)
    for k in range(1, peers):
        greet(dp=lax.rem(spot + k, peers))
    pl.semaphore_wait(barrier, jnp.where(has_left, 1, 0) + jnp.where(has_right, 1, 0) + peers)

    mine = spot * 2 + core
    plain, part = bundles.shape[1] - heads.shape[1], heads.shape[2]

    def head_place(layer, o):
        return bundle_out.at[layer, pl.ds(plain, heads.shape[1]), pl.ds(o * part, part)]

    def places(o):
        return first_out.at[mine, o], second_out.at[o], head_place(core, o), head_place(other, o)

    sides = [
        pltpu.make_async_remote_copy(
            src_ref=src,
            dst_ref=dst,
            send_sem=side_send.at[i],
            recv_sem=side_recv.at[i],
            device_id={"section": other},
            device_id_type=MESH,
        )
        for i, (src, dst) in enumerate(
            (
                (bundles.at[other, pl.ds(0, plain)], bundle_out.at[core, pl.ds(0, plain)]),
                (heads.at[other], head_place(core, me)),
            )
        )
    ]
    side_keep = pltpu.make_async_copy(
        bundles.at[core, pl.ds(0, plain)], bundle_out.at[core, pl.ds(0, plain)], side_own
    )
    sources = (attn.at[0], attn.at[1], heads.at[core], head_place(other, me))
    keeps = [
        pltpu.make_async_copy(src, dst, own_sem.at[i]) for i, (src, dst) in enumerate(zip(sources[:3], places(me)))
    ]

    def remote(src, dst, send, recv, **where):
        return pltpu.make_async_remote_copy(
            src_ref=src, dst_ref=dst, send_sem=send, recv_sem=recv, device_id=where, device_id_type=MESH
        )

    def along(i, o, side, own):
        dst = places(o)[i]
        return remote(
            sources[i] if own else dst,
            dst,
            (z_right if side > 0 else z_left).at[i, o],
            z_recv.at[i, o],
            tensor=me + side,
        )

    def to_peer(k, o, own):
        dst = first_out.at[mine, o]
        return remote(
            attn.at[0] if own else dst, dst, dp_send.at[k, o], dp_recv.at[spot, o], dp=lax.rem(spot + k, peers)
        )

    def to_core(p, o, own):
        dst = first_out.at[p * 2 + core, o]
        return remote(attn.at[0] if own else dst, dst, core_send.at[p, o], core_recv.at[p, o], section=other)

    def spread_first(o, own):
        for k in range(1, peers):
            to_peer(k, o, own).start()
        to_core(spot, o, own).start()

    for side in sides:
        side.start()
    for i in range(4):
        if i == 3:
            sides[1].wait_recv()

        @pl.when(has_right)
        def _():
            along(i, me, 1, True).start()

        @pl.when(has_left)
        def _():
            along(i, me, -1, True).start()

        if i == 0:
            spread_first(me, True)
    for keep in keeps:
        keep.start()
    side_keep.start()
    for d in range(1, line):
        for i in range(4):

            @pl.when(me >= d)
            def _():
                along(i, me - d, 1, False).wait_recv()

                @pl.when(has_right)
                def _():
                    along(i, me - d, 1, False).start()

                if i == 0:
                    spread_first(me - d, False)

            @pl.when(me + d < line)
            def _():
                along(i, me + d, -1, False).wait_recv()

                @pl.when(has_left)
                def _():
                    along(i, me + d, -1, False).start()

                if i == 0:
                    spread_first(me + d, False)

    def pass_on(o, carry):
        for k in range(1, peers):
            p = lax.rem(spot + peers - k, peers)
            remote(
                first_out.at[p * 2 + core, o], first_out.at[p * 2 + core, o], dp_send.at[k, o], dp_recv.at[p, o], dp=p
            ).wait_recv()
            to_core(p, o, False).start()
        return carry

    lax.fori_loop(0, line, pass_on, 0)

    def finish(o, carry):
        for k in range(1, peers):
            to_peer(k, o, False).wait_send()
        for p in range(peers):
            to_core(p, o, False).wait_send()
            remote(
                first_out.at[p * 2 + other, o],
                first_out.at[p * 2 + other, o],
                core_send.at[p, o],
                core_recv.at[p, o],
                section=other,
            ).wait_recv()
        for i in range(4):

            @pl.when(jnp.logical_and(has_right, me >= o))
            def _():
                along(i, o, 1, False).wait_send()

            @pl.when(jnp.logical_and(has_left, me <= o))
            def _():
                along(i, o, -1, False).wait_send()

        return carry

    lax.fori_loop(0, line, finish, 0)
    for keep in keeps:
        keep.wait()
    side_keep.wait()
    sides[0].wait_recv()
    for side in sides:
        side.wait_send()


def gather_first(attn, bundles, heads):
    line, peers = lax.axis_size("tensor"), lax.axis_size("dp")
    cores, part, cols = attn.shape
    dma = pltpu.SemaphoreType.DMA
    return pl.pallas_call(
        partial(gather_kernel, line, peers),
        in_specs=[vspec()] * 3,
        out_specs=[hspec()] * 3,
        out_shape=[
            jax.ShapeDtypeStruct((peers * cores, line, part, cols), BF),
            jax.ShapeDtypeStruct((line, part, cols), BF),
            jax.ShapeDtypeStruct(bundles.shape, BF),
        ],
        scratch_shapes=[dma((3,)), dma((4, line)), dma((4, line)), dma((4, line))]
        + [dma((peers, line))] * 4
        + [dma((2,)), dma((2,)), dma],
        compiler_params=pltpu.CompilerParams(
            collective_id=4, has_side_effects=True, vmem_limit_bytes=VMEM_LIMIT
        ),
    )(attn, bundles, heads)


def rotated(x, cos, sin):
    return x * cos + pltpu.roll(x, HEAD_DIM // 2, 1) * sin


def head_cols(h):
    return pl.ds(pl.multiple_of(h * HEAD_DIM, HEAD_DIM), HEAD_DIM)


def weight_loads(packed, wq, wo, wkv, wsem):
    cols, kv_cols = wq.shape[-1], wkv.shape[-1]
    loads = []
    for i, (ref, start, size) in enumerate(((wkv, 2 * cols, kv_cols), (wq, 0, cols), (wo, cols, cols))):
        loads.append(
            [
                pltpu.make_async_copy(packed.at[:, t, :, pl.ds(start, size)], ref.at[t], wsem.at[i, t])
                for t in range(ref.shape[0])
            ]
        )
    return loads


def flat(ref, t):
    groups, rows, cols = ref.shape[1:]
    return ref[t].reshape(groups * rows, cols)


def allowed_keys(info_ref, block, keys, rows):
    row = info_ref[0] + lax.broadcasted_iota(jnp.int32, (1, rows), 1)
    last = jnp.minimum(row, info_ref[1] - 1)
    return block * keys + lax.broadcasted_iota(jnp.int32, (keys, rows), 0) <= last


def one_way_barrier(me, line, side):
    barrier = pltpu.get_barrier_semaphore()
    first, last = (0, line - 1) if side > 0 else (line - 1, 0)

    @pl.when(me != first)
    def _():
        pl.semaphore_signal(barrier, inc=1, device_id={"tensor": me - side}, device_id_type=MESH)

    @pl.when(me != last)
    def _():
        pl.semaphore_wait(barrier, 1)


def spread_qkv(bundle_ref, bq_ref, bkv_ref):
    kv_half = bkv_ref.shape[1] // 2
    bq_ref[...] = jnp.zeros_like(bq_ref)
    bkv_ref[...] = jnp.zeros_like(bkv_ref)
    bq_ref[rows_of(0)] = bundle_ref[rows_of(B_HEADS)]
    for i in range(2):
        span = slice(i * kv_half, (i + 1) * kv_half)
        bkv_ref[rows_of(1 + i), span] = bundle_ref[rows_of(B_KV), span]


def kv_exchange(me, line, kvbuf, recv, send):
    def move(o):
        return pltpu.make_async_remote_copy(
            src_ref=kvbuf.at[o],
            dst_ref=kvbuf.at[o],
            send_sem=send.at[o],
            recv_sem=recv.at[o],
            device_id={"tensor": me + 1},
            device_id_type=MESH,
        )

    return move


def attend_kernel(
    line, group,
    info_ref, x_ref, bundle_ref, cos_ref, sin_ref, packed,
    mid_ref, n2_ref, normed_ref, lowr_ref, rank_ref, q_ref, kv_out, attended_ref, log_ref,
    wq, wo, wkv, kvbuf, acc, peak, total, bq_ref, bkv_ref, wsem, recv, send, ksem,
):
    rows, width = x_ref.shape
    heads = width // HEAD_DIM
    cols = wq.shape[-1]
    kv_cols = wkv.shape[-1]
    scale = HEAD_DIM**-0.5
    me = lax.axis_index("tensor")
    one_way_barrier(me, line, 1)
    kv_loads, q_loads, o_loads = weight_loads(packed, wq, wo, wkv, wsem)
    for load in kv_loads + q_loads + o_loads:
        load.start()
    move = kv_exchange(me, line, kvbuf, recv, send)
    spread_qkv(bundle_ref, bq_ref, bkv_ref)
    misc = bundle_ref[rows_of(B_MISC)].astype(F32)
    q_bias = bundle_ref[rows_of(B_HEADS + 2)].astype(F32)[:1]
    low_in = bundle_ref[rows_of(B_INPUT, 3)]
    x = x_ref[...].astype(F32)
    inverse = lax.rsqrt(jnp.mean(x * x, axis=-1, keepdims=True) + EPSILON)
    normed_ref[...] = (x * inverse * misc[0:1]).astype(BF)
    low = dot_t(normed_ref[...], low_in).astype(BF)
    cos, sin = cos_ref[...], sin_ref[...]
    for load in kv_loads:
        load.wait()
    for t in range(line):
        span = slice(t * kv_cols, (t + 1) * kv_cols)
        kv = dot(normed_ref[...], flat(wkv, t)) + misc[2:3, span] + dot(low, bkv_ref[:, span])
        for h in range(kv_cols // HEAD_DIM):
            at = t * kv_cols + h * HEAD_DIM
            one = kv[:, h * HEAD_DIM : (h + 1) * HEAD_DIM]
            if at < KV_HEADS * HEAD_DIM:
                one = rotated(one, cos, sin)
            kvbuf[me, :, at : at + HEAD_DIM] = one.astype(BF)

    @pl.when(me < line - 1)
    def _():
        move(me).start()

    for load in q_loads:
        load.wait()
    for t in range(line):
        span = slice(t * cols, (t + 1) * cols)
        q = dot(normed_ref[...], flat(wq, t)) + q_bias[:, span] + dot(low, bq_ref[:, span])
        for h in range(cols // HEAD_DIM):
            at = t * cols + h * HEAD_DIM
            q_ref[:, at : at + HEAD_DIM] = rotated(
                q[:, h * HEAD_DIM : (h + 1) * HEAD_DIM], cos, sin
            ).astype(BF)
    acc[...] = jnp.zeros_like(acc)
    total[...] = jnp.zeros_like(total)
    peak[...] = jnp.full_like(peak, MASKED_SCORE)

    def block(o):
        allowed = allowed_keys(info_ref, o, rows, rows)

        def one(h, carry):
            kv_head = h // group
            k = kvbuf[o, :, head_cols(kv_head)]
            v = kvbuf[o, :, head_cols(KV_HEADS + kv_head)]
            scores = jnp.where(allowed, dot_t(k, q_ref[:, head_cols(h)]) * scale, MASKED_SCORE)
            top = jnp.maximum(peak[h], jnp.max(scores, axis=0, keepdims=True))
            soft = jnp.exp(scores - top)
            shift = jnp.exp(peak[h] - top)
            total[h] = total[h] * shift + jnp.sum(soft, axis=0, keepdims=True)
            acc[h] = acc[h] * shift + t_dot(v, soft.astype(BF))
            peak[h] = top
            return carry

        lax.fori_loop(0, heads, one, 0)

    for d in range(line):

        @pl.when(me >= d)
        def _():
            if d > 0:
                move(me - d).wait_recv()

                @pl.when(me < line - 1)
                def _():
                    move(me - d).start()

            block(me - d)

    keep = pltpu.make_async_copy(kvbuf, kv_out, ksem)
    keep.start()
    for h in range(heads):
        attended_ref[:, h * HEAD_DIM : (h + 1) * HEAD_DIM] = (acc[h] * (1.0 / total[h])).T.astype(BF)
        log_ref[h] = peak[h] + jnp.log(total[h])
    rank = dot_t(attended_ref[...], bundle_ref[rows_of(B_HEADS + 1)]).astype(BF)
    lowr_ref[...] = low
    rank_ref[...] = rank
    middle = x_ref[...].astype(F32) + dot(rank, bundle_ref[rows_of(B_RES_ONE)])
    for load in o_loads:
        load.wait()
    for t in range(line):
        middle = middle + dot_t(attended_ref[:, t * cols : (t + 1) * cols], flat(wo, t))
    mid_ref[...] = middle
    inverse = lax.rsqrt(jnp.mean(middle * middle, axis=-1, keepdims=True) + EPSILON)
    n2_ref[...] = (middle * inverse * misc[1:2]).astype(BF)
    keep.wait()
    for o in range(line):

        @pl.when(jnp.logical_and(me < line - 1, me >= o))
        def _():
            move(o).wait_send()


def attend_forward(x, w, info, tables):
    line = lax.axis_size("tensor")
    rows, width = x.shape
    heads = width // HEAD_DIM
    kv_width = 2 * KV_HEADS * HEAD_DIM
    groups, low_rows = w["packed"].shape[0], w["packed"].shape[2]
    outs = pl.pallas_call(
        partial(attend_kernel, line, heads // KV_HEADS),
        in_specs=[pl.BlockSpec(memory_space=pltpu.SMEM)] + [vspec()] * 4 + [hspec()],
        out_specs=[vspec()] * 6 + [hspec()] + [vspec()] * 2,
        out_shape=[
            jax.ShapeDtypeStruct((rows, width), F32),
            jax.ShapeDtypeStruct((rows, width), BF),
            jax.ShapeDtypeStruct((rows, width), BF),
            jax.ShapeDtypeStruct((rows, 3 * RANK), BF),
            jax.ShapeDtypeStruct((rows, RANK), BF),
            jax.ShapeDtypeStruct((rows, width), BF),
            jax.ShapeDtypeStruct((line, rows, kv_width), BF),
            jax.ShapeDtypeStruct((rows, width), BF),
            jax.ShapeDtypeStruct((heads, 1, rows), F32),
        ],
        scratch_shapes=[
            pltpu.VMEM((line, groups, low_rows, width // line), BF),
            pltpu.VMEM((line, groups, low_rows, width // line), BF),
            pltpu.VMEM((line, groups, low_rows, kv_width // line), BF),
            pltpu.VMEM((line, rows, kv_width), BF),
            pltpu.VMEM((heads, HEAD_DIM, rows), F32),
            pltpu.VMEM((heads, 1, rows), F32),
            pltpu.VMEM((heads, 1, rows), F32),
            pltpu.VMEM((3 * RANK, width), BF),
            pltpu.VMEM((3 * RANK, kv_width), BF),
            pltpu.SemaphoreType.DMA((3, line)),
            pltpu.SemaphoreType.DMA((line,)),
            pltpu.SemaphoreType.DMA((line,)),
            pltpu.SemaphoreType.DMA,
        ],
        compiler_params=pltpu.CompilerParams(
            collective_id=2, has_side_effects=True, vmem_limit_bytes=VMEM_LIMIT
        ),
        cost_estimate=pl.CostEstimate(
            flops=4 * rows * width * width * 2, bytes_accessed=5 * width * width, transcendentals=0
        ),
    )(
        info, x, w["bundle"], tables[0], tables[1], w["packed"],
    )
    return outs[0], outs[1], outs[2:]


def attend_back_kernel(
    line, group,
    info_ref, x_ref, mid_ref, dy_ref, dn2_ref, bundle_ref, cos_ref, sin_ref,
    normed_ref, lowr_ref, rank_ref, q_ref, kv_ref, attended_ref, log_ref, packed,
    dx_ref, dx_low_ref, grads_ref,
    wq, wo, wkv, do_ref, dq_acc, dq_ref, dkv_acc, partial_ref, from_right, delta, bq_ref, bkv_ref, wsem, recv, send,
):
    rows, width = x_ref.shape
    heads = width // HEAD_DIM
    cols = wq.shape[-1]
    kv_cols = wkv.shape[-1]
    kv_half = KV_HEADS * HEAD_DIM
    scale = HEAD_DIM**-0.5
    me = lax.axis_index("tensor")
    one_way_barrier(me, line, -1)
    kv_loads, q_loads, o_loads = weight_loads(packed, wq, wo, wkv, wsem)
    for load in o_loads + q_loads + kv_loads:
        load.start()

    def move(o):
        return pltpu.make_async_remote_copy(
            src_ref=partial_ref.at[o],
            dst_ref=from_right.at[o],
            send_sem=send.at[o],
            recv_sem=recv.at[o],
            device_id={"tensor": me - 1},
            device_id_type=MESH,
        )

    def through_norm(values, gain, grad_out):
        inverse = lax.rsqrt(jnp.mean(values * values, axis=-1, keepdims=True) + EPSILON)
        weighted = gain * grad_out
        return inverse * weighted - inverse * inverse * inverse * values * jnp.mean(
            weighted * values, axis=-1, keepdims=True
        )

    spread_qkv(bundle_ref, bq_ref, bkv_ref)
    misc = bundle_ref[rows_of(B_MISC)].astype(F32)
    att = bundle_ref[rows_of(B_HEADS + 1)]
    middle_grad = dy_ref[...].astype(F32) + through_norm(mid_ref[...], misc[1:2], dn2_ref[...])
    dx_ref[...] = middle_grad
    branch_grad = middle_grad.astype(BF)
    low, rank = lowr_ref[...], rank_ref[...]
    rank_grad = dot_t(branch_grad, bundle_ref[rows_of(B_RES_ONE)]).astype(BF)
    grads_ref[3 * RANK : 4 * RANK] = t_dot(rank, branch_grad).astype(BF)
    grads_ref[6 * RANK :] = t_dot(rank_grad, attended_ref[...]).astype(BF)
    for load in o_loads:
        load.wait()
    for t in range(line):
        span = slice(t * cols, (t + 1) * cols)
        do_ref[:, span] = (dot(branch_grad, flat(wo, t)) + dot(rank_grad, att[:, span])).astype(BF)
    for h in range(heads):
        span = slice(h * HEAD_DIM, (h + 1) * HEAD_DIM)
        both = do_ref[:, span].astype(F32) * attended_ref[:, span].astype(F32)
        delta[h] = jnp.sum(both.T, axis=0, keepdims=True)
    dq_acc[...] = jnp.zeros_like(dq_acc)

    def block(o):
        allowed = allowed_keys(info_ref, o, rows, rows)
        dkv_acc[...] = jnp.zeros_like(dkv_acc)

        def one(h, carry):
            kv_head = h // group
            k = kv_ref[o, :, head_cols(kv_head)]
            v = kv_ref[o, :, head_cols(KV_HEADS + kv_head)]
            q = q_ref[:, head_cols(h)]
            do = do_ref[:, head_cols(h)]
            scores = dot_t(k, q) * scale - log_ref[h]
            soft = jnp.exp(jnp.where(allowed, scores, MASKED_SCORE))
            grad = (soft * (dot_t(v, do) - delta[h])).astype(BF)
            dq_acc[h] += t_dot(k, grad)
            dkv_acc[:, head_cols(kv_head)] += dot(grad, q) * scale
            dkv_acc[:, head_cols(KV_HEADS + kv_head)] += dot(soft.astype(BF), do)
            return carry

        lax.fori_loop(0, heads, one, 0)
        partial_ref[o] = dkv_acc[...].astype(BF)

    for s in range(2 * line - 1):
        if s < line:

            @pl.when(me >= s)
            def _():
                block(s)

        for h in range(line - 1):
            o = s - h
            if 0 <= o < line - 1 - h:

                @pl.when(me == line - 1 - h)
                def _():
                    if h > 0:
                        move(o).wait_recv()
                        partial_ref[o] = (partial_ref[o].astype(F32) + from_right[o].astype(F32)).astype(BF)
                    move(o).start()

    cos, sin = cos_ref[...], -sin_ref[...]
    for h in range(heads):
        dq_ref[:, h * HEAD_DIM : (h + 1) * HEAD_DIM] = rotated(dq_acc[h].T * scale, cos, sin).astype(BF)
    dq = dq_ref[...]
    grads_ref[5 * RANK : 6 * RANK] = t_dot(low, dq)[:RANK].astype(BF)
    low_grad = dot_t(dq, bq_ref[...])
    for load in q_loads:
        load.wait()
    normed_grad = dot_t(dq[:, :cols], flat(wq, 0))
    for t in range(1, line):
        normed_grad = normed_grad + dot_t(dq[:, t * cols : (t + 1) * cols], flat(wq, t))
    dkv_acc[...] = partial_ref[me].astype(F32)

    @pl.when(me < line - 1)
    def _():
        move(me).wait_recv()
        dkv_acc[...] += from_right[me].astype(F32)

    for h in range(KV_HEADS):
        span = slice(h * HEAD_DIM, (h + 1) * HEAD_DIM)
        dkv_acc[:, span] = rotated(dkv_acc[:, span], cos, sin)
    dkv = dkv_acc[...].astype(BF)
    kv_grad = t_dot(low, dkv).astype(BF)
    grads_ref[4 * RANK : 5 * RANK, :kv_half] = kv_grad[RANK : 2 * RANK, :kv_half]
    grads_ref[4 * RANK : 5 * RANK, kv_half : 2 * kv_half] = kv_grad[2 * RANK :, kv_half:]
    grads_ref[4 * RANK : 5 * RANK, 2 * kv_half :] = jnp.zeros((RANK, width - 2 * kv_half), BF)
    low_grad = (low_grad + dot_t(dkv, bkv_ref[...])).astype(BF)
    grads_ref[: 3 * RANK] = t_dot(low_grad, normed_ref[...]).astype(BF)
    for load in kv_loads:
        load.wait()
    for t in range(line):
        normed_grad = normed_grad + dot_t(dkv[:, t * kv_cols : (t + 1) * kv_cols], flat(wkv, t))
    normed_grad = normed_grad + dot(low_grad, bundle_ref[rows_of(B_INPUT, 3)])
    dx = dx_ref[...] + through_norm(x_ref[...].astype(F32), misc[0:1], normed_grad)
    dx_ref[...] = dx
    dx_low_ref[...] = dx.astype(BF)
    for o in range(line - 1):

        @pl.when(me > o)
        def _():
            move(o).wait_send()


def attend_backward(x, middle, dy, dn2, w, kept, info, tables):
    line = lax.axis_size("tensor")
    rows, width = x.shape
    heads = width // HEAD_DIM
    kv_width = 2 * KV_HEADS * HEAD_DIM
    groups, low_rows = w["packed"].shape[0], w["packed"].shape[2]
    return pl.pallas_call(
        partial(attend_back_kernel, line, heads // KV_HEADS),
        in_specs=[pl.BlockSpec(memory_space=pltpu.SMEM)] + [vspec()] * 14 + [hspec()],
        out_specs=[vspec()] * 3,
        out_shape=[
            jax.ShapeDtypeStruct((rows, width), F32),
            jax.ShapeDtypeStruct((rows, width), BF),
            jax.ShapeDtypeStruct((7 * RANK, width), BF),
        ],
        scratch_shapes=[
            pltpu.VMEM((line, groups, low_rows, width // line), BF),
            pltpu.VMEM((line, groups, low_rows, width // line), BF),
            pltpu.VMEM((line, groups, low_rows, kv_width // line), BF),
            pltpu.VMEM((rows, width), BF),
            pltpu.VMEM((heads, HEAD_DIM, rows), F32),
            pltpu.VMEM((rows, width), BF),
            pltpu.VMEM((rows, kv_width), F32),
            pltpu.VMEM((line, rows, kv_width), BF),
            pltpu.VMEM((line, rows, kv_width), BF),
            pltpu.VMEM((heads, 1, rows), F32),
            pltpu.VMEM((3 * RANK, width), BF),
            pltpu.VMEM((3 * RANK, kv_width), BF),
            pltpu.SemaphoreType.DMA((3, line)),
            pltpu.SemaphoreType.DMA((line,)),
            pltpu.SemaphoreType.DMA((line,)),
        ],
        compiler_params=pltpu.CompilerParams(
            collective_id=3 if dy.dtype == F32 else 5, has_side_effects=True, vmem_limit_bytes=VMEM_LIMIT
        ),
        cost_estimate=pl.CostEstimate(
            flops=4 * rows * width * width * 2, bytes_accessed=5 * width * width, transcendentals=0
        ),
    )(
        info, x, middle, dy, dn2, w["bundle"], tables[0], tables[1], *kept, w["packed"],
    )


def reduce_kernel(
    line, peers, extra,
    attn_ref, whole_ref, parts_ref, names_ref, y_first, y_second, g_first, g_second,
    out, y_out, g_out,
    mine, z_in, quarter, z_recv, z_send, dp_recv, dp_send, own_sem, t_recv, t_right, t_left,
    side_recv, side_send, side_own,
):
    r = RANK
    me, spot, core = lax.axis_index("tensor"), lax.axis_index("dp"), lax.axis_index("section")
    width = mine.shape[1]
    cols = width // line
    seqs = out.shape[0]
    seq = spot * 2 + core
    has_left, has_right = me > 0, me < line - 1
    barrier = pltpu.get_barrier_semaphore()

    def greet(**where):
        pl.semaphore_signal(barrier, inc=1, device_id=where, device_id_type=MESH)

    for k in range(1, line):
        greet(tensor=lax.rem(me + k, line))

    greet(section=1 - core)

    @pl.when(core == 0)
    def _():
        for k in range(1, peers):
            for c in range(2):
                greet(section=c, dp=lax.rem(spot + k, peers))

    pl.semaphore_wait(barrier, line - 1 + peers)

    def remote(src, dst, send, recv, **where):
        return pltpu.make_async_remote_copy(
            src_ref=src, dst_ref=dst, send_sem=send, recv_sem=recv, device_id=where, device_id_type=MESH
        )

    def lanes(t):
        return pl.ds(pl.multiple_of(t * cols, LANES), cols)

    def pieces(s):
        return (
            (parts_ref.at[pl.ds(0, 3 * r)], out.at[s, pl.ds(8 * r, 3 * r)]),
            (parts_ref.at[pl.ds(3 * r, 3 * r), pl.ds(0, extra)], out.at[s, pl.ds(11 * r, 3 * r), pl.ds(0, extra)]),
            (names_ref, out.at[s, pl.ds(13 * r, r), pl.ds(extra, LANES)]),
            (quarter.at[pl.ds(0, 8 * r)], out.at[s, pl.ds(0, 8 * r), lanes(me)]),
            (quarter.at[pl.ds(8 * r, 2 * r)], out.at[s, pl.ds(11 * r, 2 * r), pl.ds(extra, cols)]),
        )

    def to_peer(k, i):
        src, dst = pieces(seq)[i]
        return remote(src, dst, dp_send.at[k, i], dp_recv.at[seq, i], section=0, dp=lax.rem(spot + k, peers))

    def stay(i):
        src, dst = pieces(seq)[i]
        return pltpu.make_async_copy(src, dst, own_sem.at[i])

    def send_pieces(which):
        for i in which:
            for k in range(1, peers):
                to_peer(k, i).start()

            @pl.when(core != 0)
            def _():
                to_peer(0, i).start()

            @pl.when(core == 0)
            def _():
                stay(i).start()

    def across(k):
        to = lax.rem(me + k, line)
        return remote(mine.at[:, lanes(to)], z_in.at[me], z_send.at[k], z_recv.at[me], tensor=to)

    def incoming(k):
        o = lax.rem(me + k, line)
        return remote(mine.at[:, lanes(me)], z_in.at[o], z_send.at[k], z_recv.at[o], tensor=o)

    def side(i, src, dst):
        return remote(src, dst.at[core], side_send.at[i], side_recv.at[i], section=1 - core)

    def side_keep(i, src, dst):
        return pltpu.make_async_copy(src, dst.at[core], side_own.at[i])

    pairs = ((y_first, y_second, y_out), (g_first, g_second, g_out))

    for first, rows, ref, start in (
        (0, 3, attn_ref, 0), (3, 2, whole_ref, 0), (5, 1, attn_ref, 3), (6, 1, whole_ref, 2), (7, 3, attn_ref, 4),
    ):
        mine[rows_of(first, rows)] = ref[rows_of(start, rows)]
    for k in range(1, line):
        across(k).start()
    send_pieces((0, 1, 2))
    for c in range(2):

        @pl.when(core == c)
        def _():
            for i, (first, second, dst) in enumerate(pairs):
                side(i, first if c == 1 else second, dst).start()
                side_keep(i, second if c == 1 else first, dst).start()

    total = mine[:, lanes(me)].astype(F32)
    for k in range(1, line):
        incoming(k).wait_recv()
        total = total + z_in[lax.rem(me + k, line)].astype(F32)
    quarter[...] = total.astype(BF)
    send_pieces((3, 4))

    def arrived(s, i):
        src, dst = pieces(s)[i]
        return remote(src, dst, dp_send.at[0, i], dp_recv.at[s, i], section=0)

    def along(s, o, side):
        place = out.at[s, pl.ds(0, 8 * r), lanes(o)]
        return remote(
            place, place, (t_right if side > 0 else t_left).at[s, o], t_recv.at[s, o], tensor=me + side
        )

    @pl.when(core == 0)
    def _():
        def own_rows(n, carry):
            s = lax.rem(seq + n, seqs)

            @pl.when(n == 0)
            def _():
                stay(3).wait()

            @pl.when(n > 0)
            def _():
                arrived(s, 3).wait_recv()

            @pl.when(has_right)
            def _():
                along(s, me, 1).start()

            @pl.when(has_left)
            def _():
                along(s, me, -1).start()

            return carry

        lax.fori_loop(0, seqs, own_rows, 0)
        for d in range(1, line):

            def others(n, carry):
                s = lax.rem(seq + n, seqs)

                @pl.when(me >= d)
                def _():
                    along(s, me - d, 1).wait_recv()

                    @pl.when(has_right)
                    def _():
                        along(s, me - d, 1).start()

                @pl.when(me + d < line)
                def _():
                    along(s, me + d, -1).wait_recv()

                    @pl.when(has_left)
                    def _():
                        along(s, me + d, -1).start()

                return carry

            lax.fori_loop(0, seqs, others, 0)

        def finish(n, carry):
            s = lax.rem(seq + n, seqs)

            @pl.when(n > 0)
            def _():
                for i in (0, 1, 2, 4):
                    arrived(s, i).wait_recv()

            for o in range(line):

                @pl.when(jnp.logical_and(has_right, me >= o))
                def _():
                    along(s, o, 1).wait_send()

                @pl.when(jnp.logical_and(has_left, me <= o))
                def _():
                    along(s, o, -1).wait_send()

            return carry

        lax.fori_loop(0, seqs, finish, 0)
        for i in (0, 1, 2, 4):
            stay(i).wait()

    for k in range(1, line):
        across(k).wait_send()
    for i in range(5):
        for k in range(1, peers):
            to_peer(k, i).wait_send()

        @pl.when(core != 0)
        def _():
            to_peer(0, i).wait_send()
    for i, (first, _, dst) in enumerate(pairs):
        side(i, first, dst).wait()
        side_keep(i, first, dst).wait()


def reduce_first(attn_part, whole, parts, names, extra, outs, grads):
    line, peers = lax.axis_size("tensor"), lax.axis_size("dp")
    width = parts.shape[1]
    seqs = 2 * peers
    dma = pltpu.SemaphoreType.DMA
    return pl.pallas_call(
        partial(reduce_kernel, line, peers, extra),
        in_specs=[vspec()] * 8,
        out_specs=[hspec()] * 3,
        out_shape=[
            jax.ShapeDtypeStruct((seqs, 14 * RANK, width), BF),
            jax.ShapeDtypeStruct((2,) + outs[0].shape, outs[0].dtype),
            jax.ShapeDtypeStruct((2,) + grads[0].shape, grads[0].dtype),
        ],
        scratch_shapes=[
            pltpu.VMEM((10 * RANK, width), BF),
            pltpu.VMEM((line, 10 * RANK, width // line), BF),
            pltpu.VMEM((10 * RANK, width // line), BF),
            dma((line,)),
            dma((line,)),
            dma((seqs, 5)),
            dma((peers, 5)),
            dma((5,)),
            dma((seqs, line)),
            dma((seqs, line)),
            dma((seqs, line)),
            dma((2,)),
            dma((2,)),
            dma((2,)),
        ],
        compiler_params=pltpu.CompilerParams(
            collective_id=6, has_side_effects=True, vmem_limit_bytes=VMEM_LIMIT
        ),
    )(attn_part, whole, parts, names, *outs, *grads)


def total_kernel(
    scale, hidden, q_cols,
    first, second,
    input_ref, query_ref, kv_ref, expand_ref, attend_ref, shrink_ref, res_ref,
    block, sem,
):
    r = RANK
    a = pl.program_id(0)
    core = lax.axis_index("section")
    width = block.shape[2]
    extra = hidden - width
    pad = extra + -hidden % (2 * LANES)

    @pl.when(jnp.logical_and(a == 0, core == 0))
    def _():
        load = pltpu.make_async_copy(first, block, sem)
        load.start()
        load.wait()

    @pl.when(jnp.logical_and(a == 0, core != 0))
    def _():
        load = pltpu.make_async_copy(second, block, sem)
        load.start()
        load.wait()

    lane = lax.broadcasted_iota(jnp.int32, (1, LANES), 1)
    weights = []
    for i in range(block.shape[0]):
        names = block[i, 13 * r : 14 * r, pad : pad + LANES][:1].astype(F32)
        weights.append(jnp.sum(jnp.where(lane == a, names, 0.0), axis=1, keepdims=True) * scale)

    def summed(row, rows, col, cols):
        result = weights[0] * block[0, row : row + rows, col : col + cols].astype(F32)
        for i in range(1, block.shape[0]):
            result = result + weights[i] * block[i, row : row + rows, col : col + cols].astype(F32)
        return result

    step = 4 * LANES
    for col in range(0, width, step):
        input_ref[0, :, col : col + step] = summed(0, 5 * r, col, step)
    res_ref[0, 0] = summed(5 * r, r, 0, width)
    res_ref[0, 1] = summed(6 * r, r, 0, width)
    kv = summed(7 * r, r, 0, 2 * kv_ref.shape[3])
    kv_ref[0, 0] = kv[:, : kv_ref.shape[3]]
    kv_ref[0, 1] = kv[:, kv_ref.shape[3] :]
    for i in range(2):
        expand_ref[0, i, :, :width] = summed((8 + i) * r, r, 0, width)
        expand_ref[0, i, :, width:] = summed((11 + i) * r, r, 0, pad)[:, :extra]
    shrink_ref[0, :, :width] = summed(10 * r, r, 0, width)
    shrink_ref[0, :, width:] = summed(13 * r, r, 0, pad)[:, :extra]
    query_ref[0] = summed(11 * r, r, pad, q_cols)
    attend_ref[0] = summed(12 * r, r, pad, q_cols)


def total_by_adapter(first, second, count, scale, hidden, q_cols, kv_half):
    width = first.shape[2]
    r = RANK
    shapes = [
        (5 * r, width), (r, q_cols), (2, r, kv_half), (2, r, hidden), (r, q_cols), (r, hidden), (2, r, width),
    ]
    return pl.pallas_call(
        partial(total_kernel, scale, hidden, q_cols),
        grid=(count,),
        in_specs=[hspec()] * 2,
        out_specs=[pl.BlockSpec((1,) + s, lambda a, n=len(s): (a,) + (0,) * n) for s in shapes],
        out_shape=[jax.ShapeDtypeStruct((count,) + s, F32) for s in shapes],
        scratch_shapes=[pltpu.VMEM(first.shape, BF), pltpu.SemaphoreType.DMA],
        compiler_params=pltpu.CompilerParams(vmem_limit_bytes=VMEM_LIMIT),
    )(first, second)


def swap(pair):
    return lax.all_to_all(pair, "section", split_axis=0, concat_axis=0, tiled=True)


def local(
    inputs,
    lengths,
    adapter_ids,
    cotangent,
    norm_gain,
    query_weight,
    query_bias,
    keyvalue_weight,
    keyvalue_bias,
    output_weight,
    expand_weight,
    shrink_weight,
    adapter_input,
    adapter_query,
    adapter_keyvalue,
    adapter_expand,
    adapter_attend,
    adapter_shrink,
    adapter_residual,
):
    layers = lax.axis_size("section")
    tensor = lax.axis_size("tensor")
    core = lax.axis_index("section")
    place = lax.axis_index("tensor")
    rows, width = inputs.shape[1:]
    tokens = layers * rows * tensor * lax.axis_size("dp")
    kv_half = KV_HEADS * HEAD_DIM
    hidden = expand_weight.shape[3]
    r = RANK

    def turned(stack):
        return jnp.swapaxes(stack[0], 1, 2)

    def lined(stack):
        return stack[0].reshape(stack.shape[1], -1, stack.shape[-1])

    bundles, heads = pick_adapters(
        adapter_ids,
        (
            turned(adapter_input), lined(adapter_residual), lined(adapter_keyvalue), lined(adapter_expand),
            turned(adapter_shrink), adapter_query[0], turned(adapter_attend),
        ),
        (norm_gain[0], keyvalue_bias.reshape(1, -1), query_bias),
    )

    ff = jnp.concatenate(
        [m.reshape(layers, 1, hidden // layers, m.shape[1]) for m in (*turned(expand_weight), shrink_weight[0])],
        axis=1,
    )
    ff = swap(ff)
    kv = jnp.concatenate([keyvalue_weight[0, 0], keyvalue_weight[0, 1]], axis=1)
    kv_cols = kv.shape[1] // tensor
    kv = lax.dynamic_slice_in_dim(kv, place * kv_cols, kv_cols, 1)
    attn = jnp.concatenate([query_weight[0], output_weight[0].T, kv], axis=1)
    q_cols = query_weight.shape[2]
    attn = swap(attn.reshape(layers, attn.shape[0] // layers, attn.shape[1]))
    first_attn, line_attn, bundle = gather_first(attn, bundles, heads)

    def weights(layer):
        packed = first_attn if layer == 0 else lax.all_gather(line_attn, ("dp", "section"), axis=0)
        mlp = lax.all_gather(ff[layer], ("section", "dp"), axis=0)
        mlp = mlp.reshape(layers, -1, *mlp.shape[1:])
        if mlp.shape[4] % LANES:
            mlp = jnp.moveaxis(mlp, 1, 3)
            mlp = mlp.reshape(layers, 1, *mlp.shape[1:3], width)
        return dict(packed=packed, mlp=mlp, bundle=bundle[layer])

    x = lax.dynamic_index_in_dim(inputs, core, 0, keepdims=False)
    cot = lax.dynamic_index_in_dim(cotangent, core, 0, keepdims=False)
    length = lax.dynamic_index_in_dim(lengths, core, 0, keepdims=False)
    own_id = lax.dynamic_index_in_dim(adapter_ids, core, 0, keepdims=False)
    first_slot = place * rows
    info = jnp.stack([first_slot, length]).astype(jnp.int32)
    tables = rotary_tables(first_slot, rows)
    slot_ids = first_slot + jnp.arange(rows, dtype=jnp.int32)

    w = [weights(layer) for layer in range(layers)]
    outs, kept = [], []
    for layer in range(layers):
        middle, normed_two, attn_kept = attend_forward(x, w[layer], info, tables)
        shrunk, mlp_kept = mlp_forward(normed_two, w[layer])
        outs.append((middle + shrunk).astype(BF))
        kept.append((x, middle, attn_kept, mlp_kept))
        x = outs[-1]
    count = adapter_input.shape[1]
    extra = hidden + -hidden % (2 * LANES) - width
    names = (jnp.arange(LANES, dtype=jnp.int32) == own_id).astype(BF)[None]

    def gather_block(attn_part, whole, parts):
        mine = lax.dynamic_slice_in_dim(attn_part[5 * r :], place * q_cols, q_cols, 1)
        parts = lax.dynamic_update_slice(parts, mine, (3 * r, extra))
        parts = lax.dynamic_update_slice(parts, names, (5 * r, extra))
        block = jnp.concatenate(
            [attn_part[: 3 * r], whole[: 2 * r], attn_part[3 * r : 4 * r], whole[2 * r :], attn_part[4 * r : 5 * r]]
            + [parts],
            axis=0,
        )
        return lax.all_gather(block, ("section", "dp"), axis=0)

    grad = low_grad = jnp.where((slot_ids < length)[:, None], cot, jnp.zeros_like(cot))
    grads, gathered = [None] * layers, [None] * layers
    for layer in reversed(range(layers)):
        x, middle, attn_kept, mlp_kept = kept[layer]
        if layer < layers - 1:
            low_grad, here = lax.optimization_barrier((low_grad, here))
        dn2, whole, parts = mlp_backward(low_grad, w[layer], mlp_kept)
        if layer < layers - 1:
            total, dn2 = lax.optimization_barrier((total, dn2))
            gathered[layer + 1] = gather_block(*total, last_parts)
        grad, low_grad, attn_part = attend_backward(x, middle, grad, dn2, w[layer], attn_kept, info, tables)
        grads[layer] = grad
        here = (attn_part, whole)
        if layer > 0:
            total = lax.psum(here, "tensor")
            last_parts = parts
    gathered[0], layer_output, input_grad = reduce_first(
        *here, parts, jnp.pad(names, [(0, r - 1), (0, 0)]), extra, outs, grads
    )
    totals = total_by_adapter(
        gathered[0], gathered[1], count, 1.0 / math.sqrt(tokens), hidden, q_cols, kv_half
    )
    turned = (0, 4, 5)
    totals = [jnp.swapaxes(total, 1, 2) if i in turned else total for i, total in enumerate(totals)]
    return (layer_output[None], input_grad[None]) + tuple(total[None] for total in totals)


def solution(mesh):
    placed = (
        P("dp", "tensor", None),
        P("dp"),
        P("dp"),
        P("dp", "tensor", None),
        P("section", None, None),
        P("section", "dp", "tensor"),
        P("section", "tensor"),
        P("section", None, "dp", None),
        P("section", None, None),
        P("section", "tensor", "dp"),
        P("section", None, "dp", "tensor"),
        P("section", "tensor", "dp"),
        P("section", None, None, None),
        P("section", None, None, "tensor"),
        P("section", None, None, None, None),
        P("section", None, None, None, "tensor"),
        P("section", None, "tensor", None),
        P("section", None, "tensor", None),
        P("section", None, None, None, None),
    )
    return jax.shard_map(
        local,
        mesh=mesh,
        in_specs=placed,
        out_specs=(
            P("section", "dp", "tensor", None),
            P("section", "dp", "tensor", None),
            P("section", None, None, None),
            P("section", None, None, "tensor"),
            P("section", None, None, None, None),
            P("section", None, None, None, "tensor"),
            P("section", None, "tensor", None),
            P("section", None, "tensor", None),
            P("section", None, None, None, None),
        ),
        check_vma=False,
    )
```

```python
from functools import partial
import math

import jax
import jax.numpy as jnp
from jax import lax
from jax.experimental import pallas as pl
from jax.experimental.pallas import tpu as pltpu
from jax.sharding import PartitionSpec as P

KV_HEADS = 2
HEAD_DIM = 128
RANK = 16
EPSILON = 1e-06
ROPE_BASE = 1000000.0
MASKED_SCORE = -1e30
CHUNKS = 4
LANES = 128
VMEM_LIMIT = 60 * 2**20
MESH = pl.DeviceIdType.MESH
BF = jnp.bfloat16
F32 = jnp.float32


def dot(a, b):
    return jnp.dot(a, b, preferred_element_type=F32)


def dot_t(a, b):
    return lax.dot_general(a, b, (((1,), (1,)), ((), ())), preferred_element_type=F32)


def t_dot(a, b):
    return lax.dot_general(a, b, (((0,), (0,)), ((), ())), preferred_element_type=F32)


def rotary_tables(first_slot, rows):
    half = HEAD_DIM // 2
    frequency = jnp.exp(-math.log(ROPE_BASE) * (2.0 * jnp.arange(half, dtype=F32) / HEAD_DIM))
    slots = (first_slot + jnp.arange(rows, dtype=jnp.int32)).astype(F32)
    angles = slots[:, None] * frequency[None, :]
    cos, sin = jnp.cos(angles), jnp.sin(angles)
    return jnp.concatenate([cos, cos], axis=1), jnp.concatenate([-sin, sin], axis=1)


B_INPUT, B_RES_ONE, B_RES_TWO, B_KV, B_MISC, B_FF, B_FF_TAIL, B_HEADS, B_ROWS = 0, 5, 6, 7, 8, 9, 12, 15, 18


def rows_of(first, count=1):
    return slice(first * RANK, (first + count) * RANK)


def pick_kernel(
    ids_ref, input_ref, res_ref, kv_ref, expand_ref, shrink_ref, query_ref, attend_ref, gain_ref, kvb_ref, qb_ref,
    out_ref, heads_ref,
):
    width = out_ref.shape[2]
    out_ref[0] = jnp.zeros(out_ref.shape[1:], BF)
    out_ref[0, rows_of(B_INPUT, 5)] = input_ref[0]
    out_ref[0, rows_of(B_RES_ONE, 2)] = res_ref[0]
    kv_half = kv_ref.shape[2]
    for i in range(2):
        out_ref[0, rows_of(B_KV), i * kv_half : (i + 1) * kv_half] = kv_ref[0, rows_of(i)]
    misc = rows_of(B_MISC).start
    out_ref[0, misc : misc + 2] = gain_ref[...]
    out_ref[0, misc + 2 : misc + 3, : 2 * kv_half] = kvb_ref[...]
    tail = expand_ref.shape[2] - width
    for i in range(3):
        part = expand_ref[0, rows_of(i)] if i < 2 else shrink_ref[0]
        out_ref[0, rows_of(B_FF + i)] = part[:, :width]
        out_ref[0, rows_of(B_FF_TAIL + i), :tail] = part[:, width:]
    heads_ref[0] = jnp.zeros(heads_ref.shape[1:], BF)
    heads_ref[0, rows_of(0)] = query_ref[0]
    heads_ref[0, rows_of(1)] = attend_ref[0]
    heads_ref[0, 2 * RANK : 2 * RANK + 1] = qb_ref[...]


def pick_adapters(ids, stacks, shared):
    count = ids.shape[0]
    width = stacks[0].shape[2]
    q_cols = stacks[5].shape[2]
    shapes = [(B_ROWS * RANK, width), (3 * RANK, q_cols)]
    return pl.pallas_call(
        pick_kernel,
        grid_spec=pltpu.PrefetchScalarGridSpec(
            num_scalar_prefetch=1,
            grid=(count,),
            in_specs=[pl.BlockSpec((1,) + a.shape[1:], lambda i, ids: (ids[i], 0, 0)) for a in stacks]
            + [pl.BlockSpec(a.shape, lambda i, ids: (0, 0)) for a in shared],
            out_specs=[pl.BlockSpec((1,) + a, lambda i, ids: (i, 0, 0)) for a in shapes],
        ),
        out_shape=[jax.ShapeDtypeStruct((count,) + a, BF) for a in shapes],
    )(ids, *stacks, *shared)


def spread_factors(bundle_ref, expand_ref, ash_ref):
    width = bundle_ref.shape[1]
    tail = ash_ref.shape[1] - width
    expand_ref[...] = jnp.zeros_like(expand_ref)
    for i in range(2):
        expand_ref[i, rows_of(i), :width] = bundle_ref[rows_of(B_FF + i)]
        expand_ref[i, rows_of(i), width:] = bundle_ref[rows_of(B_FF_TAIL + i), :tail]
    ash_ref[:, :width] = bundle_ref[rows_of(B_FF + 2)]
    ash_ref[:, width:] = bundle_ref[rows_of(B_FF_TAIL + 2), :tail]


def vspec():
    return pl.BlockSpec(memory_space=pltpu.VMEM)


def hspec():
    return pl.BlockSpec(memory_space=pl.ANY)


def line_barrier(me, line):
    barrier = pltpu.get_barrier_semaphore()

    @pl.when(me > 0)
    def _():
        pl.semaphore_signal(barrier, inc=1, device_id={"tensor": me - 1}, device_id_type=MESH)

    @pl.when(me < line - 1)
    def _():
        pl.semaphore_signal(barrier, inc=1, device_id={"tensor": me + 1}, device_id_type=MESH)

    pl.semaphore_wait(barrier, jnp.where(me > 0, 1, 0) + jnp.where(me < line - 1, 1, 0))


def within(c, chunks):
    return jnp.logical_and(c >= 0, c < chunks)


def line_exchange(line, chunks, gathered, partial_ref, from_left, from_right, own_out, sems, begin, work):
    ag_recv, ag_right, ag_left, r_recv, r_send, l_recv, l_send = sems
    me = lax.axis_index("tensor")

    def copy(ref, src, c, o, send, recv, side):
        return pltpu.make_async_remote_copy(
            src_ref=src.at[c, o],
            dst_ref=ref.at[c, o],
            send_sem=send.at[c, o],
            recv_sem=recv.at[c, o],
            device_id={"tensor": me + side},
            device_id_type=MESH,
        )

    def ag(c, o, side):
        return copy(gathered, gathered, c, o, ag_right if side > 0 else ag_left, ag_recv, side)

    def rs(c, o, side):
        if side > 0:
            return copy(from_left, partial_ref, c, o, r_send, r_recv, 1)
        return copy(from_right, partial_ref, c, o, l_send, l_recv, -1)

    has_left, has_right = me > 0, me < line - 1

    def step(s, carry):
        first = s + line - 1

        @pl.when(jnp.logical_and(within(first, chunks), has_right))
        def _():
            ag(first, me, 1).start()

        @pl.when(jnp.logical_and(within(first, chunks), has_left))
        def _():
            ag(first, me, -1).start()

        for d in range(1, line):
            c = s + line - 1 - d

            @pl.when(jnp.logical_and(within(c, chunks), me - d >= 0))
            def _():
                ag(c, me - d, 1).wait_recv()

                @pl.when(has_right)
                def _():
                    ag(c, me - d, 1).start()

            @pl.when(jnp.logical_and(within(c, chunks), me + d < line))
            def _():
                ag(c, me + d, -1).wait_recv()

                @pl.when(has_left)
                def _():
                    ag(c, me + d, -1).start()

        @pl.when(within(s, chunks))
        def _():
            work(s)

        for h in range(line):
            c = s - h

            @pl.when(jnp.logical_and(within(c, chunks), me == h))
            def _():
                for j in range(line - 1, h, -1):
                    if h > 0:
                        rs(c, j, 1).wait_recv()
                        partial_ref[c, j] = (
                            partial_ref[c, j].astype(F32) + from_left[c, j].astype(F32)
                        ).astype(BF)
                    if h < line - 1:
                        rs(c, j, 1).start()

            @pl.when(jnp.logical_and(within(c, chunks), me == line - 1 - h))
            def _():
                for j in range(line - 1 - h):
                    if h > 0:
                        rs(c, j, -1).wait_recv()
                        partial_ref[c, j] = (
                            partial_ref[c, j].astype(F32) + from_right[c, j].astype(F32)
                        ).astype(BF)
                    if h < line - 1:
                        rs(c, j, -1).start()

        last = s - (line - 1)

        @pl.when(within(last, chunks))
        def _():
            own_out[last] = partial_ref[last, me].astype(F32)

            @pl.when(has_left)
            def _():
                rs(last, me, 1).wait_recv()
                own_out[last] += from_left[last, me].astype(F32)

            @pl.when(has_right)
            def _():
                rs(last, me, -1).wait_recv()
                own_out[last] += from_right[last, me].astype(F32)

        return carry

    line_barrier(me, line)
    begin()
    lax.fori_loop(-(line - 1), chunks + line - 1, step, 0)

    def drain(c, carry):
        for o in range(line):

            @pl.when(jnp.logical_and(has_right, me >= o))
            def _():
                ag(c, o, 1).wait_send()

            @pl.when(jnp.logical_and(has_left, me <= o))
            def _():
                ag(c, o, -1).wait_send()

            @pl.when(me < o)
            def _():
                rs(c, o, 1).wait_send()

            @pl.when(me > o)
            def _():
                rs(c, o, -1).wait_send()

        return carry

    lax.fori_loop(0, chunks, drain, 0)


def exchange_scratch(line, chunks, rows, width):
    slots = (chunks, line, rows, width)
    return [pltpu.VMEM(slots, BF)] * 4 + [pltpu.SemaphoreType.DMA((chunks, line))] * 7


def ff_loads(packed, refs, wsem):
    halves, parts, _, rows, cols = packed.shape
    return [
        pltpu.make_async_copy(
            packed.at[h, p, i],
            ref.at[pl.ds(h * rows, rows), pl.ds(p * cols, cols)],
            wsem.at[i, h, p],
        )
        for i, ref in enumerate(refs)
        for h in range(halves)
        for p in range(parts)
    ]


def clear_tail(packed, refs):
    hidden = packed.shape[0] * packed.shape[3]
    for ref in refs:
        if ref.shape[0] > hidden:
            ref[hidden:] = jnp.zeros((ref.shape[0] - hidden, ref.shape[1]), BF)


def mlp_kernel(
    line, chunks, tile,
    n2_ref, packed, bundle_ref,
    out_ref, n2_out, gate_out, up_out,
    gathered, partial_ref, from_left, from_right, s0, s1, s2, s3, s4, s5, s6,
    wg, wu, ws, gate_st, up_st, acc, expand_ref, ash_ref, wsem, osem, nsem,
):
    rows, width = n2_ref.shape[1:]
    every = line * rows
    tiles = wg.shape[0] // tile
    high = bundle_ref[rows_of(B_INPUT + 3, 2)]
    res = bundle_ref[rows_of(B_RES_TWO)]
    me = lax.axis_index("tensor")
    loads = ff_loads(packed, (wg, wu, ws), wsem)

    def begin():
        for load in loads:
            load.start()
        clear_tail(packed, (wg, wu, ws))
        spread_factors(bundle_ref, expand_ref, ash_ref)
        for c in range(chunks):
            gathered[c, me] = n2_ref[c]

    def saves(c, slot):
        return (
            pltpu.make_async_copy(gate_st.at[slot], gate_out.at[c], osem.at[0, slot]),
            pltpu.make_async_copy(up_st.at[slot], up_out.at[c], osem.at[1, slot]),
        )

    def keep(c):
        return pltpu.make_async_copy(gathered.at[c], n2_out.at[c], nsem.at[c])

    def work(c):
        slot = c % 2

        @pl.when(c == 0)
        def _():
            for load in loads:
                load.wait()

        @pl.when(c >= 2)
        def _():
            for save in saves(c - 2, slot):
                save.wait()

        keep(c).start()
        x = gathered[c].reshape(every, width)
        er = dot_t(x, high).astype(BF)

        def one(f, rank):
            cols = pl.ds(pl.multiple_of(f * tile, tile), tile)
            gate = dot_t(x, wg[cols]) + dot(er, expand_ref[0, :, cols])
            up = dot_t(x, wu[cols]) + dot(er, expand_ref[1, :, cols])
            gate_st[slot, :, cols] = gate.astype(BF)
            up_st[slot, :, cols] = up.astype(BF)
            act = (gate * (1.0 / (1.0 + jnp.exp(-gate))) * up).astype(BF)
            now = dot(act, ws[cols])

            @pl.when(f == 0)
            def _():
                acc[...] = now

            @pl.when(f > 0)
            def _():
                acc[...] += now

            return rank + dot_t(act, ash_ref[:, cols])

        rank = lax.fori_loop(0, tiles, one, jnp.zeros((every, ash_ref.shape[0]), F32))
        total = acc[...] + dot(rank.astype(BF), res)
        partial_ref[c] = total.astype(BF).reshape(line, rows, width)
        for save in saves(c, slot):
            save.start()

    line_exchange(
        line, chunks, gathered, partial_ref, from_left, from_right, out_ref,
        (s0, s1, s2, s3, s4, s5, s6), begin, work,
    )
    for c in range(chunks):
        keep(c).wait()
    for c in range(max(chunks - 2, 0), chunks):
        for save in saves(c, c % 2):
            save.wait()


def ff_tile(hidden):
    return hidden


def mlp_forward(n2, w):
    line = lax.axis_size("tensor")
    rows, width = n2.shape
    halves, groups, _, low_rows, _ = w["mlp"].shape
    hidden = halves * low_rows + -(halves * low_rows) % (2 * LANES)
    part = rows // CHUNKS
    every = line * part
    out, n2_all, gate, up = pl.pallas_call(
        partial(mlp_kernel, line, CHUNKS, ff_tile(hidden)),
        in_specs=[vspec(), hspec(), vspec()],
        out_specs=[vspec()] + [hspec()] * 3,
        out_shape=[
            jax.ShapeDtypeStruct((CHUNKS, part, width), F32),
            jax.ShapeDtypeStruct((CHUNKS, line, part, width), BF),
            jax.ShapeDtypeStruct((CHUNKS, every, hidden), BF),
            jax.ShapeDtypeStruct((CHUNKS, every, hidden), BF),
        ],
        scratch_shapes=exchange_scratch(line, CHUNKS, part, width)
        + [pltpu.VMEM((hidden, width), BF)] * 3
        + [pltpu.VMEM((2, every, hidden), BF)] * 2
        + [
            pltpu.VMEM((every, width), F32),
            pltpu.VMEM((2, 2 * RANK, hidden), BF),
            pltpu.VMEM((RANK, hidden), BF),
            pltpu.SemaphoreType.DMA((3, halves, groups)),
            pltpu.SemaphoreType.DMA((2, 2)),
            pltpu.SemaphoreType.DMA((CHUNKS,)),
        ],
        compiler_params=pltpu.CompilerParams(
            collective_id=0, has_side_effects=True, vmem_limit_bytes=VMEM_LIMIT
        ),
        cost_estimate=pl.CostEstimate(
            flops=6 * line * rows * width * hidden,
            bytes_accessed=6 * width * hidden + 4 * line * rows * hidden,
            transcendentals=line * rows * hidden,
        ),
    )(
        n2.reshape(CHUNKS, part, width), w["mlp"], w["bundle"],
    )
    return out.reshape(rows, width), (n2_all.reshape(CHUNKS, every, width), gate, up)


def mlp_back_kernel(
    line, chunks, tile,
    ds_ref, packed, n2_hbm, gate_in, up_in, bundle_ref, names_ref,
    out_ref, whole_ref, parts_ref,
    gathered, partial_ref, from_left, from_right, s0, s1, s2, s3, s4, s5, s6,
    wg, wu, ws, gate_st, up_st, n2_st, acc, ghigh_ref, gexp_ref, gsh_ref, gres_ref, expand_ref, ash_ref, wsem, isem,
):
    rows, width = ds_ref.shape[1:]
    every = line * rows
    tiles = wg.shape[0] // tile
    high = bundle_ref[rows_of(B_INPUT + 3, 2)]
    res = bundle_ref[rows_of(B_RES_TWO)]
    me = lax.axis_index("tensor")
    loads = ff_loads(packed, (wg, wu, ws), wsem)

    def fetch(c):
        slot = c % 2
        return (
            pltpu.make_async_copy(gate_in.at[c], gate_st.at[slot], isem.at[0, slot]),
            pltpu.make_async_copy(up_in.at[c], up_st.at[slot], isem.at[1, slot]),
            pltpu.make_async_copy(n2_hbm.at[c], n2_st.at[slot], isem.at[2, slot]),
        )

    def begin():
        for load in loads:
            load.start()
        clear_tail(packed, (wg, wu, ws))
        spread_factors(bundle_ref, expand_ref, ash_ref)
        for one in fetch(0):
            one.start()
        for c in range(chunks):
            gathered[c, me] = ds_ref[c]
        for ref in (ghigh_ref, gexp_ref, gsh_ref, gres_ref):
            ref[...] = jnp.zeros_like(ref)

    def work(c):
        slot = c % 2

        @pl.when(c == 0)
        def _():
            for load in loads:
                load.wait()

        for one in fetch(c):
            one.wait()

        @pl.when(c + 1 < chunks)
        def _():
            for one in fetch(c + 1):
                one.start()

        ds = gathered[c].reshape(every, width)
        n2 = n2_st[slot]
        er = dot_t(n2, high).astype(BF)
        rank_in = dot_t(ds, res).astype(BF)

        def one(f, carry):
            rank_out, srank = carry
            cols = pl.ds(pl.multiple_of(f * tile, tile), tile)
            act_grad = dot_t(ds, ws[cols]) + dot(rank_in, ash_ref[:, cols])
            gate = gate_st[slot, :, cols].astype(F32)
            up = up_st[slot, :, cols].astype(F32)
            sig = 1.0 / (1.0 + jnp.exp(-gate))
            silu = gate * sig
            act = (silu * up).astype(BF)
            gate_grad = (act_grad * up * (sig + silu * (1.0 - sig))).astype(BF)
            up_grad = (act_grad * silu).astype(BF)
            now = dot(gate_grad, wg[cols]) + dot(up_grad, wu[cols])

            @pl.when(f == 0)
            def _():
                acc[...] = now

            @pl.when(f > 0)
            def _():
                acc[...] += now

            gexp_ref[0, :, cols] += t_dot(er, gate_grad)
            gexp_ref[1, :, cols] += t_dot(er, up_grad)
            gsh_ref[:, cols] += t_dot(rank_in, act)
            rank_out = rank_out + dot_t(gate_grad, expand_ref[0, :, cols])
            rank_out = rank_out + dot_t(up_grad, expand_ref[1, :, cols])
            return rank_out, srank + dot_t(act, ash_ref[:, cols])

        rank_out, srank = lax.fori_loop(
            0,
            tiles,
            one,
            (
                jnp.zeros((every, expand_ref.shape[1]), F32),
                jnp.zeros((every, ash_ref.shape[0]), F32),
            ),
        )
        rank_out = rank_out.astype(BF)
        total = acc[...] + dot(rank_out, high)
        partial_ref[c] = total.astype(BF).reshape(line, rows, width)
        ghigh_ref[...] += t_dot(rank_out, n2)
        gres_ref[...] += t_dot(srank.astype(BF), ds)

    line_exchange(
        line, chunks, gathered, partial_ref, from_left, from_right, out_ref,
        (s0, s1, s2, s3, s4, s5, s6), begin, work,
    )
    whole_ref[: 2 * RANK] = ghigh_ref[...].astype(BF)
    whole_ref[2 * RANK :] = gres_ref[...].astype(BF)
    extra = gsh_ref.shape[1] - width
    parts_ref[3 * RANK :, extra:] = jnp.zeros((3 * RANK, width - extra), BF)
    for i, part in enumerate((gexp_ref[0, :RANK], gexp_ref[1, RANK:], gsh_ref[...])):
        part = part.astype(BF)
        parts_ref[i * RANK : (i + 1) * RANK] = part[:, :width]
        parts_ref[(3 + i) * RANK : (4 + i) * RANK, :extra] = part[:, width:]
    parts_ref[rows_of(5), extra : extra + LANES] = names_ref[...]


def mlp_backward(ds, w, saved, names):
    n2_all, gate, up = saved
    line = lax.axis_size("tensor")
    rows, width = ds.shape
    halves, groups, _, low_rows, _ = w["mlp"].shape
    hidden = halves * low_rows + -(halves * low_rows) % (2 * LANES)
    part = rows // CHUNKS
    every = line * part
    out, whole, parts = pl.pallas_call(
        partial(mlp_back_kernel, line, CHUNKS, ff_tile(hidden)),
        in_specs=[vspec()] + [hspec()] * 4 + [vspec()] * 2,
        out_specs=[vspec()] * 3,
        out_shape=[
            jax.ShapeDtypeStruct((CHUNKS, part, width), F32),
            jax.ShapeDtypeStruct((3 * RANK, width), BF),
            jax.ShapeDtypeStruct((6 * RANK, width), BF),
        ],
        scratch_shapes=exchange_scratch(line, CHUNKS, part, width)
        + [pltpu.VMEM((hidden, width), BF)] * 3
        + [pltpu.VMEM((2, every, hidden), BF)] * 2
        + [
            pltpu.VMEM((2, every, width), BF),
            pltpu.VMEM((every, width), F32),
            pltpu.VMEM((2 * RANK, width), F32),
            pltpu.VMEM((2, 2 * RANK, hidden), F32),
            pltpu.VMEM((RANK, hidden), F32),
            pltpu.VMEM((RANK, width), F32),
            pltpu.VMEM((2, 2 * RANK, hidden), BF),
            pltpu.VMEM((RANK, hidden), BF),
            pltpu.SemaphoreType.DMA((3, halves, groups)),
            pltpu.SemaphoreType.DMA((3, 2)),
        ],
        compiler_params=pltpu.CompilerParams(
            collective_id=1, has_side_effects=True, vmem_limit_bytes=VMEM_LIMIT
        ),
        cost_estimate=pl.CostEstimate(
            flops=6 * line * rows * width * hidden,
            bytes_accessed=6 * width * hidden + 4 * line * rows * hidden,
            transcendentals=line * rows * hidden,
        ),
    )(
        ds.reshape(CHUNKS, part, width), w["mlp"], n2_all, gate, up, w["bundle"], names,
    )
    return out.reshape(rows, width), whole, parts


def gather_kernel(
    line, peers,
    attn, bundles, heads,
    first_out, second_out, bundle_out,
    own_sem, z_recv, z_right, z_left, dp_recv, dp_send, core_recv, core_send, side_recv, side_send, side_own,
):
    me, spot, core = lax.axis_index("tensor"), lax.axis_index("dp"), lax.axis_index("section")
    other = 1 - core
    has_left, has_right = me > 0, me < line - 1
    barrier = pltpu.get_barrier_semaphore()

    def greet(**where):
        pl.semaphore_signal(barrier, inc=1, device_id=where, device_id_type=MESH)

    @pl.when(has_left)
    def _():
        greet(tensor=me - 1)

    @pl.when(has_right)
    def _():
        greet(tensor=me + 1)

    greet(section=other)
    square = peers == 4

    def partner(k):
        if square:
            return (None, spot + 1 - 2 * lax.rem(spot, 2), lax.rem(spot + 2, 4), 3 - spot)[k]
        return lax.rem(spot + k, peers)

    def origin(k):
        return partner(k) if square else lax.rem(spot + peers - k, peers)

    direct = (1, 2) if square else tuple(range(1, peers))
    for k in range(1, peers):
        greet(dp=partner(k))
    pl.semaphore_wait(barrier, jnp.where(has_left, 1, 0) + jnp.where(has_right, 1, 0) + peers)

    mine = spot * 2 + core
    plain, part = bundles.shape[1] - heads.shape[1], heads.shape[2]

    def head_place(layer, o):
        return bundle_out.at[layer, pl.ds(plain, heads.shape[1]), pl.ds(o * part, part)]

    def places(o):
        return first_out.at[mine, o], second_out.at[o], head_place(core, o), head_place(other, o)

    sides = [
        pltpu.make_async_remote_copy(
            src_ref=src,
            dst_ref=dst,
            send_sem=side_send.at[i],
            recv_sem=side_recv.at[i],
            device_id={"section": other},
            device_id_type=MESH,
        )
        for i, (src, dst) in enumerate(
            (
                (bundles.at[other, pl.ds(0, plain)], bundle_out.at[core, pl.ds(0, plain)]),
                (heads.at[other], head_place(core, me)),
            )
        )
    ]
    side_keep = pltpu.make_async_copy(
        bundles.at[core, pl.ds(0, plain)], bundle_out.at[core, pl.ds(0, plain)], side_own
    )
    sources = (attn.at[0], attn.at[1], heads.at[core], head_place(other, me))
    keeps = [
        pltpu.make_async_copy(src, dst, own_sem.at[i]) for i, (src, dst) in enumerate(zip(sources[:3], places(me)))
    ]

    def remote(src, dst, send, recv, **where):
        return pltpu.make_async_remote_copy(
            src_ref=src, dst_ref=dst, send_sem=send, recv_sem=recv, device_id=where, device_id_type=MESH
        )

    def along(i, o, side, own):
        dst = places(o)[i]
        return remote(
            sources[i] if own else dst,
            dst,
            (z_right if side > 0 else z_left).at[i, o],
            z_recv.at[i, o],
            tensor=me + side,
        )

    outs = (first_out,)

    def to_peer(lay, k, o, own):
        dst = outs[lay].at[mine, o]
        return remote(
            attn.at[lay] if own else dst, dst, dp_send.at[lay, k, o], dp_recv.at[lay, spot, o], dp=partner(k)
        )

    def from_peer(lay, k, o):
        p = origin(k)
        slot = outs[lay].at[p * 2 + core, o]
        to = partner(3 - k) if square and k < 3 else p
        return remote(slot, slot, dp_send.at[lay, peers - 1, o], dp_recv.at[lay, p, o], dp=to)

    def to_core(lay, p, o, own):
        dst = outs[lay].at[p * 2 + core, o]
        return remote(
            attn.at[lay] if own else dst, dst, core_send.at[lay, p, o], core_recv.at[lay, p, o], section=other
        )

    def spread(lay, o, own):
        for k in direct:
            to_peer(lay, k, o, own).start()
        to_core(lay, spot, o, own).start()

    for side in sides:
        side.start()
    for i in range(4):
        if i == 3:
            sides[1].wait_recv()

        @pl.when(has_right)
        def _():
            along(i, me, 1, True).start()

        @pl.when(has_left)
        def _():
            along(i, me, -1, True).start()

        if i == 0:
            spread(i, me, True)
    for keep in keeps:
        keep.start()
    side_keep.start()
    for d in range(1, line):
        for i in range(4):

            @pl.when(me >= d)
            def _():
                along(i, me - d, 1, False).wait_recv()

                @pl.when(has_right)
                def _():
                    along(i, me - d, 1, False).start()

                if i == 0:
                    spread(i, me - d, False)

            @pl.when(me + d < line)
            def _():
                along(i, me + d, -1, False).wait_recv()

                @pl.when(has_left)
                def _():
                    along(i, me + d, -1, False).start()

                if i == 0:
                    spread(i, me + d, False)

    half = line // 2

    def pass_on(n, carry):
        o = lax.rem(me + n, line)
        for lay in range(1):
            for k in direct:
                from_peer(lay, k, o).wait_recv()
                if square:

                    @pl.when(o < half if k == 1 else o >= half)
                    def _():
                        from_peer(lay, k, o).start()

                to_core(lay, origin(k), o, False).start()
        return carry

    lax.fori_loop(0, line, pass_on, 0)

    def pass_last(n, carry):
        o = lax.rem(me + n, line)
        for lay in range(1):
            from_peer(lay, 3, o).wait_recv()
            to_core(lay, origin(3), o, False).start()
        return carry

    if square:
        lax.fori_loop(0, line, pass_last, 0)

    def finish(o, carry):
        for lay in range(1):
            for k in direct:
                to_peer(lay, k, o, False).wait_send()
            if square:
                from_peer(lay, 1, o).wait_send()
            for p in range(peers):
                to_core(lay, p, o, False).wait_send()
                slot = outs[lay].at[p * 2 + other, o]
                remote(slot, slot, core_send.at[lay, p, o], core_recv.at[lay, p, o], section=other).wait_recv()
        for i in range(4):

            @pl.when(jnp.logical_and(has_right, me >= o))
            def _():
                along(i, o, 1, False).wait_send()

            @pl.when(jnp.logical_and(has_left, me <= o))
            def _():
                along(i, o, -1, False).wait_send()

        return carry

    lax.fori_loop(0, line, finish, 0)
    for keep in keeps:
        keep.wait()
    side_keep.wait()
    sides[0].wait_recv()
    for side in sides:
        side.wait_send()


def gather_first(attn, bundles, heads):
    line, peers = lax.axis_size("tensor"), lax.axis_size("dp")
    cores, part, cols = attn.shape
    dma = pltpu.SemaphoreType.DMA
    return pl.pallas_call(
        partial(gather_kernel, line, peers),
        in_specs=[vspec()] * 3,
        out_specs=[hspec()] * 3,
        out_shape=[
            jax.ShapeDtypeStruct((peers * cores, line, part, cols), BF),
            jax.ShapeDtypeStruct((line, part, cols), BF),
            jax.ShapeDtypeStruct(bundles.shape, BF),
        ],
        scratch_shapes=[dma((3,)), dma((4, line)), dma((4, line)), dma((4, line))]
        + [dma((1, peers, line))] * 4
        + [dma((2,)), dma((2,)), dma],
        compiler_params=pltpu.CompilerParams(
            collective_id=4, has_side_effects=True, vmem_limit_bytes=VMEM_LIMIT
        ),
    )(attn, bundles, heads)


def rotated(x, cos, sin):
    return x * cos + pltpu.roll(x, HEAD_DIM // 2, 1) * sin


def head_cols(h):
    return pl.ds(pl.multiple_of(h * HEAD_DIM, HEAD_DIM), HEAD_DIM)


def weight_loads(packed, wq, wo, wkv, wsem):
    cols, kv_cols = wq.shape[-1], wkv.shape[-1]
    loads = []
    for i, (ref, start, size) in enumerate(((wkv, 2 * cols, kv_cols), (wq, 0, cols), (wo, cols, cols))):
        loads.append(
            [
                pltpu.make_async_copy(packed.at[:, t, :, pl.ds(start, size)], ref.at[t], wsem.at[i, t])
                for t in range(ref.shape[0])
            ]
        )
    return loads


def flat(ref, t):
    groups, rows, cols = ref.shape[1:]
    return ref[t].reshape(groups * rows, cols)


def allowed_keys(info_ref, block, keys, rows):
    row = info_ref[0] + lax.broadcasted_iota(jnp.int32, (1, rows), 1)
    last = jnp.minimum(row, info_ref[1] - 1)
    return block * keys + lax.broadcasted_iota(jnp.int32, (keys, rows), 0) <= last


def one_way_barrier(me, line, side):
    barrier = pltpu.get_barrier_semaphore()
    first, last = (0, line - 1) if side > 0 else (line - 1, 0)

    @pl.when(me != first)
    def _():
        pl.semaphore_signal(barrier, inc=1, device_id={"tensor": me - side}, device_id_type=MESH)

    @pl.when(me != last)
    def _():
        pl.semaphore_wait(barrier, 1)


def spread_qkv(bundle_ref, bq_ref, bkv_ref):
    kv_half = bkv_ref.shape[1] // 2
    bq_ref[...] = jnp.zeros_like(bq_ref)
    bkv_ref[...] = jnp.zeros_like(bkv_ref)
    bq_ref[rows_of(0)] = bundle_ref[rows_of(B_HEADS)]
    for i in range(2):
        span = slice(i * kv_half, (i + 1) * kv_half)
        bkv_ref[rows_of(1 + i), span] = bundle_ref[rows_of(B_KV), span]


def kv_exchange(me, line, kvbuf, recv, send):
    def move(o):
        return pltpu.make_async_remote_copy(
            src_ref=kvbuf.at[o],
            dst_ref=kvbuf.at[o],
            send_sem=send.at[o],
            recv_sem=recv.at[o],
            device_id={"tensor": me + 1},
            device_id_type=MESH,
        )

    return move


def attend_kernel(
    line, group,
    info_ref, x_ref, bundle_ref, cos_ref, sin_ref, packed,
    mid_ref, n2_ref, normed_ref, lowr_ref, rank_ref, q_ref, kv_out, attended_ref, log_ref,
    wq, wo, wkv, kvbuf, acc, peak, total, bq_ref, bkv_ref, wsem, recv, send, ksem,
):
    rows, width = x_ref.shape
    heads = width // HEAD_DIM
    cols = wq.shape[-1]
    kv_cols = wkv.shape[-1]
    scale = HEAD_DIM**-0.5
    me = lax.axis_index("tensor")
    one_way_barrier(me, line, 1)
    kv_loads, q_loads, o_loads = weight_loads(packed, wq, wo, wkv, wsem)
    for load in kv_loads + q_loads + o_loads:
        load.start()
    move = kv_exchange(me, line, kvbuf, recv, send)
    spread_qkv(bundle_ref, bq_ref, bkv_ref)
    misc = bundle_ref[rows_of(B_MISC)].astype(F32)
    q_bias = bundle_ref[rows_of(B_HEADS + 2)].astype(F32)[:1]
    low_in = bundle_ref[rows_of(B_INPUT, 3)]
    x = x_ref[...].astype(F32)
    inverse = lax.rsqrt(jnp.mean(x * x, axis=-1, keepdims=True) + EPSILON)
    normed_ref[...] = (x * inverse * misc[0:1]).astype(BF)
    low = dot_t(normed_ref[...], low_in).astype(BF)
    cos, sin = cos_ref[...], sin_ref[...]
    for load in kv_loads:
        load.wait()
    for t in range(line):
        span = slice(t * kv_cols, (t + 1) * kv_cols)
        kv = dot(normed_ref[...], flat(wkv, t)) + misc[2:3, span] + dot(low, bkv_ref[:, span])
        for h in range(kv_cols // HEAD_DIM):
            at = t * kv_cols + h * HEAD_DIM
            one = kv[:, h * HEAD_DIM : (h + 1) * HEAD_DIM]
            if at < KV_HEADS * HEAD_DIM:
                one = rotated(one, cos, sin)
            kvbuf[me, :, at : at + HEAD_DIM] = one.astype(BF)

    @pl.when(me < line - 1)
    def _():
        move(me).start()

    for load in q_loads:
        load.wait()
    for t in range(line):
        span = slice(t * cols, (t + 1) * cols)
        q = dot(normed_ref[...], flat(wq, t)) + q_bias[:, span] + dot(low, bq_ref[:, span])
        for h in range(cols // HEAD_DIM):
            at = t * cols + h * HEAD_DIM
            q_ref[:, at : at + HEAD_DIM] = rotated(
                q[:, h * HEAD_DIM : (h + 1) * HEAD_DIM], cos, sin
            ).astype(BF)
    acc[...] = jnp.zeros_like(acc)
    total[...] = jnp.zeros_like(total)
    peak[...] = jnp.full_like(peak, MASKED_SCORE)

    def block(o):
        allowed = allowed_keys(info_ref, o, rows, rows)

        def one(h, carry):
            kv_head = h // group
            k = kvbuf[o, :, head_cols(kv_head)]
            v = kvbuf[o, :, head_cols(KV_HEADS + kv_head)]
            scores = jnp.where(allowed, dot_t(k, q_ref[:, head_cols(h)]) * scale, MASKED_SCORE)
            top = jnp.maximum(peak[h], jnp.max(scores, axis=0, keepdims=True))
            soft = jnp.exp(scores - top)
            shift = jnp.exp(peak[h] - top)
            total[h] = total[h] * shift + jnp.sum(soft, axis=0, keepdims=True)
            acc[h] = acc[h] * shift + t_dot(v, soft.astype(BF))
            peak[h] = top
            return carry

        lax.fori_loop(0, heads, one, 0)

    for d in range(line):

        @pl.when(me >= d)
        def _():
            if d > 0:
                move(me - d).wait_recv()

                @pl.when(me < line - 1)
                def _():
                    move(me - d).start()

            block(me - d)

    keep = pltpu.make_async_copy(kvbuf, kv_out, ksem)
    keep.start()
    for h in range(heads):
        attended_ref[:, h * HEAD_DIM : (h + 1) * HEAD_DIM] = (acc[h] * (1.0 / total[h])).T.astype(BF)
        log_ref[h] = peak[h] + jnp.log(total[h])
    rank = dot_t(attended_ref[...], bundle_ref[rows_of(B_HEADS + 1)]).astype(BF)
    lowr_ref[...] = low
    rank_ref[...] = rank
    middle = x_ref[...].astype(F32) + dot(rank, bundle_ref[rows_of(B_RES_ONE)])
    for load in o_loads:
        load.wait()
    for t in range(line):
        middle = middle + dot_t(attended_ref[:, t * cols : (t + 1) * cols], flat(wo, t))
    mid_ref[...] = middle
    inverse = lax.rsqrt(jnp.mean(middle * middle, axis=-1, keepdims=True) + EPSILON)
    n2_ref[...] = (middle * inverse * misc[1:2]).astype(BF)
    keep.wait()
    for o in range(line):

        @pl.when(jnp.logical_and(me < line - 1, me >= o))
        def _():
            move(o).wait_send()


def attend_forward(x, w, info, tables):
    line = lax.axis_size("tensor")
    rows, width = x.shape
    heads = width // HEAD_DIM
    kv_width = 2 * KV_HEADS * HEAD_DIM
    groups, low_rows = w["packed"].shape[0], w["packed"].shape[2]
    outs = pl.pallas_call(
        partial(attend_kernel, line, heads // KV_HEADS),
        in_specs=[pl.BlockSpec(memory_space=pltpu.SMEM)] + [vspec()] * 4 + [hspec()],
        out_specs=[vspec()] * 6 + [hspec()] + [vspec()] * 2,
        out_shape=[
            jax.ShapeDtypeStruct((rows, width), F32),
            jax.ShapeDtypeStruct((rows, width), BF),
            jax.ShapeDtypeStruct((rows, width), BF),
            jax.ShapeDtypeStruct((rows, 3 * RANK), BF),
            jax.ShapeDtypeStruct((rows, RANK), BF),
            jax.ShapeDtypeStruct((rows, width), BF),
            jax.ShapeDtypeStruct((line, rows, kv_width), BF),
            jax.ShapeDtypeStruct((rows, width), BF),
            jax.ShapeDtypeStruct((heads, 1, rows), F32),
        ],
        scratch_shapes=[
            pltpu.VMEM((line, groups, low_rows, width // line), BF),
            pltpu.VMEM((line, groups, low_rows, width // line), BF),
            pltpu.VMEM((line, groups, low_rows, kv_width // line), BF),
            pltpu.VMEM((line, rows, kv_width), BF),
            pltpu.VMEM((heads, HEAD_DIM, rows), F32),
            pltpu.VMEM((heads, 1, rows), F32),
            pltpu.VMEM((heads, 1, rows), F32),
            pltpu.VMEM((3 * RANK, width), BF),
            pltpu.VMEM((3 * RANK, kv_width), BF),
            pltpu.SemaphoreType.DMA((3, line)),
            pltpu.SemaphoreType.DMA((line,)),
            pltpu.SemaphoreType.DMA((line,)),
            pltpu.SemaphoreType.DMA,
        ],
        compiler_params=pltpu.CompilerParams(
            collective_id=2, has_side_effects=True, vmem_limit_bytes=VMEM_LIMIT
        ),
        cost_estimate=pl.CostEstimate(
            flops=4 * rows * width * width * 2, bytes_accessed=5 * width * width, transcendentals=0
        ),
    )(
        info, x, w["bundle"], tables[0], tables[1], w["packed"],
    )
    return outs[0], outs[1], outs[2:]


def attend_back_kernel(
    line, group,
    info_ref, x_ref, mid_ref, dy_ref, dn2_ref, bundle_ref, cos_ref, sin_ref,
    normed_ref, lowr_ref, rank_ref, q_ref, kv_ref, attended_ref, log_ref, packed,
    dx_ref, dx_low_ref, grads_ref,
    wq, wo, wkv, do_ref, dq_acc, dq_ref, dkv_acc, partial_ref, from_right, delta, bq_ref, bkv_ref, wsem, recv, send,
):
    rows, width = x_ref.shape
    heads = width // HEAD_DIM
    cols = wq.shape[-1]
    kv_cols = wkv.shape[-1]
    kv_half = KV_HEADS * HEAD_DIM
    scale = HEAD_DIM**-0.5
    me = lax.axis_index("tensor")
    one_way_barrier(me, line, -1)
    kv_loads, q_loads, o_loads = weight_loads(packed, wq, wo, wkv, wsem)
    for load in o_loads + q_loads + kv_loads:
        load.start()

    def move(o):
        return pltpu.make_async_remote_copy(
            src_ref=partial_ref.at[o],
            dst_ref=from_right.at[o],
            send_sem=send.at[o],
            recv_sem=recv.at[o],
            device_id={"tensor": me - 1},
            device_id_type=MESH,
        )

    def through_norm(values, gain, grad_out):
        inverse = lax.rsqrt(jnp.mean(values * values, axis=-1, keepdims=True) + EPSILON)
        weighted = gain * grad_out
        return inverse * weighted - inverse * inverse * inverse * values * jnp.mean(
            weighted * values, axis=-1, keepdims=True
        )

    spread_qkv(bundle_ref, bq_ref, bkv_ref)
    misc = bundle_ref[rows_of(B_MISC)].astype(F32)
    att = bundle_ref[rows_of(B_HEADS + 1)]
    middle_grad = dy_ref[...].astype(F32) + through_norm(mid_ref[...], misc[1:2], dn2_ref[...])
    dx_ref[...] = middle_grad
    branch_grad = middle_grad.astype(BF)
    low, rank = lowr_ref[...], rank_ref[...]
    rank_grad = dot_t(branch_grad, bundle_ref[rows_of(B_RES_ONE)]).astype(BF)
    grads_ref[3 * RANK : 4 * RANK] = t_dot(rank, branch_grad).astype(BF)
    grads_ref[6 * RANK :] = t_dot(rank_grad, attended_ref[...]).astype(BF)
    for load in o_loads:
        load.wait()
    for t in range(line):
        span = slice(t * cols, (t + 1) * cols)
        do_ref[:, span] = (dot(branch_grad, flat(wo, t)) + dot(rank_grad, att[:, span])).astype(BF)
    for h in range(heads):
        span = slice(h * HEAD_DIM, (h + 1) * HEAD_DIM)
        both = do_ref[:, span].astype(F32) * attended_ref[:, span].astype(F32)
        delta[h] = jnp.sum(both.T, axis=0, keepdims=True)
    dq_acc[...] = jnp.zeros_like(dq_acc)

    def block(o):
        allowed = allowed_keys(info_ref, o, rows, rows)
        dkv_acc[...] = jnp.zeros_like(dkv_acc)

        def one(h, carry):
            kv_head = h // group
            k = kv_ref[o, :, head_cols(kv_head)]
            v = kv_ref[o, :, head_cols(KV_HEADS + kv_head)]
            q = q_ref[:, head_cols(h)]
            do = do_ref[:, head_cols(h)]
            scores = dot_t(k, q) * scale - log_ref[h]
            soft = jnp.exp(jnp.where(allowed, scores, MASKED_SCORE))
            grad = (soft * (dot_t(v, do) - delta[h])).astype(BF)
            dq_acc[h] += t_dot(k, grad)
            dkv_acc[:, head_cols(kv_head)] += dot(grad, q) * scale
            dkv_acc[:, head_cols(KV_HEADS + kv_head)] += dot(soft.astype(BF), do)
            return carry

        lax.fori_loop(0, heads, one, 0)
        partial_ref[o] = dkv_acc[...].astype(BF)

    for s in range(2 * line - 1):
        if s < line:

            @pl.when(me >= s)
            def _():
                block(s)

        for h in range(line - 1):
            o = s - h
            if 0 <= o < line - 1 - h:

                @pl.when(me == line - 1 - h)
                def _():
                    if h > 0:
                        move(o).wait_recv()
                        partial_ref[o] = (partial_ref[o].astype(F32) + from_right[o].astype(F32)).astype(BF)
                    move(o).start()

    cos, sin = cos_ref[...], -sin_ref[...]
    for h in range(heads):
        dq_ref[:, h * HEAD_DIM : (h + 1) * HEAD_DIM] = rotated(dq_acc[h].T * scale, cos, sin).astype(BF)
    dq = dq_ref[...]
    grads_ref[5 * RANK : 6 * RANK] = t_dot(low, dq)[:RANK].astype(BF)
    low_grad = dot_t(dq, bq_ref[...])
    for load in q_loads:
        load.wait()
    normed_grad = dot_t(dq[:, :cols], flat(wq, 0))
    for t in range(1, line):
        normed_grad = normed_grad + dot_t(dq[:, t * cols : (t + 1) * cols], flat(wq, t))
    dkv_acc[...] = partial_ref[me].astype(F32)

    @pl.when(me < line - 1)
    def _():
        move(me).wait_recv()
        dkv_acc[...] += from_right[me].astype(F32)

    for h in range(KV_HEADS):
        span = slice(h * HEAD_DIM, (h + 1) * HEAD_DIM)
        dkv_acc[:, span] = rotated(dkv_acc[:, span], cos, sin)
    dkv = dkv_acc[...].astype(BF)
    kv_grad = t_dot(low, dkv).astype(BF)
    grads_ref[4 * RANK : 5 * RANK, :kv_half] = kv_grad[RANK : 2 * RANK, :kv_half]
    grads_ref[4 * RANK : 5 * RANK, kv_half : 2 * kv_half] = kv_grad[2 * RANK :, kv_half:]
    grads_ref[4 * RANK : 5 * RANK, 2 * kv_half :] = jnp.zeros((RANK, width - 2 * kv_half), BF)
    low_grad = (low_grad + dot_t(dkv, bkv_ref[...])).astype(BF)
    grads_ref[: 3 * RANK] = t_dot(low_grad, normed_ref[...]).astype(BF)
    for load in kv_loads:
        load.wait()
    for t in range(line):
        normed_grad = normed_grad + dot_t(dkv[:, t * kv_cols : (t + 1) * kv_cols], flat(wkv, t))
    normed_grad = normed_grad + dot(low_grad, bundle_ref[rows_of(B_INPUT, 3)])
    dx = dx_ref[...] + through_norm(x_ref[...].astype(F32), misc[0:1], normed_grad)
    dx_ref[...] = dx
    dx_low_ref[...] = dx.astype(BF)
    for o in range(line - 1):

        @pl.when(me > o)
        def _():
            move(o).wait_send()


def attend_backward(x, middle, dy, dn2, w, kept, info, tables):
    line = lax.axis_size("tensor")
    rows, width = x.shape
    heads = width // HEAD_DIM
    kv_width = 2 * KV_HEADS * HEAD_DIM
    groups, low_rows = w["packed"].shape[0], w["packed"].shape[2]
    return pl.pallas_call(
        partial(attend_back_kernel, line, heads // KV_HEADS),
        in_specs=[pl.BlockSpec(memory_space=pltpu.SMEM)] + [vspec()] * 14 + [hspec()],
        out_specs=[vspec()] * 3,
        out_shape=[
            jax.ShapeDtypeStruct((rows, width), F32),
            jax.ShapeDtypeStruct((rows, width), BF),
            jax.ShapeDtypeStruct((7 * RANK, width), BF),
        ],
        scratch_shapes=[
            pltpu.VMEM((line, groups, low_rows, width // line), BF),
            pltpu.VMEM((line, groups, low_rows, width // line), BF),
            pltpu.VMEM((line, groups, low_rows, kv_width // line), BF),
            pltpu.VMEM((rows, width), BF),
            pltpu.VMEM((heads, HEAD_DIM, rows), F32),
            pltpu.VMEM((rows, width), BF),
            pltpu.VMEM((rows, kv_width), F32),
            pltpu.VMEM((line, rows, kv_width), BF),
            pltpu.VMEM((line, rows, kv_width), BF),
            pltpu.VMEM((heads, 1, rows), F32),
            pltpu.VMEM((3 * RANK, width), BF),
            pltpu.VMEM((3 * RANK, kv_width), BF),
            pltpu.SemaphoreType.DMA((3, line)),
            pltpu.SemaphoreType.DMA((line,)),
            pltpu.SemaphoreType.DMA((line,)),
        ],
        compiler_params=pltpu.CompilerParams(
            collective_id=3 if dy.dtype == F32 else 5, has_side_effects=True, vmem_limit_bytes=VMEM_LIMIT
        ),
        cost_estimate=pl.CostEstimate(
            flops=4 * rows * width * width * 2, bytes_accessed=5 * width * width, transcendentals=0
        ),
    )(
        info, x, middle, dy, dn2, w["bundle"], tables[0], tables[1], *kept, w["packed"],
    )


def reduce_kernel(
    line, peers, extra,
    attn_ref, whole_ref, parts_ref, y_first, y_second, g_first, g_second,
    out, y_out, g_out,
    mine, z_in, quarter, z_recv, z_send, dp_recv, dp_send, own_sem, t_recv, t_right, t_left,
    side_recv, side_send, side_own,
):
    r = RANK
    me, spot, core = lax.axis_index("tensor"), lax.axis_index("dp"), lax.axis_index("section")
    width = mine.shape[1]
    cols = width // line
    seqs = out.shape[0]
    seq = spot * 2 + core
    has_left, has_right = me > 0, me < line - 1
    barrier = pltpu.get_barrier_semaphore()

    def greet(**where):
        pl.semaphore_signal(barrier, inc=1, device_id=where, device_id_type=MESH)

    for k in range(1, line):
        greet(tensor=lax.rem(me + k, line))

    greet(section=1 - core)

    @pl.when(core == 0)
    def _():
        for k in range(1, peers):
            for c in range(2):
                greet(section=c, dp=lax.rem(spot + k, peers))

    pl.semaphore_wait(barrier, line - 1 + peers)

    def remote(src, dst, send, recv, **where):
        return pltpu.make_async_remote_copy(
            src_ref=src, dst_ref=dst, send_sem=send, recv_sem=recv, device_id=where, device_id_type=MESH
        )

    def lanes(t):
        return pl.ds(pl.multiple_of(t * cols, LANES), cols)

    def pieces(s):
        return (
            (parts_ref.at[pl.ds(0, 3 * r)], out.at[s, pl.ds(8 * r, 3 * r)]),
            (parts_ref.at[pl.ds(3 * r, 3 * r), pl.ds(0, extra)], out.at[s, pl.ds(11 * r, 3 * r), pl.ds(0, extra)]),
            (
                parts_ref.at[pl.ds(5 * r, r), pl.ds(extra, LANES)],
                out.at[s, pl.ds(13 * r, r), pl.ds(extra, LANES)],
            ),
            (quarter.at[pl.ds(0, 8 * r)], out.at[s, pl.ds(0, 8 * r), lanes(me)]),
            (quarter.at[pl.ds(8 * r, 2 * r)], out.at[s, pl.ds(11 * r, 2 * r), pl.ds(extra, cols)]),
        )

    def to_peer(k, i):
        src, dst = pieces(seq)[i]
        return remote(src, dst, dp_send.at[k, i], dp_recv.at[seq, i], section=0, dp=lax.rem(spot + k, peers))

    def stay(i):
        src, dst = pieces(seq)[i]
        return pltpu.make_async_copy(src, dst, own_sem.at[i])

    def send_pieces(which):
        for i in which:
            for k in range(1, peers):
                to_peer(k, i).start()

            @pl.when(core != 0)
            def _():
                to_peer(0, i).start()

            @pl.when(core == 0)
            def _():
                stay(i).start()

    def across(k):
        to = lax.rem(me + k, line)
        return remote(mine.at[:, lanes(to)], z_in.at[me], z_send.at[k], z_recv.at[me], tensor=to)

    def incoming(k):
        o = lax.rem(me + k, line)
        return remote(mine.at[:, lanes(me)], z_in.at[o], z_send.at[k], z_recv.at[o], tensor=o)

    def side(i, src, dst):
        return remote(src, dst.at[core], side_send.at[i], side_recv.at[i], section=1 - core)

    def side_keep(i, src, dst):
        return pltpu.make_async_copy(src, dst.at[core], side_own.at[i])

    pairs = ((y_first, y_second, y_out), (g_first, g_second, g_out))

    for first, rows, ref, start in (
        (0, 3, attn_ref, 0), (3, 2, whole_ref, 0), (5, 1, attn_ref, 3), (6, 1, whole_ref, 2), (7, 3, attn_ref, 4),
    ):
        mine[rows_of(first, rows)] = ref[rows_of(start, rows)]
    for k in range(1, line):
        across(k).start()
    send_pieces((0, 1, 2))
    for c in range(2):

        @pl.when(core == c)
        def _():
            for i, (first, second, dst) in enumerate(pairs):
                side(i, first if c == 1 else second, dst).start()
                side_keep(i, second if c == 1 else first, dst).start()

    total = mine[:, lanes(me)].astype(F32)
    for k in range(1, line):
        incoming(k).wait_recv()
        total = total + z_in[lax.rem(me + k, line)].astype(F32)
    quarter[...] = total.astype(BF)
    send_pieces((3, 4))

    def arrived(s, i):
        src, dst = pieces(s)[i]
        return remote(src, dst, dp_send.at[0, i], dp_recv.at[s, i], section=0)

    def along(s, o, side):
        place = out.at[s, pl.ds(0, 8 * r), lanes(o)]
        return remote(
            place, place, (t_right if side > 0 else t_left).at[s, o], t_recv.at[s, o], tensor=me + side
        )

    @pl.when(core == 0)
    def _():
        def own_rows(n, carry):
            s = lax.rem(seq + n, seqs)

            @pl.when(n == 0)
            def _():
                stay(3).wait()

            @pl.when(n > 0)
            def _():
                arrived(s, 3).wait_recv()

            @pl.when(has_right)
            def _():
                along(s, me, 1).start()

            @pl.when(has_left)
            def _():
                along(s, me, -1).start()

            return carry

        lax.fori_loop(0, seqs, own_rows, 0)
        for d in range(1, line):

            def others(n, carry):
                s = lax.rem(seq + n, seqs)

                @pl.when(me >= d)
                def _():
                    along(s, me - d, 1).wait_recv()

                    @pl.when(has_right)
                    def _():
                        along(s, me - d, 1).start()

                @pl.when(me + d < line)
                def _():
                    along(s, me + d, -1).wait_recv()

                    @pl.when(has_left)
                    def _():
                        along(s, me + d, -1).start()

                return carry

            lax.fori_loop(0, seqs, others, 0)

        def finish(n, carry):
            s = lax.rem(seq + n, seqs)

            @pl.when(n > 0)
            def _():
                for i in (0, 1, 2, 4):
                    arrived(s, i).wait_recv()

            for o in range(line):

                @pl.when(jnp.logical_and(has_right, me >= o))
                def _():
                    along(s, o, 1).wait_send()

                @pl.when(jnp.logical_and(has_left, me <= o))
                def _():
                    along(s, o, -1).wait_send()

            return carry

        lax.fori_loop(0, seqs, finish, 0)
        for i in (0, 1, 2, 4):
            stay(i).wait()

    for k in range(1, line):
        across(k).wait_send()
    for i in range(5):
        for k in range(1, peers):
            to_peer(k, i).wait_send()

        @pl.when(core != 0)
        def _():
            to_peer(0, i).wait_send()
    for i, (first, _, dst) in enumerate(pairs):
        side(i, first, dst).wait()
        side_keep(i, first, dst).wait()


def reduce_first(attn_part, whole, parts, extra, outs, grads):
    line, peers = lax.axis_size("tensor"), lax.axis_size("dp")
    width = parts.shape[1]
    seqs = 2 * peers
    dma = pltpu.SemaphoreType.DMA
    return pl.pallas_call(
        partial(reduce_kernel, line, peers, extra),
        in_specs=[vspec()] * 7,
        out_specs=[hspec()] * 3,
        out_shape=[
            jax.ShapeDtypeStruct((seqs, 14 * RANK, width), BF),
            jax.ShapeDtypeStruct((2,) + outs[0].shape, outs[0].dtype),
            jax.ShapeDtypeStruct((2,) + grads[0].shape, grads[0].dtype),
        ],
        scratch_shapes=[
            pltpu.VMEM((10 * RANK, width), BF),
            pltpu.VMEM((line, 10 * RANK, width // line), BF),
            pltpu.VMEM((10 * RANK, width // line), BF),
            dma((line,)),
            dma((line,)),
            dma((seqs, 5)),
            dma((peers, 5)),
            dma((5,)),
            dma((seqs, line)),
            dma((seqs, line)),
            dma((seqs, line)),
            dma((2,)),
            dma((2,)),
            dma((2,)),
        ],
        compiler_params=pltpu.CompilerParams(
            collective_id=6, has_side_effects=True, vmem_limit_bytes=VMEM_LIMIT
        ),
    )(attn_part, whole, parts, *outs, *grads)


def total_kernel(
    scale, hidden, q_cols,
    first, attn_in, whole_in, parts_in,
    input_ref, query_ref, kv_ref, expand_ref, attend_ref, shrink_ref, res_ref,
    block, ids, sem,
):
    r = RANK
    a = pl.program_id(0)
    core = lax.axis_index("section")
    width = block.shape[2]
    extra = hidden - width
    pad = extra + -hidden % (2 * LANES)

    @pl.when(jnp.logical_and(a == 0, core == 0))
    def _():
        load = pltpu.make_async_copy(first, block, sem.at[0])
        load.start()
        load.wait()

    @pl.when(jnp.logical_and(a == 0, core != 0))
    def _():
        def load(src, start, first, count, at):
            return pltpu.make_async_copy(src.at[:, rows_of(start, count)], block.at[:, rows_of(first, count)], sem.at[at])

        loads = [
            load(attn_in, 0, 0, 3, 1), load(whole_in, 0, 3, 2, 2), load(attn_in, 3, 5, 1, 3),
            load(whole_in, 2, 6, 1, 4), load(attn_in, 4, 7, 1, 5), load(parts_in, 0, 8, 6, 6),
        ]
        for one in loads:
            one.start()
        for one in loads:
            one.wait()
        mine = pl.ds(pl.multiple_of(lax.axis_index("tensor") * q_cols, LANES), q_cols)
        last = pltpu.make_async_copy(
            attn_in.at[:, rows_of(5, 2), mine], block.at[:, rows_of(11, 2), pl.ds(pad, q_cols)], sem.at[7]
        )
        last.start()
        last.wait()

    @pl.when(a == 0)
    def _():
        lane = lax.broadcasted_iota(jnp.int32, (1, LANES), 1).astype(F32)
        for i in range(block.shape[0]):
            names = block[i, 13 * r : 14 * r, pad : pad + LANES][:1].astype(F32)
            ids[i] = jnp.sum(lane * names).astype(jnp.int32)

    for ref in (input_ref, query_ref, kv_ref, expand_ref, attend_ref, shrink_ref, res_ref):
        ref[...] = jnp.zeros_like(ref)

    for i in range(block.shape[0]):

        @pl.when(ids[i] == a)
        def _():
            def part(row, rows, col, cols):
                return block[i, row : row + rows, col : col + cols].astype(F32) * scale

            input_ref[0] += part(0, 5 * r, 0, width)
            res_ref[0, 0] += part(5 * r, r, 0, width)
            res_ref[0, 1] += part(6 * r, r, 0, width)
            kv = part(7 * r, r, 0, 2 * kv_ref.shape[3])
            kv_ref[0, 0] += kv[:, : kv_ref.shape[3]]
            kv_ref[0, 1] += kv[:, kv_ref.shape[3] :]
            for j in range(2):
                expand_ref[0, j, :, :width] += part((8 + j) * r, r, 0, width)
                expand_ref[0, j, :, width:] += part((11 + j) * r, r, 0, pad)[:, :extra]
            shrink_ref[0, :, :width] += part(10 * r, r, 0, width)
            shrink_ref[0, :, width:] += part(13 * r, r, 0, pad)[:, :extra]
            query_ref[0] += part(11 * r, r, pad, q_cols)
            attend_ref[0] += part(12 * r, r, pad, q_cols)


def total_by_adapter(first, attn_in, whole_in, parts_in, count, scale, hidden, q_cols, kv_half):
    width = first.shape[2]
    r = RANK
    shapes = [
        (5 * r, width), (r, q_cols), (2, r, kv_half), (2, r, hidden), (r, q_cols), (r, hidden), (2, r, width),
    ]
    return pl.pallas_call(
        partial(total_kernel, scale, hidden, q_cols),
        grid=(count,),
        in_specs=[hspec()] * 4,
        out_specs=[pl.BlockSpec((1,) + s, lambda a, n=len(s): (a,) + (0,) * n) for s in shapes],
        out_shape=[jax.ShapeDtypeStruct((count,) + s, F32) for s in shapes],
        scratch_shapes=[
            pltpu.VMEM(first.shape, BF),
            pltpu.SMEM((first.shape[0],), jnp.int32),
            pltpu.SemaphoreType.DMA((8,)),
        ],
        compiler_params=pltpu.CompilerParams(vmem_limit_bytes=VMEM_LIMIT),
    )(first, attn_in, whole_in, parts_in)


def swap(pair):
    return lax.all_to_all(pair, "section", split_axis=0, concat_axis=0, tiled=True)


def local(
    inputs,
    lengths,
    adapter_ids,
    cotangent,
    norm_gain,
    query_weight,
    query_bias,
    keyvalue_weight,
    keyvalue_bias,
    output_weight,
    expand_weight,
    shrink_weight,
    adapter_input,
    adapter_query,
    adapter_keyvalue,
    adapter_expand,
    adapter_attend,
    adapter_shrink,
    adapter_residual,
):
    layers = lax.axis_size("section")
    tensor = lax.axis_size("tensor")
    core = lax.axis_index("section")
    place = lax.axis_index("tensor")
    rows, width = inputs.shape[1:]
    tokens = layers * rows * tensor * lax.axis_size("dp")
    kv_half = KV_HEADS * HEAD_DIM
    hidden = expand_weight.shape[3]
    r = RANK

    def turned(stack):
        return jnp.swapaxes(stack[0], 1, 2)

    def lined(stack):
        return stack[0].reshape(stack.shape[1], -1, stack.shape[-1])

    bundles, heads = pick_adapters(
        adapter_ids,
        (
            turned(adapter_input), lined(adapter_residual), lined(adapter_keyvalue), lined(adapter_expand),
            turned(adapter_shrink), adapter_query[0], turned(adapter_attend),
        ),
        (norm_gain[0], keyvalue_bias.reshape(1, -1), query_bias),
    )

    ff = jnp.concatenate(
        [m.reshape(layers, 1, hidden // layers, m.shape[1]) for m in (*turned(expand_weight), shrink_weight[0])],
        axis=1,
    )
    ff = swap(ff)
    kv = jnp.concatenate([keyvalue_weight[0, 0], keyvalue_weight[0, 1]], axis=1)
    kv_cols = kv.shape[1] // tensor
    kv = lax.dynamic_slice_in_dim(kv, place * kv_cols, kv_cols, 1)
    attn = jnp.concatenate([query_weight[0], output_weight[0].T, kv], axis=1)
    q_cols = query_weight.shape[2]
    attn = swap(attn.reshape(layers, attn.shape[0] // layers, attn.shape[1]))
    first_attn, line_attn, bundle = gather_first(attn, bundles, heads)

    def weights(layer):
        packed = first_attn if layer == 0 else lax.all_gather(line_attn, ("dp", "section"), axis=0)
        mlp = lax.all_gather(ff[layer], ("section", "dp"), axis=0)
        mlp = mlp.reshape(layers, -1, *mlp.shape[1:])
        if mlp.shape[4] % LANES:
            mlp = jnp.moveaxis(mlp, 1, 3)
            mlp = mlp.reshape(layers, 1, *mlp.shape[1:3], width)
        return dict(packed=packed, mlp=mlp, bundle=bundle[layer])

    x = lax.dynamic_index_in_dim(inputs, core, 0, keepdims=False)
    cot = lax.dynamic_index_in_dim(cotangent, core, 0, keepdims=False)
    length = lax.dynamic_index_in_dim(lengths, core, 0, keepdims=False)
    own_id = lax.dynamic_index_in_dim(adapter_ids, core, 0, keepdims=False)
    first_slot = place * rows
    info = jnp.stack([first_slot, length]).astype(jnp.int32)
    tables = rotary_tables(first_slot, rows)
    slot_ids = first_slot + jnp.arange(rows, dtype=jnp.int32)

    w = [weights(layer) for layer in range(layers)]
    outs, kept = [], []
    for layer in range(layers):
        middle, normed_two, attn_kept = attend_forward(x, w[layer], info, tables)
        shrunk, mlp_kept = mlp_forward(normed_two, w[layer])
        outs.append((middle + shrunk).astype(BF))
        kept.append((x, middle, attn_kept, mlp_kept))
        x = outs[-1]
    count = adapter_input.shape[1]
    extra = hidden + -hidden % (2 * LANES) - width
    names = jnp.broadcast_to((jnp.arange(LANES, dtype=jnp.int32) == own_id).astype(BF)[None], (r, LANES))

    def gather_all(*arrays):
        return [lax.all_gather(a, ("section", "dp"), axis=0) for a in arrays]

    grad = low_grad = jnp.where((slot_ids < length)[:, None], cot, jnp.zeros_like(cot))
    grads, gathered = [None] * layers, [None] * layers
    for layer in reversed(range(layers)):
        x, middle, attn_kept, mlp_kept = kept[layer]
        if layer < layers - 1:
            low_grad, here = lax.optimization_barrier((low_grad, here))
        dn2, whole, parts = mlp_backward(low_grad, w[layer], mlp_kept, names)
        if layer < layers - 1:
            total, dn2 = lax.optimization_barrier((total, dn2))
            gathered[layer + 1] = gather_all(*total, last_parts)
        grad, low_grad, attn_part = attend_backward(x, middle, grad, dn2, w[layer], attn_kept, info, tables)
        grads[layer] = grad
        here = (attn_part, whole)
        if layer > 0:
            total = lax.psum(here, "tensor")
            last_parts = parts
    gathered[0], layer_output, input_grad = reduce_first(*here, parts, extra, outs, grads)
    totals = total_by_adapter(
        gathered[0], *gathered[1], count, 1.0 / math.sqrt(tokens), hidden, q_cols, kv_half
    )
    turned = (0, 4, 5)
    totals = [jnp.swapaxes(total, 1, 2) if i in turned else total for i, total in enumerate(totals)]
    return (layer_output[None], input_grad[None]) + tuple(total[None] for total in totals)


def solution(mesh):
    placed = (
        P("dp", "tensor", None),
        P("dp"),
        P("dp"),
        P("dp", "tensor", None),
        P("section", None, None),
        P("section", "dp", "tensor"),
        P("section", "tensor"),
        P("section", None, "dp", None),
        P("section", None, None),
        P("section", "tensor", "dp"),
        P("section", None, "dp", "tensor"),
        P("section", "tensor", "dp"),
        P("section", None, None, None),
        P("section", None, None, "tensor"),
        P("section", None, None, None, None),
        P("section", None, None, None, "tensor"),
        P("section", None, "tensor", None),
        P("section", None, "tensor", None),
        P("section", None, None, None, None),
    )
    return jax.shard_map(
        local,
        mesh=mesh,
        in_specs=placed,
        out_specs=(
            P("section", "dp", "tensor", None),
            P("section", "dp", "tensor", None),
            P("section", None, None, None),
            P("section", None, None, "tensor"),
            P("section", None, None, None, None),
            P("section", None, None, None, "tensor"),
            P("section", None, "tensor", None),
            P("section", None, "tensor", None),
            P("section", None, None, None, None),
        ),
        check_vma=False,
    )
```

```python
from functools import partial
import math

import jax
import jax.numpy as jnp
from jax import lax
from jax.experimental import pallas as pl
from jax.experimental.pallas import tpu as pltpu
from jax.sharding import PartitionSpec as P

KV_HEADS = 2
HEAD_DIM = 128
RANK = 16
EPSILON = 1e-06
ROPE_BASE = 1000000.0
MASKED_SCORE = -1e30
CHUNKS = 4
LANES = 128
VMEM_LIMIT = 60 * 2**20
MESH = pl.DeviceIdType.MESH
BF = jnp.bfloat16
F32 = jnp.float32


def dot(a, b):
    return jnp.dot(a, b, preferred_element_type=F32)


def dot_t(a, b):
    return lax.dot_general(a, b, (((1,), (1,)), ((), ())), preferred_element_type=F32)


def t_dot(a, b):
    return lax.dot_general(a, b, (((0,), (0,)), ((), ())), preferred_element_type=F32)


def rotary_tables(first_slot, rows):
    half = HEAD_DIM // 2
    frequency = jnp.exp(-math.log(ROPE_BASE) * (2.0 * jnp.arange(half, dtype=F32) / HEAD_DIM))
    slots = (first_slot + jnp.arange(rows, dtype=jnp.int32)).astype(F32)
    angles = slots[:, None] * frequency[None, :]
    cos, sin = jnp.cos(angles), jnp.sin(angles)
    return jnp.concatenate([cos, cos], axis=1), jnp.concatenate([-sin, sin], axis=1)


B_INPUT, B_RES_ONE, B_RES_TWO, B_KV, B_MISC, B_FF, B_FF_TAIL, B_HEADS, B_ROWS = 0, 5, 6, 7, 8, 9, 12, 15, 18


def rows_of(first, count=1):
    return slice(first * RANK, (first + count) * RANK)


def pick_kernel(
    ids_ref, input_ref, res_ref, kv_ref, expand_ref, shrink_ref, query_ref, attend_ref, gain_ref, kvb_ref, qb_ref,
    out_ref, heads_ref,
):
    width = out_ref.shape[2]
    out_ref[0] = jnp.zeros(out_ref.shape[1:], BF)
    out_ref[0, rows_of(B_INPUT, 5)] = input_ref[0]
    out_ref[0, rows_of(B_RES_ONE, 2)] = res_ref[0]
    kv_half = kv_ref.shape[2]
    for i in range(2):
        out_ref[0, rows_of(B_KV), i * kv_half : (i + 1) * kv_half] = kv_ref[0, rows_of(i)]
    misc = rows_of(B_MISC).start
    out_ref[0, misc : misc + 2] = gain_ref[...]
    out_ref[0, misc + 2 : misc + 3, : 2 * kv_half] = kvb_ref[...]
    tail = expand_ref.shape[2] - width
    for i in range(3):
        part = expand_ref[0, rows_of(i)] if i < 2 else shrink_ref[0]
        out_ref[0, rows_of(B_FF + i)] = part[:, :width]
        out_ref[0, rows_of(B_FF_TAIL + i), :tail] = part[:, width:]
    heads_ref[0] = jnp.zeros(heads_ref.shape[1:], BF)
    heads_ref[0, rows_of(0)] = query_ref[0]
    heads_ref[0, rows_of(1)] = attend_ref[0]
    heads_ref[0, 2 * RANK : 2 * RANK + 1] = qb_ref[...]


def pick_adapters(ids, stacks, shared):
    count = ids.shape[0]
    width = stacks[0].shape[2]
    q_cols = stacks[5].shape[2]
    shapes = [(B_ROWS * RANK, width), (3 * RANK, q_cols)]
    return pl.pallas_call(
        pick_kernel,
        grid_spec=pltpu.PrefetchScalarGridSpec(
            num_scalar_prefetch=1,
            grid=(count,),
            in_specs=[pl.BlockSpec((1,) + a.shape[1:], lambda i, ids: (ids[i], 0, 0)) for a in stacks]
            + [pl.BlockSpec(a.shape, lambda i, ids: (0, 0)) for a in shared],
            out_specs=[pl.BlockSpec((1,) + a, lambda i, ids: (i, 0, 0)) for a in shapes],
        ),
        out_shape=[jax.ShapeDtypeStruct((count,) + a, BF) for a in shapes],
    )(ids, *stacks, *shared)


def spread_factors(bundle_ref, expand_ref, ash_ref):
    width = bundle_ref.shape[1]
    tail = ash_ref.shape[1] - width
    expand_ref[...] = jnp.zeros_like(expand_ref)
    for i in range(2):
        expand_ref[i, rows_of(i), :width] = bundle_ref[rows_of(B_FF + i)]
        expand_ref[i, rows_of(i), width:] = bundle_ref[rows_of(B_FF_TAIL + i), :tail]
    ash_ref[:, :width] = bundle_ref[rows_of(B_FF + 2)]
    ash_ref[:, width:] = bundle_ref[rows_of(B_FF_TAIL + 2), :tail]


def vspec():
    return pl.BlockSpec(memory_space=pltpu.VMEM)


def hspec():
    return pl.BlockSpec(memory_space=pl.ANY)


def line_barrier(me, line):
    barrier = pltpu.get_barrier_semaphore()

    @pl.when(me > 0)
    def _():
        pl.semaphore_signal(barrier, inc=1, device_id={"tensor": me - 1}, device_id_type=MESH)

    @pl.when(me < line - 1)
    def _():
        pl.semaphore_signal(barrier, inc=1, device_id={"tensor": me + 1}, device_id_type=MESH)

    pl.semaphore_wait(barrier, jnp.where(me > 0, 1, 0) + jnp.where(me < line - 1, 1, 0))


def within(c, chunks):
    return jnp.logical_and(c >= 0, c < chunks)


def line_exchange(line, chunks, gathered, partial_ref, from_left, from_right, own_out, sems, begin, work):
    ag_recv, ag_right, ag_left, r_recv, r_send, l_recv, l_send = sems
    me = lax.axis_index("tensor")

    def copy(ref, src, c, o, send, recv, side):
        return pltpu.make_async_remote_copy(
            src_ref=src.at[c, o],
            dst_ref=ref.at[c, o],
            send_sem=send.at[c, o],
            recv_sem=recv.at[c, o],
            device_id={"tensor": me + side},
            device_id_type=MESH,
        )

    def ag(c, o, side):
        return copy(gathered, gathered, c, o, ag_right if side > 0 else ag_left, ag_recv, side)

    def rs(c, o, side):
        if side > 0:
            return copy(from_left, partial_ref, c, o, r_send, r_recv, 1)
        return copy(from_right, partial_ref, c, o, l_send, l_recv, -1)

    has_left, has_right = me > 0, me < line - 1

    def step(s, carry):
        first = s + line - 1

        @pl.when(jnp.logical_and(within(first, chunks), has_right))
        def _():
            ag(first, me, 1).start()

        @pl.when(jnp.logical_and(within(first, chunks), has_left))
        def _():
            ag(first, me, -1).start()

        for d in range(1, line):
            c = s + line - 1 - d

            @pl.when(jnp.logical_and(within(c, chunks), me - d >= 0))
            def _():
                ag(c, me - d, 1).wait_recv()

                @pl.when(has_right)
                def _():
                    ag(c, me - d, 1).start()

            @pl.when(jnp.logical_and(within(c, chunks), me + d < line))
            def _():
                ag(c, me + d, -1).wait_recv()

                @pl.when(has_left)
                def _():
                    ag(c, me + d, -1).start()

        @pl.when(within(s, chunks))
        def _():
            work(s)

        for h in range(line):
            c = s - h

            @pl.when(jnp.logical_and(within(c, chunks), me == h))
            def _():
                for j in range(line - 1, h, -1):
                    if h > 0:
                        rs(c, j, 1).wait_recv()
                        partial_ref[c, j] = (
                            partial_ref[c, j].astype(F32) + from_left[c, j].astype(F32)
                        ).astype(BF)
                    if h < line - 1:
                        rs(c, j, 1).start()

            @pl.when(jnp.logical_and(within(c, chunks), me == line - 1 - h))
            def _():
                for j in range(line - 1 - h):
                    if h > 0:
                        rs(c, j, -1).wait_recv()
                        partial_ref[c, j] = (
                            partial_ref[c, j].astype(F32) + from_right[c, j].astype(F32)
                        ).astype(BF)
                    if h < line - 1:
                        rs(c, j, -1).start()

        last = s - (line - 1)

        @pl.when(within(last, chunks))
        def _():
            own_out[last] = partial_ref[last, me].astype(F32)

            @pl.when(has_left)
            def _():
                rs(last, me, 1).wait_recv()
                own_out[last] += from_left[last, me].astype(F32)

            @pl.when(has_right)
            def _():
                rs(last, me, -1).wait_recv()
                own_out[last] += from_right[last, me].astype(F32)

        return carry

    line_barrier(me, line)
    begin()
    lax.fori_loop(-(line - 1), chunks + line - 1, step, 0)

    def drain(c, carry):
        for o in range(line):

            @pl.when(jnp.logical_and(has_right, me >= o))
            def _():
                ag(c, o, 1).wait_send()

            @pl.when(jnp.logical_and(has_left, me <= o))
            def _():
                ag(c, o, -1).wait_send()

            @pl.when(me < o)
            def _():
                rs(c, o, 1).wait_send()

            @pl.when(me > o)
            def _():
                rs(c, o, -1).wait_send()

        return carry

    lax.fori_loop(0, chunks, drain, 0)


def exchange_scratch(line, chunks, rows, width):
    slots = (chunks, line, rows, width)
    return [pltpu.VMEM(slots, BF)] * 4 + [pltpu.SemaphoreType.DMA((chunks, line))] * 7


def ff_loads(packed, refs, wsem):
    halves, parts, _, rows, cols = packed.shape
    return [
        pltpu.make_async_copy(
            packed.at[h, p, i],
            ref.at[pl.ds(h * rows, rows), pl.ds(p * cols, cols)],
            wsem.at[i, h, p],
        )
        for i, ref in enumerate(refs)
        for h in range(halves)
        for p in range(parts)
    ]


def clear_tail(packed, refs):
    hidden = packed.shape[0] * packed.shape[3]
    for ref in refs:
        if ref.shape[0] > hidden:
            ref[hidden:] = jnp.zeros((ref.shape[0] - hidden, ref.shape[1]), BF)


def mlp_kernel(
    line, chunks, tile,
    n2_ref, packed, bundle_ref,
    out_ref, n2_out, gate_out, up_out,
    gathered, partial_ref, from_left, from_right, s0, s1, s2, s3, s4, s5, s6,
    wg, wu, ws, gate_st, up_st, acc, expand_ref, ash_ref, wsem, osem, nsem,
):
    rows, width = n2_ref.shape[1:]
    every = line * rows
    tiles = wg.shape[0] // tile
    high = bundle_ref[rows_of(B_INPUT + 3, 2)]
    res = bundle_ref[rows_of(B_RES_TWO)]
    me = lax.axis_index("tensor")
    loads = ff_loads(packed, (wg, wu, ws), wsem)

    def begin():
        for load in loads:
            load.start()
        clear_tail(packed, (wg, wu, ws))
        spread_factors(bundle_ref, expand_ref, ash_ref)
        for c in range(chunks):
            gathered[c, me] = n2_ref[c]

    def saves(c, slot):
        return (
            pltpu.make_async_copy(gate_st.at[slot], gate_out.at[c], osem.at[0, slot]),
            pltpu.make_async_copy(up_st.at[slot], up_out.at[c], osem.at[1, slot]),
        )

    def keep(c):
        return pltpu.make_async_copy(gathered.at[c], n2_out.at[c], nsem.at[c])

    def work(c):
        slot = c % 2

        @pl.when(c == 0)
        def _():
            for load in loads:
                load.wait()

        @pl.when(c >= 2)
        def _():
            for save in saves(c - 2, slot):
                save.wait()

        keep(c).start()
        x = gathered[c].reshape(every, width)
        er = dot_t(x, high).astype(BF)

        def one(f, rank):
            cols = pl.ds(pl.multiple_of(f * tile, tile), tile)
            gate = dot_t(x, wg[cols]) + dot(er, expand_ref[0, :, cols])
            up = dot_t(x, wu[cols]) + dot(er, expand_ref[1, :, cols])
            gate_st[slot, :, cols] = gate.astype(BF)
            up_st[slot, :, cols] = up.astype(BF)
            act = (gate * (1.0 / (1.0 + jnp.exp(-gate))) * up).astype(BF)
            now = dot(act, ws[cols])

            @pl.when(f == 0)
            def _():
                acc[...] = now

            @pl.when(f > 0)
            def _():
                acc[...] += now

            return rank + dot_t(act, ash_ref[:, cols])

        rank = lax.fori_loop(0, tiles, one, jnp.zeros((every, ash_ref.shape[0]), F32))
        total = acc[...] + dot(rank.astype(BF), res)
        partial_ref[c] = total.astype(BF).reshape(line, rows, width)
        for save in saves(c, slot):
            save.start()

    line_exchange(
        line, chunks, gathered, partial_ref, from_left, from_right, out_ref,
        (s0, s1, s2, s3, s4, s5, s6), begin, work,
    )
    for c in range(chunks):
        keep(c).wait()
    for c in range(max(chunks - 2, 0), chunks):
        for save in saves(c, c % 2):
            save.wait()


def ff_tile(hidden):
    return hidden


def mlp_forward(n2, w):
    line = lax.axis_size("tensor")
    rows, width = n2.shape
    halves, groups, _, low_rows, _ = w["mlp"].shape
    hidden = halves * low_rows + -(halves * low_rows) % (2 * LANES)
    part = rows // CHUNKS
    every = line * part
    out, n2_all, gate, up = pl.pallas_call(
        partial(mlp_kernel, line, CHUNKS, ff_tile(hidden)),
        in_specs=[vspec(), hspec(), vspec()],
        out_specs=[vspec()] + [hspec()] * 3,
        out_shape=[
            jax.ShapeDtypeStruct((CHUNKS, part, width), F32),
            jax.ShapeDtypeStruct((CHUNKS, line, part, width), BF),
            jax.ShapeDtypeStruct((CHUNKS, every, hidden), BF),
            jax.ShapeDtypeStruct((CHUNKS, every, hidden), BF),
        ],
        scratch_shapes=exchange_scratch(line, CHUNKS, part, width)
        + [pltpu.VMEM((hidden, width), BF)] * 3
        + [pltpu.VMEM((2, every, hidden), BF)] * 2
        + [
            pltpu.VMEM((every, width), F32),
            pltpu.VMEM((2, 2 * RANK, hidden), BF),
            pltpu.VMEM((RANK, hidden), BF),
            pltpu.SemaphoreType.DMA((3, halves, groups)),
            pltpu.SemaphoreType.DMA((2, 2)),
            pltpu.SemaphoreType.DMA((CHUNKS,)),
        ],
        compiler_params=pltpu.CompilerParams(
            collective_id=0, has_side_effects=True, vmem_limit_bytes=VMEM_LIMIT
        ),
        cost_estimate=pl.CostEstimate(
            flops=6 * line * rows * width * hidden,
            bytes_accessed=6 * width * hidden + 4 * line * rows * hidden,
            transcendentals=line * rows * hidden,
        ),
    )(
        n2.reshape(CHUNKS, part, width), w["mlp"], w["bundle"],
    )
    return out.reshape(rows, width), (n2_all.reshape(CHUNKS, every, width), gate, up)


def mlp_back_kernel(
    line, chunks, tile,
    ds_ref, packed, n2_hbm, gate_in, up_in, bundle_ref, names_ref,
    out_ref, whole_ref, parts_ref,
    gathered, partial_ref, from_left, from_right, s0, s1, s2, s3, s4, s5, s6,
    wg, wu, ws, gate_st, up_st, n2_st, acc, ghigh_ref, gexp_ref, gsh_ref, gres_ref, expand_ref, ash_ref, wsem, isem,
):
    rows, width = ds_ref.shape[1:]
    every = line * rows
    tiles = wg.shape[0] // tile
    high = bundle_ref[rows_of(B_INPUT + 3, 2)]
    res = bundle_ref[rows_of(B_RES_TWO)]
    me = lax.axis_index("tensor")
    loads = ff_loads(packed, (wg, wu, ws), wsem)

    def fetch(c):
        slot = c % 2
        return (
            pltpu.make_async_copy(gate_in.at[c], gate_st.at[slot], isem.at[0, slot]),
            pltpu.make_async_copy(up_in.at[c], up_st.at[slot], isem.at[1, slot]),
            pltpu.make_async_copy(n2_hbm.at[c], n2_st.at[slot], isem.at[2, slot]),
        )

    def begin():
        for load in loads:
            load.start()
        clear_tail(packed, (wg, wu, ws))
        spread_factors(bundle_ref, expand_ref, ash_ref)
        for one in fetch(0):
            one.start()
        for c in range(chunks):
            gathered[c, me] = ds_ref[c]
        for ref in (ghigh_ref, gexp_ref, gsh_ref, gres_ref):
            ref[...] = jnp.zeros_like(ref)

    def work(c):
        slot = c % 2

        @pl.when(c == 0)
        def _():
            for load in loads:
                load.wait()

        for one in fetch(c):
            one.wait()

        @pl.when(c + 1 < chunks)
        def _():
            for one in fetch(c + 1):
                one.start()

        ds = gathered[c].reshape(every, width)
        n2 = n2_st[slot]
        er = dot_t(n2, high).astype(BF)
        rank_in = dot_t(ds, res).astype(BF)

        def one(f, carry):
            rank_out, srank = carry
            cols = pl.ds(pl.multiple_of(f * tile, tile), tile)
            act_grad = dot_t(ds, ws[cols]) + dot(rank_in, ash_ref[:, cols])
            gate = gate_st[slot, :, cols].astype(F32)
            up = up_st[slot, :, cols].astype(F32)
            sig = 1.0 / (1.0 + jnp.exp(-gate))
            silu = gate * sig
            act = (silu * up).astype(BF)
            gate_grad = (act_grad * up * (sig + silu * (1.0 - sig))).astype(BF)
            up_grad = (act_grad * silu).astype(BF)
            now = dot(gate_grad, wg[cols]) + dot(up_grad, wu[cols])

            @pl.when(f == 0)
            def _():
                acc[...] = now

            @pl.when(f > 0)
            def _():
                acc[...] += now

            gexp_ref[0, :, cols] += t_dot(er, gate_grad)
            gexp_ref[1, :, cols] += t_dot(er, up_grad)
            gsh_ref[:, cols] += t_dot(rank_in, act)
            rank_out = rank_out + dot_t(gate_grad, expand_ref[0, :, cols])
            rank_out = rank_out + dot_t(up_grad, expand_ref[1, :, cols])
            return rank_out, srank + dot_t(act, ash_ref[:, cols])

        rank_out, srank = lax.fori_loop(
            0,
            tiles,
            one,
            (
                jnp.zeros((every, expand_ref.shape[1]), F32),
                jnp.zeros((every, ash_ref.shape[0]), F32),
            ),
        )
        rank_out = rank_out.astype(BF)
        total = acc[...] + dot(rank_out, high)
        partial_ref[c] = total.astype(BF).reshape(line, rows, width)
        ghigh_ref[...] += t_dot(rank_out, n2)
        gres_ref[...] += t_dot(srank.astype(BF), ds)

    line_exchange(
        line, chunks, gathered, partial_ref, from_left, from_right, out_ref,
        (s0, s1, s2, s3, s4, s5, s6), begin, work,
    )
    whole_ref[: 2 * RANK] = ghigh_ref[...].astype(BF)
    whole_ref[2 * RANK :] = gres_ref[...].astype(BF)
    extra = gsh_ref.shape[1] - width
    parts_ref[3 * RANK :, extra:] = jnp.zeros((3 * RANK, width - extra), BF)
    for i, part in enumerate((gexp_ref[0, :RANK], gexp_ref[1, RANK:], gsh_ref[...])):
        part = part.astype(BF)
        parts_ref[i * RANK : (i + 1) * RANK] = part[:, :width]
        parts_ref[(3 + i) * RANK : (4 + i) * RANK, :extra] = part[:, width:]
    parts_ref[rows_of(5), extra : extra + LANES] = names_ref[...]


def mlp_backward(ds, w, saved, names):
    n2_all, gate, up = saved
    line = lax.axis_size("tensor")
    rows, width = ds.shape
    halves, groups, _, low_rows, _ = w["mlp"].shape
    hidden = halves * low_rows + -(halves * low_rows) % (2 * LANES)
    part = rows // CHUNKS
    every = line * part
    out, whole, parts = pl.pallas_call(
        partial(mlp_back_kernel, line, CHUNKS, ff_tile(hidden)),
        in_specs=[vspec()] + [hspec()] * 4 + [vspec()] * 2,
        out_specs=[vspec()] * 3,
        out_shape=[
            jax.ShapeDtypeStruct((CHUNKS, part, width), F32),
            jax.ShapeDtypeStruct((3 * RANK, width), BF),
            jax.ShapeDtypeStruct((6 * RANK, width), BF),
        ],
        scratch_shapes=exchange_scratch(line, CHUNKS, part, width)
        + [pltpu.VMEM((hidden, width), BF)] * 3
        + [pltpu.VMEM((2, every, hidden), BF)] * 2
        + [
            pltpu.VMEM((2, every, width), BF),
            pltpu.VMEM((every, width), F32),
            pltpu.VMEM((2 * RANK, width), F32),
            pltpu.VMEM((2, 2 * RANK, hidden), F32),
            pltpu.VMEM((RANK, hidden), F32),
            pltpu.VMEM((RANK, width), F32),
            pltpu.VMEM((2, 2 * RANK, hidden), BF),
            pltpu.VMEM((RANK, hidden), BF),
            pltpu.SemaphoreType.DMA((3, halves, groups)),
            pltpu.SemaphoreType.DMA((3, 2)),
        ],
        compiler_params=pltpu.CompilerParams(
            collective_id=1, has_side_effects=True, vmem_limit_bytes=VMEM_LIMIT
        ),
        cost_estimate=pl.CostEstimate(
            flops=6 * line * rows * width * hidden,
            bytes_accessed=6 * width * hidden + 4 * line * rows * hidden,
            transcendentals=line * rows * hidden,
        ),
    )(
        ds.reshape(CHUNKS, part, width), w["mlp"], n2_all, gate, up, w["bundle"], names,
    )
    return out.reshape(rows, width), whole, parts


def gather_kernel(
    line, peers,
    attn, bundles, heads,
    first_out, second_out, bundle_out,
    own_sem, z_recv, z_right, z_left, dp_recv, dp_send, core_recv, core_send, side_recv, side_send, side_own,
):
    me, spot, core = lax.axis_index("tensor"), lax.axis_index("dp"), lax.axis_index("section")
    other = 1 - core
    has_left, has_right = me > 0, me < line - 1
    barrier = pltpu.get_barrier_semaphore()

    def greet(**where):
        pl.semaphore_signal(barrier, inc=1, device_id=where, device_id_type=MESH)

    @pl.when(has_left)
    def _():
        greet(tensor=me - 1)

    @pl.when(has_right)
    def _():
        greet(tensor=me + 1)

    greet(section=other)
    square = peers == 4

    def partner(k):
        if square:
            return (None, spot + 1 - 2 * lax.rem(spot, 2), lax.rem(spot + 2, 4), 3 - spot)[k]
        return lax.rem(spot + k, peers)

    def origin(k):
        return partner(k) if square else lax.rem(spot + peers - k, peers)

    direct = (1, 2) if square else tuple(range(1, peers))
    for k in range(1, peers):
        greet(dp=partner(k))
    pl.semaphore_wait(barrier, jnp.where(has_left, 1, 0) + jnp.where(has_right, 1, 0) + peers)

    mine = spot * 2 + core
    plain, part = bundles.shape[1] - heads.shape[1], heads.shape[2]

    def head_place(layer, o):
        return bundle_out.at[layer, pl.ds(plain, heads.shape[1]), pl.ds(o * part, part)]

    def places(o):
        return first_out.at[mine, o], second_out.at[o], head_place(core, o), head_place(other, o)

    sides = [
        pltpu.make_async_remote_copy(
            src_ref=src,
            dst_ref=dst,
            send_sem=side_send.at[i],
            recv_sem=side_recv.at[i],
            device_id={"section": other},
            device_id_type=MESH,
        )
        for i, (src, dst) in enumerate(
            (
                (bundles.at[other, pl.ds(0, plain)], bundle_out.at[core, pl.ds(0, plain)]),
                (heads.at[other], head_place(core, me)),
            )
        )
    ]
    side_keep = pltpu.make_async_copy(
        bundles.at[core, pl.ds(0, plain)], bundle_out.at[core, pl.ds(0, plain)], side_own
    )
    sources = (attn.at[0], attn.at[1], heads.at[core], head_place(other, me))
    keeps = [
        pltpu.make_async_copy(src, dst, own_sem.at[i]) for i, (src, dst) in enumerate(zip(sources[:3], places(me)))
    ]

    def remote(src, dst, send, recv, **where):
        return pltpu.make_async_remote_copy(
            src_ref=src, dst_ref=dst, send_sem=send, recv_sem=recv, device_id=where, device_id_type=MESH
        )

    def along(i, o, side, own):
        dst = places(o)[i]
        return remote(
            sources[i] if own else dst,
            dst,
            (z_right if side > 0 else z_left).at[i, o],
            z_recv.at[i, o],
            tensor=me + side,
        )

    outs = (first_out,)

    def to_peer(lay, k, o, own):
        dst = outs[lay].at[mine, o]
        return remote(
            attn.at[lay] if own else dst, dst, dp_send.at[lay, k, o], dp_recv.at[lay, spot, o], dp=partner(k)
        )

    def from_peer(lay, k, o):
        p = origin(k)
        slot = outs[lay].at[p * 2 + core, o]
        to = partner(3 - k) if square and k < 3 else p
        return remote(slot, slot, dp_send.at[lay, peers - 1, o], dp_recv.at[lay, p, o], dp=to)

    def to_core(lay, p, o, own):
        dst = outs[lay].at[p * 2 + core, o]
        return remote(
            attn.at[lay] if own else dst, dst, core_send.at[lay, p, o], core_recv.at[lay, p, o], section=other
        )

    def spread(lay, o, own):
        for k in direct:
            to_peer(lay, k, o, own).start()
        to_core(lay, spot, o, own).start()

    for side in sides:
        side.start()
    for i in range(4):
        if i == 3:
            sides[1].wait_recv()

        @pl.when(has_right)
        def _():
            along(i, me, 1, True).start()

        @pl.when(has_left)
        def _():
            along(i, me, -1, True).start()

        if i == 0:
            spread(i, me, True)
    for keep in keeps:
        keep.start()
    side_keep.start()
    for d in range(1, line):
        for i in range(4):

            @pl.when(me >= d)
            def _():
                along(i, me - d, 1, False).wait_recv()

                @pl.when(has_right)
                def _():
                    along(i, me - d, 1, False).start()

                if i == 0:
                    spread(i, me - d, False)

            @pl.when(me + d < line)
            def _():
                along(i, me + d, -1, False).wait_recv()

                @pl.when(has_left)
                def _():
                    along(i, me + d, -1, False).start()

                if i == 0:
                    spread(i, me + d, False)

    half = line // 2

    def pass_on(n, carry):
        o = lax.rem(me + n, line)
        for lay in range(1):
            for k in direct:
                from_peer(lay, k, o).wait_recv()
                if square:

                    @pl.when(o < half if k == 1 else o >= half)
                    def _():
                        from_peer(lay, k, o).start()

                to_core(lay, origin(k), o, False).start()
        return carry

    lax.fori_loop(0, line, pass_on, 0)

    def pass_last(n, carry):
        o = lax.rem(me + n, line)
        for lay in range(1):
            from_peer(lay, 3, o).wait_recv()
            to_core(lay, origin(3), o, False).start()
        return carry

    if square:
        lax.fori_loop(0, line, pass_last, 0)

    def finish(o, carry):
        for lay in range(1):
            for k in direct:
                to_peer(lay, k, o, False).wait_send()
            if square:
                from_peer(lay, 1, o).wait_send()
            for p in range(peers):
                to_core(lay, p, o, False).wait_send()
                slot = outs[lay].at[p * 2 + other, o]
                remote(slot, slot, core_send.at[lay, p, o], core_recv.at[lay, p, o], section=other).wait_recv()
        for i in range(4):

            @pl.when(jnp.logical_and(has_right, me >= o))
            def _():
                along(i, o, 1, False).wait_send()

            @pl.when(jnp.logical_and(has_left, me <= o))
            def _():
                along(i, o, -1, False).wait_send()

        return carry

    lax.fori_loop(0, line, finish, 0)
    for keep in keeps:
        keep.wait()
    side_keep.wait()
    sides[0].wait_recv()
    for side in sides:
        side.wait_send()


def gather_first(attn, bundles, heads):
    line, peers = lax.axis_size("tensor"), lax.axis_size("dp")
    cores, part, cols = attn.shape
    dma = pltpu.SemaphoreType.DMA
    return pl.pallas_call(
        partial(gather_kernel, line, peers),
        in_specs=[vspec()] * 3,
        out_specs=[hspec()] * 3,
        out_shape=[
            jax.ShapeDtypeStruct((peers * cores, line, part, cols), BF),
            jax.ShapeDtypeStruct((line, part, cols), BF),
            jax.ShapeDtypeStruct(bundles.shape, BF),
        ],
        scratch_shapes=[dma((3,)), dma((4, line)), dma((4, line)), dma((4, line))]
        + [dma((1, peers, line))] * 4
        + [dma((2,)), dma((2,)), dma],
        compiler_params=pltpu.CompilerParams(
            collective_id=4, has_side_effects=True, vmem_limit_bytes=VMEM_LIMIT
        ),
    )(attn, bundles, heads)


def rotated(x, cos, sin):
    return x * cos + pltpu.roll(x, HEAD_DIM // 2, 1) * sin


def head_cols(h):
    return pl.ds(pl.multiple_of(h * HEAD_DIM, HEAD_DIM), HEAD_DIM)


def weight_loads(packed, wq, wo, wkv, wsem):
    cols, kv_cols = wq.shape[-1], wkv.shape[-1]
    loads = []
    for i, (ref, start, size) in enumerate(((wkv, 2 * cols, kv_cols), (wq, 0, cols), (wo, cols, cols))):
        loads.append(
            [
                pltpu.make_async_copy(packed.at[:, t, :, pl.ds(start, size)], ref.at[t], wsem.at[i, t])
                for t in range(ref.shape[0])
            ]
        )
    return loads


def flat(ref, t):
    groups, rows, cols = ref.shape[1:]
    return ref[t].reshape(groups * rows, cols)


def allowed_keys(info_ref, block, keys, rows):
    row = info_ref[0] + lax.broadcasted_iota(jnp.int32, (1, rows), 1)
    last = jnp.minimum(row, info_ref[1] - 1)
    return block * keys + lax.broadcasted_iota(jnp.int32, (keys, rows), 0) <= last


def one_way_barrier(me, line, side):
    barrier = pltpu.get_barrier_semaphore()
    first, last = (0, line - 1) if side > 0 else (line - 1, 0)

    @pl.when(me != first)
    def _():
        pl.semaphore_signal(barrier, inc=1, device_id={"tensor": me - side}, device_id_type=MESH)

    @pl.when(me != last)
    def _():
        pl.semaphore_wait(barrier, 1)


def spread_qkv(bundle_ref, bq_ref, bkv_ref):
    kv_half = bkv_ref.shape[1] // 2
    bq_ref[...] = jnp.zeros_like(bq_ref)
    bkv_ref[...] = jnp.zeros_like(bkv_ref)
    bq_ref[rows_of(0)] = bundle_ref[rows_of(B_HEADS)]
    for i in range(2):
        span = slice(i * kv_half, (i + 1) * kv_half)
        bkv_ref[rows_of(1 + i), span] = bundle_ref[rows_of(B_KV), span]


def kv_exchange(me, line, kvbuf, recv, send):
    def move(o):
        return pltpu.make_async_remote_copy(
            src_ref=kvbuf.at[o],
            dst_ref=kvbuf.at[o],
            send_sem=send.at[o],
            recv_sem=recv.at[o],
            device_id={"tensor": me + 1},
            device_id_type=MESH,
        )

    return move


def attend_kernel(
    line, group,
    info_ref, x_ref, bundle_ref, cos_ref, sin_ref, packed,
    mid_ref, n2_ref, normed_ref, lowr_ref, rank_ref, q_ref, kv_out, attended_ref, log_ref,
    wq, wo, wkv, kvbuf, acc, peak, total, bq_ref, bkv_ref, wsem, recv, send, ksem,
):
    rows, width = x_ref.shape
    heads = width // HEAD_DIM
    cols = wq.shape[-1]
    kv_cols = wkv.shape[-1]
    scale = HEAD_DIM**-0.5
    me = lax.axis_index("tensor")
    one_way_barrier(me, line, 1)
    kv_loads, q_loads, o_loads = weight_loads(packed, wq, wo, wkv, wsem)
    for load in kv_loads + q_loads + o_loads:
        load.start()
    move = kv_exchange(me, line, kvbuf, recv, send)
    spread_qkv(bundle_ref, bq_ref, bkv_ref)
    misc = bundle_ref[rows_of(B_MISC)].astype(F32)
    q_bias = bundle_ref[rows_of(B_HEADS + 2)].astype(F32)[:1]
    low_in = bundle_ref[rows_of(B_INPUT, 3)]
    x = x_ref[...].astype(F32)
    inverse = lax.rsqrt(jnp.mean(x * x, axis=-1, keepdims=True) + EPSILON)
    normed_ref[...] = (x * inverse * misc[0:1]).astype(BF)
    low = dot_t(normed_ref[...], low_in).astype(BF)
    cos, sin = cos_ref[...], sin_ref[...]
    for load in kv_loads:
        load.wait()
    for t in range(line):
        span = slice(t * kv_cols, (t + 1) * kv_cols)
        kv = dot(normed_ref[...], flat(wkv, t)) + misc[2:3, span] + dot(low, bkv_ref[:, span])
        for h in range(kv_cols // HEAD_DIM):
            at = t * kv_cols + h * HEAD_DIM
            one = kv[:, h * HEAD_DIM : (h + 1) * HEAD_DIM]
            if at < KV_HEADS * HEAD_DIM:
                one = rotated(one, cos, sin)
            kvbuf[me, :, at : at + HEAD_DIM] = one.astype(BF)

    @pl.when(me < line - 1)
    def _():
        move(me).start()

    for load in q_loads:
        load.wait()
    for t in range(line):
        span = slice(t * cols, (t + 1) * cols)
        q = dot(normed_ref[...], flat(wq, t)) + q_bias[:, span] + dot(low, bq_ref[:, span])
        for h in range(cols // HEAD_DIM):
            at = t * cols + h * HEAD_DIM
            q_ref[:, at : at + HEAD_DIM] = rotated(
                q[:, h * HEAD_DIM : (h + 1) * HEAD_DIM], cos, sin
            ).astype(BF)
    acc[...] = jnp.zeros_like(acc)
    total[...] = jnp.zeros_like(total)
    peak[...] = jnp.full_like(peak, MASKED_SCORE)

    def block(o):
        allowed = allowed_keys(info_ref, o, rows, rows)

        def one(h, carry):
            kv_head = h // group
            k = kvbuf[o, :, head_cols(kv_head)]
            v = kvbuf[o, :, head_cols(KV_HEADS + kv_head)]
            scores = jnp.where(allowed, dot_t(k, q_ref[:, head_cols(h)]) * scale, MASKED_SCORE)
            top = jnp.maximum(peak[h], jnp.max(scores, axis=0, keepdims=True))
            soft = jnp.exp(scores - top)
            shift = jnp.exp(peak[h] - top)
            total[h] = total[h] * shift + jnp.sum(soft, axis=0, keepdims=True)
            acc[h] = acc[h] * shift + t_dot(v, soft.astype(BF))
            peak[h] = top
            return carry

        lax.fori_loop(0, heads, one, 0, unroll=12)

    for d in range(line):

        @pl.when(me >= d)
        def _():
            if d > 0:
                move(me - d).wait_recv()

                @pl.when(me < line - 1)
                def _():
                    move(me - d).start()

            block(me - d)

    keep = pltpu.make_async_copy(kvbuf, kv_out, ksem)
    keep.start()
    for h in range(heads):
        attended_ref[:, h * HEAD_DIM : (h + 1) * HEAD_DIM] = (acc[h] * (1.0 / total[h])).T.astype(BF)
        log_ref[h] = peak[h] + jnp.log(total[h])
    rank = dot_t(attended_ref[...], bundle_ref[rows_of(B_HEADS + 1)]).astype(BF)
    lowr_ref[...] = low
    rank_ref[...] = rank
    middle = x_ref[...].astype(F32) + dot(rank, bundle_ref[rows_of(B_RES_ONE)])
    for load in o_loads:
        load.wait()
    for t in range(line):
        middle = middle + dot_t(attended_ref[:, t * cols : (t + 1) * cols], flat(wo, t))
    mid_ref[...] = middle
    inverse = lax.rsqrt(jnp.mean(middle * middle, axis=-1, keepdims=True) + EPSILON)
    n2_ref[...] = (middle * inverse * misc[1:2]).astype(BF)
    keep.wait()
    for o in range(line):

        @pl.when(jnp.logical_and(me < line - 1, me >= o))
        def _():
            move(o).wait_send()


def attend_forward(x, w, info, tables):
    line = lax.axis_size("tensor")
    rows, width = x.shape
    heads = width // HEAD_DIM
    kv_width = 2 * KV_HEADS * HEAD_DIM
    groups, low_rows = w["packed"].shape[0], w["packed"].shape[2]
    outs = pl.pallas_call(
        partial(attend_kernel, line, heads // KV_HEADS),
        in_specs=[pl.BlockSpec(memory_space=pltpu.SMEM)] + [vspec()] * 4 + [hspec()],
        out_specs=[vspec()] * 6 + [hspec()] + [vspec()] * 2,
        out_shape=[
            jax.ShapeDtypeStruct((rows, width), F32),
            jax.ShapeDtypeStruct((rows, width), BF),
            jax.ShapeDtypeStruct((rows, width), BF),
            jax.ShapeDtypeStruct((rows, 3 * RANK), BF),
            jax.ShapeDtypeStruct((rows, RANK), BF),
            jax.ShapeDtypeStruct((rows, width), BF),
            jax.ShapeDtypeStruct((line, rows, kv_width), BF),
            jax.ShapeDtypeStruct((rows, width), BF),
            jax.ShapeDtypeStruct((heads, 1, rows), F32),
        ],
        scratch_shapes=[
            pltpu.VMEM((line, groups, low_rows, width // line), BF),
            pltpu.VMEM((line, groups, low_rows, width // line), BF),
            pltpu.VMEM((line, groups, low_rows, kv_width // line), BF),
            pltpu.VMEM((line, rows, kv_width), BF),
            pltpu.VMEM((heads, HEAD_DIM, rows), F32),
            pltpu.VMEM((heads, 1, rows), F32),
            pltpu.VMEM((heads, 1, rows), F32),
            pltpu.VMEM((3 * RANK, width), BF),
            pltpu.VMEM((3 * RANK, kv_width), BF),
            pltpu.SemaphoreType.DMA((3, line)),
            pltpu.SemaphoreType.DMA((line,)),
            pltpu.SemaphoreType.DMA((line,)),
            pltpu.SemaphoreType.DMA,
        ],
        compiler_params=pltpu.CompilerParams(
            collective_id=2, has_side_effects=True, vmem_limit_bytes=VMEM_LIMIT
        ),
        cost_estimate=pl.CostEstimate(
            flops=4 * rows * width * width * 2, bytes_accessed=5 * width * width, transcendentals=0
        ),
    )(
        info, x, w["bundle"], tables[0], tables[1], w["packed"],
    )
    return outs[0], outs[1], outs[2:]


def attend_back_kernel(
    line, group,
    info_ref, x_ref, mid_ref, dy_ref, dn2_ref, bundle_ref, cos_ref, sin_ref,
    normed_ref, lowr_ref, rank_ref, q_ref, kv_ref, attended_ref, log_ref, packed,
    dx_ref, dx_low_ref, grads_ref,
    wq, wo, wkv, do_ref, dq_acc, dq_ref, dkv_acc, partial_ref, from_right, delta, bq_ref, bkv_ref, wsem, recv, send,
):
    rows, width = x_ref.shape
    heads = width // HEAD_DIM
    cols = wq.shape[-1]
    kv_cols = wkv.shape[-1]
    kv_half = KV_HEADS * HEAD_DIM
    scale = HEAD_DIM**-0.5
    me = lax.axis_index("tensor")
    one_way_barrier(me, line, -1)
    kv_loads, q_loads, o_loads = weight_loads(packed, wq, wo, wkv, wsem)
    for load in o_loads + q_loads + kv_loads:
        load.start()

    def move(o):
        return pltpu.make_async_remote_copy(
            src_ref=partial_ref.at[o],
            dst_ref=from_right.at[o],
            send_sem=send.at[o],
            recv_sem=recv.at[o],
            device_id={"tensor": me - 1},
            device_id_type=MESH,
        )

    def through_norm(values, gain, grad_out):
        inverse = lax.rsqrt(jnp.mean(values * values, axis=-1, keepdims=True) + EPSILON)
        weighted = gain * grad_out
        return inverse * weighted - inverse * inverse * inverse * values * jnp.mean(
            weighted * values, axis=-1, keepdims=True
        )

    spread_qkv(bundle_ref, bq_ref, bkv_ref)
    misc = bundle_ref[rows_of(B_MISC)].astype(F32)
    att = bundle_ref[rows_of(B_HEADS + 1)]
    middle_grad = dy_ref[...].astype(F32) + through_norm(mid_ref[...], misc[1:2], dn2_ref[...])
    dx_ref[...] = middle_grad
    branch_grad = middle_grad.astype(BF)
    low, rank = lowr_ref[...], rank_ref[...]
    rank_grad = dot_t(branch_grad, bundle_ref[rows_of(B_RES_ONE)]).astype(BF)
    grads_ref[3 * RANK : 4 * RANK] = t_dot(rank, branch_grad).astype(BF)
    grads_ref[6 * RANK :] = t_dot(rank_grad, attended_ref[...]).astype(BF)
    for load in o_loads:
        load.wait()
    for t in range(line):
        span = slice(t * cols, (t + 1) * cols)
        do_ref[:, span] = (dot(branch_grad, flat(wo, t)) + dot(rank_grad, att[:, span])).astype(BF)
    for h in range(heads):
        span = slice(h * HEAD_DIM, (h + 1) * HEAD_DIM)
        both = do_ref[:, span].astype(F32) * attended_ref[:, span].astype(F32)
        delta[h] = jnp.sum(both.T, axis=0, keepdims=True)
    dq_acc[...] = jnp.zeros_like(dq_acc)

    def block(o):
        allowed = allowed_keys(info_ref, o, rows, rows)
        dkv_acc[...] = jnp.zeros_like(dkv_acc)

        def one(h, carry):
            kv_head = h // group
            k = kv_ref[o, :, head_cols(kv_head)]
            v = kv_ref[o, :, head_cols(KV_HEADS + kv_head)]
            q = q_ref[:, head_cols(h)]
            do = do_ref[:, head_cols(h)]
            scores = dot_t(k, q) * scale - log_ref[h]
            soft = jnp.exp(jnp.where(allowed, scores, MASKED_SCORE))
            grad = (soft * (dot_t(v, do) - delta[h])).astype(BF)
            dq_acc[h] += t_dot(k, grad)
            dkv_acc[:, head_cols(kv_head)] += dot(grad, q) * scale
            dkv_acc[:, head_cols(KV_HEADS + kv_head)] += dot(soft.astype(BF), do)
            return carry

        lax.fori_loop(0, heads, one, 0, unroll=12)
        partial_ref[o] = dkv_acc[...].astype(BF)

    for s in range(2 * line - 1):
        if s < line:

            @pl.when(me >= s)
            def _():
                block(s)

        for h in range(line - 1):
            o = s - h
            if 0 <= o < line - 1 - h:

                @pl.when(me == line - 1 - h)
                def _():
                    if h > 0:
                        move(o).wait_recv()
                        partial_ref[o] = (partial_ref[o].astype(F32) + from_right[o].astype(F32)).astype(BF)
                    move(o).start()

    cos, sin = cos_ref[...], -sin_ref[...]
    for h in range(heads):
        dq_ref[:, h * HEAD_DIM : (h + 1) * HEAD_DIM] = rotated(dq_acc[h].T * scale, cos, sin).astype(BF)
    dq = dq_ref[...]
    grads_ref[5 * RANK : 6 * RANK] = t_dot(low, dq)[:RANK].astype(BF)
    low_grad = dot_t(dq, bq_ref[...])
    for load in q_loads:
        load.wait()
    normed_grad = dot_t(dq[:, :cols], flat(wq, 0))
    for t in range(1, line):
        normed_grad = normed_grad + dot_t(dq[:, t * cols : (t + 1) * cols], flat(wq, t))
    dkv_acc[...] = partial_ref[me].astype(F32)

    @pl.when(me < line - 1)
    def _():
        move(me).wait_recv()
        dkv_acc[...] += from_right[me].astype(F32)

    for h in range(KV_HEADS):
        span = slice(h * HEAD_DIM, (h + 1) * HEAD_DIM)
        dkv_acc[:, span] = rotated(dkv_acc[:, span], cos, sin)
    dkv = dkv_acc[...].astype(BF)
    kv_grad = t_dot(low, dkv).astype(BF)
    grads_ref[4 * RANK : 5 * RANK, :kv_half] = kv_grad[RANK : 2 * RANK, :kv_half]
    grads_ref[4 * RANK : 5 * RANK, kv_half : 2 * kv_half] = kv_grad[2 * RANK :, kv_half:]
    grads_ref[4 * RANK : 5 * RANK, 2 * kv_half :] = jnp.zeros((RANK, width - 2 * kv_half), BF)
    low_grad = (low_grad + dot_t(dkv, bkv_ref[...])).astype(BF)
    grads_ref[: 3 * RANK] = t_dot(low_grad, normed_ref[...]).astype(BF)
    for load in kv_loads:
        load.wait()
    for t in range(line):
        normed_grad = normed_grad + dot_t(dkv[:, t * kv_cols : (t + 1) * kv_cols], flat(wkv, t))
    normed_grad = normed_grad + dot(low_grad, bundle_ref[rows_of(B_INPUT, 3)])
    dx = dx_ref[...] + through_norm(x_ref[...].astype(F32), misc[0:1], normed_grad)
    dx_ref[...] = dx
    dx_low_ref[...] = dx.astype(BF)
    for o in range(line - 1):

        @pl.when(me > o)
        def _():
            move(o).wait_send()


def attend_backward(x, middle, dy, dn2, w, kept, info, tables):
    line = lax.axis_size("tensor")
    rows, width = x.shape
    heads = width // HEAD_DIM
    kv_width = 2 * KV_HEADS * HEAD_DIM
    groups, low_rows = w["packed"].shape[0], w["packed"].shape[2]
    return pl.pallas_call(
        partial(attend_back_kernel, line, heads // KV_HEADS),
        in_specs=[pl.BlockSpec(memory_space=pltpu.SMEM)] + [vspec()] * 14 + [hspec()],
        out_specs=[vspec()] * 3,
        out_shape=[
            jax.ShapeDtypeStruct((rows, width), F32),
            jax.ShapeDtypeStruct((rows, width), BF),
            jax.ShapeDtypeStruct((7 * RANK, width), BF),
        ],
        scratch_shapes=[
            pltpu.VMEM((line, groups, low_rows, width // line), BF),
            pltpu.VMEM((line, groups, low_rows, width // line), BF),
            pltpu.VMEM((line, groups, low_rows, kv_width // line), BF),
            pltpu.VMEM((rows, width), BF),
            pltpu.VMEM((heads, HEAD_DIM, rows), F32),
            pltpu.VMEM((rows, width), BF),
            pltpu.VMEM((rows, kv_width), F32),
            pltpu.VMEM((line, rows, kv_width), BF),
            pltpu.VMEM((line, rows, kv_width), BF),
            pltpu.VMEM((heads, 1, rows), F32),
            pltpu.VMEM((3 * RANK, width), BF),
            pltpu.VMEM((3 * RANK, kv_width), BF),
            pltpu.SemaphoreType.DMA((3, line)),
            pltpu.SemaphoreType.DMA((line,)),
            pltpu.SemaphoreType.DMA((line,)),
        ],
        compiler_params=pltpu.CompilerParams(
            collective_id=3 if dy.dtype == F32 else 5, has_side_effects=True, vmem_limit_bytes=VMEM_LIMIT
        ),
        cost_estimate=pl.CostEstimate(
            flops=4 * rows * width * width * 2, bytes_accessed=5 * width * width, transcendentals=0
        ),
    )(
        info, x, middle, dy, dn2, w["bundle"], tables[0], tables[1], *kept, w["packed"],
    )


def reduce_kernel(
    line, peers, extra,
    attn_ref, whole_ref, parts_ref, y_first, y_second, g_first, g_second,
    out, y_out, g_out,
    mine, z_in, quarter, z_recv, z_send, dp_recv, dp_send, own_sem, t_recv, t_right, t_left,
    side_recv, side_send, side_own,
):
    r = RANK
    me, spot, core = lax.axis_index("tensor"), lax.axis_index("dp"), lax.axis_index("section")
    width = mine.shape[1]
    cols = width // line
    seqs = out.shape[0]
    seq = spot * 2 + core
    has_left, has_right = me > 0, me < line - 1
    barrier = pltpu.get_barrier_semaphore()

    def greet(**where):
        pl.semaphore_signal(barrier, inc=1, device_id=where, device_id_type=MESH)

    for k in range(1, line):
        greet(tensor=lax.rem(me + k, line))

    greet(section=1 - core)

    @pl.when(core == 0)
    def _():
        for k in range(1, peers):
            for c in range(2):
                greet(section=c, dp=lax.rem(spot + k, peers))

    pl.semaphore_wait(barrier, line - 1 + peers)

    def remote(src, dst, send, recv, **where):
        return pltpu.make_async_remote_copy(
            src_ref=src, dst_ref=dst, send_sem=send, recv_sem=recv, device_id=where, device_id_type=MESH
        )

    def lanes(t):
        return pl.ds(pl.multiple_of(t * cols, LANES), cols)

    def pieces(s):
        return (
            (parts_ref.at[pl.ds(0, 3 * r)], out.at[s, pl.ds(8 * r, 3 * r)]),
            (parts_ref.at[pl.ds(3 * r, 3 * r), pl.ds(0, extra)], out.at[s, pl.ds(11 * r, 3 * r), pl.ds(0, extra)]),
            (
                parts_ref.at[pl.ds(5 * r, r), pl.ds(extra, LANES)],
                out.at[s, pl.ds(13 * r, r), pl.ds(extra, LANES)],
            ),
            (quarter.at[pl.ds(0, 8 * r)], out.at[s, pl.ds(0, 8 * r), lanes(me)]),
            (quarter.at[pl.ds(8 * r, 2 * r)], out.at[s, pl.ds(11 * r, 2 * r), pl.ds(extra, cols)]),
        )

    def to_peer(k, i):
        src, dst = pieces(seq)[i]
        return remote(src, dst, dp_send.at[k, i], dp_recv.at[seq, i], section=0, dp=lax.rem(spot + k, peers))

    def stay(i):
        src, dst = pieces(seq)[i]
        return pltpu.make_async_copy(src, dst, own_sem.at[i])

    def send_pieces(which):
        for i in which:
            for k in range(1, peers):
                to_peer(k, i).start()

            @pl.when(core != 0)
            def _():
                to_peer(0, i).start()

            @pl.when(core == 0)
            def _():
                stay(i).start()

    def across(k):
        to = lax.rem(me + k, line)
        return remote(mine.at[:, lanes(to)], z_in.at[me], z_send.at[k], z_recv.at[me], tensor=to)

    def incoming(k):
        o = lax.rem(me + k, line)
        return remote(mine.at[:, lanes(me)], z_in.at[o], z_send.at[k], z_recv.at[o], tensor=o)

    def side(i, src, dst):
        return remote(src, dst.at[core], side_send.at[i], side_recv.at[i], section=1 - core)

    def side_keep(i, src, dst):
        return pltpu.make_async_copy(src, dst.at[core], side_own.at[i])

    pairs = ((y_first, y_second, y_out), (g_first, g_second, g_out))

    for first, rows, ref, start in (
        (0, 3, attn_ref, 0), (3, 2, whole_ref, 0), (5, 1, attn_ref, 3), (6, 1, whole_ref, 2), (7, 3, attn_ref, 4),
    ):
        mine[rows_of(first, rows)] = ref[rows_of(start, rows)]
    for k in range(1, line):
        across(k).start()
    send_pieces((0, 1, 2))
    for c in range(2):

        @pl.when(core == c)
        def _():
            for i, (first, second, dst) in enumerate(pairs):
                side(i, first if c == 1 else second, dst).start()
                side_keep(i, second if c == 1 else first, dst).start()

    total = mine[:, lanes(me)].astype(F32)
    for k in range(1, line):
        incoming(k).wait_recv()
        total = total + z_in[lax.rem(me + k, line)].astype(F32)
    quarter[...] = total.astype(BF)
    send_pieces((3, 4))

    def arrived(s, i):
        src, dst = pieces(s)[i]
        return remote(src, dst, dp_send.at[0, i], dp_recv.at[s, i], section=0)

    def along(s, o, side):
        place = out.at[s, pl.ds(0, 8 * r), lanes(o)]
        return remote(
            place, place, (t_right if side > 0 else t_left).at[s, o], t_recv.at[s, o], tensor=me + side
        )

    @pl.when(core == 0)
    def _():
        def own_rows(n, carry):
            s = lax.rem(seq + n, seqs)

            @pl.when(n == 0)
            def _():
                stay(3).wait()

            @pl.when(n > 0)
            def _():
                arrived(s, 3).wait_recv()

            @pl.when(has_right)
            def _():
                along(s, me, 1).start()

            @pl.when(has_left)
            def _():
                along(s, me, -1).start()

            return carry

        lax.fori_loop(0, seqs, own_rows, 0)
        for d in range(1, line):

            def others(n, carry):
                s = lax.rem(seq + n, seqs)

                @pl.when(me >= d)
                def _():
                    along(s, me - d, 1).wait_recv()

                    @pl.when(has_right)
                    def _():
                        along(s, me - d, 1).start()

                @pl.when(me + d < line)
                def _():
                    along(s, me + d, -1).wait_recv()

                    @pl.when(has_left)
                    def _():
                        along(s, me + d, -1).start()

                return carry

            lax.fori_loop(0, seqs, others, 0)

        def finish(n, carry):
            s = lax.rem(seq + n, seqs)

            @pl.when(n > 0)
            def _():
                for i in (0, 1, 2, 4):
                    arrived(s, i).wait_recv()

            for o in range(line):

                @pl.when(jnp.logical_and(has_right, me >= o))
                def _():
                    along(s, o, 1).wait_send()

                @pl.when(jnp.logical_and(has_left, me <= o))
                def _():
                    along(s, o, -1).wait_send()

            return carry

        lax.fori_loop(0, seqs, finish, 0)
        for i in (0, 1, 2, 4):
            stay(i).wait()

    for k in range(1, line):
        across(k).wait_send()
    for i in range(5):
        for k in range(1, peers):
            to_peer(k, i).wait_send()

        @pl.when(core != 0)
        def _():
            to_peer(0, i).wait_send()
    for i, (first, _, dst) in enumerate(pairs):
        side(i, first, dst).wait()
        side_keep(i, first, dst).wait()


def reduce_first(attn_part, whole, parts, extra, outs, grads):
    line, peers = lax.axis_size("tensor"), lax.axis_size("dp")
    width = parts.shape[1]
    seqs = 2 * peers
    dma = pltpu.SemaphoreType.DMA
    return pl.pallas_call(
        partial(reduce_kernel, line, peers, extra),
        in_specs=[vspec()] * 7,
        out_specs=[hspec()] * 3,
        out_shape=[
            jax.ShapeDtypeStruct((seqs, 14 * RANK, width), BF),
            jax.ShapeDtypeStruct((2,) + outs[0].shape, outs[0].dtype),
            jax.ShapeDtypeStruct((2,) + grads[0].shape, grads[0].dtype),
        ],
        scratch_shapes=[
            pltpu.VMEM((10 * RANK, width), BF),
            pltpu.VMEM((line, 10 * RANK, width // line), BF),
            pltpu.VMEM((10 * RANK, width // line), BF),
            dma((line,)),
            dma((line,)),
            dma((seqs, 5)),
            dma((peers, 5)),
            dma((5,)),
            dma((seqs, line)),
            dma((seqs, line)),
            dma((seqs, line)),
            dma((2,)),
            dma((2,)),
            dma((2,)),
        ],
        compiler_params=pltpu.CompilerParams(
            collective_id=6, has_side_effects=True, vmem_limit_bytes=VMEM_LIMIT
        ),
    )(attn_part, whole, parts, *outs, *grads)


def total_kernel(
    scale, hidden, q_cols,
    first, attn_in, whole_in, parts_in,
    input_ref, query_ref, kv_ref, expand_ref, attend_ref, shrink_ref, res_ref,
    block, ids, sem,
):
    r = RANK
    a = pl.program_id(0)
    core = lax.axis_index("section")
    width = block.shape[2]
    extra = hidden - width
    pad = extra + -hidden % (2 * LANES)

    @pl.when(jnp.logical_and(a == 0, core == 0))
    def _():
        load = pltpu.make_async_copy(first, block, sem.at[0])
        load.start()
        load.wait()

    @pl.when(jnp.logical_and(a == 0, core != 0))
    def _():
        def load(src, start, first, count, at):
            return pltpu.make_async_copy(src.at[:, rows_of(start, count)], block.at[:, rows_of(first, count)], sem.at[at])

        loads = [
            load(attn_in, 0, 0, 3, 1), load(whole_in, 0, 3, 2, 2), load(attn_in, 3, 5, 1, 3),
            load(whole_in, 2, 6, 1, 4), load(attn_in, 4, 7, 1, 5), load(parts_in, 0, 8, 6, 6),
        ]
        for one in loads:
            one.start()
        for one in loads:
            one.wait()
        mine = pl.ds(pl.multiple_of(lax.axis_index("tensor") * q_cols, LANES), q_cols)
        last = pltpu.make_async_copy(
            attn_in.at[:, rows_of(5, 2), mine], block.at[:, rows_of(11, 2), pl.ds(pad, q_cols)], sem.at[7]
        )
        last.start()
        last.wait()

    @pl.when(a == 0)
    def _():
        lane = lax.broadcasted_iota(jnp.int32, (1, LANES), 1).astype(F32)
        for i in range(block.shape[0]):
            names = block[i, 13 * r : 14 * r, pad : pad + LANES][:1].astype(F32)
            ids[i] = jnp.sum(lane * names).astype(jnp.int32)

    for ref in (input_ref, query_ref, kv_ref, expand_ref, attend_ref, shrink_ref, res_ref):
        ref[...] = jnp.zeros_like(ref)

    for i in range(block.shape[0]):

        @pl.when(ids[i] == a)
        def _():
            def part(row, rows, col, cols):
                return block[i, row : row + rows, col : col + cols].astype(F32) * scale

            input_ref[0] += part(0, 5 * r, 0, width)
            res_ref[0, 0] += part(5 * r, r, 0, width)
            res_ref[0, 1] += part(6 * r, r, 0, width)
            kv = part(7 * r, r, 0, 2 * kv_ref.shape[3])
            kv_ref[0, 0] += kv[:, : kv_ref.shape[3]]
            kv_ref[0, 1] += kv[:, kv_ref.shape[3] :]
            for j in range(2):
                expand_ref[0, j, :, :width] += part((8 + j) * r, r, 0, width)
                expand_ref[0, j, :, width:] += part((11 + j) * r, r, 0, pad)[:, :extra]
            shrink_ref[0, :, :width] += part(10 * r, r, 0, width)
            shrink_ref[0, :, width:] += part(13 * r, r, 0, pad)[:, :extra]
            query_ref[0] += part(11 * r, r, pad, q_cols)
            attend_ref[0] += part(12 * r, r, pad, q_cols)


def total_by_adapter(first, attn_in, whole_in, parts_in, count, scale, hidden, q_cols, kv_half):
    width = first.shape[2]
    r = RANK
    shapes = [
        (5 * r, width), (r, q_cols), (2, r, kv_half), (2, r, hidden), (r, q_cols), (r, hidden), (2, r, width),
    ]
    return pl.pallas_call(
        partial(total_kernel, scale, hidden, q_cols),
        grid=(count,),
        in_specs=[hspec()] * 4,
        out_specs=[pl.BlockSpec((1,) + s, lambda a, n=len(s): (a,) + (0,) * n) for s in shapes],
        out_shape=[jax.ShapeDtypeStruct((count,) + s, F32) for s in shapes],
        scratch_shapes=[
            pltpu.VMEM(first.shape, BF),
            pltpu.SMEM((first.shape[0],), jnp.int32),
            pltpu.SemaphoreType.DMA((8,)),
        ],
        compiler_params=pltpu.CompilerParams(vmem_limit_bytes=VMEM_LIMIT),
    )(first, attn_in, whole_in, parts_in)


def swap(pair):
    return lax.all_to_all(pair, "section", split_axis=0, concat_axis=0, tiled=True)


def local(
    inputs,
    lengths,
    adapter_ids,
    cotangent,
    norm_gain,
    query_weight,
    query_bias,
    keyvalue_weight,
    keyvalue_bias,
    output_weight,
    expand_weight,
    shrink_weight,
    adapter_input,
    adapter_query,
    adapter_keyvalue,
    adapter_expand,
    adapter_attend,
    adapter_shrink,
    adapter_residual,
):
    layers = lax.axis_size("section")
    tensor = lax.axis_size("tensor")
    core = lax.axis_index("section")
    place = lax.axis_index("tensor")
    rows, width = inputs.shape[1:]
    tokens = layers * rows * tensor * lax.axis_size("dp")
    kv_half = KV_HEADS * HEAD_DIM
    hidden = expand_weight.shape[3]
    r = RANK

    def turned(stack):
        return jnp.swapaxes(stack[0], 1, 2)

    def lined(stack):
        return stack[0].reshape(stack.shape[1], -1, stack.shape[-1])

    bundles, heads = pick_adapters(
        adapter_ids,
        (
            turned(adapter_input), lined(adapter_residual), lined(adapter_keyvalue), lined(adapter_expand),
            turned(adapter_shrink), adapter_query[0], turned(adapter_attend),
        ),
        (norm_gain[0], keyvalue_bias.reshape(1, -1), query_bias),
    )

    ff = jnp.concatenate(
        [m.reshape(layers, 1, hidden // layers, m.shape[1]) for m in (*turned(expand_weight), shrink_weight[0])],
        axis=1,
    )
    ff = swap(ff)
    kv = jnp.concatenate([keyvalue_weight[0, 0], keyvalue_weight[0, 1]], axis=1)
    kv_cols = kv.shape[1] // tensor
    kv = lax.dynamic_slice_in_dim(kv, place * kv_cols, kv_cols, 1)
    attn = jnp.concatenate([query_weight[0], output_weight[0].T, kv], axis=1)
    q_cols = query_weight.shape[2]
    attn = swap(attn.reshape(layers, attn.shape[0] // layers, attn.shape[1]))
    first_attn, line_attn, bundle = gather_first(attn, bundles, heads)

    def weights(layer):
        packed = first_attn if layer == 0 else lax.all_gather(line_attn, ("dp", "section"), axis=0)
        mlp = lax.all_gather(ff[layer], ("section", "dp"), axis=0)
        mlp = mlp.reshape(layers, -1, *mlp.shape[1:])
        if mlp.shape[4] % LANES:
            mlp = jnp.moveaxis(mlp, 1, 3)
            mlp = mlp.reshape(layers, 1, *mlp.shape[1:3], width)
        return dict(packed=packed, mlp=mlp, bundle=bundle[layer])

    x = lax.dynamic_index_in_dim(inputs, core, 0, keepdims=False)
    cot = lax.dynamic_index_in_dim(cotangent, core, 0, keepdims=False)
    length = lax.dynamic_index_in_dim(lengths, core, 0, keepdims=False)
    own_id = lax.dynamic_index_in_dim(adapter_ids, core, 0, keepdims=False)
    first_slot = place * rows
    info = jnp.stack([first_slot, length]).astype(jnp.int32)
    tables = rotary_tables(first_slot, rows)
    slot_ids = first_slot + jnp.arange(rows, dtype=jnp.int32)

    w = [weights(layer) for layer in range(layers)]
    outs, kept = [], []
    for layer in range(layers):
        middle, normed_two, attn_kept = attend_forward(x, w[layer], info, tables)
        shrunk, mlp_kept = mlp_forward(normed_two, w[layer])
        outs.append((middle + shrunk).astype(BF))
        kept.append((x, middle, attn_kept, mlp_kept))
        x = outs[-1]
    count = adapter_input.shape[1]
    extra = hidden + -hidden % (2 * LANES) - width
    names = jnp.broadcast_to((jnp.arange(LANES, dtype=jnp.int32) == own_id).astype(BF)[None], (r, LANES))

    def gather_all(*arrays):
        return [lax.all_gather(a, ("section", "dp"), axis=0) for a in arrays]

    grad = low_grad = jnp.where((slot_ids < length)[:, None], cot, jnp.zeros_like(cot))
    grads, gathered = [None] * layers, [None] * layers
    for layer in reversed(range(layers)):
        x, middle, attn_kept, mlp_kept = kept[layer]
        if layer < layers - 1:
            low_grad, here = lax.optimization_barrier((low_grad, here))
        dn2, whole, parts = mlp_backward(low_grad, w[layer], mlp_kept, names)
        if layer < layers - 1:
            total, dn2 = lax.optimization_barrier((total, dn2))
            gathered[layer + 1] = gather_all(*total, last_parts)
        grad, low_grad, attn_part = attend_backward(x, middle, grad, dn2, w[layer], attn_kept, info, tables)
        grads[layer] = grad
        here = (attn_part, whole)
        if layer > 0:
            total = lax.psum(here, "tensor")
            last_parts = parts
    gathered[0], layer_output, input_grad = reduce_first(*here, parts, extra, outs, grads)
    totals = total_by_adapter(
        gathered[0], *gathered[1], count, 1.0 / math.sqrt(tokens), hidden, q_cols, kv_half
    )
    turned = (0, 4, 5)
    totals = [jnp.swapaxes(total, 1, 2) if i in turned else total for i, total in enumerate(totals)]
    return (layer_output[None], input_grad[None]) + tuple(total[None] for total in totals)


def solution(mesh):
    placed = (
        P("dp", "tensor", None),
        P("dp"),
        P("dp"),
        P("dp", "tensor", None),
        P("section", None, None),
        P("section", "dp", "tensor"),
        P("section", "tensor"),
        P("section", None, "dp", None),
        P("section", None, None),
        P("section", "tensor", "dp"),
        P("section", None, "dp", "tensor"),
        P("section", "tensor", "dp"),
        P("section", None, None, None),
        P("section", None, None, "tensor"),
        P("section", None, None, None, None),
        P("section", None, None, None, "tensor"),
        P("section", None, "tensor", None),
        P("section", None, "tensor", None),
        P("section", None, None, None, None),
    )
    return jax.shard_map(
        local,
        mesh=mesh,
        in_specs=placed,
        out_specs=(
            P("section", "dp", "tensor", None),
            P("section", "dp", "tensor", None),
            P("section", None, None, None),
            P("section", None, None, "tensor"),
            P("section", None, None, None, None),
            P("section", None, None, None, "tensor"),
            P("section", None, "tensor", None),
            P("section", None, "tensor", None),
            P("section", None, None, None, None),
        ),
        check_vma=False,
    )
```

```python
from functools import partial
import math

import jax
import jax.numpy as jnp
from jax import lax
from jax.experimental import pallas as pl
from jax.experimental.pallas import tpu as pltpu
from jax.sharding import PartitionSpec as P

KV_HEADS = 2
HEAD_DIM = 128
RANK = 16
EPSILON = 1e-06
ROPE_BASE = 1000000.0
MASKED_SCORE = -1e30
CHUNKS = 8
LANES = 128
VMEM_LIMIT = 60 * 2**20
MESH = pl.DeviceIdType.MESH
BF = jnp.bfloat16
F32 = jnp.float32


def dot(a, b):
    return jnp.dot(a, b, preferred_element_type=F32)


def dot_t(a, b):
    return lax.dot_general(a, b, (((1,), (1,)), ((), ())), preferred_element_type=F32)


def t_dot(a, b):
    return lax.dot_general(a, b, (((0,), (0,)), ((), ())), preferred_element_type=F32)


def rotary_tables(first_slot, rows):
    half = HEAD_DIM // 2
    frequency = jnp.exp(-math.log(ROPE_BASE) * (2.0 * jnp.arange(half, dtype=F32) / HEAD_DIM))
    slots = (first_slot + jnp.arange(rows, dtype=jnp.int32)).astype(F32)
    angles = slots[:, None] * frequency[None, :]
    cos, sin = jnp.cos(angles), jnp.sin(angles)
    return jnp.concatenate([cos, cos], axis=1), jnp.concatenate([-sin, sin], axis=1)


B_INPUT, B_RES_ONE, B_RES_TWO, B_KV, B_MISC, B_FF, B_FF_TAIL, B_HEADS, B_ROWS = 0, 5, 6, 7, 8, 9, 12, 15, 18


def rows_of(first, count=1):
    return slice(first * RANK, (first + count) * RANK)


def pick_kernel(
    ids_ref, input_ref, res_ref, kv_ref, expand_ref, shrink_ref, query_ref, attend_ref, gain_ref, kvb_ref, qb_ref,
    out_ref, heads_ref,
):
    width = out_ref.shape[2]
    out_ref[0] = jnp.zeros(out_ref.shape[1:], BF)
    out_ref[0, rows_of(B_INPUT, 5)] = input_ref[0]
    out_ref[0, rows_of(B_RES_ONE, 2)] = res_ref[0]
    kv_half = kv_ref.shape[2]
    for i in range(2):
        out_ref[0, rows_of(B_KV), i * kv_half : (i + 1) * kv_half] = kv_ref[0, rows_of(i)]
    misc = rows_of(B_MISC).start
    out_ref[0, misc : misc + 2] = gain_ref[...]
    out_ref[0, misc + 2 : misc + 3, : 2 * kv_half] = kvb_ref[...]
    tail = expand_ref.shape[2] - width
    for i in range(3):
        part = expand_ref[0, rows_of(i)] if i < 2 else shrink_ref[0]
        out_ref[0, rows_of(B_FF + i)] = part[:, :width]
        out_ref[0, rows_of(B_FF_TAIL + i), :tail] = part[:, width:]
    heads_ref[0] = jnp.zeros(heads_ref.shape[1:], BF)
    heads_ref[0, rows_of(0)] = query_ref[0]
    heads_ref[0, rows_of(1)] = attend_ref[0]
    heads_ref[0, 2 * RANK : 2 * RANK + 1] = qb_ref[...]


def pick_adapters(ids, stacks, shared):
    count = ids.shape[0]
    width = stacks[0].shape[2]
    q_cols = stacks[5].shape[2]
    shapes = [(B_ROWS * RANK, width), (3 * RANK, q_cols)]
    return pl.pallas_call(
        pick_kernel,
        grid_spec=pltpu.PrefetchScalarGridSpec(
            num_scalar_prefetch=1,
            grid=(count,),
            in_specs=[pl.BlockSpec((1,) + a.shape[1:], lambda i, ids: (ids[i], 0, 0)) for a in stacks]
            + [pl.BlockSpec(a.shape, lambda i, ids: (0, 0)) for a in shared],
            out_specs=[pl.BlockSpec((1,) + a, lambda i, ids: (i, 0, 0)) for a in shapes],
        ),
        out_shape=[jax.ShapeDtypeStruct((count,) + a, BF) for a in shapes],
    )(ids, *stacks, *shared)


def spread_factors(bundle_ref, expand_ref, ash_ref):
    width = bundle_ref.shape[1]
    tail = ash_ref.shape[1] - width
    expand_ref[...] = jnp.zeros_like(expand_ref)
    for i in range(2):
        expand_ref[i, rows_of(i), :width] = bundle_ref[rows_of(B_FF + i)]
        expand_ref[i, rows_of(i), width:] = bundle_ref[rows_of(B_FF_TAIL + i), :tail]
    ash_ref[:, :width] = bundle_ref[rows_of(B_FF + 2)]
    ash_ref[:, width:] = bundle_ref[rows_of(B_FF_TAIL + 2), :tail]


def vspec():
    return pl.BlockSpec(memory_space=pltpu.VMEM)


def hspec():
    return pl.BlockSpec(memory_space=pl.ANY)


def line_barrier(me, line):
    barrier = pltpu.get_barrier_semaphore()

    @pl.when(me > 0)
    def _():
        pl.semaphore_signal(barrier, inc=1, device_id={"tensor": me - 1}, device_id_type=MESH)

    @pl.when(me < line - 1)
    def _():
        pl.semaphore_signal(barrier, inc=1, device_id={"tensor": me + 1}, device_id_type=MESH)

    pl.semaphore_wait(barrier, jnp.where(me > 0, 1, 0) + jnp.where(me < line - 1, 1, 0))


def within(c, chunks):
    return jnp.logical_and(c >= 0, c < chunks)


def line_exchange(line, chunks, gathered, partial_ref, from_left, from_right, own_out, sems, begin, work):
    ag_recv, ag_right, ag_left, r_recv, r_send, l_recv, l_send = sems
    me = lax.axis_index("tensor")

    def copy(ref, src, c, o, send, recv, side):
        return pltpu.make_async_remote_copy(
            src_ref=src.at[c, o],
            dst_ref=ref.at[c, o],
            send_sem=send.at[c, o],
            recv_sem=recv.at[c, o],
            device_id={"tensor": me + side},
            device_id_type=MESH,
        )

    def ag(c, o, side):
        return copy(gathered, gathered, c, o, ag_right if side > 0 else ag_left, ag_recv, side)

    def rs(c, o, side):
        if side > 0:
            return copy(from_left, partial_ref, c, o, r_send, r_recv, 1)
        return copy(from_right, partial_ref, c, o, l_send, l_recv, -1)

    has_left, has_right = me > 0, me < line - 1

    def step(s, carry):
        first = s + line - 1

        @pl.when(jnp.logical_and(within(first, chunks), has_right))
        def _():
            ag(first, me, 1).start()

        @pl.when(jnp.logical_and(within(first, chunks), has_left))
        def _():
            ag(first, me, -1).start()

        for d in range(1, line):
            c = s + line - 1 - d

            @pl.when(jnp.logical_and(within(c, chunks), me - d >= 0))
            def _():
                ag(c, me - d, 1).wait_recv()

                @pl.when(has_right)
                def _():
                    ag(c, me - d, 1).start()

            @pl.when(jnp.logical_and(within(c, chunks), me + d < line))
            def _():
                ag(c, me + d, -1).wait_recv()

                @pl.when(has_left)
                def _():
                    ag(c, me + d, -1).start()

        @pl.when(within(s, chunks))
        def _():
            work(s)

        for h in range(line):
            c = s - h

            @pl.when(jnp.logical_and(within(c, chunks), me == h))
            def _():
                for j in range(line - 1, h, -1):
                    if h > 0:
                        rs(c, j, 1).wait_recv()
                        partial_ref[c, j] = (
                            partial_ref[c, j].astype(F32) + from_left[c, j].astype(F32)
                        ).astype(BF)
                    if h < line - 1:
                        rs(c, j, 1).start()

            @pl.when(jnp.logical_and(within(c, chunks), me == line - 1 - h))
            def _():
                for j in range(line - 1 - h):
                    if h > 0:
                        rs(c, j, -1).wait_recv()
                        partial_ref[c, j] = (
                            partial_ref[c, j].astype(F32) + from_right[c, j].astype(F32)
                        ).astype(BF)
                    if h < line - 1:
                        rs(c, j, -1).start()

        last = s - (line - 1)

        @pl.when(within(last, chunks))
        def _():
            own_out[last] = partial_ref[last, me].astype(F32)

            @pl.when(has_left)
            def _():
                rs(last, me, 1).wait_recv()
                own_out[last] += from_left[last, me].astype(F32)

            @pl.when(has_right)
            def _():
                rs(last, me, -1).wait_recv()
                own_out[last] += from_right[last, me].astype(F32)

        return carry

    line_barrier(me, line)
    begin()
    lax.fori_loop(-(line - 1), chunks + line - 1, step, 0)

    def drain(c, carry):
        for o in range(line):

            @pl.when(jnp.logical_and(has_right, me >= o))
            def _():
                ag(c, o, 1).wait_send()

            @pl.when(jnp.logical_and(has_left, me <= o))
            def _():
                ag(c, o, -1).wait_send()

            @pl.when(me < o)
            def _():
                rs(c, o, 1).wait_send()

            @pl.when(me > o)
            def _():
                rs(c, o, -1).wait_send()

        return carry

    lax.fori_loop(0, chunks, drain, 0)


def exchange_scratch(line, chunks, rows, width):
    slots = (chunks, line, rows, width)
    return [pltpu.VMEM(slots, BF)] * 4 + [pltpu.SemaphoreType.DMA((chunks, line))] * 7


def ff_loads(packed, refs, wsem):
    halves, parts, _, rows, cols = packed.shape
    return [
        pltpu.make_async_copy(
            packed.at[h, p, i],
            ref.at[pl.ds(h * rows, rows), pl.ds(p * cols, cols)],
            wsem.at[i, h, p],
        )
        for i, ref in enumerate(refs)
        for h in range(halves)
        for p in range(parts)
    ]


def clear_tail(packed, refs):
    hidden = packed.shape[0] * packed.shape[3]
    for ref in refs:
        if ref.shape[0] > hidden:
            ref[hidden:] = jnp.zeros((ref.shape[0] - hidden, ref.shape[1]), BF)


def mlp_kernel(
    line, chunks, tile,
    n2_ref, packed, bundle_ref,
    out_ref, n2_out, gate_out, up_out,
    gathered, partial_ref, from_left, from_right, s0, s1, s2, s3, s4, s5, s6,
    wg, wu, ws, gate_st, up_st, acc, expand_ref, ash_ref, wsem, osem, nsem,
):
    rows, width = n2_ref.shape[1:]
    every = line * rows
    tiles = wg.shape[0] // tile
    high = bundle_ref[rows_of(B_INPUT + 3, 2)]
    res = bundle_ref[rows_of(B_RES_TWO)]
    me = lax.axis_index("tensor")
    loads = ff_loads(packed, (wg, wu, ws), wsem)

    def begin():
        for load in loads:
            load.start()
        clear_tail(packed, (wg, wu, ws))
        spread_factors(bundle_ref, expand_ref, ash_ref)
        for c in range(chunks):
            gathered[c, me] = n2_ref[c]

    def saves(c, slot):
        return (
            pltpu.make_async_copy(gate_st.at[slot], gate_out.at[c], osem.at[0, slot]),
            pltpu.make_async_copy(up_st.at[slot], up_out.at[c], osem.at[1, slot]),
        )

    def keep(c):
        return pltpu.make_async_copy(gathered.at[c], n2_out.at[c], nsem.at[c])

    def work(c):
        slot = c % 2

        @pl.when(c == 0)
        def _():
            for load in loads:
                load.wait()

        @pl.when(c >= 2)
        def _():
            for save in saves(c - 2, slot):
                save.wait()

        keep(c).start()
        x = gathered[c].reshape(every, width)
        er = dot_t(x, high).astype(BF)

        def one(f, rank):
            cols = pl.ds(pl.multiple_of(f * tile, tile), tile)
            gate = dot_t(x, wg[cols]) + dot(er, expand_ref[0, :, cols])
            up = dot_t(x, wu[cols]) + dot(er, expand_ref[1, :, cols])
            gate_st[slot, :, cols] = gate.astype(BF)
            up_st[slot, :, cols] = up.astype(BF)
            act = (gate * (1.0 / (1.0 + jnp.exp(-gate))) * up).astype(BF)
            now = dot(act, ws[cols])

            @pl.when(f == 0)
            def _():
                acc[...] = now

            @pl.when(f > 0)
            def _():
                acc[...] += now

            return rank + dot_t(act, ash_ref[:, cols])

        rank = lax.fori_loop(0, tiles, one, jnp.zeros((every, ash_ref.shape[0]), F32))
        total = acc[...] + dot(rank.astype(BF), res)
        partial_ref[c] = total.astype(BF).reshape(line, rows, width)
        for save in saves(c, slot):
            save.start()

    line_exchange(
        line, chunks, gathered, partial_ref, from_left, from_right, out_ref,
        (s0, s1, s2, s3, s4, s5, s6), begin, work,
    )
    for c in range(chunks):
        keep(c).wait()
    for c in range(max(chunks - 2, 0), chunks):
        for save in saves(c, c % 2):
            save.wait()


def ff_tile(hidden):
    return hidden


def mlp_forward(n2, w):
    line = lax.axis_size("tensor")
    rows, width = n2.shape
    halves, groups, _, low_rows, _ = w["mlp"].shape
    hidden = halves * low_rows + -(halves * low_rows) % (2 * LANES)
    part = rows // CHUNKS
    every = line * part
    out, n2_all, gate, up = pl.pallas_call(
        partial(mlp_kernel, line, CHUNKS, ff_tile(hidden)),
        in_specs=[vspec(), hspec(), vspec()],
        out_specs=[vspec()] + [hspec()] * 3,
        out_shape=[
            jax.ShapeDtypeStruct((CHUNKS, part, width), F32),
            jax.ShapeDtypeStruct((CHUNKS, line, part, width), BF),
            jax.ShapeDtypeStruct((CHUNKS, every, hidden), BF),
            jax.ShapeDtypeStruct((CHUNKS, every, hidden), BF),
        ],
        scratch_shapes=exchange_scratch(line, CHUNKS, part, width)
        + [pltpu.VMEM((hidden, width), BF)] * 3
        + [pltpu.VMEM((2, every, hidden), BF)] * 2
        + [
            pltpu.VMEM((every, width), F32),
            pltpu.VMEM((2, 2 * RANK, hidden), BF),
            pltpu.VMEM((RANK, hidden), BF),
            pltpu.SemaphoreType.DMA((3, halves, groups)),
            pltpu.SemaphoreType.DMA((2, 2)),
            pltpu.SemaphoreType.DMA((CHUNKS,)),
        ],
        compiler_params=pltpu.CompilerParams(
            collective_id=0, has_side_effects=True, vmem_limit_bytes=VMEM_LIMIT
        ),
        cost_estimate=pl.CostEstimate(
            flops=6 * line * rows * width * hidden,
            bytes_accessed=6 * width * hidden + 4 * line * rows * hidden,
            transcendentals=line * rows * hidden,
        ),
    )(
        n2.reshape(CHUNKS, part, width), w["mlp"], w["bundle"],
    )
    return out.reshape(rows, width), (n2_all.reshape(CHUNKS, every, width), gate, up)


def mlp_back_kernel(
    line, chunks, tile,
    ds_ref, packed, n2_hbm, gate_in, up_in, bundle_ref, names_ref,
    out_ref, whole_ref, parts_ref,
    gathered, partial_ref, from_left, from_right, s0, s1, s2, s3, s4, s5, s6,
    wg, wu, ws, gate_st, up_st, n2_st, acc, ghigh_ref, gexp_ref, gsh_ref, gres_ref, expand_ref, ash_ref, wsem, isem,
):
    rows, width = ds_ref.shape[1:]
    every = line * rows
    tiles = wg.shape[0] // tile
    high = bundle_ref[rows_of(B_INPUT + 3, 2)]
    res = bundle_ref[rows_of(B_RES_TWO)]
    me = lax.axis_index("tensor")
    loads = ff_loads(packed, (wg, wu, ws), wsem)

    def fetch(c):
        slot = c % 2
        return (
            pltpu.make_async_copy(gate_in.at[c], gate_st.at[slot], isem.at[0, slot]),
            pltpu.make_async_copy(up_in.at[c], up_st.at[slot], isem.at[1, slot]),
            pltpu.make_async_copy(n2_hbm.at[c], n2_st.at[slot], isem.at[2, slot]),
        )

    def begin():
        for load in loads:
            load.start()
        clear_tail(packed, (wg, wu, ws))
        spread_factors(bundle_ref, expand_ref, ash_ref)
        for one in fetch(0):
            one.start()
        for c in range(chunks):
            gathered[c, me] = ds_ref[c]
        for ref in (ghigh_ref, gexp_ref, gsh_ref, gres_ref):
            ref[...] = jnp.zeros_like(ref)

    def work(c):
        slot = c % 2

        @pl.when(c == 0)
        def _():
            for load in loads:
                load.wait()

        for one in fetch(c):
            one.wait()

        @pl.when(c + 1 < chunks)
        def _():
            for one in fetch(c + 1):
                one.start()

        ds = gathered[c].reshape(every, width)
        n2 = n2_st[slot]
        er = dot_t(n2, high).astype(BF)
        rank_in = dot_t(ds, res).astype(BF)

        def one(f, carry):
            rank_out, srank = carry
            cols = pl.ds(pl.multiple_of(f * tile, tile), tile)
            act_grad = dot_t(ds, ws[cols]) + dot(rank_in, ash_ref[:, cols])
            gate = gate_st[slot, :, cols].astype(F32)
            up = up_st[slot, :, cols].astype(F32)
            sig = 1.0 / (1.0 + jnp.exp(-gate))
            silu = gate * sig
            act = (silu * up).astype(BF)
            gate_grad = (act_grad * up * (sig + silu * (1.0 - sig))).astype(BF)
            up_grad = (act_grad * silu).astype(BF)
            now = dot(gate_grad, wg[cols]) + dot(up_grad, wu[cols])

            @pl.when(f == 0)
            def _():
                acc[...] = now

            @pl.when(f > 0)
            def _():
                acc[...] += now

            gexp_ref[0, :, cols] += t_dot(er, gate_grad)
            gexp_ref[1, :, cols] += t_dot(er, up_grad)
            gsh_ref[:, cols] += t_dot(rank_in, act)
            rank_out = rank_out + dot_t(gate_grad, expand_ref[0, :, cols])
            rank_out = rank_out + dot_t(up_grad, expand_ref[1, :, cols])
            return rank_out, srank + dot_t(act, ash_ref[:, cols])

        rank_out, srank = lax.fori_loop(
            0,
            tiles,
            one,
            (
                jnp.zeros((every, expand_ref.shape[1]), F32),
                jnp.zeros((every, ash_ref.shape[0]), F32),
            ),
        )
        rank_out = rank_out.astype(BF)
        total = acc[...] + dot(rank_out, high)
        partial_ref[c] = total.astype(BF).reshape(line, rows, width)
        ghigh_ref[...] += t_dot(rank_out, n2)
        gres_ref[...] += t_dot(srank.astype(BF), ds)

    line_exchange(
        line, chunks, gathered, partial_ref, from_left, from_right, out_ref,
        (s0, s1, s2, s3, s4, s5, s6), begin, work,
    )
    whole_ref[: 2 * RANK] = ghigh_ref[...].astype(BF)
    whole_ref[2 * RANK :] = gres_ref[...].astype(BF)
    extra = gsh_ref.shape[1] - width
    parts_ref[3 * RANK :, extra:] = jnp.zeros((3 * RANK, width - extra), BF)
    for i, part in enumerate((gexp_ref[0, :RANK], gexp_ref[1, RANK:], gsh_ref[...])):
        part = part.astype(BF)
        parts_ref[i * RANK : (i + 1) * RANK] = part[:, :width]
        parts_ref[(3 + i) * RANK : (4 + i) * RANK, :extra] = part[:, width:]
    parts_ref[rows_of(5), extra : extra + LANES] = names_ref[...]


def mlp_backward(ds, w, saved, names):
    n2_all, gate, up = saved
    line = lax.axis_size("tensor")
    rows, width = ds.shape
    halves, groups, _, low_rows, _ = w["mlp"].shape
    hidden = halves * low_rows + -(halves * low_rows) % (2 * LANES)
    part = rows // CHUNKS
    every = line * part
    out, whole, parts = pl.pallas_call(
        partial(mlp_back_kernel, line, CHUNKS, ff_tile(hidden)),
        in_specs=[vspec()] + [hspec()] * 4 + [vspec()] * 2,
        out_specs=[vspec()] * 3,
        out_shape=[
            jax.ShapeDtypeStruct((CHUNKS, part, width), F32),
            jax.ShapeDtypeStruct((3 * RANK, width), BF),
            jax.ShapeDtypeStruct((6 * RANK, width), BF),
        ],
        scratch_shapes=exchange_scratch(line, CHUNKS, part, width)
        + [pltpu.VMEM((hidden, width), BF)] * 3
        + [pltpu.VMEM((2, every, hidden), BF)] * 2
        + [
            pltpu.VMEM((2, every, width), BF),
            pltpu.VMEM((every, width), F32),
            pltpu.VMEM((2 * RANK, width), F32),
            pltpu.VMEM((2, 2 * RANK, hidden), F32),
            pltpu.VMEM((RANK, hidden), F32),
            pltpu.VMEM((RANK, width), F32),
            pltpu.VMEM((2, 2 * RANK, hidden), BF),
            pltpu.VMEM((RANK, hidden), BF),
            pltpu.SemaphoreType.DMA((3, halves, groups)),
            pltpu.SemaphoreType.DMA((3, 2)),
        ],
        compiler_params=pltpu.CompilerParams(
            collective_id=1, has_side_effects=True, vmem_limit_bytes=VMEM_LIMIT
        ),
        cost_estimate=pl.CostEstimate(
            flops=6 * line * rows * width * hidden,
            bytes_accessed=6 * width * hidden + 4 * line * rows * hidden,
            transcendentals=line * rows * hidden,
        ),
    )(
        ds.reshape(CHUNKS, part, width), w["mlp"], n2_all, gate, up, w["bundle"], names,
    )
    return out.reshape(rows, width), whole, parts


def gather_kernel(
    line, peers,
    attn, bundles, heads,
    first_out, second_out, bundle_out,
    own_sem, z_recv, z_right, z_left, dp_recv, dp_send, core_recv, core_send, side_recv, side_send, side_own,
):
    me, spot, core = lax.axis_index("tensor"), lax.axis_index("dp"), lax.axis_index("section")
    other = 1 - core
    has_left, has_right = me > 0, me < line - 1
    barrier = pltpu.get_barrier_semaphore()

    def greet(**where):
        pl.semaphore_signal(barrier, inc=1, device_id=where, device_id_type=MESH)

    @pl.when(has_left)
    def _():
        greet(tensor=me - 1)

    @pl.when(has_right)
    def _():
        greet(tensor=me + 1)

    greet(section=other)
    square = peers == 4

    def partner(k):
        if square:
            return (None, spot + 1 - 2 * lax.rem(spot, 2), lax.rem(spot + 2, 4), 3 - spot)[k]
        return lax.rem(spot + k, peers)

    def origin(k):
        return partner(k) if square else lax.rem(spot + peers - k, peers)

    direct = (1, 2) if square else tuple(range(1, peers))
    for k in range(1, peers):
        greet(dp=partner(k))
    pl.semaphore_wait(barrier, jnp.where(has_left, 1, 0) + jnp.where(has_right, 1, 0) + peers)

    mine = spot * 2 + core
    plain, part = bundles.shape[1] - heads.shape[1], heads.shape[2]

    def head_place(layer, o):
        return bundle_out.at[layer, pl.ds(plain, heads.shape[1]), pl.ds(o * part, part)]

    def places(o):
        return first_out.at[mine, o], second_out.at[o], head_place(core, o), head_place(other, o)

    sides = [
        pltpu.make_async_remote_copy(
            src_ref=src,
            dst_ref=dst,
            send_sem=side_send.at[i],
            recv_sem=side_recv.at[i],
            device_id={"section": other},
            device_id_type=MESH,
        )
        for i, (src, dst) in enumerate(
            (
                (bundles.at[other, pl.ds(0, plain)], bundle_out.at[core, pl.ds(0, plain)]),
                (heads.at[other], head_place(core, me)),
            )
        )
    ]
    side_keep = pltpu.make_async_copy(
        bundles.at[core, pl.ds(0, plain)], bundle_out.at[core, pl.ds(0, plain)], side_own
    )
    sources = (attn.at[0], attn.at[1], heads.at[core], head_place(other, me))
    keeps = [
        pltpu.make_async_copy(src, dst, own_sem.at[i]) for i, (src, dst) in enumerate(zip(sources[:3], places(me)))
    ]

    def remote(src, dst, send, recv, **where):
        return pltpu.make_async_remote_copy(
            src_ref=src, dst_ref=dst, send_sem=send, recv_sem=recv, device_id=where, device_id_type=MESH
        )

    def along(i, o, side, own):
        dst = places(o)[i]
        return remote(
            sources[i] if own else dst,
            dst,
            (z_right if side > 0 else z_left).at[i, o],
            z_recv.at[i, o],
            tensor=me + side,
        )

    outs = (first_out,)

    def to_peer(lay, k, o, own):
        dst = outs[lay].at[mine, o]
        return remote(
            attn.at[lay] if own else dst, dst, dp_send.at[lay, k, o], dp_recv.at[lay, spot, o], dp=partner(k)
        )

    def from_peer(lay, k, o):
        p = origin(k)
        slot = outs[lay].at[p * 2 + core, o]
        to = partner(3 - k) if square and k < 3 else p
        return remote(slot, slot, dp_send.at[lay, peers - 1, o], dp_recv.at[lay, p, o], dp=to)

    def to_core(lay, p, o, own):
        dst = outs[lay].at[p * 2 + core, o]
        return remote(
            attn.at[lay] if own else dst, dst, core_send.at[lay, p, o], core_recv.at[lay, p, o], section=other
        )

    def spread(lay, o, own):
        for k in direct:
            to_peer(lay, k, o, own).start()
        to_core(lay, spot, o, own).start()

    for side in sides:
        side.start()
    for i in range(4):
        if i == 3:
            sides[1].wait_recv()

        @pl.when(has_right)
        def _():
            along(i, me, 1, True).start()

        @pl.when(has_left)
        def _():
            along(i, me, -1, True).start()

        if i == 0:
            spread(i, me, True)
    for keep in keeps:
        keep.start()
    side_keep.start()
    for d in range(1, line):
        for i in range(4):

            @pl.when(me >= d)
            def _():
                along(i, me - d, 1, False).wait_recv()

                @pl.when(has_right)
                def _():
                    along(i, me - d, 1, False).start()

                if i == 0:
                    spread(i, me - d, False)

            @pl.when(me + d < line)
            def _():
                along(i, me + d, -1, False).wait_recv()

                @pl.when(has_left)
                def _():
                    along(i, me + d, -1, False).start()

                if i == 0:
                    spread(i, me + d, False)

    half = line // 2

    def pass_on(n, carry):
        o = lax.rem(me + n, line)
        for lay in range(1):
            for k in direct:
                from_peer(lay, k, o).wait_recv()
                if square:

                    @pl.when(o < half if k == 1 else o >= half)
                    def _():
                        from_peer(lay, k, o).start()

                to_core(lay, origin(k), o, False).start()
        return carry

    lax.fori_loop(0, line, pass_on, 0)

    def pass_last(n, carry):
        o = lax.rem(me + n, line)
        for lay in range(1):
            from_peer(lay, 3, o).wait_recv()
            to_core(lay, origin(3), o, False).start()
        return carry

    if square:
        lax.fori_loop(0, line, pass_last, 0)

    def finish(o, carry):
        for lay in range(1):
            for k in direct:
                to_peer(lay, k, o, False).wait_send()
            if square:
                from_peer(lay, 1, o).wait_send()
            for p in range(peers):
                to_core(lay, p, o, False).wait_send()
                slot = outs[lay].at[p * 2 + other, o]
                remote(slot, slot, core_send.at[lay, p, o], core_recv.at[lay, p, o], section=other).wait_recv()
        for i in range(4):

            @pl.when(jnp.logical_and(has_right, me >= o))
            def _():
                along(i, o, 1, False).wait_send()

            @pl.when(jnp.logical_and(has_left, me <= o))
            def _():
                along(i, o, -1, False).wait_send()

        return carry

    lax.fori_loop(0, line, finish, 0)
    for keep in keeps:
        keep.wait()
    side_keep.wait()
    sides[0].wait_recv()
    for side in sides:
        side.wait_send()


def gather_first(attn, bundles, heads):
    line, peers = lax.axis_size("tensor"), lax.axis_size("dp")
    cores, part, cols = attn.shape
    dma = pltpu.SemaphoreType.DMA
    return pl.pallas_call(
        partial(gather_kernel, line, peers),
        in_specs=[vspec()] * 3,
        out_specs=[hspec()] * 3,
        out_shape=[
            jax.ShapeDtypeStruct((peers * cores, line, part, cols), BF),
            jax.ShapeDtypeStruct((line, part, cols), BF),
            jax.ShapeDtypeStruct(bundles.shape, BF),
        ],
        scratch_shapes=[dma((3,)), dma((4, line)), dma((4, line)), dma((4, line))]
        + [dma((1, peers, line))] * 4
        + [dma((2,)), dma((2,)), dma],
        compiler_params=pltpu.CompilerParams(
            collective_id=4, has_side_effects=True, vmem_limit_bytes=VMEM_LIMIT
        ),
    )(attn, bundles, heads)


def rotated(x, cos, sin):
    return x * cos + pltpu.roll(x, HEAD_DIM // 2, 1) * sin


def head_cols(h):
    return pl.ds(pl.multiple_of(h * HEAD_DIM, HEAD_DIM), HEAD_DIM)


def weight_loads(packed, wq, wo, wkv, wsem):
    cols, kv_cols = wq.shape[-1], wkv.shape[-1]
    loads = []
    for i, (ref, start, size) in enumerate(((wkv, 2 * cols, kv_cols), (wq, 0, cols), (wo, cols, cols))):
        loads.append(
            [
                pltpu.make_async_copy(packed.at[:, t, :, pl.ds(start, size)], ref.at[t], wsem.at[i, t])
                for t in range(ref.shape[0])
            ]
        )
    return loads


def flat(ref, t):
    groups, rows, cols = ref.shape[1:]
    return ref[t].reshape(groups * rows, cols)


def allowed_keys(info_ref, block, keys, rows):
    row = info_ref[0] + lax.broadcasted_iota(jnp.int32, (1, rows), 1)
    last = jnp.minimum(row, info_ref[1] - 1)
    return block * keys + lax.broadcasted_iota(jnp.int32, (keys, rows), 0) <= last


def one_way_barrier(me, line, side):
    barrier = pltpu.get_barrier_semaphore()
    first, last = (0, line - 1) if side > 0 else (line - 1, 0)

    @pl.when(me != first)
    def _():
        pl.semaphore_signal(barrier, inc=1, device_id={"tensor": me - side}, device_id_type=MESH)

    @pl.when(me != last)
    def _():
        pl.semaphore_wait(barrier, 1)


def spread_qkv(bundle_ref, bq_ref, bkv_ref):
    kv_half = bkv_ref.shape[1] // 2
    bq_ref[...] = jnp.zeros_like(bq_ref)
    bkv_ref[...] = jnp.zeros_like(bkv_ref)
    bq_ref[rows_of(0)] = bundle_ref[rows_of(B_HEADS)]
    for i in range(2):
        span = slice(i * kv_half, (i + 1) * kv_half)
        bkv_ref[rows_of(1 + i), span] = bundle_ref[rows_of(B_KV), span]


def kv_exchange(me, line, kvbuf, recv, send):
    def move(o):
        return pltpu.make_async_remote_copy(
            src_ref=kvbuf.at[o],
            dst_ref=kvbuf.at[o],
            send_sem=send.at[o],
            recv_sem=recv.at[o],
            device_id={"tensor": me + 1},
            device_id_type=MESH,
        )

    return move


def attend_kernel(
    line, group,
    info_ref, x_ref, bundle_ref, cos_ref, sin_ref, packed,
    mid_ref, n2_ref, normed_ref, lowr_ref, rank_ref, q_ref, kv_out, attended_ref, log_ref,
    wq, wo, wkv, kvbuf, acc, peak, total, bq_ref, bkv_ref, wsem, recv, send, ksem,
):
    rows, width = x_ref.shape
    heads = width // HEAD_DIM
    cols = wq.shape[-1]
    kv_cols = wkv.shape[-1]
    scale = HEAD_DIM**-0.5
    me = lax.axis_index("tensor")
    one_way_barrier(me, line, 1)
    kv_loads, q_loads, o_loads = weight_loads(packed, wq, wo, wkv, wsem)
    for load in kv_loads + q_loads + o_loads:
        load.start()
    move = kv_exchange(me, line, kvbuf, recv, send)
    spread_qkv(bundle_ref, bq_ref, bkv_ref)
    misc = bundle_ref[rows_of(B_MISC)].astype(F32)
    q_bias = bundle_ref[rows_of(B_HEADS + 2)].astype(F32)[:1]
    low_in = bundle_ref[rows_of(B_INPUT, 3)]
    x = x_ref[...].astype(F32)
    inverse = lax.rsqrt(jnp.mean(x * x, axis=-1, keepdims=True) + EPSILON)
    normed_ref[...] = (x * inverse * misc[0:1]).astype(BF)
    low = dot_t(normed_ref[...], low_in).astype(BF)
    cos, sin = cos_ref[...], sin_ref[...]
    for load in kv_loads:
        load.wait()
    for t in range(line):
        span = slice(t * kv_cols, (t + 1) * kv_cols)
        kv = dot(normed_ref[...], flat(wkv, t)) + misc[2:3, span] + dot(low, bkv_ref[:, span])
        for h in range(kv_cols // HEAD_DIM):
            at = t * kv_cols + h * HEAD_DIM
            one = kv[:, h * HEAD_DIM : (h + 1) * HEAD_DIM]
            if at < KV_HEADS * HEAD_DIM:
                one = rotated(one, cos, sin)
            kvbuf[me, :, at : at + HEAD_DIM] = one.astype(BF)

    @pl.when(me < line - 1)
    def _():
        move(me).start()

    for load in q_loads:
        load.wait()
    for t in range(line):
        span = slice(t * cols, (t + 1) * cols)
        q = dot(normed_ref[...], flat(wq, t)) + q_bias[:, span] + dot(low, bq_ref[:, span])
        for h in range(cols // HEAD_DIM):
            at = t * cols + h * HEAD_DIM
            q_ref[:, at : at + HEAD_DIM] = rotated(
                q[:, h * HEAD_DIM : (h + 1) * HEAD_DIM], cos, sin
            ).astype(BF)
    acc[...] = jnp.zeros_like(acc)
    total[...] = jnp.zeros_like(total)
    peak[...] = jnp.full_like(peak, MASKED_SCORE)

    def block(o):
        allowed = allowed_keys(info_ref, o, rows, rows)

        def one(h, carry):
            kv_head = h // group
            k = kvbuf[o, :, head_cols(kv_head)]
            v = kvbuf[o, :, head_cols(KV_HEADS + kv_head)]
            scores = jnp.where(allowed, dot_t(k, q_ref[:, head_cols(h)]) * scale, MASKED_SCORE)
            top = jnp.maximum(peak[h], jnp.max(scores, axis=0, keepdims=True))
            soft = jnp.exp(scores - top)
            shift = jnp.exp(peak[h] - top)
            total[h] = total[h] * shift + jnp.sum(soft, axis=0, keepdims=True)
            acc[h] = acc[h] * shift + t_dot(v, soft.astype(BF))
            peak[h] = top
            return carry

        lax.fori_loop(0, heads, one, 0, unroll=12)

    for d in range(line):

        @pl.when(me >= d)
        def _():
            if d > 0:
                move(me - d).wait_recv()

                @pl.when(me < line - 1)
                def _():
                    move(me - d).start()

            block(me - d)

    keep = pltpu.make_async_copy(kvbuf, kv_out, ksem)
    keep.start()
    for h in range(heads):
        attended_ref[:, h * HEAD_DIM : (h + 1) * HEAD_DIM] = (acc[h] * (1.0 / total[h])).T.astype(BF)
        log_ref[h] = peak[h] + jnp.log(total[h])
    rank = dot_t(attended_ref[...], bundle_ref[rows_of(B_HEADS + 1)]).astype(BF)
    lowr_ref[...] = low
    rank_ref[...] = rank
    middle = x_ref[...].astype(F32) + dot(rank, bundle_ref[rows_of(B_RES_ONE)])
    for load in o_loads:
        load.wait()
    for t in range(line):
        middle = middle + dot_t(attended_ref[:, t * cols : (t + 1) * cols], flat(wo, t))
    mid_ref[...] = middle
    inverse = lax.rsqrt(jnp.mean(middle * middle, axis=-1, keepdims=True) + EPSILON)
    n2_ref[...] = (middle * inverse * misc[1:2]).astype(BF)
    keep.wait()
    for o in range(line):

        @pl.when(jnp.logical_and(me < line - 1, me >= o))
        def _():
            move(o).wait_send()


def attend_forward(x, w, info, tables):
    line = lax.axis_size("tensor")
    rows, width = x.shape
    heads = width // HEAD_DIM
    kv_width = 2 * KV_HEADS * HEAD_DIM
    groups, low_rows = w["packed"].shape[0], w["packed"].shape[2]
    outs = pl.pallas_call(
        partial(attend_kernel, line, heads // KV_HEADS),
        in_specs=[pl.BlockSpec(memory_space=pltpu.SMEM)] + [vspec()] * 4 + [hspec()],
        out_specs=[vspec()] * 6 + [hspec()] + [vspec()] * 2,
        out_shape=[
            jax.ShapeDtypeStruct((rows, width), F32),
            jax.ShapeDtypeStruct((rows, width), BF),
            jax.ShapeDtypeStruct((rows, width), BF),
            jax.ShapeDtypeStruct((rows, 3 * RANK), BF),
            jax.ShapeDtypeStruct((rows, RANK), BF),
            jax.ShapeDtypeStruct((rows, width), BF),
            jax.ShapeDtypeStruct((line, rows, kv_width), BF),
            jax.ShapeDtypeStruct((rows, width), BF),
            jax.ShapeDtypeStruct((heads, 1, rows), F32),
        ],
        scratch_shapes=[
            pltpu.VMEM((line, groups, low_rows, width // line), BF),
            pltpu.VMEM((line, groups, low_rows, width // line), BF),
            pltpu.VMEM((line, groups, low_rows, kv_width // line), BF),
            pltpu.VMEM((line, rows, kv_width), BF),
            pltpu.VMEM((heads, HEAD_DIM, rows), F32),
            pltpu.VMEM((heads, 1, rows), F32),
            pltpu.VMEM((heads, 1, rows), F32),
            pltpu.VMEM((3 * RANK, width), BF),
            pltpu.VMEM((3 * RANK, kv_width), BF),
            pltpu.SemaphoreType.DMA((3, line)),
            pltpu.SemaphoreType.DMA((line,)),
            pltpu.SemaphoreType.DMA((line,)),
            pltpu.SemaphoreType.DMA,
        ],
        compiler_params=pltpu.CompilerParams(
            collective_id=2, has_side_effects=True, vmem_limit_bytes=VMEM_LIMIT
        ),
        cost_estimate=pl.CostEstimate(
            flops=4 * rows * width * width * 2, bytes_accessed=5 * width * width, transcendentals=0
        ),
    )(
        info, x, w["bundle"], tables[0], tables[1], w["packed"],
    )
    return outs[0], outs[1], outs[2:]


def attend_back_kernel(
    line, group,
    info_ref, x_ref, mid_ref, dy_ref, dn2_ref, bundle_ref, cos_ref, sin_ref,
    normed_ref, lowr_ref, rank_ref, q_ref, kv_ref, attended_ref, log_ref, packed,
    dx_ref, dx_low_ref, grads_ref,
    wq, wo, wkv, do_ref, dq_acc, dq_ref, dkv_acc, partial_ref, from_right, delta, bq_ref, bkv_ref, wsem, recv, send,
):
    rows, width = x_ref.shape
    heads = width // HEAD_DIM
    cols = wq.shape[-1]
    kv_cols = wkv.shape[-1]
    kv_half = KV_HEADS * HEAD_DIM
    scale = HEAD_DIM**-0.5
    me = lax.axis_index("tensor")
    one_way_barrier(me, line, -1)
    kv_loads, q_loads, o_loads = weight_loads(packed, wq, wo, wkv, wsem)
    for load in o_loads + q_loads + kv_loads:
        load.start()

    def move(o):
        return pltpu.make_async_remote_copy(
            src_ref=partial_ref.at[o],
            dst_ref=from_right.at[o],
            send_sem=send.at[o],
            recv_sem=recv.at[o],
            device_id={"tensor": me - 1},
            device_id_type=MESH,
        )

    def through_norm(values, gain, grad_out):
        inverse = lax.rsqrt(jnp.mean(values * values, axis=-1, keepdims=True) + EPSILON)
        weighted = gain * grad_out
        return inverse * weighted - inverse * inverse * inverse * values * jnp.mean(
            weighted * values, axis=-1, keepdims=True
        )

    spread_qkv(bundle_ref, bq_ref, bkv_ref)
    misc = bundle_ref[rows_of(B_MISC)].astype(F32)
    att = bundle_ref[rows_of(B_HEADS + 1)]
    middle_grad = dy_ref[...].astype(F32) + through_norm(mid_ref[...], misc[1:2], dn2_ref[...])
    dx_ref[...] = middle_grad
    branch_grad = middle_grad.astype(BF)
    low, rank = lowr_ref[...], rank_ref[...]
    rank_grad = dot_t(branch_grad, bundle_ref[rows_of(B_RES_ONE)]).astype(BF)
    grads_ref[3 * RANK : 4 * RANK] = t_dot(rank, branch_grad).astype(BF)
    grads_ref[6 * RANK :] = t_dot(rank_grad, attended_ref[...]).astype(BF)
    for load in o_loads:
        load.wait()
    for t in range(line):
        span = slice(t * cols, (t + 1) * cols)
        do_ref[:, span] = (dot(branch_grad, flat(wo, t)) + dot(rank_grad, att[:, span])).astype(BF)
    for h in range(heads):
        span = slice(h * HEAD_DIM, (h + 1) * HEAD_DIM)
        both = do_ref[:, span].astype(F32) * attended_ref[:, span].astype(F32)
        delta[h] = jnp.sum(both.T, axis=0, keepdims=True)
    dq_acc[...] = jnp.zeros_like(dq_acc)

    def block(o):
        allowed = allowed_keys(info_ref, o, rows, rows)
        dkv_acc[...] = jnp.zeros_like(dkv_acc)

        def one(h, carry):
            kv_head = h // group
            k = kv_ref[o, :, head_cols(kv_head)]
            v = kv_ref[o, :, head_cols(KV_HEADS + kv_head)]
            q = q_ref[:, head_cols(h)]
            do = do_ref[:, head_cols(h)]
            scores = dot_t(k, q) * scale - log_ref[h]
            soft = jnp.exp(jnp.where(allowed, scores, MASKED_SCORE))
            grad = (soft * (dot_t(v, do) - delta[h])).astype(BF)
            dq_acc[h] += t_dot(k, grad)
            dkv_acc[:, head_cols(kv_head)] += dot(grad, q) * scale
            dkv_acc[:, head_cols(KV_HEADS + kv_head)] += dot(soft.astype(BF), do)
            return carry

        lax.fori_loop(0, heads, one, 0, unroll=12)
        partial_ref[o] = dkv_acc[...].astype(BF)

    for s in range(2 * line - 1):
        if s < line:

            @pl.when(me >= s)
            def _():
                block(s)

        for h in range(line - 1):
            o = s - h
            if 0 <= o < line - 1 - h:

                @pl.when(me == line - 1 - h)
                def _():
                    if h > 0:
                        move(o).wait_recv()
                        partial_ref[o] = (partial_ref[o].astype(F32) + from_right[o].astype(F32)).astype(BF)
                    move(o).start()

    cos, sin = cos_ref[...], -sin_ref[...]
    for h in range(heads):
        dq_ref[:, h * HEAD_DIM : (h + 1) * HEAD_DIM] = rotated(dq_acc[h].T * scale, cos, sin).astype(BF)
    dq = dq_ref[...]
    grads_ref[5 * RANK : 6 * RANK] = t_dot(low, dq)[:RANK].astype(BF)
    low_grad = dot_t(dq, bq_ref[...])
    for load in q_loads:
        load.wait()
    normed_grad = dot_t(dq[:, :cols], flat(wq, 0))
    for t in range(1, line):
        normed_grad = normed_grad + dot_t(dq[:, t * cols : (t + 1) * cols], flat(wq, t))
    dkv_acc[...] = partial_ref[me].astype(F32)

    @pl.when(me < line - 1)
    def _():
        move(me).wait_recv()
        dkv_acc[...] += from_right[me].astype(F32)

    for h in range(KV_HEADS):
        span = slice(h * HEAD_DIM, (h + 1) * HEAD_DIM)
        dkv_acc[:, span] = rotated(dkv_acc[:, span], cos, sin)
    dkv = dkv_acc[...].astype(BF)
    kv_grad = t_dot(low, dkv).astype(BF)
    grads_ref[4 * RANK : 5 * RANK, :kv_half] = kv_grad[RANK : 2 * RANK, :kv_half]
    grads_ref[4 * RANK : 5 * RANK, kv_half : 2 * kv_half] = kv_grad[2 * RANK :, kv_half:]
    grads_ref[4 * RANK : 5 * RANK, 2 * kv_half :] = jnp.zeros((RANK, width - 2 * kv_half), BF)
    low_grad = (low_grad + dot_t(dkv, bkv_ref[...])).astype(BF)
    grads_ref[: 3 * RANK] = t_dot(low_grad, normed_ref[...]).astype(BF)
    for load in kv_loads:
        load.wait()
    for t in range(line):
        normed_grad = normed_grad + dot_t(dkv[:, t * kv_cols : (t + 1) * kv_cols], flat(wkv, t))
    normed_grad = normed_grad + dot(low_grad, bundle_ref[rows_of(B_INPUT, 3)])
    dx = dx_ref[...] + through_norm(x_ref[...].astype(F32), misc[0:1], normed_grad)
    dx_ref[...] = dx
    dx_low_ref[...] = dx.astype(BF)
    for o in range(line - 1):

        @pl.when(me > o)
        def _():
            move(o).wait_send()


def attend_backward(x, middle, dy, dn2, w, kept, info, tables):
    line = lax.axis_size("tensor")
    rows, width = x.shape
    heads = width // HEAD_DIM
    kv_width = 2 * KV_HEADS * HEAD_DIM
    groups, low_rows = w["packed"].shape[0], w["packed"].shape[2]
    return pl.pallas_call(
        partial(attend_back_kernel, line, heads // KV_HEADS),
        in_specs=[pl.BlockSpec(memory_space=pltpu.SMEM)] + [vspec()] * 14 + [hspec()],
        out_specs=[vspec()] * 3,
        out_shape=[
            jax.ShapeDtypeStruct((rows, width), F32),
            jax.ShapeDtypeStruct((rows, width), BF),
            jax.ShapeDtypeStruct((7 * RANK, width), BF),
        ],
        scratch_shapes=[
            pltpu.VMEM((line, groups, low_rows, width // line), BF),
            pltpu.VMEM((line, groups, low_rows, width // line), BF),
            pltpu.VMEM((line, groups, low_rows, kv_width // line), BF),
            pltpu.VMEM((rows, width), BF),
            pltpu.VMEM((heads, HEAD_DIM, rows), F32),
            pltpu.VMEM((rows, width), BF),
            pltpu.VMEM((rows, kv_width), F32),
            pltpu.VMEM((line, rows, kv_width), BF),
            pltpu.VMEM((line, rows, kv_width), BF),
            pltpu.VMEM((heads, 1, rows), F32),
            pltpu.VMEM((3 * RANK, width), BF),
            pltpu.VMEM((3 * RANK, kv_width), BF),
            pltpu.SemaphoreType.DMA((3, line)),
            pltpu.SemaphoreType.DMA((line,)),
            pltpu.SemaphoreType.DMA((line,)),
        ],
        compiler_params=pltpu.CompilerParams(
            collective_id=3 if dy.dtype == F32 else 5, has_side_effects=True, vmem_limit_bytes=VMEM_LIMIT
        ),
        cost_estimate=pl.CostEstimate(
            flops=4 * rows * width * width * 2, bytes_accessed=5 * width * width, transcendentals=0
        ),
    )(
        info, x, middle, dy, dn2, w["bundle"], tables[0], tables[1], *kept, w["packed"],
    )


def reduce_kernel(
    line, peers, extra,
    attn_ref, whole_ref, parts_ref, y_first, y_second, g_first, g_second,
    out, y_out, g_out,
    mine, z_in, quarter, z_recv, z_send, dp_recv, dp_send, own_sem, t_recv, t_right, t_left,
    side_recv, side_send, side_own,
):
    r = RANK
    me, spot, core = lax.axis_index("tensor"), lax.axis_index("dp"), lax.axis_index("section")
    width = mine.shape[1]
    cols = width // line
    seqs = out.shape[0]
    seq = spot * 2 + core
    has_left, has_right = me > 0, me < line - 1
    barrier = pltpu.get_barrier_semaphore()

    def greet(**where):
        pl.semaphore_signal(barrier, inc=1, device_id=where, device_id_type=MESH)

    for k in range(1, line):
        greet(tensor=lax.rem(me + k, line))

    greet(section=1 - core)

    @pl.when(core == 0)
    def _():
        for k in range(1, peers):
            for c in range(2):
                greet(section=c, dp=lax.rem(spot + k, peers))

    pl.semaphore_wait(barrier, line - 1 + peers)

    def remote(src, dst, send, recv, **where):
        return pltpu.make_async_remote_copy(
            src_ref=src, dst_ref=dst, send_sem=send, recv_sem=recv, device_id=where, device_id_type=MESH
        )

    def lanes(t):
        return pl.ds(pl.multiple_of(t * cols, LANES), cols)

    def pieces(s):
        return (
            (parts_ref.at[pl.ds(0, 3 * r)], out.at[s, pl.ds(8 * r, 3 * r)]),
            (parts_ref.at[pl.ds(3 * r, 3 * r), pl.ds(0, extra)], out.at[s, pl.ds(11 * r, 3 * r), pl.ds(0, extra)]),
            (
                parts_ref.at[pl.ds(5 * r, r), pl.ds(extra, LANES)],
                out.at[s, pl.ds(13 * r, r), pl.ds(extra, LANES)],
            ),
            (quarter.at[pl.ds(0, 8 * r)], out.at[s, pl.ds(0, 8 * r), lanes(me)]),
            (quarter.at[pl.ds(8 * r, 2 * r)], out.at[s, pl.ds(11 * r, 2 * r), pl.ds(extra, cols)]),
        )

    def to_peer(k, i):
        src, dst = pieces(seq)[i]
        return remote(src, dst, dp_send.at[k, i], dp_recv.at[seq, i], section=0, dp=lax.rem(spot + k, peers))

    def stay(i):
        src, dst = pieces(seq)[i]
        return pltpu.make_async_copy(src, dst, own_sem.at[i])

    def send_pieces(which):
        for i in which:
            for k in range(1, peers):
                to_peer(k, i).start()

            @pl.when(core != 0)
            def _():
                to_peer(0, i).start()

            @pl.when(core == 0)
            def _():
                stay(i).start()

    def across(k):
        to = lax.rem(me + k, line)
        return remote(mine.at[:, lanes(to)], z_in.at[me], z_send.at[k], z_recv.at[me], tensor=to)

    def incoming(k):
        o = lax.rem(me + k, line)
        return remote(mine.at[:, lanes(me)], z_in.at[o], z_send.at[k], z_recv.at[o], tensor=o)

    def side(i, src, dst):
        return remote(src, dst.at[core], side_send.at[i], side_recv.at[i], section=1 - core)

    def side_keep(i, src, dst):
        return pltpu.make_async_copy(src, dst.at[core], side_own.at[i])

    pairs = ((y_first, y_second, y_out), (g_first, g_second, g_out))

    for first, rows, ref, start in (
        (0, 3, attn_ref, 0), (3, 2, whole_ref, 0), (5, 1, attn_ref, 3), (6, 1, whole_ref, 2), (7, 3, attn_ref, 4),
    ):
        mine[rows_of(first, rows)] = ref[rows_of(start, rows)]
    for k in range(1, line):
        across(k).start()
    send_pieces((0, 1, 2))
    for c in range(2):

        @pl.when(core == c)
        def _():
            for i, (first, second, dst) in enumerate(pairs):
                side(i, first if c == 1 else second, dst).start()
                side_keep(i, second if c == 1 else first, dst).start()

    total = mine[:, lanes(me)].astype(F32)
    for k in range(1, line):
        incoming(k).wait_recv()
        total = total + z_in[lax.rem(me + k, line)].astype(F32)
    quarter[...] = total.astype(BF)
    send_pieces((3, 4))

    def arrived(s, i):
        src, dst = pieces(s)[i]
        return remote(src, dst, dp_send.at[0, i], dp_recv.at[s, i], section=0)

    def along(s, o, side):
        place = out.at[s, pl.ds(0, 8 * r), lanes(o)]
        return remote(
            place, place, (t_right if side > 0 else t_left).at[s, o], t_recv.at[s, o], tensor=me + side
        )

    @pl.when(core == 0)
    def _():
        def own_rows(n, carry):
            s = lax.rem(seq + n, seqs)

            @pl.when(n == 0)
            def _():
                stay(3).wait()

            @pl.when(n > 0)
            def _():
                arrived(s, 3).wait_recv()

            @pl.when(has_right)
            def _():
                along(s, me, 1).start()

            @pl.when(has_left)
            def _():
                along(s, me, -1).start()

            return carry

        lax.fori_loop(0, seqs, own_rows, 0)
        for d in range(1, line):

            def others(n, carry):
                s = lax.rem(seq + n, seqs)

                @pl.when(me >= d)
                def _():
                    along(s, me - d, 1).wait_recv()

                    @pl.when(has_right)
                    def _():
                        along(s, me - d, 1).start()

                @pl.when(me + d < line)
                def _():
                    along(s, me + d, -1).wait_recv()

                    @pl.when(has_left)
                    def _():
                        along(s, me + d, -1).start()

                return carry

            lax.fori_loop(0, seqs, others, 0)

        def finish(n, carry):
            s = lax.rem(seq + n, seqs)

            @pl.when(n > 0)
            def _():
                for i in (0, 1, 2, 4):
                    arrived(s, i).wait_recv()

            for o in range(line):

                @pl.when(jnp.logical_and(has_right, me >= o))
                def _():
                    along(s, o, 1).wait_send()

                @pl.when(jnp.logical_and(has_left, me <= o))
                def _():
                    along(s, o, -1).wait_send()

            return carry

        lax.fori_loop(0, seqs, finish, 0)
        for i in (0, 1, 2, 4):
            stay(i).wait()

    for k in range(1, line):
        across(k).wait_send()
    for i in range(5):
        for k in range(1, peers):
            to_peer(k, i).wait_send()

        @pl.when(core != 0)
        def _():
            to_peer(0, i).wait_send()
    for i, (first, _, dst) in enumerate(pairs):
        side(i, first, dst).wait()
        side_keep(i, first, dst).wait()


def reduce_first(attn_part, whole, parts, extra, outs, grads):
    line, peers = lax.axis_size("tensor"), lax.axis_size("dp")
    width = parts.shape[1]
    seqs = 2 * peers
    dma = pltpu.SemaphoreType.DMA
    return pl.pallas_call(
        partial(reduce_kernel, line, peers, extra),
        in_specs=[vspec()] * 7,
        out_specs=[hspec()] * 3,
        out_shape=[
            jax.ShapeDtypeStruct((seqs, 14 * RANK, width), BF),
            jax.ShapeDtypeStruct((2,) + outs[0].shape, outs[0].dtype),
            jax.ShapeDtypeStruct((2,) + grads[0].shape, grads[0].dtype),
        ],
        scratch_shapes=[
            pltpu.VMEM((10 * RANK, width), BF),
            pltpu.VMEM((line, 10 * RANK, width // line), BF),
            pltpu.VMEM((10 * RANK, width // line), BF),
            dma((line,)),
            dma((line,)),
            dma((seqs, 5)),
            dma((peers, 5)),
            dma((5,)),
            dma((seqs, line)),
            dma((seqs, line)),
            dma((seqs, line)),
            dma((2,)),
            dma((2,)),
            dma((2,)),
        ],
        compiler_params=pltpu.CompilerParams(
            collective_id=6, has_side_effects=True, vmem_limit_bytes=VMEM_LIMIT
        ),
    )(attn_part, whole, parts, *outs, *grads)


def total_kernel(
    scale, hidden, q_cols,
    first, attn_in, whole_in, parts_in,
    input_ref, query_ref, kv_ref, expand_ref, attend_ref, shrink_ref, res_ref,
    block, ids, sem,
):
    r = RANK
    a = pl.program_id(0)
    core = lax.axis_index("section")
    width = block.shape[2]
    extra = hidden - width
    pad = extra + -hidden % (2 * LANES)

    @pl.when(jnp.logical_and(a == 0, core == 0))
    def _():
        load = pltpu.make_async_copy(first, block, sem.at[0])
        load.start()
        load.wait()

    @pl.when(jnp.logical_and(a == 0, core != 0))
    def _():
        def load(src, start, first, count, at):
            return pltpu.make_async_copy(src.at[:, rows_of(start, count)], block.at[:, rows_of(first, count)], sem.at[at])

        loads = [
            load(attn_in, 0, 0, 3, 1), load(whole_in, 0, 3, 2, 2), load(attn_in, 3, 5, 1, 3),
            load(whole_in, 2, 6, 1, 4), load(attn_in, 4, 7, 1, 5), load(parts_in, 0, 8, 6, 6),
        ]
        for one in loads:
            one.start()
        for one in loads:
            one.wait()
        mine = pl.ds(pl.multiple_of(lax.axis_index("tensor") * q_cols, LANES), q_cols)
        last = pltpu.make_async_copy(
            attn_in.at[:, rows_of(5, 2), mine], block.at[:, rows_of(11, 2), pl.ds(pad, q_cols)], sem.at[7]
        )
        last.start()
        last.wait()

    @pl.when(a == 0)
    def _():
        lane = lax.broadcasted_iota(jnp.int32, (1, LANES), 1).astype(F32)
        for i in range(block.shape[0]):
            names = block[i, 13 * r : 14 * r, pad : pad + LANES][:1].astype(F32)
            ids[i] = jnp.sum(lane * names).astype(jnp.int32)

    for ref in (input_ref, query_ref, kv_ref, expand_ref, attend_ref, shrink_ref, res_ref):
        ref[...] = jnp.zeros_like(ref)

    for i in range(block.shape[0]):

        @pl.when(ids[i] == a)
        def _():
            def part(row, rows, col, cols):
                return block[i, row : row + rows, col : col + cols].astype(F32) * scale

            input_ref[0] += part(0, 5 * r, 0, width)
            res_ref[0, 0] += part(5 * r, r, 0, width)
            res_ref[0, 1] += part(6 * r, r, 0, width)
            kv = part(7 * r, r, 0, 2 * kv_ref.shape[3])
            kv_ref[0, 0] += kv[:, : kv_ref.shape[3]]
            kv_ref[0, 1] += kv[:, kv_ref.shape[3] :]
            for j in range(2):
                expand_ref[0, j, :, :width] += part((8 + j) * r, r, 0, width)
                expand_ref[0, j, :, width:] += part((11 + j) * r, r, 0, pad)[:, :extra]
            shrink_ref[0, :, :width] += part(10 * r, r, 0, width)
            shrink_ref[0, :, width:] += part(13 * r, r, 0, pad)[:, :extra]
            query_ref[0] += part(11 * r, r, pad, q_cols)
            attend_ref[0] += part(12 * r, r, pad, q_cols)


def total_by_adapter(first, attn_in, whole_in, parts_in, count, scale, hidden, q_cols, kv_half):
    width = first.shape[2]
    r = RANK
    shapes = [
        (5 * r, width), (r, q_cols), (2, r, kv_half), (2, r, hidden), (r, q_cols), (r, hidden), (2, r, width),
    ]
    return pl.pallas_call(
        partial(total_kernel, scale, hidden, q_cols),
        grid=(count,),
        in_specs=[hspec()] * 4,
        out_specs=[pl.BlockSpec((1,) + s, lambda a, n=len(s): (a,) + (0,) * n) for s in shapes],
        out_shape=[jax.ShapeDtypeStruct((count,) + s, F32) for s in shapes],
        scratch_shapes=[
            pltpu.VMEM(first.shape, BF),
            pltpu.SMEM((first.shape[0],), jnp.int32),
            pltpu.SemaphoreType.DMA((8,)),
        ],
        compiler_params=pltpu.CompilerParams(vmem_limit_bytes=VMEM_LIMIT),
    )(first, attn_in, whole_in, parts_in)


def swap(pair):
    return lax.all_to_all(pair, "section", split_axis=0, concat_axis=0, tiled=True)


def local(
    inputs,
    lengths,
    adapter_ids,
    cotangent,
    norm_gain,
    query_weight,
    query_bias,
    keyvalue_weight,
    keyvalue_bias,
    output_weight,
    expand_weight,
    shrink_weight,
    adapter_input,
    adapter_query,
    adapter_keyvalue,
    adapter_expand,
    adapter_attend,
    adapter_shrink,
    adapter_residual,
):
    layers = lax.axis_size("section")
    tensor = lax.axis_size("tensor")
    core = lax.axis_index("section")
    place = lax.axis_index("tensor")
    rows, width = inputs.shape[1:]
    tokens = layers * rows * tensor * lax.axis_size("dp")
    kv_half = KV_HEADS * HEAD_DIM
    hidden = expand_weight.shape[3]
    r = RANK

    def turned(stack):
        return jnp.swapaxes(stack[0], 1, 2)

    def lined(stack):
        return stack[0].reshape(stack.shape[1], -1, stack.shape[-1])

    bundles, heads = pick_adapters(
        adapter_ids,
        (
            turned(adapter_input), lined(adapter_residual), lined(adapter_keyvalue), lined(adapter_expand),
            turned(adapter_shrink), adapter_query[0], turned(adapter_attend),
        ),
        (norm_gain[0], keyvalue_bias.reshape(1, -1), query_bias),
    )

    ff = jnp.concatenate(
        [m.reshape(layers, 1, hidden // layers, m.shape[1]) for m in (*turned(expand_weight), shrink_weight[0])],
        axis=1,
    )
    ff = swap(ff)
    kv = jnp.concatenate([keyvalue_weight[0, 0], keyvalue_weight[0, 1]], axis=1)
    kv_cols = kv.shape[1] // tensor
    kv = lax.dynamic_slice_in_dim(kv, place * kv_cols, kv_cols, 1)
    attn = jnp.concatenate([query_weight[0], output_weight[0].T, kv], axis=1)
    q_cols = query_weight.shape[2]
    attn = swap(attn.reshape(layers, attn.shape[0] // layers, attn.shape[1]))
    first_attn, line_attn, bundle = gather_first(attn, bundles, heads)

    def weights(layer):
        packed = first_attn if layer == 0 else lax.all_gather(line_attn, ("dp", "section"), axis=0)
        mlp = lax.all_gather(ff[layer], ("section", "dp"), axis=0)
        mlp = mlp.reshape(layers, -1, *mlp.shape[1:])
        if mlp.shape[4] % LANES:
            mlp = jnp.moveaxis(mlp, 1, 3)
            mlp = mlp.reshape(layers, 1, *mlp.shape[1:3], width)
        return dict(packed=packed, mlp=mlp, bundle=bundle[layer])

    x = lax.dynamic_index_in_dim(inputs, core, 0, keepdims=False)
    cot = lax.dynamic_index_in_dim(cotangent, core, 0, keepdims=False)
    length = lax.dynamic_index_in_dim(lengths, core, 0, keepdims=False)
    own_id = lax.dynamic_index_in_dim(adapter_ids, core, 0, keepdims=False)
    first_slot = place * rows
    info = jnp.stack([first_slot, length]).astype(jnp.int32)
    tables = rotary_tables(first_slot, rows)
    slot_ids = first_slot + jnp.arange(rows, dtype=jnp.int32)

    w = [weights(layer) for layer in range(layers)]
    outs, kept = [], []
    for layer in range(layers):
        middle, normed_two, attn_kept = attend_forward(x, w[layer], info, tables)
        shrunk, mlp_kept = mlp_forward(normed_two, w[layer])
        outs.append((middle + shrunk).astype(BF))
        kept.append((x, middle, attn_kept, mlp_kept))
        x = outs[-1]
    count = adapter_input.shape[1]
    extra = hidden + -hidden % (2 * LANES) - width
    names = jnp.broadcast_to((jnp.arange(LANES, dtype=jnp.int32) == own_id).astype(BF)[None], (r, LANES))

    def gather_all(*arrays):
        return [lax.all_gather(a, ("section", "dp"), axis=0) for a in arrays]

    grad = low_grad = jnp.where((slot_ids < length)[:, None], cot, jnp.zeros_like(cot))
    grads, gathered = [None] * layers, [None] * layers
    for layer in reversed(range(layers)):
        x, middle, attn_kept, mlp_kept = kept[layer]
        if layer < layers - 1:
            low_grad, here = lax.optimization_barrier((low_grad, here))
        dn2, whole, parts = mlp_backward(low_grad, w[layer], mlp_kept, names)
        if layer < layers - 1:
            total, dn2 = lax.optimization_barrier((total, dn2))
            gathered[layer + 1] = gather_all(*total, last_parts)
        grad, low_grad, attn_part = attend_backward(x, middle, grad, dn2, w[layer], attn_kept, info, tables)
        grads[layer] = grad
        here = (attn_part, whole)
        if layer > 0:
            total = lax.psum(here, "tensor")
            last_parts = parts
    gathered[0], layer_output, input_grad = reduce_first(*here, parts, extra, outs, grads)
    totals = total_by_adapter(
        gathered[0], *gathered[1], count, 1.0 / math.sqrt(tokens), hidden, q_cols, kv_half
    )
    turned = (0, 4, 5)
    totals = [jnp.swapaxes(total, 1, 2) if i in turned else total for i, total in enumerate(totals)]
    return (layer_output[None], input_grad[None]) + tuple(total[None] for total in totals)


def solution(mesh):
    placed = (
        P("dp", "tensor", None),
        P("dp"),
        P("dp"),
        P("dp", "tensor", None),
        P("section", None, None),
        P("section", "dp", "tensor"),
        P("section", "tensor"),
        P("section", None, "dp", None),
        P("section", None, None),
        P("section", "tensor", "dp"),
        P("section", None, "dp", "tensor"),
        P("section", "tensor", "dp"),
        P("section", None, None, None),
        P("section", None, None, "tensor"),
        P("section", None, None, None, None),
        P("section", None, None, None, "tensor"),
        P("section", None, "tensor", None),
        P("section", None, "tensor", None),
        P("section", None, None, None, None),
    )
    return jax.shard_map(
        local,
        mesh=mesh,
        in_specs=placed,
        out_specs=(
            P("section", "dp", "tensor", None),
            P("section", "dp", "tensor", None),
            P("section", None, None, None),
            P("section", None, None, "tensor"),
            P("section", None, None, None, None),
            P("section", None, None, None, "tensor"),
            P("section", None, "tensor", None),
            P("section", None, "tensor", None),
            P("section", None, None, None, None),
        ),
        check_vma=False,
    )
```

```python
from functools import partial
import math

import jax
import jax.numpy as jnp
from jax import lax
from jax.experimental import pallas as pl
from jax.experimental.pallas import tpu as pltpu
from jax.sharding import PartitionSpec as P

KV_HEADS = 2
HEAD_DIM = 128
RANK = 16
EPSILON = 1e-06
ROPE_BASE = 1000000.0
MASKED_SCORE = -1e30
CHUNKS = 8
LANES = 128
VMEM_LIMIT = 60 * 2**20
MESH = pl.DeviceIdType.MESH
BF = jnp.bfloat16
F32 = jnp.float32


def dot(a, b):
    return jnp.dot(a, b, preferred_element_type=F32)


def dot_t(a, b):
    return lax.dot_general(a, b, (((1,), (1,)), ((), ())), preferred_element_type=F32)


def t_dot(a, b):
    return lax.dot_general(a, b, (((0,), (0,)), ((), ())), preferred_element_type=F32)


def rotary_tables(first_slot, rows):
    half = HEAD_DIM // 2
    frequency = jnp.exp(-math.log(ROPE_BASE) * (2.0 * jnp.arange(half, dtype=F32) / HEAD_DIM))
    slots = (first_slot + jnp.arange(rows, dtype=jnp.int32)).astype(F32)
    angles = slots[:, None] * frequency[None, :]
    cos, sin = jnp.cos(angles), jnp.sin(angles)
    return jnp.concatenate([cos, cos], axis=1), jnp.concatenate([-sin, sin], axis=1)


B_INPUT, B_RES_ONE, B_RES_TWO, B_KV, B_MISC, B_FF, B_FF_TAIL, B_HEADS, B_ROWS = 0, 5, 6, 7, 8, 9, 12, 15, 18


def rows_of(first, count=1):
    return slice(first * RANK, (first + count) * RANK)


def pick_kernel(
    ids_ref, input_ref, res_ref, kv_ref, expand_ref, shrink_ref, query_ref, attend_ref, gain_ref, kvb_ref, qb_ref,
    out_ref, heads_ref,
):
    width = out_ref.shape[2]
    out_ref[0] = jnp.zeros(out_ref.shape[1:], BF)
    out_ref[0, rows_of(B_INPUT, 5)] = input_ref[0]
    out_ref[0, rows_of(B_RES_ONE, 2)] = res_ref[0]
    kv_half = kv_ref.shape[2]
    for i in range(2):
        out_ref[0, rows_of(B_KV), i * kv_half : (i + 1) * kv_half] = kv_ref[0, rows_of(i)]
    misc = rows_of(B_MISC).start
    out_ref[0, misc : misc + 2] = gain_ref[...]
    out_ref[0, misc + 2 : misc + 3, : 2 * kv_half] = kvb_ref[...]
    tail = expand_ref.shape[2] - width
    for i in range(3):
        part = expand_ref[0, rows_of(i)] if i < 2 else shrink_ref[0]
        out_ref[0, rows_of(B_FF + i)] = part[:, :width]
        out_ref[0, rows_of(B_FF_TAIL + i), :tail] = part[:, width:]
    heads_ref[0] = jnp.zeros(heads_ref.shape[1:], BF)
    heads_ref[0, rows_of(0)] = query_ref[0]
    heads_ref[0, rows_of(1)] = attend_ref[0]
    heads_ref[0, 2 * RANK : 2 * RANK + 1] = qb_ref[...]


def pick_adapters(ids, stacks, shared):
    count = ids.shape[0]
    width = stacks[0].shape[2]
    q_cols = stacks[5].shape[2]
    shapes = [(B_ROWS * RANK, width), (3 * RANK, q_cols)]
    return pl.pallas_call(
        pick_kernel,
        grid_spec=pltpu.PrefetchScalarGridSpec(
            num_scalar_prefetch=1,
            grid=(count,),
            in_specs=[pl.BlockSpec((1,) + a.shape[1:], lambda i, ids: (ids[i], 0, 0)) for a in stacks]
            + [pl.BlockSpec(a.shape, lambda i, ids: (0, 0)) for a in shared],
            out_specs=[pl.BlockSpec((1,) + a, lambda i, ids: (i, 0, 0)) for a in shapes],
        ),
        out_shape=[jax.ShapeDtypeStruct((count,) + a, BF) for a in shapes],
    )(ids, *stacks, *shared)


def spread_factors(bundle_ref, expand_ref, ash_ref):
    width = bundle_ref.shape[1]
    tail = ash_ref.shape[1] - width
    expand_ref[...] = jnp.zeros_like(expand_ref)
    for i in range(2):
        expand_ref[i, rows_of(i), :width] = bundle_ref[rows_of(B_FF + i)]
        expand_ref[i, rows_of(i), width:] = bundle_ref[rows_of(B_FF_TAIL + i), :tail]
    ash_ref[:, :width] = bundle_ref[rows_of(B_FF + 2)]
    ash_ref[:, width:] = bundle_ref[rows_of(B_FF_TAIL + 2), :tail]


def vspec():
    return pl.BlockSpec(memory_space=pltpu.VMEM)


def hspec():
    return pl.BlockSpec(memory_space=pl.ANY)


def line_barrier(me, line):
    barrier = pltpu.get_barrier_semaphore()

    @pl.when(me > 0)
    def _():
        pl.semaphore_signal(barrier, inc=1, device_id={"tensor": me - 1}, device_id_type=MESH)

    @pl.when(me < line - 1)
    def _():
        pl.semaphore_signal(barrier, inc=1, device_id={"tensor": me + 1}, device_id_type=MESH)

    pl.semaphore_wait(barrier, jnp.where(me > 0, 1, 0) + jnp.where(me < line - 1, 1, 0))


def within(c, chunks):
    return jnp.logical_and(c >= 0, c < chunks)


def line_exchange(line, chunks, gathered, partial_ref, from_left, from_right, own_out, sems, begin, work):
    ag_recv, ag_right, ag_left, r_recv, r_send, l_recv, l_send = sems
    me = lax.axis_index("tensor")

    def copy(ref, src, c, o, send, recv, side):
        return pltpu.make_async_remote_copy(
            src_ref=src.at[c, o],
            dst_ref=ref.at[c, o],
            send_sem=send.at[c, o],
            recv_sem=recv.at[c, o],
            device_id={"tensor": me + side},
            device_id_type=MESH,
        )

    def ag(c, o, side):
        return copy(gathered, gathered, c, o, ag_right if side > 0 else ag_left, ag_recv, side)

    def rs(c, o, side):
        if side > 0:
            return copy(from_left, partial_ref, c, o, r_send, r_recv, 1)
        return copy(from_right, partial_ref, c, o, l_send, l_recv, -1)

    has_left, has_right = me > 0, me < line - 1

    def step(s, carry):
        first = s + line - 1

        @pl.when(jnp.logical_and(within(first, chunks), has_right))
        def _():
            ag(first, me, 1).start()

        @pl.when(jnp.logical_and(within(first, chunks), has_left))
        def _():
            ag(first, me, -1).start()

        for d in range(1, line):
            c = s + line - 1 - d

            @pl.when(jnp.logical_and(within(c, chunks), me - d >= 0))
            def _():
                ag(c, me - d, 1).wait_recv()

                @pl.when(has_right)
                def _():
                    ag(c, me - d, 1).start()

            @pl.when(jnp.logical_and(within(c, chunks), me + d < line))
            def _():
                ag(c, me + d, -1).wait_recv()

                @pl.when(has_left)
                def _():
                    ag(c, me + d, -1).start()

        @pl.when(within(s, chunks))
        def _():
            work(s)

        for h in range(line):
            c = s - h

            @pl.when(jnp.logical_and(within(c, chunks), me == h))
            def _():
                for j in range(line - 1, h, -1):
                    if h > 0:
                        rs(c, j, 1).wait_recv()
                        partial_ref[c, j] = (
                            partial_ref[c, j].astype(F32) + from_left[c, j].astype(F32)
                        ).astype(BF)
                    if h < line - 1:
                        rs(c, j, 1).start()

            @pl.when(jnp.logical_and(within(c, chunks), me == line - 1 - h))
            def _():
                for j in range(line - 1 - h):
                    if h > 0:
                        rs(c, j, -1).wait_recv()
                        partial_ref[c, j] = (
                            partial_ref[c, j].astype(F32) + from_right[c, j].astype(F32)
                        ).astype(BF)
                    if h < line - 1:
                        rs(c, j, -1).start()

        last = s - (line - 1)

        @pl.when(within(last, chunks))
        def _():
            own_out[last] = partial_ref[last, me].astype(F32)

            @pl.when(has_left)
            def _():
                rs(last, me, 1).wait_recv()
                own_out[last] += from_left[last, me].astype(F32)

            @pl.when(has_right)
            def _():
                rs(last, me, -1).wait_recv()
                own_out[last] += from_right[last, me].astype(F32)

        return carry

    line_barrier(me, line)
    begin()
    lax.fori_loop(-(line - 1), chunks + line - 1, step, 0)

    def drain(c, carry):
        for o in range(line):

            @pl.when(jnp.logical_and(has_right, me >= o))
            def _():
                ag(c, o, 1).wait_send()

            @pl.when(jnp.logical_and(has_left, me <= o))
            def _():
                ag(c, o, -1).wait_send()

            @pl.when(me < o)
            def _():
                rs(c, o, 1).wait_send()

            @pl.when(me > o)
            def _():
                rs(c, o, -1).wait_send()

        return carry

    lax.fori_loop(0, chunks, drain, 0)


def exchange_scratch(line, chunks, rows, width):
    slots = (chunks, line, rows, width)
    return [pltpu.VMEM(slots, BF)] * 4 + [pltpu.SemaphoreType.DMA((chunks, line))] * 7


def ff_loads(packed, refs, wsem):
    halves, parts, _, rows, cols = packed.shape
    return [
        pltpu.make_async_copy(
            packed.at[h, p, i],
            ref.at[pl.ds(h * rows, rows), pl.ds(p * cols, cols)],
            wsem.at[i, h, p],
        )
        for i, ref in enumerate(refs)
        for h in range(halves)
        for p in range(parts)
    ]


def clear_tail(packed, refs):
    hidden = packed.shape[0] * packed.shape[3]
    for ref in refs:
        if ref.shape[0] > hidden:
            ref[hidden:] = jnp.zeros((ref.shape[0] - hidden, ref.shape[1]), BF)


def mlp_kernel(
    line, chunks, tile,
    n2_ref, packed, bundle_ref,
    out_ref, n2_out, gate_out, up_out,
    gathered, partial_ref, from_left, from_right, s0, s1, s2, s3, s4, s5, s6,
    wg, wu, ws, gate_st, up_st, acc, expand_ref, ash_ref, wsem, osem, nsem,
):
    rows, width = n2_ref.shape[1:]
    every = line * rows
    tiles = wg.shape[0] // tile
    high = bundle_ref[rows_of(B_INPUT + 3, 2)]
    res = bundle_ref[rows_of(B_RES_TWO)]
    me = lax.axis_index("tensor")
    loads = ff_loads(packed, (wg, wu, ws), wsem)

    def begin():
        for load in loads:
            load.start()
        clear_tail(packed, (wg, wu, ws))
        spread_factors(bundle_ref, expand_ref, ash_ref)
        for c in range(chunks):
            gathered[c, me] = n2_ref[c]

    def saves(c, slot):
        return (
            pltpu.make_async_copy(gate_st.at[slot], gate_out.at[c], osem.at[0, slot]),
            pltpu.make_async_copy(up_st.at[slot], up_out.at[c], osem.at[1, slot]),
        )

    def keep(c):
        return pltpu.make_async_copy(gathered.at[c], n2_out.at[c], nsem.at[c])

    def work(c):
        slot = c % 2

        @pl.when(c == 0)
        def _():
            for load in loads:
                load.wait()

        @pl.when(c >= 2)
        def _():
            for save in saves(c - 2, slot):
                save.wait()

        keep(c).start()
        x = gathered[c].reshape(every, width)
        er = dot_t(x, high).astype(BF)

        def one(f, rank):
            cols = pl.ds(pl.multiple_of(f * tile, tile), tile)
            gate = dot_t(x, wg[cols]) + dot(er, expand_ref[0, :, cols])
            up = dot_t(x, wu[cols]) + dot(er, expand_ref[1, :, cols])
            gate_st[slot, :, cols] = gate.astype(BF)
            up_st[slot, :, cols] = up.astype(BF)
            act = (gate * (1.0 / (1.0 + jnp.exp(-gate))) * up).astype(BF)
            now = dot(act, ws[cols])

            @pl.when(f == 0)
            def _():
                acc[...] = now

            @pl.when(f > 0)
            def _():
                acc[...] += now

            return rank + dot_t(act, ash_ref[:, cols])

        rank = lax.fori_loop(0, tiles, one, jnp.zeros((every, ash_ref.shape[0]), F32))
        total = acc[...] + dot(rank.astype(BF), res)
        partial_ref[c] = total.astype(BF).reshape(line, rows, width)
        for save in saves(c, slot):
            save.start()

    line_exchange(
        line, chunks, gathered, partial_ref, from_left, from_right, out_ref,
        (s0, s1, s2, s3, s4, s5, s6), begin, work,
    )
    for c in range(chunks):
        keep(c).wait()
    for c in range(max(chunks - 2, 0), chunks):
        for save in saves(c, c % 2):
            save.wait()


def ff_tile(hidden):
    return hidden


def mlp_forward(n2, w):
    line = lax.axis_size("tensor")
    rows, width = n2.shape
    halves, groups, _, low_rows, _ = w["mlp"].shape
    hidden = halves * low_rows + -(halves * low_rows) % (2 * LANES)
    part = rows // CHUNKS
    every = line * part
    out, n2_all, gate, up = pl.pallas_call(
        partial(mlp_kernel, line, CHUNKS, ff_tile(hidden)),
        in_specs=[vspec(), hspec(), vspec()],
        out_specs=[vspec()] + [hspec()] * 3,
        out_shape=[
            jax.ShapeDtypeStruct((CHUNKS, part, width), F32),
            jax.ShapeDtypeStruct((CHUNKS, line, part, width), BF),
            jax.ShapeDtypeStruct((CHUNKS, every, hidden), BF),
            jax.ShapeDtypeStruct((CHUNKS, every, hidden), BF),
        ],
        scratch_shapes=exchange_scratch(line, CHUNKS, part, width)
        + [pltpu.VMEM((hidden, width), BF)] * 3
        + [pltpu.VMEM((2, every, hidden), BF)] * 2
        + [
            pltpu.VMEM((every, width), F32),
            pltpu.VMEM((2, 2 * RANK, hidden), BF),
            pltpu.VMEM((RANK, hidden), BF),
            pltpu.SemaphoreType.DMA((3, halves, groups)),
            pltpu.SemaphoreType.DMA((2, 2)),
            pltpu.SemaphoreType.DMA((CHUNKS,)),
        ],
        compiler_params=pltpu.CompilerParams(
            collective_id=0, has_side_effects=True, vmem_limit_bytes=VMEM_LIMIT
        ),
        cost_estimate=pl.CostEstimate(
            flops=6 * line * rows * width * hidden,
            bytes_accessed=6 * width * hidden + 4 * line * rows * hidden,
            transcendentals=line * rows * hidden,
        ),
    )(
        n2.reshape(CHUNKS, part, width), w["mlp"], w["bundle"],
    )
    return out.reshape(rows, width), (n2_all.reshape(CHUNKS, every, width), gate, up)


def mlp_back_kernel(
    line, chunks, tile,
    ds_ref, packed, n2_hbm, gate_in, up_in, bundle_ref, names_ref,
    out_ref, whole_ref, parts_ref,
    gathered, partial_ref, from_left, from_right, s0, s1, s2, s3, s4, s5, s6,
    wg, wu, ws, gate_st, up_st, n2_st, acc, ghigh_ref, gexp_ref, gsh_ref, gres_ref, expand_ref, ash_ref, wsem, isem,
):
    rows, width = ds_ref.shape[1:]
    every = line * rows
    tiles = wg.shape[0] // tile
    high = bundle_ref[rows_of(B_INPUT + 3, 2)]
    res = bundle_ref[rows_of(B_RES_TWO)]
    me = lax.axis_index("tensor")
    loads = ff_loads(packed, (wg, wu, ws), wsem)

    def fetch(c):
        slot = c % 2
        return (
            pltpu.make_async_copy(gate_in.at[c], gate_st.at[slot], isem.at[0, slot]),
            pltpu.make_async_copy(up_in.at[c], up_st.at[slot], isem.at[1, slot]),
            pltpu.make_async_copy(n2_hbm.at[c], n2_st.at[slot], isem.at[2, slot]),
        )

    def begin():
        for load in loads:
            load.start()
        clear_tail(packed, (wg, wu, ws))
        spread_factors(bundle_ref, expand_ref, ash_ref)
        for one in fetch(0):
            one.start()
        for c in range(chunks):
            gathered[c, me] = ds_ref[c]
        for ref in (ghigh_ref, gexp_ref, gsh_ref, gres_ref):
            ref[...] = jnp.zeros_like(ref)

    def work(c):
        slot = c % 2

        @pl.when(c == 0)
        def _():
            for load in loads:
                load.wait()

        for one in fetch(c):
            one.wait()

        @pl.when(c + 1 < chunks)
        def _():
            for one in fetch(c + 1):
                one.start()

        ds = gathered[c].reshape(every, width)
        n2 = n2_st[slot]
        er = dot_t(n2, high).astype(BF)
        rank_in = dot_t(ds, res).astype(BF)

        def one(f, carry):
            rank_out, srank = carry
            cols = pl.ds(pl.multiple_of(f * tile, tile), tile)
            act_grad = dot_t(ds, ws[cols]) + dot(rank_in, ash_ref[:, cols])
            gate = gate_st[slot, :, cols].astype(F32)
            up = up_st[slot, :, cols].astype(F32)
            sig = 1.0 / (1.0 + jnp.exp(-gate))
            silu = gate * sig
            act = (silu * up).astype(BF)
            gate_grad = (act_grad * up * (sig + silu * (1.0 - sig))).astype(BF)
            up_grad = (act_grad * silu).astype(BF)
            now = dot(gate_grad, wg[cols]) + dot(up_grad, wu[cols])

            @pl.when(f == 0)
            def _():
                acc[...] = now

            @pl.when(f > 0)
            def _():
                acc[...] += now

            gexp_ref[0, :, cols] += t_dot(er, gate_grad)
            gexp_ref[1, :, cols] += t_dot(er, up_grad)
            gsh_ref[:, cols] += t_dot(rank_in, act)
            rank_out = rank_out + dot_t(gate_grad, expand_ref[0, :, cols])
            rank_out = rank_out + dot_t(up_grad, expand_ref[1, :, cols])
            return rank_out, srank + dot_t(act, ash_ref[:, cols])

        rank_out, srank = lax.fori_loop(
            0,
            tiles,
            one,
            (
                jnp.zeros((every, expand_ref.shape[1]), F32),
                jnp.zeros((every, ash_ref.shape[0]), F32),
            ),
        )
        rank_out = rank_out.astype(BF)
        total = acc[...] + dot(rank_out, high)
        partial_ref[c] = total.astype(BF).reshape(line, rows, width)
        ghigh_ref[...] += t_dot(rank_out, n2)
        gres_ref[...] += t_dot(srank.astype(BF), ds)

    line_exchange(
        line, chunks, gathered, partial_ref, from_left, from_right, out_ref,
        (s0, s1, s2, s3, s4, s5, s6), begin, work,
    )
    whole_ref[: 2 * RANK] = ghigh_ref[...].astype(BF)
    whole_ref[2 * RANK :] = gres_ref[...].astype(BF)
    extra = gsh_ref.shape[1] - width
    parts_ref[3 * RANK :, extra:] = jnp.zeros((3 * RANK, width - extra), BF)
    for i, part in enumerate((gexp_ref[0, :RANK], gexp_ref[1, RANK:], gsh_ref[...])):
        part = part.astype(BF)
        parts_ref[i * RANK : (i + 1) * RANK] = part[:, :width]
        parts_ref[(3 + i) * RANK : (4 + i) * RANK, :extra] = part[:, width:]
    parts_ref[rows_of(5), extra : extra + LANES] = names_ref[...]


def mlp_backward(ds, w, saved, names):
    n2_all, gate, up = saved
    line = lax.axis_size("tensor")
    rows, width = ds.shape
    halves, groups, _, low_rows, _ = w["mlp"].shape
    hidden = halves * low_rows + -(halves * low_rows) % (2 * LANES)
    part = rows // CHUNKS
    every = line * part
    out, whole, parts = pl.pallas_call(
        partial(mlp_back_kernel, line, CHUNKS, ff_tile(hidden)),
        in_specs=[vspec()] + [hspec()] * 4 + [vspec()] * 2,
        out_specs=[vspec()] * 3,
        out_shape=[
            jax.ShapeDtypeStruct((CHUNKS, part, width), F32),
            jax.ShapeDtypeStruct((3 * RANK, width), BF),
            jax.ShapeDtypeStruct((6 * RANK, width), BF),
        ],
        scratch_shapes=exchange_scratch(line, CHUNKS, part, width)
        + [pltpu.VMEM((hidden, width), BF)] * 3
        + [pltpu.VMEM((2, every, hidden), BF)] * 2
        + [
            pltpu.VMEM((2, every, width), BF),
            pltpu.VMEM((every, width), F32),
            pltpu.VMEM((2 * RANK, width), F32),
            pltpu.VMEM((2, 2 * RANK, hidden), F32),
            pltpu.VMEM((RANK, hidden), F32),
            pltpu.VMEM((RANK, width), F32),
            pltpu.VMEM((2, 2 * RANK, hidden), BF),
            pltpu.VMEM((RANK, hidden), BF),
            pltpu.SemaphoreType.DMA((3, halves, groups)),
            pltpu.SemaphoreType.DMA((3, 2)),
        ],
        compiler_params=pltpu.CompilerParams(
            collective_id=1, has_side_effects=True, vmem_limit_bytes=VMEM_LIMIT
        ),
        cost_estimate=pl.CostEstimate(
            flops=6 * line * rows * width * hidden,
            bytes_accessed=6 * width * hidden + 4 * line * rows * hidden,
            transcendentals=line * rows * hidden,
        ),
    )(
        ds.reshape(CHUNKS, part, width), w["mlp"], n2_all, gate, up, w["bundle"], names,
    )
    return out.reshape(rows, width), whole, parts


def halves_kernel(expand, shrink, first, second, stage, in_sem, keep_sem, send_sem, recv_sem):
    core = lax.axis_index("section")
    half = first.shape[1]
    barrier = pltpu.get_barrier_semaphore()
    pl.semaphore_signal(barrier, inc=1, device_id={"section": 1 - core}, device_id_type=MESH)
    for c in range(2):

        @pl.when(core == c)
        def _():
            own = (expand.at[:, pl.ds(c * half, half)], shrink.at[pl.ds(c * half, half)])
            for i, dst in enumerate((stage.at[pl.ds(0, 2)], stage.at[2])):
                pltpu.make_async_copy(own[i], dst, in_sem.at[i]).start()

    pl.semaphore_wait(barrier, 1)
    for c, out in enumerate((first, second)):

        @pl.when(core == c)
        def _():
            away = (expand.at[:, pl.ds((1 - c) * half, half)], shrink.at[pl.ds((1 - c) * half, half)])
            places = (out.at[pl.ds(0, 2)], out.at[2])
            sends = [
                pltpu.make_async_remote_copy(
                    src_ref=away[i],
                    dst_ref=places[i],
                    send_sem=send_sem.at[i],
                    recv_sem=recv_sem.at[i],
                    device_id={"section": 1 - c},
                    device_id_type=MESH,
                )
                for i in range(2)
            ]
            for send in sends:
                send.start()
            own = (expand.at[:, pl.ds(c * half, half)], shrink.at[pl.ds(c * half, half)])
            for i, dst in enumerate((stage.at[pl.ds(0, 2)], stage.at[2])):
                pltpu.make_async_copy(own[i], dst, in_sem.at[i]).wait()
            keep = pltpu.make_async_copy(stage, out, keep_sem)
            keep.start()
            keep.wait()
            for send in sends:
                send.wait()


def weight_halves(expand, shrink):
    _, hidden, cols = expand.shape
    shape = (3, hidden // 2, cols)
    dma = pltpu.SemaphoreType.DMA
    return pl.pallas_call(
        halves_kernel,
        in_specs=[hspec()] * 2,
        out_specs=[hspec()] * 2,
        out_shape=[jax.ShapeDtypeStruct(shape, BF)] * 2,
        scratch_shapes=[pltpu.VMEM(shape, BF), dma((2,)), dma, dma((2,)), dma((2,))],
        compiler_params=pltpu.CompilerParams(
            collective_id=7, has_side_effects=True, vmem_limit_bytes=VMEM_LIMIT
        ),
    )(expand, shrink)


def gather_kernel(
    line, peers,
    attn, bundles, heads,
    first_out, second_out, bundle_out,
    own_sem, z_recv, z_right, z_left, dp_recv, dp_send, core_recv, core_send, side_recv, side_send, side_own,
):
    me, spot, core = lax.axis_index("tensor"), lax.axis_index("dp"), lax.axis_index("section")
    other = 1 - core
    has_left, has_right = me > 0, me < line - 1
    barrier = pltpu.get_barrier_semaphore()

    def greet(**where):
        pl.semaphore_signal(barrier, inc=1, device_id=where, device_id_type=MESH)

    @pl.when(has_left)
    def _():
        greet(tensor=me - 1)

    @pl.when(has_right)
    def _():
        greet(tensor=me + 1)

    greet(section=other)
    square = peers == 4

    def partner(k):
        if square:
            return (None, spot + 1 - 2 * lax.rem(spot, 2), lax.rem(spot + 2, 4), 3 - spot)[k]
        return lax.rem(spot + k, peers)

    def origin(k):
        return partner(k) if square else lax.rem(spot + peers - k, peers)

    direct = (1, 2) if square else tuple(range(1, peers))
    for k in range(1, peers):
        greet(dp=partner(k))
    pl.semaphore_wait(barrier, jnp.where(has_left, 1, 0) + jnp.where(has_right, 1, 0) + peers)

    mine = spot * 2 + core
    plain, part = bundles.shape[1] - heads.shape[1], heads.shape[2]

    def head_place(layer, o):
        return bundle_out.at[layer, pl.ds(plain, heads.shape[1]), pl.ds(o * part, part)]

    def places(o):
        return first_out.at[mine, o], second_out.at[o], head_place(core, o), head_place(other, o)

    sides = [
        pltpu.make_async_remote_copy(
            src_ref=src,
            dst_ref=dst,
            send_sem=side_send.at[i],
            recv_sem=side_recv.at[i],
            device_id={"section": other},
            device_id_type=MESH,
        )
        for i, (src, dst) in enumerate(
            (
                (bundles.at[other, pl.ds(0, plain)], bundle_out.at[core, pl.ds(0, plain)]),
                (heads.at[other], head_place(core, me)),
            )
        )
    ]
    side_keep = pltpu.make_async_copy(
        bundles.at[core, pl.ds(0, plain)], bundle_out.at[core, pl.ds(0, plain)], side_own
    )
    sources = (attn.at[0], attn.at[1], heads.at[core], head_place(other, me))
    keeps = [
        pltpu.make_async_copy(src, dst, own_sem.at[i]) for i, (src, dst) in enumerate(zip(sources[:3], places(me)))
    ]

    def remote(src, dst, send, recv, **where):
        return pltpu.make_async_remote_copy(
            src_ref=src, dst_ref=dst, send_sem=send, recv_sem=recv, device_id=where, device_id_type=MESH
        )

    def along(i, o, side, own):
        dst = places(o)[i]
        return remote(
            sources[i] if own else dst,
            dst,
            (z_right if side > 0 else z_left).at[i, o],
            z_recv.at[i, o],
            tensor=me + side,
        )

    outs = (first_out,)

    def to_peer(lay, k, o, own):
        dst = outs[lay].at[mine, o]
        return remote(
            attn.at[lay] if own else dst, dst, dp_send.at[lay, k, o], dp_recv.at[lay, spot, o], dp=partner(k)
        )

    def from_peer(lay, k, o):
        p = origin(k)
        slot = outs[lay].at[p * 2 + core, o]
        to = partner(3 - k) if square and k < 3 else p
        return remote(slot, slot, dp_send.at[lay, peers - 1, o], dp_recv.at[lay, p, o], dp=to)

    def to_core(lay, p, o, own):
        dst = outs[lay].at[p * 2 + core, o]
        return remote(
            attn.at[lay] if own else dst, dst, core_send.at[lay, p, o], core_recv.at[lay, p, o], section=other
        )

    def spread(lay, o, own):
        for k in direct:
            to_peer(lay, k, o, own).start()
        to_core(lay, spot, o, own).start()

    for side in sides:
        side.start()
    for i in range(4):
        if i == 3:
            sides[1].wait_recv()

        @pl.when(has_right)
        def _():
            along(i, me, 1, True).start()

        @pl.when(has_left)
        def _():
            along(i, me, -1, True).start()

        if i == 0:
            spread(i, me, True)
    for keep in keeps:
        keep.start()
    side_keep.start()
    for d in range(1, line):
        for i in range(4):

            @pl.when(me >= d)
            def _():
                along(i, me - d, 1, False).wait_recv()

                @pl.when(has_right)
                def _():
                    along(i, me - d, 1, False).start()

                if i == 0:
                    spread(i, me - d, False)

            @pl.when(me + d < line)
            def _():
                along(i, me + d, -1, False).wait_recv()

                @pl.when(has_left)
                def _():
                    along(i, me + d, -1, False).start()

                if i == 0:
                    spread(i, me + d, False)

    half = line // 2

    def pass_on(n, carry):
        o = lax.rem(me + n, line)
        for lay in range(1):
            for k in direct:
                from_peer(lay, k, o).wait_recv()
                if square:

                    @pl.when(o < half if k == 1 else o >= half)
                    def _():
                        from_peer(lay, k, o).start()

                to_core(lay, origin(k), o, False).start()
        return carry

    lax.fori_loop(0, line, pass_on, 0)

    def pass_last(n, carry):
        o = lax.rem(me + n, line)
        for lay in range(1):
            from_peer(lay, 3, o).wait_recv()
            to_core(lay, origin(3), o, False).start()
        return carry

    if square:
        lax.fori_loop(0, line, pass_last, 0)

    def finish(o, carry):
        for lay in range(1):
            for k in direct:
                to_peer(lay, k, o, False).wait_send()
            if square:
                from_peer(lay, 1, o).wait_send()
            for p in range(peers):
                to_core(lay, p, o, False).wait_send()
                slot = outs[lay].at[p * 2 + other, o]
                remote(slot, slot, core_send.at[lay, p, o], core_recv.at[lay, p, o], section=other).wait_recv()
        for i in range(4):

            @pl.when(jnp.logical_and(has_right, me >= o))
            def _():
                along(i, o, 1, False).wait_send()

            @pl.when(jnp.logical_and(has_left, me <= o))
            def _():
                along(i, o, -1, False).wait_send()

        return carry

    lax.fori_loop(0, line, finish, 0)
    for keep in keeps:
        keep.wait()
    side_keep.wait()
    sides[0].wait_recv()
    for side in sides:
        side.wait_send()


def gather_first(attn, bundles, heads):
    line, peers = lax.axis_size("tensor"), lax.axis_size("dp")
    cores, part, cols = attn.shape
    dma = pltpu.SemaphoreType.DMA
    return pl.pallas_call(
        partial(gather_kernel, line, peers),
        in_specs=[vspec()] * 3,
        out_specs=[hspec()] * 3,
        out_shape=[
            jax.ShapeDtypeStruct((peers * cores, line, part, cols), BF),
            jax.ShapeDtypeStruct((line, part, cols), BF),
            jax.ShapeDtypeStruct(bundles.shape, BF),
        ],
        scratch_shapes=[dma((3,)), dma((4, line)), dma((4, line)), dma((4, line))]
        + [dma((1, peers, line))] * 4
        + [dma((2,)), dma((2,)), dma],
        compiler_params=pltpu.CompilerParams(
            collective_id=4, has_side_effects=True, vmem_limit_bytes=VMEM_LIMIT
        ),
    )(attn, bundles, heads)


def rotated(x, cos, sin):
    return x * cos + pltpu.roll(x, HEAD_DIM // 2, 1) * sin


def head_cols(h):
    return pl.ds(pl.multiple_of(h * HEAD_DIM, HEAD_DIM), HEAD_DIM)


def weight_loads(packed, wq, wo, wkv, wsem):
    cols, kv_cols = wq.shape[-1], wkv.shape[-1]
    loads = []
    for i, (ref, start, size) in enumerate(((wkv, 2 * cols, kv_cols), (wq, 0, cols), (wo, cols, cols))):
        loads.append(
            [
                pltpu.make_async_copy(packed.at[:, t, :, pl.ds(start, size)], ref.at[t], wsem.at[i, t])
                for t in range(ref.shape[0])
            ]
        )
    return loads


def flat(ref, t):
    groups, rows, cols = ref.shape[1:]
    return ref[t].reshape(groups * rows, cols)


def allowed_keys(info_ref, block, keys, rows):
    row = info_ref[0] + lax.broadcasted_iota(jnp.int32, (1, rows), 1)
    last = jnp.minimum(row, info_ref[1] - 1)
    return block * keys + lax.broadcasted_iota(jnp.int32, (keys, rows), 0) <= last


def one_way_barrier(me, line, side):
    barrier = pltpu.get_barrier_semaphore()
    first, last = (0, line - 1) if side > 0 else (line - 1, 0)

    @pl.when(me != first)
    def _():
        pl.semaphore_signal(barrier, inc=1, device_id={"tensor": me - side}, device_id_type=MESH)

    @pl.when(me != last)
    def _():
        pl.semaphore_wait(barrier, 1)


def spread_qkv(bundle_ref, bq_ref, bkv_ref):
    kv_half = bkv_ref.shape[1] // 2
    bq_ref[...] = jnp.zeros_like(bq_ref)
    bkv_ref[...] = jnp.zeros_like(bkv_ref)
    bq_ref[rows_of(0)] = bundle_ref[rows_of(B_HEADS)]
    for i in range(2):
        span = slice(i * kv_half, (i + 1) * kv_half)
        bkv_ref[rows_of(1 + i), span] = bundle_ref[rows_of(B_KV), span]


def kv_exchange(me, line, kvbuf, recv, send):
    def move(o):
        return pltpu.make_async_remote_copy(
            src_ref=kvbuf.at[o],
            dst_ref=kvbuf.at[o],
            send_sem=send.at[o],
            recv_sem=recv.at[o],
            device_id={"tensor": me + 1},
            device_id_type=MESH,
        )

    return move


def attend_kernel(
    line, group,
    info_ref, x_ref, bundle_ref, cos_ref, sin_ref, packed,
    mid_ref, n2_ref, normed_ref, lowr_ref, rank_ref, q_ref, kv_out, attended_ref, log_ref,
    wq, wo, wkv, kvbuf, acc, peak, total, bq_ref, bkv_ref, wsem, recv, send, ksem,
):
    rows, width = x_ref.shape
    heads = width // HEAD_DIM
    cols = wq.shape[-1]
    kv_cols = wkv.shape[-1]
    scale = HEAD_DIM**-0.5
    me = lax.axis_index("tensor")
    one_way_barrier(me, line, 1)
    kv_loads, q_loads, o_loads = weight_loads(packed, wq, wo, wkv, wsem)
    for load in kv_loads + q_loads + o_loads:
        load.start()
    move = kv_exchange(me, line, kvbuf, recv, send)
    spread_qkv(bundle_ref, bq_ref, bkv_ref)
    misc = bundle_ref[rows_of(B_MISC)].astype(F32)
    q_bias = bundle_ref[rows_of(B_HEADS + 2)].astype(F32)[:1]
    low_in = bundle_ref[rows_of(B_INPUT, 3)]
    x = x_ref[...].astype(F32)
    inverse = lax.rsqrt(jnp.mean(x * x, axis=-1, keepdims=True) + EPSILON)
    normed_ref[...] = (x * inverse * misc[0:1]).astype(BF)
    low = dot_t(normed_ref[...], low_in).astype(BF)
    cos, sin = cos_ref[...], sin_ref[...]
    for load in kv_loads:
        load.wait()
    for t in range(line):
        span = slice(t * kv_cols, (t + 1) * kv_cols)
        kv = dot(normed_ref[...], flat(wkv, t)) + misc[2:3, span] + dot(low, bkv_ref[:, span])
        for h in range(kv_cols // HEAD_DIM):
            at = t * kv_cols + h * HEAD_DIM
            one = kv[:, h * HEAD_DIM : (h + 1) * HEAD_DIM]
            if at < KV_HEADS * HEAD_DIM:
                one = rotated(one, cos, sin)
            kvbuf[me, :, at : at + HEAD_DIM] = one.astype(BF)

    @pl.when(me < line - 1)
    def _():
        move(me).start()

    for load in q_loads:
        load.wait()
    for t in range(line):
        span = slice(t * cols, (t + 1) * cols)
        q = dot(normed_ref[...], flat(wq, t)) + q_bias[:, span] + dot(low, bq_ref[:, span])
        for h in range(cols // HEAD_DIM):
            at = t * cols + h * HEAD_DIM
            q_ref[:, at : at + HEAD_DIM] = rotated(
                q[:, h * HEAD_DIM : (h + 1) * HEAD_DIM], cos, sin
            ).astype(BF)
    acc[...] = jnp.zeros_like(acc)
    total[...] = jnp.zeros_like(total)
    peak[...] = jnp.full_like(peak, MASKED_SCORE)

    def block(o):
        allowed = allowed_keys(info_ref, o, rows, rows)

        def one(h, carry):
            kv_head = h // group
            k = kvbuf[o, :, head_cols(kv_head)]
            v = kvbuf[o, :, head_cols(KV_HEADS + kv_head)]
            scores = jnp.where(allowed, dot_t(k, q_ref[:, head_cols(h)]) * scale, MASKED_SCORE)
            top = jnp.maximum(peak[h], jnp.max(scores, axis=0, keepdims=True))
            soft = jnp.exp(scores - top)
            shift = jnp.exp(peak[h] - top)
            total[h] = total[h] * shift + jnp.sum(soft, axis=0, keepdims=True)
            acc[h] = acc[h] * shift + t_dot(v, soft.astype(BF))
            peak[h] = top
            return carry

        lax.fori_loop(0, heads, one, 0, unroll=12)

    for d in range(line):

        @pl.when(me >= d)
        def _():
            if d > 0:
                move(me - d).wait_recv()

                @pl.when(me < line - 1)
                def _():
                    move(me - d).start()

            block(me - d)

    keep = pltpu.make_async_copy(kvbuf, kv_out, ksem)
    keep.start()
    for h in range(heads):
        attended_ref[:, h * HEAD_DIM : (h + 1) * HEAD_DIM] = (acc[h] * (1.0 / total[h])).T.astype(BF)
        log_ref[h] = peak[h] + jnp.log(total[h])
    rank = dot_t(attended_ref[...], bundle_ref[rows_of(B_HEADS + 1)]).astype(BF)
    lowr_ref[...] = low
    rank_ref[...] = rank
    middle = x_ref[...].astype(F32) + dot(rank, bundle_ref[rows_of(B_RES_ONE)])
    for load in o_loads:
        load.wait()
    for t in range(line):
        middle = middle + dot_t(attended_ref[:, t * cols : (t + 1) * cols], flat(wo, t))
    mid_ref[...] = middle
    inverse = lax.rsqrt(jnp.mean(middle * middle, axis=-1, keepdims=True) + EPSILON)
    n2_ref[...] = (middle * inverse * misc[1:2]).astype(BF)
    keep.wait()
    for o in range(line):

        @pl.when(jnp.logical_and(me < line - 1, me >= o))
        def _():
            move(o).wait_send()


def attend_forward(x, w, info, tables):
    line = lax.axis_size("tensor")
    rows, width = x.shape
    heads = width // HEAD_DIM
    kv_width = 2 * KV_HEADS * HEAD_DIM
    groups, low_rows = w["packed"].shape[0], w["packed"].shape[2]
    outs = pl.pallas_call(
        partial(attend_kernel, line, heads // KV_HEADS),
        in_specs=[pl.BlockSpec(memory_space=pltpu.SMEM)] + [vspec()] * 4 + [hspec()],
        out_specs=[vspec()] * 6 + [hspec()] + [vspec()] * 2,
        out_shape=[
            jax.ShapeDtypeStruct((rows, width), F32),
            jax.ShapeDtypeStruct((rows, width), BF),
            jax.ShapeDtypeStruct((rows, width), BF),
            jax.ShapeDtypeStruct((rows, 3 * RANK), BF),
            jax.ShapeDtypeStruct((rows, RANK), BF),
            jax.ShapeDtypeStruct((rows, width), BF),
            jax.ShapeDtypeStruct((line, rows, kv_width), BF),
            jax.ShapeDtypeStruct((rows, width), BF),
            jax.ShapeDtypeStruct((heads, 1, rows), F32),
        ],
        scratch_shapes=[
            pltpu.VMEM((line, groups, low_rows, width // line), BF),
            pltpu.VMEM((line, groups, low_rows, width // line), BF),
            pltpu.VMEM((line, groups, low_rows, kv_width // line), BF),
            pltpu.VMEM((line, rows, kv_width), BF),
            pltpu.VMEM((heads, HEAD_DIM, rows), F32),
            pltpu.VMEM((heads, 1, rows), F32),
            pltpu.VMEM((heads, 1, rows), F32),
            pltpu.VMEM((3 * RANK, width), BF),
            pltpu.VMEM((3 * RANK, kv_width), BF),
            pltpu.SemaphoreType.DMA((3, line)),
            pltpu.SemaphoreType.DMA((line,)),
            pltpu.SemaphoreType.DMA((line,)),
            pltpu.SemaphoreType.DMA,
        ],
        compiler_params=pltpu.CompilerParams(
            collective_id=2, has_side_effects=True, vmem_limit_bytes=VMEM_LIMIT
        ),
        cost_estimate=pl.CostEstimate(
            flops=4 * rows * width * width * 2, bytes_accessed=5 * width * width, transcendentals=0
        ),
    )(
        info, x, w["bundle"], tables[0], tables[1], w["packed"],
    )
    return outs[0], outs[1], outs[2:]


def attend_back_kernel(
    line, group,
    info_ref, x_ref, mid_ref, dy_ref, dn2_ref, bundle_ref, cos_ref, sin_ref,
    normed_ref, lowr_ref, rank_ref, q_ref, kv_ref, attended_ref, log_ref, packed,
    dx_ref, dx_low_ref, grads_ref,
    wq, wo, wkv, do_ref, dq_acc, dq_ref, dkv_acc, partial_ref, from_right, delta, bq_ref, bkv_ref, wsem, recv, send,
):
    rows, width = x_ref.shape
    heads = width // HEAD_DIM
    cols = wq.shape[-1]
    kv_cols = wkv.shape[-1]
    kv_half = KV_HEADS * HEAD_DIM
    scale = HEAD_DIM**-0.5
    me = lax.axis_index("tensor")
    one_way_barrier(me, line, -1)
    kv_loads, q_loads, o_loads = weight_loads(packed, wq, wo, wkv, wsem)
    for load in o_loads + q_loads + kv_loads:
        load.start()

    def move(o):
        return pltpu.make_async_remote_copy(
            src_ref=partial_ref.at[o],
            dst_ref=from_right.at[o],
            send_sem=send.at[o],
            recv_sem=recv.at[o],
            device_id={"tensor": me - 1},
            device_id_type=MESH,
        )

    def through_norm(values, gain, grad_out):
        inverse = lax.rsqrt(jnp.mean(values * values, axis=-1, keepdims=True) + EPSILON)
        weighted = gain * grad_out
        return inverse * weighted - inverse * inverse * inverse * values * jnp.mean(
            weighted * values, axis=-1, keepdims=True
        )

    spread_qkv(bundle_ref, bq_ref, bkv_ref)
    misc = bundle_ref[rows_of(B_MISC)].astype(F32)
    att = bundle_ref[rows_of(B_HEADS + 1)]
    middle_grad = dy_ref[...].astype(F32) + through_norm(mid_ref[...], misc[1:2], dn2_ref[...])
    dx_ref[...] = middle_grad
    branch_grad = middle_grad.astype(BF)
    low, rank = lowr_ref[...], rank_ref[...]
    rank_grad = dot_t(branch_grad, bundle_ref[rows_of(B_RES_ONE)]).astype(BF)
    grads_ref[3 * RANK : 4 * RANK] = t_dot(rank, branch_grad).astype(BF)
    grads_ref[6 * RANK :] = t_dot(rank_grad, attended_ref[...]).astype(BF)
    for load in o_loads:
        load.wait()
    for t in range(line):
        span = slice(t * cols, (t + 1) * cols)
        do_ref[:, span] = (dot(branch_grad, flat(wo, t)) + dot(rank_grad, att[:, span])).astype(BF)
    for h in range(heads):
        span = slice(h * HEAD_DIM, (h + 1) * HEAD_DIM)
        both = do_ref[:, span].astype(F32) * attended_ref[:, span].astype(F32)
        delta[h] = jnp.sum(both.T, axis=0, keepdims=True)
    dq_acc[...] = jnp.zeros_like(dq_acc)

    def block(o):
        allowed = allowed_keys(info_ref, o, rows, rows)
        dkv_acc[...] = jnp.zeros_like(dkv_acc)

        def one(h, carry):
            kv_head = h // group
            k = kv_ref[o, :, head_cols(kv_head)]
            v = kv_ref[o, :, head_cols(KV_HEADS + kv_head)]
            q = q_ref[:, head_cols(h)]
            do = do_ref[:, head_cols(h)]
            scores = dot_t(k, q) * scale - log_ref[h]
            soft = jnp.exp(jnp.where(allowed, scores, MASKED_SCORE))
            grad = (soft * (dot_t(v, do) - delta[h])).astype(BF)
            dq_acc[h] += t_dot(k, grad)
            dkv_acc[:, head_cols(kv_head)] += dot(grad, q) * scale
            dkv_acc[:, head_cols(KV_HEADS + kv_head)] += dot(soft.astype(BF), do)
            return carry

        lax.fori_loop(0, heads, one, 0, unroll=12)
        partial_ref[o] = dkv_acc[...].astype(BF)

    for s in range(2 * line - 1):
        if s < line:

            @pl.when(me >= s)
            def _():
                block(s)

        for h in range(line - 1):
            o = s - h
            if 0 <= o < line - 1 - h:

                @pl.when(me == line - 1 - h)
                def _():
                    if h > 0:
                        move(o).wait_recv()
                        partial_ref[o] = (partial_ref[o].astype(F32) + from_right[o].astype(F32)).astype(BF)
                    move(o).start()

    cos, sin = cos_ref[...], -sin_ref[...]
    for h in range(heads):
        dq_ref[:, h * HEAD_DIM : (h + 1) * HEAD_DIM] = rotated(dq_acc[h].T * scale, cos, sin).astype(BF)
    dq = dq_ref[...]
    grads_ref[5 * RANK : 6 * RANK] = t_dot(low, dq)[:RANK].astype(BF)
    low_grad = dot_t(dq, bq_ref[...])
    for load in q_loads:
        load.wait()
    normed_grad = dot_t(dq[:, :cols], flat(wq, 0))
    for t in range(1, line):
        normed_grad = normed_grad + dot_t(dq[:, t * cols : (t + 1) * cols], flat(wq, t))
    dkv_acc[...] = partial_ref[me].astype(F32)

    @pl.when(me < line - 1)
    def _():
        move(me).wait_recv()
        dkv_acc[...] += from_right[me].astype(F32)

    for h in range(KV_HEADS):
        span = slice(h * HEAD_DIM, (h + 1) * HEAD_DIM)
        dkv_acc[:, span] = rotated(dkv_acc[:, span], cos, sin)
    dkv = dkv_acc[...].astype(BF)
    kv_grad = t_dot(low, dkv).astype(BF)
    grads_ref[4 * RANK : 5 * RANK, :kv_half] = kv_grad[RANK : 2 * RANK, :kv_half]
    grads_ref[4 * RANK : 5 * RANK, kv_half : 2 * kv_half] = kv_grad[2 * RANK :, kv_half:]
    grads_ref[4 * RANK : 5 * RANK, 2 * kv_half :] = jnp.zeros((RANK, width - 2 * kv_half), BF)
    low_grad = (low_grad + dot_t(dkv, bkv_ref[...])).astype(BF)
    grads_ref[: 3 * RANK] = t_dot(low_grad, normed_ref[...]).astype(BF)
    for load in kv_loads:
        load.wait()
    for t in range(line):
        normed_grad = normed_grad + dot_t(dkv[:, t * kv_cols : (t + 1) * kv_cols], flat(wkv, t))
    normed_grad = normed_grad + dot(low_grad, bundle_ref[rows_of(B_INPUT, 3)])
    dx = dx_ref[...] + through_norm(x_ref[...].astype(F32), misc[0:1], normed_grad)
    dx_ref[...] = dx
    dx_low_ref[...] = dx.astype(BF)
    for o in range(line - 1):

        @pl.when(me > o)
        def _():
            move(o).wait_send()


def attend_backward(x, middle, dy, dn2, w, kept, info, tables):
    line = lax.axis_size("tensor")
    rows, width = x.shape
    heads = width // HEAD_DIM
    kv_width = 2 * KV_HEADS * HEAD_DIM
    groups, low_rows = w["packed"].shape[0], w["packed"].shape[2]
    return pl.pallas_call(
        partial(attend_back_kernel, line, heads // KV_HEADS),
        in_specs=[pl.BlockSpec(memory_space=pltpu.SMEM)] + [vspec()] * 14 + [hspec()],
        out_specs=[vspec()] * 3,
        out_shape=[
            jax.ShapeDtypeStruct((rows, width), F32),
            jax.ShapeDtypeStruct((rows, width), BF),
            jax.ShapeDtypeStruct((7 * RANK, width), BF),
        ],
        scratch_shapes=[
            pltpu.VMEM((line, groups, low_rows, width // line), BF),
            pltpu.VMEM((line, groups, low_rows, width // line), BF),
            pltpu.VMEM((line, groups, low_rows, kv_width // line), BF),
            pltpu.VMEM((rows, width), BF),
            pltpu.VMEM((heads, HEAD_DIM, rows), F32),
            pltpu.VMEM((rows, width), BF),
            pltpu.VMEM((rows, kv_width), F32),
            pltpu.VMEM((line, rows, kv_width), BF),
            pltpu.VMEM((line, rows, kv_width), BF),
            pltpu.VMEM((heads, 1, rows), F32),
            pltpu.VMEM((3 * RANK, width), BF),
            pltpu.VMEM((3 * RANK, kv_width), BF),
            pltpu.SemaphoreType.DMA((3, line)),
            pltpu.SemaphoreType.DMA((line,)),
            pltpu.SemaphoreType.DMA((line,)),
        ],
        compiler_params=pltpu.CompilerParams(
            collective_id=3 if dy.dtype == F32 else 5, has_side_effects=True, vmem_limit_bytes=VMEM_LIMIT
        ),
        cost_estimate=pl.CostEstimate(
            flops=4 * rows * width * width * 2, bytes_accessed=5 * width * width, transcendentals=0
        ),
    )(
        info, x, middle, dy, dn2, w["bundle"], tables[0], tables[1], *kept, w["packed"],
    )


def reduce_kernel(
    line, peers, extra,
    attn_ref, whole_ref, parts_ref, y_first, y_second, g_first, g_second,
    out, y_out, g_out,
    mine, z_in, quarter, z_recv, z_send, dp_recv, dp_send, own_sem, t_recv, t_right, t_left,
    side_recv, side_send, side_own,
):
    r = RANK
    me, spot, core = lax.axis_index("tensor"), lax.axis_index("dp"), lax.axis_index("section")
    width = mine.shape[1]
    cols = width // line
    seqs = out.shape[0]
    seq = spot * 2 + core
    has_left, has_right = me > 0, me < line - 1
    barrier = pltpu.get_barrier_semaphore()

    def greet(**where):
        pl.semaphore_signal(barrier, inc=1, device_id=where, device_id_type=MESH)

    for k in range(1, line):
        greet(tensor=lax.rem(me + k, line))

    greet(section=1 - core)

    @pl.when(core == 0)
    def _():
        for k in range(1, peers):
            for c in range(2):
                greet(section=c, dp=lax.rem(spot + k, peers))

    pl.semaphore_wait(barrier, line - 1 + peers)

    def remote(src, dst, send, recv, **where):
        return pltpu.make_async_remote_copy(
            src_ref=src, dst_ref=dst, send_sem=send, recv_sem=recv, device_id=where, device_id_type=MESH
        )

    def lanes(t):
        return pl.ds(pl.multiple_of(t * cols, LANES), cols)

    def pieces(s):
        return (
            (parts_ref.at[pl.ds(0, 3 * r)], out.at[s, pl.ds(8 * r, 3 * r)]),
            (parts_ref.at[pl.ds(3 * r, 3 * r), pl.ds(0, extra)], out.at[s, pl.ds(11 * r, 3 * r), pl.ds(0, extra)]),
            (
                parts_ref.at[pl.ds(5 * r, r), pl.ds(extra, LANES)],
                out.at[s, pl.ds(13 * r, r), pl.ds(extra, LANES)],
            ),
            (quarter.at[pl.ds(0, 8 * r)], out.at[s, pl.ds(0, 8 * r), lanes(me)]),
            (quarter.at[pl.ds(8 * r, 2 * r)], out.at[s, pl.ds(11 * r, 2 * r), pl.ds(extra, cols)]),
        )

    def to_peer(k, i):
        src, dst = pieces(seq)[i]
        return remote(src, dst, dp_send.at[k, i], dp_recv.at[seq, i], section=0, dp=lax.rem(spot + k, peers))

    def stay(i):
        src, dst = pieces(seq)[i]
        return pltpu.make_async_copy(src, dst, own_sem.at[i])

    def send_pieces(which):
        for i in which:
            for k in range(1, peers):
                to_peer(k, i).start()

            @pl.when(core != 0)
            def _():
                to_peer(0, i).start()

            @pl.when(core == 0)
            def _():
                stay(i).start()

    def across(k):
        to = lax.rem(me + k, line)
        return remote(mine.at[:, lanes(to)], z_in.at[me], z_send.at[k], z_recv.at[me], tensor=to)

    def incoming(k):
        o = lax.rem(me + k, line)
        return remote(mine.at[:, lanes(me)], z_in.at[o], z_send.at[k], z_recv.at[o], tensor=o)

    def side(i, src, dst):
        return remote(src, dst.at[core], side_send.at[i], side_recv.at[i], section=1 - core)

    def side_keep(i, src, dst):
        return pltpu.make_async_copy(src, dst.at[core], side_own.at[i])

    pairs = ((y_first, y_second, y_out), (g_first, g_second, g_out))

    for first, rows, ref, start in (
        (0, 3, attn_ref, 0), (3, 2, whole_ref, 0), (5, 1, attn_ref, 3), (6, 1, whole_ref, 2), (7, 3, attn_ref, 4),
    ):
        mine[rows_of(first, rows)] = ref[rows_of(start, rows)]
    for k in range(1, line):
        across(k).start()
    send_pieces((0, 1, 2))
    for c in range(2):

        @pl.when(core == c)
        def _():
            for i, (first, second, dst) in enumerate(pairs):
                side(i, first if c == 1 else second, dst).start()
                side_keep(i, second if c == 1 else first, dst).start()

    total = mine[:, lanes(me)].astype(F32)
    for k in range(1, line):
        incoming(k).wait_recv()
        total = total + z_in[lax.rem(me + k, line)].astype(F32)
    quarter[...] = total.astype(BF)
    send_pieces((3, 4))

    def arrived(s, i):
        src, dst = pieces(s)[i]
        return remote(src, dst, dp_send.at[0, i], dp_recv.at[s, i], section=0)

    def along(s, o, side):
        place = out.at[s, pl.ds(0, 8 * r), lanes(o)]
        return remote(
            place, place, (t_right if side > 0 else t_left).at[s, o], t_recv.at[s, o], tensor=me + side
        )

    @pl.when(core == 0)
    def _():
        def own_rows(n, carry):
            s = lax.rem(seq + n, seqs)

            @pl.when(n == 0)
            def _():
                stay(3).wait()

            @pl.when(n > 0)
            def _():
                arrived(s, 3).wait_recv()

            @pl.when(has_right)
            def _():
                along(s, me, 1).start()

            @pl.when(has_left)
            def _():
                along(s, me, -1).start()

            return carry

        lax.fori_loop(0, seqs, own_rows, 0)
        for d in range(1, line):

            def others(n, carry):
                s = lax.rem(seq + n, seqs)

                @pl.when(me >= d)
                def _():
                    along(s, me - d, 1).wait_recv()

                    @pl.when(has_right)
                    def _():
                        along(s, me - d, 1).start()

                @pl.when(me + d < line)
                def _():
                    along(s, me + d, -1).wait_recv()

                    @pl.when(has_left)
                    def _():
                        along(s, me + d, -1).start()

                return carry

            lax.fori_loop(0, seqs, others, 0)

        def finish(n, carry):
            s = lax.rem(seq + n, seqs)

            @pl.when(n > 0)
            def _():
                for i in (0, 1, 2, 4):
                    arrived(s, i).wait_recv()

            for o in range(line):

                @pl.when(jnp.logical_and(has_right, me >= o))
                def _():
                    along(s, o, 1).wait_send()

                @pl.when(jnp.logical_and(has_left, me <= o))
                def _():
                    along(s, o, -1).wait_send()

            return carry

        lax.fori_loop(0, seqs, finish, 0)
        for i in (0, 1, 2, 4):
            stay(i).wait()

    for k in range(1, line):
        across(k).wait_send()
    for i in range(5):
        for k in range(1, peers):
            to_peer(k, i).wait_send()

        @pl.when(core != 0)
        def _():
            to_peer(0, i).wait_send()
    for i, (first, _, dst) in enumerate(pairs):
        side(i, first, dst).wait()
        side_keep(i, first, dst).wait()


def reduce_first(attn_part, whole, parts, extra, outs, grads):
    line, peers = lax.axis_size("tensor"), lax.axis_size("dp")
    width = parts.shape[1]
    seqs = 2 * peers
    dma = pltpu.SemaphoreType.DMA
    return pl.pallas_call(
        partial(reduce_kernel, line, peers, extra),
        in_specs=[vspec()] * 7,
        out_specs=[hspec()] * 3,
        out_shape=[
            jax.ShapeDtypeStruct((seqs, 14 * RANK, width), BF),
            jax.ShapeDtypeStruct((2,) + outs[0].shape, outs[0].dtype),
            jax.ShapeDtypeStruct((2,) + grads[0].shape, grads[0].dtype),
        ],
        scratch_shapes=[
            pltpu.VMEM((10 * RANK, width), BF),
            pltpu.VMEM((line, 10 * RANK, width // line), BF),
            pltpu.VMEM((10 * RANK, width // line), BF),
            dma((line,)),
            dma((line,)),
            dma((seqs, 5)),
            dma((peers, 5)),
            dma((5,)),
            dma((seqs, line)),
            dma((seqs, line)),
            dma((seqs, line)),
            dma((2,)),
            dma((2,)),
            dma((2,)),
        ],
        compiler_params=pltpu.CompilerParams(
            collective_id=6, has_side_effects=True, vmem_limit_bytes=VMEM_LIMIT
        ),
    )(attn_part, whole, parts, *outs, *grads)


def total_kernel(
    scale, hidden, q_cols,
    first, attn_in, whole_in, parts_in,
    input_ref, query_ref, kv_ref, expand_ref, attend_ref, shrink_ref, res_ref,
    block, ids, sem,
):
    r = RANK
    a = pl.program_id(0)
    core = lax.axis_index("section")
    width = block.shape[2]
    extra = hidden - width
    pad = extra + -hidden % (2 * LANES)

    @pl.when(jnp.logical_and(a == 0, core == 0))
    def _():
        load = pltpu.make_async_copy(first, block, sem.at[0])
        load.start()
        load.wait()

    @pl.when(jnp.logical_and(a == 0, core != 0))
    def _():
        def load(src, start, first, count, at):
            return pltpu.make_async_copy(src.at[:, rows_of(start, count)], block.at[:, rows_of(first, count)], sem.at[at])

        loads = [
            load(attn_in, 0, 0, 3, 1), load(whole_in, 0, 3, 2, 2), load(attn_in, 3, 5, 1, 3),
            load(whole_in, 2, 6, 1, 4), load(attn_in, 4, 7, 1, 5), load(parts_in, 0, 8, 6, 6),
        ]
        for one in loads:
            one.start()
        for one in loads:
            one.wait()
        mine = pl.ds(pl.multiple_of(lax.axis_index("tensor") * q_cols, LANES), q_cols)
        last = pltpu.make_async_copy(
            attn_in.at[:, rows_of(5, 2), mine], block.at[:, rows_of(11, 2), pl.ds(pad, q_cols)], sem.at[7]
        )
        last.start()
        last.wait()

    @pl.when(a == 0)
    def _():
        lane = lax.broadcasted_iota(jnp.int32, (1, LANES), 1).astype(F32)
        for i in range(block.shape[0]):
            names = block[i, 13 * r : 14 * r, pad : pad + LANES][:1].astype(F32)
            ids[i] = jnp.sum(lane * names).astype(jnp.int32)

    for ref in (input_ref, query_ref, kv_ref, expand_ref, attend_ref, shrink_ref, res_ref):
        ref[...] = jnp.zeros_like(ref)

    for i in range(block.shape[0]):

        @pl.when(ids[i] == a)
        def _():
            def part(row, rows, col, cols):
                return block[i, row : row + rows, col : col + cols].astype(F32) * scale

            input_ref[0] += part(0, 5 * r, 0, width)
            res_ref[0, 0] += part(5 * r, r, 0, width)
            res_ref[0, 1] += part(6 * r, r, 0, width)
            kv = part(7 * r, r, 0, 2 * kv_ref.shape[3])
            kv_ref[0, 0] += kv[:, : kv_ref.shape[3]]
            kv_ref[0, 1] += kv[:, kv_ref.shape[3] :]
            for j in range(2):
                expand_ref[0, j, :, :width] += part((8 + j) * r, r, 0, width)
                expand_ref[0, j, :, width:] += part((11 + j) * r, r, 0, pad)[:, :extra]
            shrink_ref[0, :, :width] += part(10 * r, r, 0, width)
            shrink_ref[0, :, width:] += part(13 * r, r, 0, pad)[:, :extra]
            query_ref[0] += part(11 * r, r, pad, q_cols)
            attend_ref[0] += part(12 * r, r, pad, q_cols)


def total_by_adapter(first, attn_in, whole_in, parts_in, count, scale, hidden, q_cols, kv_half):
    width = first.shape[2]
    r = RANK
    shapes = [
        (5 * r, width), (r, q_cols), (2, r, kv_half), (2, r, hidden), (r, q_cols), (r, hidden), (2, r, width),
    ]
    return pl.pallas_call(
        partial(total_kernel, scale, hidden, q_cols),
        grid=(count,),
        in_specs=[hspec()] * 4,
        out_specs=[pl.BlockSpec((1,) + s, lambda a, n=len(s): (a,) + (0,) * n) for s in shapes],
        out_shape=[jax.ShapeDtypeStruct((count,) + s, F32) for s in shapes],
        scratch_shapes=[
            pltpu.VMEM(first.shape, BF),
            pltpu.SMEM((first.shape[0],), jnp.int32),
            pltpu.SemaphoreType.DMA((8,)),
        ],
        compiler_params=pltpu.CompilerParams(vmem_limit_bytes=VMEM_LIMIT),
    )(first, attn_in, whole_in, parts_in)


def swap(pair):
    return lax.all_to_all(pair, "section", split_axis=0, concat_axis=0, tiled=True)


def local(
    inputs,
    lengths,
    adapter_ids,
    cotangent,
    norm_gain,
    query_weight,
    query_bias,
    keyvalue_weight,
    keyvalue_bias,
    output_weight,
    expand_weight,
    shrink_weight,
    adapter_input,
    adapter_query,
    adapter_keyvalue,
    adapter_expand,
    adapter_attend,
    adapter_shrink,
    adapter_residual,
):
    layers = lax.axis_size("section")
    tensor = lax.axis_size("tensor")
    core = lax.axis_index("section")
    place = lax.axis_index("tensor")
    rows, width = inputs.shape[1:]
    tokens = layers * rows * tensor * lax.axis_size("dp")
    kv_half = KV_HEADS * HEAD_DIM
    hidden = expand_weight.shape[3]
    r = RANK

    def turned(stack):
        return jnp.swapaxes(stack[0], 1, 2)

    def lined(stack):
        return stack[0].reshape(stack.shape[1], -1, stack.shape[-1])

    bundles, heads = pick_adapters(
        adapter_ids,
        (
            turned(adapter_input), lined(adapter_residual), lined(adapter_keyvalue), lined(adapter_expand),
            turned(adapter_shrink), adapter_query[0], turned(adapter_attend),
        ),
        (norm_gain[0], keyvalue_bias.reshape(1, -1), query_bias),
    )

    ff = weight_halves(turned(expand_weight), shrink_weight[0])
    kv = jnp.concatenate([keyvalue_weight[0, 0], keyvalue_weight[0, 1]], axis=1)
    kv_cols = kv.shape[1] // tensor
    kv = lax.dynamic_slice_in_dim(kv, place * kv_cols, kv_cols, 1)
    attn = jnp.concatenate([query_weight[0], output_weight[0].T, kv], axis=1)
    q_cols = query_weight.shape[2]
    attn = swap(attn.reshape(layers, attn.shape[0] // layers, attn.shape[1]))
    first_attn, line_attn, bundle = gather_first(attn, bundles, heads)

    def weights(layer):
        packed = first_attn if layer == 0 else lax.all_gather(line_attn, ("dp", "section"), axis=0)
        mlp = lax.all_gather(ff[layer], ("section", "dp"), axis=0)
        mlp = mlp.reshape(layers, -1, *mlp.shape[1:])
        if mlp.shape[4] % LANES:
            mlp = jnp.moveaxis(mlp, 1, 3)
            mlp = mlp.reshape(layers, 1, *mlp.shape[1:3], width)
        return dict(packed=packed, mlp=mlp, bundle=bundle[layer])

    x = lax.dynamic_index_in_dim(inputs, core, 0, keepdims=False)
    cot = lax.dynamic_index_in_dim(cotangent, core, 0, keepdims=False)
    length = lax.dynamic_index_in_dim(lengths, core, 0, keepdims=False)
    own_id = lax.dynamic_index_in_dim(adapter_ids, core, 0, keepdims=False)
    first_slot = place * rows
    info = jnp.stack([first_slot, length]).astype(jnp.int32)
    tables = rotary_tables(first_slot, rows)
    slot_ids = first_slot + jnp.arange(rows, dtype=jnp.int32)

    w = [weights(layer) for layer in range(layers)]
    outs, kept = [], []
    for layer in range(layers):
        middle, normed_two, attn_kept = attend_forward(x, w[layer], info, tables)
        shrunk, mlp_kept = mlp_forward(normed_two, w[layer])
        outs.append((middle + shrunk).astype(BF))
        kept.append((x, middle, attn_kept, mlp_kept))
        x = outs[-1]
    count = adapter_input.shape[1]
    extra = hidden + -hidden % (2 * LANES) - width
    names = jnp.broadcast_to((jnp.arange(LANES, dtype=jnp.int32) == own_id).astype(BF)[None], (r, LANES))

    def gather_all(*arrays):
        return [lax.all_gather(a, ("section", "dp"), axis=0) for a in arrays]

    grad = low_grad = jnp.where((slot_ids < length)[:, None], cot, jnp.zeros_like(cot))
    grads, gathered = [None] * layers, [None] * layers
    for layer in reversed(range(layers)):
        x, middle, attn_kept, mlp_kept = kept[layer]
        if layer < layers - 1:
            low_grad, here = lax.optimization_barrier((low_grad, here))
        dn2, whole, parts = mlp_backward(low_grad, w[layer], mlp_kept, names)
        if layer < layers - 1:
            total, dn2 = lax.optimization_barrier((total, dn2))
            gathered[layer + 1] = gather_all(*total, last_parts)
        grad, low_grad, attn_part = attend_backward(x, middle, grad, dn2, w[layer], attn_kept, info, tables)
        grads[layer] = grad
        here = (attn_part, whole)
        if layer > 0:
            total = lax.psum(here, "tensor")
            last_parts = parts
    gathered[0], layer_output, input_grad = reduce_first(*here, parts, extra, outs, grads)
    totals = total_by_adapter(
        gathered[0], *gathered[1], count, 1.0 / math.sqrt(tokens), hidden, q_cols, kv_half
    )
    turned = (0, 4, 5)
    totals = [jnp.swapaxes(total, 1, 2) if i in turned else total for i, total in enumerate(totals)]
    return (layer_output[None], input_grad[None]) + tuple(total[None] for total in totals)


def solution(mesh):
    placed = (
        P("dp", "tensor", None),
        P("dp"),
        P("dp"),
        P("dp", "tensor", None),
        P("section", None, None),
        P("section", "dp", "tensor"),
        P("section", "tensor"),
        P("section", None, "dp", None),
        P("section", None, None),
        P("section", "tensor", "dp"),
        P("section", None, "dp", "tensor"),
        P("section", "tensor", "dp"),
        P("section", None, None, None),
        P("section", None, None, "tensor"),
        P("section", None, None, None, None),
        P("section", None, None, None, "tensor"),
        P("section", None, "tensor", None),
        P("section", None, "tensor", None),
        P("section", None, None, None, None),
    )
    return jax.shard_map(
        local,
        mesh=mesh,
        in_specs=placed,
        out_specs=(
            P("section", "dp", "tensor", None),
            P("section", "dp", "tensor", None),
            P("section", None, None, None),
            P("section", None, None, "tensor"),
            P("section", None, None, None, None),
            P("section", None, None, None, "tensor"),
            P("section", None, "tensor", None),
            P("section", None, "tensor", None),
            P("section", None, None, None, None),
        ),
        check_vma=False,
    )
```

```python
from functools import partial
import math

import jax
import jax.numpy as jnp
from jax import lax
from jax.experimental import pallas as pl
from jax.experimental.pallas import tpu as pltpu
from jax.sharding import PartitionSpec as P

KV_HEADS = 2
HEAD_DIM = 128
RANK = 16
EPSILON = 1e-06
ROPE_BASE = 1000000.0
MASKED_SCORE = -1e30
CHUNKS = 8
LANES = 128
VMEM_LIMIT = 60 * 2**20
MESH = pl.DeviceIdType.MESH
BF = jnp.bfloat16
F32 = jnp.float32


def dot(a, b):
    return jnp.dot(a, b, preferred_element_type=F32)


def dot_t(a, b):
    return lax.dot_general(a, b, (((1,), (1,)), ((), ())), preferred_element_type=F32)


def t_dot(a, b):
    return lax.dot_general(a, b, (((0,), (0,)), ((), ())), preferred_element_type=F32)


def rotary_tables(first_slot, rows):
    half = HEAD_DIM // 2
    frequency = jnp.exp(-math.log(ROPE_BASE) * (2.0 * jnp.arange(half, dtype=F32) / HEAD_DIM))
    slots = (first_slot + jnp.arange(rows, dtype=jnp.int32)).astype(F32)
    angles = slots[:, None] * frequency[None, :]
    cos, sin = jnp.cos(angles), jnp.sin(angles)
    return jnp.concatenate([cos, cos], axis=1), jnp.concatenate([-sin, sin], axis=1)


B_INPUT, B_RES_ONE, B_RES_TWO, B_KV, B_MISC, B_FF, B_FF_TAIL, B_HEADS, B_ROWS = 0, 5, 6, 7, 8, 9, 12, 15, 18


def rows_of(first, count=1):
    return slice(first * RANK, (first + count) * RANK)


def pick_kernel(
    ids_ref, input_ref, res_ref, kv_ref, expand_ref, shrink_ref, query_ref, attend_ref, gain_ref, kvb_ref, qb_ref,
    out_ref, heads_ref,
):
    width = out_ref.shape[2]
    out_ref[0] = jnp.zeros(out_ref.shape[1:], BF)
    out_ref[0, rows_of(B_INPUT, 5)] = input_ref[0]
    out_ref[0, rows_of(B_RES_ONE, 2)] = res_ref[0]
    kv_half = kv_ref.shape[2]
    for i in range(2):
        out_ref[0, rows_of(B_KV), i * kv_half : (i + 1) * kv_half] = kv_ref[0, rows_of(i)]
    misc = rows_of(B_MISC).start
    out_ref[0, misc : misc + 2] = gain_ref[...]
    out_ref[0, misc + 2 : misc + 3, : 2 * kv_half] = kvb_ref[...]
    tail = expand_ref.shape[2] - width
    for i in range(3):
        part = expand_ref[0, rows_of(i)] if i < 2 else shrink_ref[0]
        out_ref[0, rows_of(B_FF + i)] = part[:, :width]
        out_ref[0, rows_of(B_FF_TAIL + i), :tail] = part[:, width:]
    heads_ref[0] = jnp.zeros(heads_ref.shape[1:], BF)
    heads_ref[0, rows_of(0)] = query_ref[0]
    heads_ref[0, rows_of(1)] = attend_ref[0]
    heads_ref[0, 2 * RANK : 2 * RANK + 1] = qb_ref[...]


def pick_adapters(ids, stacks, shared):
    count = ids.shape[0]
    width = stacks[0].shape[2]
    q_cols = stacks[5].shape[2]
    shapes = [(B_ROWS * RANK, width), (3 * RANK, q_cols)]
    return pl.pallas_call(
        pick_kernel,
        grid_spec=pltpu.PrefetchScalarGridSpec(
            num_scalar_prefetch=1,
            grid=(count,),
            in_specs=[pl.BlockSpec((1,) + a.shape[1:], lambda i, ids: (ids[i], 0, 0)) for a in stacks]
            + [pl.BlockSpec(a.shape, lambda i, ids: (0, 0)) for a in shared],
            out_specs=[pl.BlockSpec((1,) + a, lambda i, ids: (i, 0, 0)) for a in shapes],
        ),
        out_shape=[jax.ShapeDtypeStruct((count,) + a, BF) for a in shapes],
    )(ids, *stacks, *shared)


def spread_factors(bundle_ref, expand_ref, ash_ref):
    width = bundle_ref.shape[1]
    tail = ash_ref.shape[1] - width
    expand_ref[...] = jnp.zeros_like(expand_ref)
    for i in range(2):
        expand_ref[i, rows_of(i), :width] = bundle_ref[rows_of(B_FF + i)]
        expand_ref[i, rows_of(i), width:] = bundle_ref[rows_of(B_FF_TAIL + i), :tail]
    ash_ref[:, :width] = bundle_ref[rows_of(B_FF + 2)]
    ash_ref[:, width:] = bundle_ref[rows_of(B_FF_TAIL + 2), :tail]


def vspec():
    return pl.BlockSpec(memory_space=pltpu.VMEM)


def hspec():
    return pl.BlockSpec(memory_space=pl.ANY)


def line_barrier(me, line):
    barrier = pltpu.get_barrier_semaphore()

    @pl.when(me > 0)
    def _():
        pl.semaphore_signal(barrier, inc=1, device_id={"tensor": me - 1}, device_id_type=MESH)

    @pl.when(me < line - 1)
    def _():
        pl.semaphore_signal(barrier, inc=1, device_id={"tensor": me + 1}, device_id_type=MESH)

    pl.semaphore_wait(barrier, jnp.where(me > 0, 1, 0) + jnp.where(me < line - 1, 1, 0))


def within(c, chunks):
    return jnp.logical_and(c >= 0, c < chunks)


def line_exchange(line, chunks, gathered, partial_ref, from_left, from_right, own_out, sems, begin, work):
    ag_recv, ag_right, ag_left, r_recv, r_send, l_recv, l_send = sems
    me = lax.axis_index("tensor")

    def copy(ref, src, c, o, send, recv, side):
        return pltpu.make_async_remote_copy(
            src_ref=src.at[c, o],
            dst_ref=ref.at[c, o],
            send_sem=send.at[c, o],
            recv_sem=recv.at[c, o],
            device_id={"tensor": me + side},
            device_id_type=MESH,
        )

    def ag(c, o, side):
        return copy(gathered, gathered, c, o, ag_right if side > 0 else ag_left, ag_recv, side)

    def rs(c, o, side):
        if side > 0:
            return copy(from_left, partial_ref, c, o, r_send, r_recv, 1)
        return copy(from_right, partial_ref, c, o, l_send, l_recv, -1)

    has_left, has_right = me > 0, me < line - 1

    def step(s, carry):
        first = s + line - 1

        @pl.when(jnp.logical_and(within(first, chunks), has_right))
        def _():
            ag(first, me, 1).start()

        @pl.when(jnp.logical_and(within(first, chunks), has_left))
        def _():
            ag(first, me, -1).start()

        for d in range(1, line):
            c = s + line - 1 - d

            @pl.when(jnp.logical_and(within(c, chunks), me - d >= 0))
            def _():
                ag(c, me - d, 1).wait_recv()

                @pl.when(has_right)
                def _():
                    ag(c, me - d, 1).start()

            @pl.when(jnp.logical_and(within(c, chunks), me + d < line))
            def _():
                ag(c, me + d, -1).wait_recv()

                @pl.when(has_left)
                def _():
                    ag(c, me + d, -1).start()

        @pl.when(within(s, chunks))
        def _():
            work(s)

        for h in range(line):
            c = s - h

            @pl.when(jnp.logical_and(within(c, chunks), me == h))
            def _():
                for j in range(line - 1, h, -1):
                    if h > 0:
                        rs(c, j, 1).wait_recv()
                        partial_ref[c, j] = (
                            partial_ref[c, j].astype(F32) + from_left[c, j].astype(F32)
                        ).astype(BF)
                    if h < line - 1:
                        rs(c, j, 1).start()

            @pl.when(jnp.logical_and(within(c, chunks), me == line - 1 - h))
            def _():
                for j in range(line - 1 - h):
                    if h > 0:
                        rs(c, j, -1).wait_recv()
                        partial_ref[c, j] = (
                            partial_ref[c, j].astype(F32) + from_right[c, j].astype(F32)
                        ).astype(BF)
                    if h < line - 1:
                        rs(c, j, -1).start()

        last = s - (line - 1)

        @pl.when(within(last, chunks))
        def _():
            own_out[last] = partial_ref[last, me].astype(F32)

            @pl.when(has_left)
            def _():
                rs(last, me, 1).wait_recv()
                own_out[last] += from_left[last, me].astype(F32)

            @pl.when(has_right)
            def _():
                rs(last, me, -1).wait_recv()
                own_out[last] += from_right[last, me].astype(F32)

        return carry

    line_barrier(me, line)
    begin()
    lax.fori_loop(-(line - 1), chunks + line - 1, step, 0)

    def drain(c, carry):
        for o in range(line):

            @pl.when(jnp.logical_and(has_right, me >= o))
            def _():
                ag(c, o, 1).wait_send()

            @pl.when(jnp.logical_and(has_left, me <= o))
            def _():
                ag(c, o, -1).wait_send()

            @pl.when(me < o)
            def _():
                rs(c, o, 1).wait_send()

            @pl.when(me > o)
            def _():
                rs(c, o, -1).wait_send()

        return carry

    lax.fori_loop(0, chunks, drain, 0)


def exchange_scratch(line, chunks, rows, width):
    slots = (chunks, line, rows, width)
    return [pltpu.VMEM(slots, BF)] * 4 + [pltpu.SemaphoreType.DMA((chunks, line))] * 7


def ff_loads(packed, refs, wsem):
    halves, parts, _, rows, cols = packed.shape
    return [
        pltpu.make_async_copy(
            packed.at[h, p, i],
            ref.at[pl.ds(h * rows, rows), pl.ds(p * cols, cols)],
            wsem.at[i, h, p],
        )
        for i, ref in enumerate(refs)
        for h in range(halves)
        for p in range(parts)
    ]


def clear_tail(packed, refs):
    hidden = packed.shape[0] * packed.shape[3]
    for ref in refs:
        if ref.shape[0] > hidden:
            ref[hidden:] = jnp.zeros((ref.shape[0] - hidden, ref.shape[1]), BF)


def mlp_kernel(
    line, chunks, tile,
    n2_ref, packed, bundle_ref,
    out_ref, n2_out, gate_out, up_out,
    gathered, partial_ref, from_left, from_right, s0, s1, s2, s3, s4, s5, s6,
    wg, wu, ws, gate_st, up_st, acc, expand_ref, ash_ref, wsem, osem, nsem,
):
    rows, width = n2_ref.shape[1:]
    every = line * rows
    tiles = wg.shape[0] // tile
    high = bundle_ref[rows_of(B_INPUT + 3, 2)]
    res = bundle_ref[rows_of(B_RES_TWO)]
    me = lax.axis_index("tensor")
    loads = ff_loads(packed, (wg, wu, ws), wsem)

    def begin():
        for load in loads:
            load.start()
        clear_tail(packed, (wg, wu, ws))
        spread_factors(bundle_ref, expand_ref, ash_ref)
        for c in range(chunks):
            gathered[c, me] = n2_ref[c]

    def saves(c, slot):
        return (
            pltpu.make_async_copy(gate_st.at[slot], gate_out.at[c], osem.at[0, slot]),
            pltpu.make_async_copy(up_st.at[slot], up_out.at[c], osem.at[1, slot]),
        )

    def keep(c):
        return pltpu.make_async_copy(gathered.at[c], n2_out.at[c], nsem.at[c])

    def work(c):
        slot = c % 2

        @pl.when(c == 0)
        def _():
            for load in loads:
                load.wait()

        @pl.when(c >= 2)
        def _():
            for save in saves(c - 2, slot):
                save.wait()

        keep(c).start()
        x = gathered[c].reshape(every, width)
        er = dot_t(x, high).astype(BF)

        def one(f, rank):
            cols = pl.ds(pl.multiple_of(f * tile, tile), tile)
            gate = dot_t(x, wg[cols]) + dot(er, expand_ref[0, :, cols])
            up = dot_t(x, wu[cols]) + dot(er, expand_ref[1, :, cols])
            gate_st[slot, :, cols] = gate.astype(BF)
            up_st[slot, :, cols] = up.astype(BF)
            act = (gate * (1.0 / (1.0 + jnp.exp(-gate))) * up).astype(BF)
            now = dot(act, ws[cols])

            @pl.when(f == 0)
            def _():
                acc[...] = now

            @pl.when(f > 0)
            def _():
                acc[...] += now

            return rank + dot_t(act, ash_ref[:, cols])

        rank = lax.fori_loop(0, tiles, one, jnp.zeros((every, ash_ref.shape[0]), F32))
        total = acc[...] + dot(rank.astype(BF), res)
        partial_ref[c] = total.astype(BF).reshape(line, rows, width)
        for save in saves(c, slot):
            save.start()

    line_exchange(
        line, chunks, gathered, partial_ref, from_left, from_right, out_ref,
        (s0, s1, s2, s3, s4, s5, s6), begin, work,
    )
    for c in range(chunks):
        keep(c).wait()
    for c in range(max(chunks - 2, 0), chunks):
        for save in saves(c, c % 2):
            save.wait()


def ff_tile(hidden):
    return hidden


def mlp_forward(n2, w):
    line = lax.axis_size("tensor")
    rows, width = n2.shape
    halves, groups, _, low_rows, _ = w["mlp"].shape
    hidden = halves * low_rows + -(halves * low_rows) % (2 * LANES)
    part = rows // CHUNKS
    every = line * part
    out, n2_all, gate, up = pl.pallas_call(
        partial(mlp_kernel, line, CHUNKS, ff_tile(hidden)),
        in_specs=[vspec(), hspec(), vspec()],
        out_specs=[vspec()] + [hspec()] * 3,
        out_shape=[
            jax.ShapeDtypeStruct((CHUNKS, part, width), F32),
            jax.ShapeDtypeStruct((CHUNKS, line, part, width), BF),
            jax.ShapeDtypeStruct((CHUNKS, every, hidden), BF),
            jax.ShapeDtypeStruct((CHUNKS, every, hidden), BF),
        ],
        scratch_shapes=exchange_scratch(line, CHUNKS, part, width)
        + [pltpu.VMEM((hidden, width), BF)] * 3
        + [pltpu.VMEM((2, every, hidden), BF)] * 2
        + [
            pltpu.VMEM((every, width), F32),
            pltpu.VMEM((2, 2 * RANK, hidden), BF),
            pltpu.VMEM((RANK, hidden), BF),
            pltpu.SemaphoreType.DMA((3, halves, groups)),
            pltpu.SemaphoreType.DMA((2, 2)),
            pltpu.SemaphoreType.DMA((CHUNKS,)),
        ],
        compiler_params=pltpu.CompilerParams(
            collective_id=0, has_side_effects=True, vmem_limit_bytes=VMEM_LIMIT
        ),
        cost_estimate=pl.CostEstimate(
            flops=6 * line * rows * width * hidden,
            bytes_accessed=6 * width * hidden + 4 * line * rows * hidden,
            transcendentals=line * rows * hidden,
        ),
    )(
        n2.reshape(CHUNKS, part, width), w["mlp"], w["bundle"],
    )
    return out.reshape(rows, width), (n2_all.reshape(CHUNKS, every, width), gate, up)


def mlp_back_kernel(
    line, chunks, tile,
    ds_ref, packed, n2_hbm, gate_in, up_in, bundle_ref, names_ref,
    out_ref, whole_ref, parts_ref,
    gathered, partial_ref, from_left, from_right, s0, s1, s2, s3, s4, s5, s6,
    wg, wu, ws, gate_st, up_st, n2_st, acc, ghigh_ref, gexp_ref, gsh_ref, gres_ref, expand_ref, ash_ref, wsem, isem,
):
    rows, width = ds_ref.shape[1:]
    every = line * rows
    tiles = wg.shape[0] // tile
    high = bundle_ref[rows_of(B_INPUT + 3, 2)]
    res = bundle_ref[rows_of(B_RES_TWO)]
    me = lax.axis_index("tensor")
    loads = ff_loads(packed, (wg, wu, ws), wsem)

    def fetch(c):
        slot = c % 2
        return (
            pltpu.make_async_copy(gate_in.at[c], gate_st.at[slot], isem.at[0, slot]),
            pltpu.make_async_copy(up_in.at[c], up_st.at[slot], isem.at[1, slot]),
            pltpu.make_async_copy(n2_hbm.at[c], n2_st.at[slot], isem.at[2, slot]),
        )

    def begin():
        for load in loads:
            load.start()
        clear_tail(packed, (wg, wu, ws))
        spread_factors(bundle_ref, expand_ref, ash_ref)
        for one in fetch(0):
            one.start()
        for c in range(chunks):
            gathered[c, me] = ds_ref[c]
        for ref in (ghigh_ref, gexp_ref, gsh_ref, gres_ref):
            ref[...] = jnp.zeros_like(ref)

    def work(c):
        slot = c % 2

        @pl.when(c == 0)
        def _():
            for load in loads:
                load.wait()

        for one in fetch(c):
            one.wait()

        @pl.when(c + 1 < chunks)
        def _():
            for one in fetch(c + 1):
                one.start()

        ds = gathered[c].reshape(every, width)
        n2 = n2_st[slot]
        er = dot_t(n2, high).astype(BF)
        rank_in = dot_t(ds, res).astype(BF)

        def one(f, carry):
            rank_out, srank = carry
            cols = pl.ds(pl.multiple_of(f * tile, tile), tile)
            act_grad = dot_t(ds, ws[cols]) + dot(rank_in, ash_ref[:, cols])
            gate = gate_st[slot, :, cols].astype(F32)
            up = up_st[slot, :, cols].astype(F32)
            sig = 1.0 / (1.0 + jnp.exp(-gate))
            silu = gate * sig
            act = (silu * up).astype(BF)
            gate_grad = (act_grad * up * (sig + silu * (1.0 - sig))).astype(BF)
            up_grad = (act_grad * silu).astype(BF)
            now = dot(gate_grad, wg[cols]) + dot(up_grad, wu[cols])

            @pl.when(f == 0)
            def _():
                acc[...] = now

            @pl.when(f > 0)
            def _():
                acc[...] += now

            gexp_ref[0, :, cols] += t_dot(er, gate_grad)
            gexp_ref[1, :, cols] += t_dot(er, up_grad)
            gsh_ref[:, cols] += t_dot(rank_in, act)
            rank_out = rank_out + dot_t(gate_grad, expand_ref[0, :, cols])
            rank_out = rank_out + dot_t(up_grad, expand_ref[1, :, cols])
            return rank_out, srank + dot_t(act, ash_ref[:, cols])

        rank_out, srank = lax.fori_loop(
            0,
            tiles,
            one,
            (
                jnp.zeros((every, expand_ref.shape[1]), F32),
                jnp.zeros((every, ash_ref.shape[0]), F32),
            ),
        )
        rank_out = rank_out.astype(BF)
        total = acc[...] + dot(rank_out, high)
        partial_ref[c] = total.astype(BF).reshape(line, rows, width)
        ghigh_ref[...] += t_dot(rank_out, n2)
        gres_ref[...] += t_dot(srank.astype(BF), ds)

    line_exchange(
        line, chunks, gathered, partial_ref, from_left, from_right, out_ref,
        (s0, s1, s2, s3, s4, s5, s6), begin, work,
    )
    whole_ref[: 2 * RANK] = ghigh_ref[...].astype(BF)
    whole_ref[2 * RANK :] = gres_ref[...].astype(BF)
    extra = gsh_ref.shape[1] - width
    parts_ref[3 * RANK :, extra:] = jnp.zeros((3 * RANK, width - extra), BF)
    for i, part in enumerate((gexp_ref[0, :RANK], gexp_ref[1, RANK:], gsh_ref[...])):
        part = part.astype(BF)
        parts_ref[i * RANK : (i + 1) * RANK] = part[:, :width]
        parts_ref[(3 + i) * RANK : (4 + i) * RANK, :extra] = part[:, width:]
    parts_ref[rows_of(5), extra : extra + LANES] = names_ref[...]


def mlp_backward(ds, w, saved, names):
    n2_all, gate, up = saved
    line = lax.axis_size("tensor")
    rows, width = ds.shape
    halves, groups, _, low_rows, _ = w["mlp"].shape
    hidden = halves * low_rows + -(halves * low_rows) % (2 * LANES)
    part = rows // CHUNKS
    every = line * part
    out, whole, parts = pl.pallas_call(
        partial(mlp_back_kernel, line, CHUNKS, ff_tile(hidden)),
        in_specs=[vspec()] + [hspec()] * 4 + [vspec()] * 2,
        out_specs=[vspec()] * 3,
        out_shape=[
            jax.ShapeDtypeStruct((CHUNKS, part, width), F32),
            jax.ShapeDtypeStruct((3 * RANK, width), BF),
            jax.ShapeDtypeStruct((6 * RANK, width), BF),
        ],
        scratch_shapes=exchange_scratch(line, CHUNKS, part, width)
        + [pltpu.VMEM((hidden, width), BF)] * 3
        + [pltpu.VMEM((2, every, hidden), BF)] * 2
        + [
            pltpu.VMEM((2, every, width), BF),
            pltpu.VMEM((every, width), F32),
            pltpu.VMEM((2 * RANK, width), F32),
            pltpu.VMEM((2, 2 * RANK, hidden), F32),
            pltpu.VMEM((RANK, hidden), F32),
            pltpu.VMEM((RANK, width), F32),
            pltpu.VMEM((2, 2 * RANK, hidden), BF),
            pltpu.VMEM((RANK, hidden), BF),
            pltpu.SemaphoreType.DMA((3, halves, groups)),
            pltpu.SemaphoreType.DMA((3, 2)),
        ],
        compiler_params=pltpu.CompilerParams(
            collective_id=1, has_side_effects=True, vmem_limit_bytes=VMEM_LIMIT
        ),
        cost_estimate=pl.CostEstimate(
            flops=6 * line * rows * width * hidden,
            bytes_accessed=6 * width * hidden + 4 * line * rows * hidden,
            transcendentals=line * rows * hidden,
        ),
    )(
        ds.reshape(CHUNKS, part, width), w["mlp"], n2_all, gate, up, w["bundle"], names,
    )
    return out.reshape(rows, width), whole, parts


def halves_kernel(expand, shrink, first, second, stage, in_sem, keep_sem, send_sem, recv_sem):
    core = lax.axis_index("section")
    half = first.shape[1]
    barrier = pltpu.get_barrier_semaphore()
    pl.semaphore_signal(barrier, inc=1, device_id={"section": 1 - core}, device_id_type=MESH)
    for c in range(2):

        @pl.when(core == c)
        def _():
            own = (expand.at[:, pl.ds(c * half, half)], shrink.at[pl.ds(c * half, half)])
            for i, dst in enumerate((stage.at[pl.ds(0, 2)], stage.at[2])):
                pltpu.make_async_copy(own[i], dst, in_sem.at[i]).start()

    pl.semaphore_wait(barrier, 1)
    for c, out in enumerate((first, second)):

        @pl.when(core == c)
        def _():
            away = (expand.at[:, pl.ds((1 - c) * half, half)], shrink.at[pl.ds((1 - c) * half, half)])
            places = (out.at[pl.ds(0, 2)], out.at[2])
            sends = [
                pltpu.make_async_remote_copy(
                    src_ref=away[i],
                    dst_ref=places[i],
                    send_sem=send_sem.at[i],
                    recv_sem=recv_sem.at[i],
                    device_id={"section": 1 - c},
                    device_id_type=MESH,
                )
                for i in range(2)
            ]
            for send in sends:
                send.start()
            own = (expand.at[:, pl.ds(c * half, half)], shrink.at[pl.ds(c * half, half)])
            for i, dst in enumerate((stage.at[pl.ds(0, 2)], stage.at[2])):
                pltpu.make_async_copy(own[i], dst, in_sem.at[i]).wait()
            keep = pltpu.make_async_copy(stage, out, keep_sem)
            keep.start()
            keep.wait()
            for send in sends:
                send.wait()


def weight_halves(expand, shrink):
    _, hidden, cols = expand.shape
    shape = (3, hidden // 2, cols)
    dma = pltpu.SemaphoreType.DMA
    return pl.pallas_call(
        halves_kernel,
        in_specs=[hspec()] * 2,
        out_specs=[hspec()] * 2,
        out_shape=[jax.ShapeDtypeStruct(shape, BF)] * 2,
        scratch_shapes=[pltpu.VMEM(shape, BF), dma((2,)), dma, dma((2,)), dma((2,))],
        compiler_params=pltpu.CompilerParams(
            collective_id=7, has_side_effects=True, vmem_limit_bytes=VMEM_LIMIT
        ),
    )(expand, shrink)


def gather_kernel(
    line, peers,
    attn, bundles, heads,
    first_out, second_out, bundle_out,
    own_sem, z_recv, z_right, z_left, dp_recv, dp_send, core_recv, core_send, side_recv, side_send, side_own,
):
    me, spot, core = lax.axis_index("tensor"), lax.axis_index("dp"), lax.axis_index("section")
    other = 1 - core
    has_left, has_right = me > 0, me < line - 1
    barrier = pltpu.get_barrier_semaphore()

    def greet(**where):
        pl.semaphore_signal(barrier, inc=1, device_id=where, device_id_type=MESH)

    @pl.when(has_left)
    def _():
        greet(tensor=me - 1)

    @pl.when(has_right)
    def _():
        greet(tensor=me + 1)

    greet(section=other)
    square = peers == 4

    def partner(k):
        if square:
            return (None, spot + 1 - 2 * lax.rem(spot, 2), lax.rem(spot + 2, 4), 3 - spot)[k]
        return lax.rem(spot + k, peers)

    def origin(k):
        return partner(k) if square else lax.rem(spot + peers - k, peers)

    direct = (1, 2) if square else tuple(range(1, peers))
    for k in range(1, peers):
        greet(dp=partner(k))
    pl.semaphore_wait(barrier, jnp.where(has_left, 1, 0) + jnp.where(has_right, 1, 0) + peers)

    mine = spot * 2 + core
    plain, part = bundles.shape[1] - heads.shape[1], heads.shape[2]

    def head_place(layer, o):
        return bundle_out.at[layer, pl.ds(plain, heads.shape[1]), pl.ds(o * part, part)]

    def places(o):
        return first_out.at[mine, o], second_out.at[o], head_place(core, o), head_place(other, o)

    sides = [
        pltpu.make_async_remote_copy(
            src_ref=src,
            dst_ref=dst,
            send_sem=side_send.at[i],
            recv_sem=side_recv.at[i],
            device_id={"section": other},
            device_id_type=MESH,
        )
        for i, (src, dst) in enumerate(
            (
                (bundles.at[other, pl.ds(0, plain)], bundle_out.at[core, pl.ds(0, plain)]),
                (heads.at[other], head_place(core, me)),
            )
        )
    ]
    side_keep = pltpu.make_async_copy(
        bundles.at[core, pl.ds(0, plain)], bundle_out.at[core, pl.ds(0, plain)], side_own
    )
    sources = (attn.at[0], attn.at[1], heads.at[core], head_place(other, me))
    keeps = [
        pltpu.make_async_copy(src, dst, own_sem.at[i]) for i, (src, dst) in enumerate(zip(sources[:3], places(me)))
    ]

    def remote(src, dst, send, recv, **where):
        return pltpu.make_async_remote_copy(
            src_ref=src, dst_ref=dst, send_sem=send, recv_sem=recv, device_id=where, device_id_type=MESH
        )

    def along(i, o, side, own):
        dst = places(o)[i]
        return remote(
            sources[i] if own else dst,
            dst,
            (z_right if side > 0 else z_left).at[i, o],
            z_recv.at[i, o],
            tensor=me + side,
        )

    outs = (first_out,)

    def to_peer(lay, k, o, own):
        dst = outs[lay].at[mine, o]
        return remote(
            attn.at[lay] if own else dst, dst, dp_send.at[lay, k, o], dp_recv.at[lay, spot, o], dp=partner(k)
        )

    def from_peer(lay, k, o):
        p = origin(k)
        slot = outs[lay].at[p * 2 + core, o]
        to = partner(3 - k) if square and k < 3 else p
        return remote(slot, slot, dp_send.at[lay, peers - 1, o], dp_recv.at[lay, p, o], dp=to)

    def to_core(lay, p, o, own):
        dst = outs[lay].at[p * 2 + core, o]
        return remote(
            attn.at[lay] if own else dst, dst, core_send.at[lay, p, o], core_recv.at[lay, p, o], section=other
        )

    def spread(lay, o, own):
        for k in direct:
            to_peer(lay, k, o, own).start()
        to_core(lay, spot, o, own).start()

    for side in sides:
        side.start()
    for i in range(4):
        if i == 3:
            sides[1].wait_recv()

        @pl.when(has_right)
        def _():
            along(i, me, 1, True).start()

        @pl.when(has_left)
        def _():
            along(i, me, -1, True).start()

        if i == 0:
            spread(i, me, True)
    for keep in keeps:
        keep.start()
    side_keep.start()
    for d in range(1, line):
        for i in range(4):

            @pl.when(me >= d)
            def _():
                along(i, me - d, 1, False).wait_recv()

                @pl.when(has_right)
                def _():
                    along(i, me - d, 1, False).start()

                if i == 0:
                    spread(i, me - d, False)

            @pl.when(me + d < line)
            def _():
                along(i, me + d, -1, False).wait_recv()

                @pl.when(has_left)
                def _():
                    along(i, me + d, -1, False).start()

                if i == 0:
                    spread(i, me + d, False)

    half = line // 2

    def pass_on(n, carry):
        o = lax.rem(me + n, line)
        for lay in range(1):
            for k in direct:
                from_peer(lay, k, o).wait_recv()
                if square:

                    @pl.when(o < half if k == 1 else o >= half)
                    def _():
                        from_peer(lay, k, o).start()

                to_core(lay, origin(k), o, False).start()
        return carry

    lax.fori_loop(0, line, pass_on, 0)

    def pass_last(n, carry):
        o = lax.rem(me + n, line)
        for lay in range(1):
            from_peer(lay, 3, o).wait_recv()
            to_core(lay, origin(3), o, False).start()
        return carry

    if square:
        lax.fori_loop(0, line, pass_last, 0)

    def finish(o, carry):
        for lay in range(1):
            for k in direct:
                to_peer(lay, k, o, False).wait_send()
            if square:
                from_peer(lay, 1, o).wait_send()
            for p in range(peers):
                to_core(lay, p, o, False).wait_send()
                slot = outs[lay].at[p * 2 + other, o]
                remote(slot, slot, core_send.at[lay, p, o], core_recv.at[lay, p, o], section=other).wait_recv()
        for i in range(4):

            @pl.when(jnp.logical_and(has_right, me >= o))
            def _():
                along(i, o, 1, False).wait_send()

            @pl.when(jnp.logical_and(has_left, me <= o))
            def _():
                along(i, o, -1, False).wait_send()

        return carry

    lax.fori_loop(0, line, finish, 0)
    for keep in keeps:
        keep.wait()
    side_keep.wait()
    sides[0].wait_recv()
    for side in sides:
        side.wait_send()


def gather_first(attn, bundles, heads):
    line, peers = lax.axis_size("tensor"), lax.axis_size("dp")
    cores, part, cols = attn.shape
    dma = pltpu.SemaphoreType.DMA
    return pl.pallas_call(
        partial(gather_kernel, line, peers),
        in_specs=[vspec()] * 3,
        out_specs=[hspec()] * 3,
        out_shape=[
            jax.ShapeDtypeStruct((peers * cores, line, part, cols), BF),
            jax.ShapeDtypeStruct((line, part, cols), BF),
            jax.ShapeDtypeStruct(bundles.shape, BF),
        ],
        scratch_shapes=[dma((3,)), dma((4, line)), dma((4, line)), dma((4, line))]
        + [dma((1, peers, line))] * 4
        + [dma((2,)), dma((2,)), dma],
        compiler_params=pltpu.CompilerParams(
            collective_id=4, has_side_effects=True, vmem_limit_bytes=VMEM_LIMIT
        ),
    )(attn, bundles, heads)


def rotated(x, cos, sin):
    return x * cos + pltpu.roll(x, HEAD_DIM // 2, 1) * sin


def head_cols(h):
    return pl.ds(pl.multiple_of(h * HEAD_DIM, HEAD_DIM), HEAD_DIM)


def weight_loads(packed, wq, wo, wkv, wsem):
    cols, kv_cols = wq.shape[-1], wkv.shape[-1]
    loads = []
    for i, (ref, start, size) in enumerate(((wkv, 2 * cols, kv_cols), (wq, 0, cols), (wo, cols, cols))):
        loads.append(
            [
                pltpu.make_async_copy(packed.at[:, t, :, pl.ds(start, size)], ref.at[t], wsem.at[i, t])
                for t in range(ref.shape[0])
            ]
        )
    return loads


def flat(ref, t):
    groups, rows, cols = ref.shape[1:]
    return ref[t].reshape(groups * rows, cols)


def allowed_keys(info_ref, block, keys, rows):
    row = info_ref[0] + lax.broadcasted_iota(jnp.int32, (1, rows), 1)
    last = jnp.minimum(row, info_ref[1] - 1)
    return block * keys + lax.broadcasted_iota(jnp.int32, (keys, rows), 0) <= last


def one_way_barrier(me, line, side):
    barrier = pltpu.get_barrier_semaphore()
    first, last = (0, line - 1) if side > 0 else (line - 1, 0)

    @pl.when(me != first)
    def _():
        pl.semaphore_signal(barrier, inc=1, device_id={"tensor": me - side}, device_id_type=MESH)

    @pl.when(me != last)
    def _():
        pl.semaphore_wait(barrier, 1)


def spread_qkv(bundle_ref, bq_ref, bkv_ref):
    kv_half = bkv_ref.shape[1] // 2
    bq_ref[...] = jnp.zeros_like(bq_ref)
    bkv_ref[...] = jnp.zeros_like(bkv_ref)
    bq_ref[rows_of(0)] = bundle_ref[rows_of(B_HEADS)]
    for i in range(2):
        span = slice(i * kv_half, (i + 1) * kv_half)
        bkv_ref[rows_of(1 + i), span] = bundle_ref[rows_of(B_KV), span]


def kv_exchange(me, line, kvbuf, recv, send):
    def move(o):
        return pltpu.make_async_remote_copy(
            src_ref=kvbuf.at[o],
            dst_ref=kvbuf.at[o],
            send_sem=send.at[o],
            recv_sem=recv.at[o],
            device_id={"tensor": me + 1},
            device_id_type=MESH,
        )

    return move


def attend_kernel(
    line, group,
    info_ref, x_ref, bundle_ref, cos_ref, sin_ref, packed,
    mid_ref, n2_ref, normed_ref, lowr_ref, rank_ref, q_ref, kv_out, attended_ref, log_ref,
    wq, wo, wkv, kvbuf, acc, peak, total, bq_ref, bkv_ref, wsem, recv, send, ksem,
):
    rows, width = x_ref.shape
    heads = width // HEAD_DIM
    cols = wq.shape[-1]
    kv_cols = wkv.shape[-1]
    scale = HEAD_DIM**-0.5
    me = lax.axis_index("tensor")
    one_way_barrier(me, line, 1)
    kv_loads, q_loads, o_loads = weight_loads(packed, wq, wo, wkv, wsem)
    for load in kv_loads + q_loads + o_loads:
        load.start()
    move = kv_exchange(me, line, kvbuf, recv, send)
    spread_qkv(bundle_ref, bq_ref, bkv_ref)
    misc = bundle_ref[rows_of(B_MISC)].astype(F32)
    q_bias = bundle_ref[rows_of(B_HEADS + 2)].astype(F32)[:1]
    low_in = bundle_ref[rows_of(B_INPUT, 3)]
    x = x_ref[...].astype(F32)
    inverse = lax.rsqrt(jnp.mean(x * x, axis=-1, keepdims=True) + EPSILON)
    normed_ref[...] = (x * inverse * misc[0:1]).astype(BF)
    low = dot_t(normed_ref[...], low_in).astype(BF)
    cos, sin = cos_ref[...], sin_ref[...]
    for load in kv_loads:
        load.wait()
    for t in range(line):
        span = slice(t * kv_cols, (t + 1) * kv_cols)
        kv = dot(normed_ref[...], flat(wkv, t)) + misc[2:3, span] + dot(low, bkv_ref[:, span])
        for h in range(kv_cols // HEAD_DIM):
            at = t * kv_cols + h * HEAD_DIM
            one = kv[:, h * HEAD_DIM : (h + 1) * HEAD_DIM]
            if at < KV_HEADS * HEAD_DIM:
                one = rotated(one, cos, sin)
            kvbuf[me, :, at : at + HEAD_DIM] = one.astype(BF)

    @pl.when(me < line - 1)
    def _():
        move(me).start()

    for load in q_loads:
        load.wait()
    for t in range(line):
        span = slice(t * cols, (t + 1) * cols)
        q = dot(normed_ref[...], flat(wq, t)) + q_bias[:, span] + dot(low, bq_ref[:, span])
        for h in range(cols // HEAD_DIM):
            at = t * cols + h * HEAD_DIM
            q_ref[:, at : at + HEAD_DIM] = rotated(
                q[:, h * HEAD_DIM : (h + 1) * HEAD_DIM], cos, sin
            ).astype(BF)
    acc[...] = jnp.zeros_like(acc)
    total[...] = jnp.zeros_like(total)
    peak[...] = jnp.full_like(peak, MASKED_SCORE)

    def block(o):
        allowed = allowed_keys(info_ref, o, rows, rows)

        def one(h, carry):
            kv_head = h // group
            k = kvbuf[o, :, head_cols(kv_head)]
            v = kvbuf[o, :, head_cols(KV_HEADS + kv_head)]
            scores = jnp.where(allowed, dot_t(k, q_ref[:, head_cols(h)]) * scale, MASKED_SCORE)
            top = jnp.maximum(peak[h], jnp.max(scores, axis=0, keepdims=True))
            soft = jnp.exp(scores - top)
            shift = jnp.exp(peak[h] - top)
            total[h] = total[h] * shift + jnp.sum(soft, axis=0, keepdims=True)
            acc[h] = acc[h] * shift + t_dot(v, soft.astype(BF))
            peak[h] = top
            return carry

        lax.fori_loop(0, heads, one, 0, unroll=12)

    for d in range(line):

        @pl.when(me >= d)
        def _():
            if d > 0:
                move(me - d).wait_recv()

                @pl.when(me < line - 1)
                def _():
                    move(me - d).start()

            block(me - d)

    keep = pltpu.make_async_copy(kvbuf, kv_out, ksem)
    keep.start()
    for h in range(heads):
        attended_ref[:, h * HEAD_DIM : (h + 1) * HEAD_DIM] = (acc[h] * (1.0 / total[h])).T.astype(BF)
        log_ref[h] = peak[h] + jnp.log(total[h])
    rank = dot_t(attended_ref[...], bundle_ref[rows_of(B_HEADS + 1)]).astype(BF)
    lowr_ref[...] = low
    rank_ref[...] = rank
    middle = x_ref[...].astype(F32) + dot(rank, bundle_ref[rows_of(B_RES_ONE)])
    for load in o_loads:
        load.wait()
    for t in range(line):
        middle = middle + dot_t(attended_ref[:, t * cols : (t + 1) * cols], flat(wo, t))
    mid_ref[...] = middle
    inverse = lax.rsqrt(jnp.mean(middle * middle, axis=-1, keepdims=True) + EPSILON)
    n2_ref[...] = (middle * inverse * misc[1:2]).astype(BF)
    keep.wait()
    for o in range(line):

        @pl.when(jnp.logical_and(me < line - 1, me >= o))
        def _():
            move(o).wait_send()


def attend_forward(x, w, info, tables):
    line = lax.axis_size("tensor")
    rows, width = x.shape
    heads = width // HEAD_DIM
    kv_width = 2 * KV_HEADS * HEAD_DIM
    groups, low_rows = w["packed"].shape[0], w["packed"].shape[2]
    outs = pl.pallas_call(
        partial(attend_kernel, line, heads // KV_HEADS),
        in_specs=[pl.BlockSpec(memory_space=pltpu.SMEM)] + [vspec()] * 4 + [hspec()],
        out_specs=[vspec()] * 6 + [hspec()] + [vspec()] * 2,
        out_shape=[
            jax.ShapeDtypeStruct((rows, width), F32),
            jax.ShapeDtypeStruct((rows, width), BF),
            jax.ShapeDtypeStruct((rows, width), BF),
            jax.ShapeDtypeStruct((rows, 3 * RANK), BF),
            jax.ShapeDtypeStruct((rows, RANK), BF),
            jax.ShapeDtypeStruct((rows, width), BF),
            jax.ShapeDtypeStruct((line, rows, kv_width), BF),
            jax.ShapeDtypeStruct((rows, width), BF),
            jax.ShapeDtypeStruct((heads, 1, rows), F32),
        ],
        scratch_shapes=[
            pltpu.VMEM((line, groups, low_rows, width // line), BF),
            pltpu.VMEM((line, groups, low_rows, width // line), BF),
            pltpu.VMEM((line, groups, low_rows, kv_width // line), BF),
            pltpu.VMEM((line, rows, kv_width), BF),
            pltpu.VMEM((heads, HEAD_DIM, rows), F32),
            pltpu.VMEM((heads, 1, rows), F32),
            pltpu.VMEM((heads, 1, rows), F32),
            pltpu.VMEM((3 * RANK, width), BF),
            pltpu.VMEM((3 * RANK, kv_width), BF),
            pltpu.SemaphoreType.DMA((3, line)),
            pltpu.SemaphoreType.DMA((line,)),
            pltpu.SemaphoreType.DMA((line,)),
            pltpu.SemaphoreType.DMA,
        ],
        compiler_params=pltpu.CompilerParams(
            collective_id=2, has_side_effects=True, vmem_limit_bytes=VMEM_LIMIT
        ),
        cost_estimate=pl.CostEstimate(
            flops=4 * rows * width * width * 2, bytes_accessed=5 * width * width, transcendentals=0
        ),
    )(
        info, x, w["bundle"], tables[0], tables[1], w["packed"],
    )
    return outs[0], outs[1], outs[2:]


def attend_back_kernel(
    line, group,
    info_ref, x_ref, mid_ref, dy_ref, dn2_ref, bundle_ref, cos_ref, sin_ref,
    normed_ref, lowr_ref, rank_ref, q_ref, kv_ref, attended_ref, log_ref, packed,
    dx_ref, dx_low_ref, grads_ref,
    wq, wo, wkv, do_ref, dq_acc, dq_ref, dkv_acc, partial_ref, from_right, delta, bq_ref, bkv_ref, wsem, recv, send,
):
    rows, width = x_ref.shape
    heads = width // HEAD_DIM
    cols = wq.shape[-1]
    kv_cols = wkv.shape[-1]
    kv_half = KV_HEADS * HEAD_DIM
    scale = HEAD_DIM**-0.5
    me = lax.axis_index("tensor")
    one_way_barrier(me, line, -1)
    kv_loads, q_loads, o_loads = weight_loads(packed, wq, wo, wkv, wsem)
    for load in o_loads + q_loads + kv_loads:
        load.start()

    def move(o):
        return pltpu.make_async_remote_copy(
            src_ref=partial_ref.at[o],
            dst_ref=from_right.at[o],
            send_sem=send.at[o],
            recv_sem=recv.at[o],
            device_id={"tensor": me - 1},
            device_id_type=MESH,
        )

    def through_norm(values, gain, grad_out):
        inverse = lax.rsqrt(jnp.mean(values * values, axis=-1, keepdims=True) + EPSILON)
        weighted = gain * grad_out
        return inverse * weighted - inverse * inverse * inverse * values * jnp.mean(
            weighted * values, axis=-1, keepdims=True
        )

    spread_qkv(bundle_ref, bq_ref, bkv_ref)
    misc = bundle_ref[rows_of(B_MISC)].astype(F32)
    att = bundle_ref[rows_of(B_HEADS + 1)]
    middle_grad = dy_ref[...].astype(F32) + through_norm(mid_ref[...], misc[1:2], dn2_ref[...])
    dx_ref[...] = middle_grad
    branch_grad = middle_grad.astype(BF)
    low, rank = lowr_ref[...], rank_ref[...]
    rank_grad = dot_t(branch_grad, bundle_ref[rows_of(B_RES_ONE)]).astype(BF)
    grads_ref[3 * RANK : 4 * RANK] = t_dot(rank, branch_grad).astype(BF)
    grads_ref[6 * RANK :] = t_dot(rank_grad, attended_ref[...]).astype(BF)
    for load in o_loads:
        load.wait()
    for t in range(line):
        span = slice(t * cols, (t + 1) * cols)
        do_ref[:, span] = (dot(branch_grad, flat(wo, t)) + dot(rank_grad, att[:, span])).astype(BF)
    for h in range(heads):
        span = slice(h * HEAD_DIM, (h + 1) * HEAD_DIM)
        both = do_ref[:, span].astype(F32) * attended_ref[:, span].astype(F32)
        delta[h] = jnp.sum(both.T, axis=0, keepdims=True)
    dq_acc[...] = jnp.zeros_like(dq_acc)

    def block(o):
        allowed = allowed_keys(info_ref, o, rows, rows)
        dkv_acc[...] = jnp.zeros_like(dkv_acc)

        def one(h, carry):
            kv_head = h // group
            k = kv_ref[o, :, head_cols(kv_head)]
            v = kv_ref[o, :, head_cols(KV_HEADS + kv_head)]
            q = q_ref[:, head_cols(h)]
            do = do_ref[:, head_cols(h)]
            scores = dot_t(k, q) * scale - log_ref[h]
            soft = jnp.exp(jnp.where(allowed, scores, MASKED_SCORE))
            grad = (soft * (dot_t(v, do) - delta[h])).astype(BF)
            dq_acc[h] += t_dot(k, grad)
            dkv_acc[:, head_cols(kv_head)] += dot(grad, q) * scale
            dkv_acc[:, head_cols(KV_HEADS + kv_head)] += dot(soft.astype(BF), do)
            return carry

        lax.fori_loop(0, heads, one, 0, unroll=12)
        partial_ref[o] = dkv_acc[...].astype(BF)

    for s in range(2 * line - 1):
        if s < line:

            @pl.when(me >= s)
            def _():
                block(s)

        for h in range(line - 1):
            o = s - h
            if 0 <= o < line - 1 - h:

                @pl.when(me == line - 1 - h)
                def _():
                    if h > 0:
                        move(o).wait_recv()
                        partial_ref[o] = (partial_ref[o].astype(F32) + from_right[o].astype(F32)).astype(BF)
                    move(o).start()

    cos, sin = cos_ref[...], -sin_ref[...]
    for h in range(heads):
        dq_ref[:, h * HEAD_DIM : (h + 1) * HEAD_DIM] = rotated(dq_acc[h].T * scale, cos, sin).astype(BF)
    dq = dq_ref[...]
    grads_ref[5 * RANK : 6 * RANK] = t_dot(low, dq)[:RANK].astype(BF)
    low_grad = dot_t(dq, bq_ref[...])
    for load in q_loads:
        load.wait()
    normed_grad = dot_t(dq[:, :cols], flat(wq, 0))
    for t in range(1, line):
        normed_grad = normed_grad + dot_t(dq[:, t * cols : (t + 1) * cols], flat(wq, t))
    dkv_acc[...] = partial_ref[me].astype(F32)

    @pl.when(me < line - 1)
    def _():
        move(me).wait_recv()
        dkv_acc[...] += from_right[me].astype(F32)

    for h in range(KV_HEADS):
        span = slice(h * HEAD_DIM, (h + 1) * HEAD_DIM)
        dkv_acc[:, span] = rotated(dkv_acc[:, span], cos, sin)
    dkv = dkv_acc[...].astype(BF)
    kv_grad = t_dot(low, dkv).astype(BF)
    grads_ref[4 * RANK : 5 * RANK, :kv_half] = kv_grad[RANK : 2 * RANK, :kv_half]
    grads_ref[4 * RANK : 5 * RANK, kv_half : 2 * kv_half] = kv_grad[2 * RANK :, kv_half:]
    grads_ref[4 * RANK : 5 * RANK, 2 * kv_half :] = jnp.zeros((RANK, width - 2 * kv_half), BF)
    low_grad = (low_grad + dot_t(dkv, bkv_ref[...])).astype(BF)
    grads_ref[: 3 * RANK] = t_dot(low_grad, normed_ref[...]).astype(BF)
    for load in kv_loads:
        load.wait()
    for t in range(line):
        normed_grad = normed_grad + dot_t(dkv[:, t * kv_cols : (t + 1) * kv_cols], flat(wkv, t))
    normed_grad = normed_grad + dot(low_grad, bundle_ref[rows_of(B_INPUT, 3)])
    dx = dx_ref[...] + through_norm(x_ref[...].astype(F32), misc[0:1], normed_grad)
    dx_ref[...] = dx
    dx_low_ref[...] = dx.astype(BF)
    for o in range(line - 1):

        @pl.when(me > o)
        def _():
            move(o).wait_send()


def attend_backward(x, middle, dy, dn2, w, kept, info, tables):
    line = lax.axis_size("tensor")
    rows, width = x.shape
    heads = width // HEAD_DIM
    kv_width = 2 * KV_HEADS * HEAD_DIM
    groups, low_rows = w["packed"].shape[0], w["packed"].shape[2]
    return pl.pallas_call(
        partial(attend_back_kernel, line, heads // KV_HEADS),
        in_specs=[pl.BlockSpec(memory_space=pltpu.SMEM)] + [vspec()] * 14 + [hspec()],
        out_specs=[vspec()] * 3,
        out_shape=[
            jax.ShapeDtypeStruct((rows, width), F32),
            jax.ShapeDtypeStruct((rows, width), BF),
            jax.ShapeDtypeStruct((7 * RANK, width), BF),
        ],
        scratch_shapes=[
            pltpu.VMEM((line, groups, low_rows, width // line), BF),
            pltpu.VMEM((line, groups, low_rows, width // line), BF),
            pltpu.VMEM((line, groups, low_rows, kv_width // line), BF),
            pltpu.VMEM((rows, width), BF),
            pltpu.VMEM((heads, HEAD_DIM, rows), F32),
            pltpu.VMEM((rows, width), BF),
            pltpu.VMEM((rows, kv_width), F32),
            pltpu.VMEM((line, rows, kv_width), BF),
            pltpu.VMEM((line, rows, kv_width), BF),
            pltpu.VMEM((heads, 1, rows), F32),
            pltpu.VMEM((3 * RANK, width), BF),
            pltpu.VMEM((3 * RANK, kv_width), BF),
            pltpu.SemaphoreType.DMA((3, line)),
            pltpu.SemaphoreType.DMA((line,)),
            pltpu.SemaphoreType.DMA((line,)),
        ],
        compiler_params=pltpu.CompilerParams(
            collective_id=3 if dy.dtype == F32 else 5, has_side_effects=True, vmem_limit_bytes=VMEM_LIMIT
        ),
        cost_estimate=pl.CostEstimate(
            flops=4 * rows * width * width * 2, bytes_accessed=5 * width * width, transcendentals=0
        ),
    )(
        info, x, middle, dy, dn2, w["bundle"], tables[0], tables[1], *kept, w["packed"],
    )


def reduce_kernel(
    line, peers, extra,
    attn_ref, whole_ref, parts_ref, y_first, y_second, g_first, g_second,
    out, y_out, g_out,
    mine, z_in, quarter, z_recv, z_send, dp_recv, dp_send, own_sem, t_recv, t_right, t_left,
    side_recv, side_send, side_own,
):
    r = RANK
    me, spot, core = lax.axis_index("tensor"), lax.axis_index("dp"), lax.axis_index("section")
    width = mine.shape[1]
    cols = width // line
    seqs = out.shape[0]
    seq = spot * 2 + core
    has_left, has_right = me > 0, me < line - 1
    barrier = pltpu.get_barrier_semaphore()

    def greet(**where):
        pl.semaphore_signal(barrier, inc=1, device_id=where, device_id_type=MESH)

    for k in range(1, line):
        greet(tensor=lax.rem(me + k, line))

    greet(section=1 - core)

    @pl.when(core == 0)
    def _():
        for k in range(1, peers):
            for c in range(2):
                greet(section=c, dp=lax.rem(spot + k, peers))

    pl.semaphore_wait(barrier, line - 1 + peers)

    def remote(src, dst, send, recv, **where):
        return pltpu.make_async_remote_copy(
            src_ref=src, dst_ref=dst, send_sem=send, recv_sem=recv, device_id=where, device_id_type=MESH
        )

    def lanes(t):
        return pl.ds(pl.multiple_of(t * cols, LANES), cols)

    def pieces(s):
        return (
            (parts_ref.at[pl.ds(0, 3 * r)], out.at[s, pl.ds(8 * r, 3 * r)]),
            (parts_ref.at[pl.ds(3 * r, 3 * r), pl.ds(0, extra)], out.at[s, pl.ds(11 * r, 3 * r), pl.ds(0, extra)]),
            (
                parts_ref.at[pl.ds(5 * r, r), pl.ds(extra, LANES)],
                out.at[s, pl.ds(13 * r, r), pl.ds(extra, LANES)],
            ),
            (quarter.at[pl.ds(0, 8 * r)], out.at[s, pl.ds(0, 8 * r), lanes(me)]),
            (quarter.at[pl.ds(8 * r, 2 * r)], out.at[s, pl.ds(11 * r, 2 * r), pl.ds(extra, cols)]),
        )

    def to_peer(k, i):
        src, dst = pieces(seq)[i]
        return remote(src, dst, dp_send.at[k, i], dp_recv.at[seq, i], section=0, dp=lax.rem(spot + k, peers))

    def stay(i):
        src, dst = pieces(seq)[i]
        return pltpu.make_async_copy(src, dst, own_sem.at[i])

    def send_pieces(which):
        for i in which:
            for k in range(1, peers):
                to_peer(k, i).start()

            @pl.when(core != 0)
            def _():
                to_peer(0, i).start()

            @pl.when(core == 0)
            def _():
                stay(i).start()

    def across(k):
        to = lax.rem(me + k, line)
        return remote(mine.at[:, lanes(to)], z_in.at[me], z_send.at[k], z_recv.at[me], tensor=to)

    def incoming(k):
        o = lax.rem(me + k, line)
        return remote(mine.at[:, lanes(me)], z_in.at[o], z_send.at[k], z_recv.at[o], tensor=o)

    def side(i, src, dst):
        return remote(src, dst.at[core], side_send.at[i], side_recv.at[i], section=1 - core)

    def side_keep(i, src, dst):
        return pltpu.make_async_copy(src, dst.at[core], side_own.at[i])

    pairs = ((y_first, y_second, y_out), (g_first, g_second, g_out))

    for first, rows, ref, start in (
        (0, 3, attn_ref, 0), (3, 2, whole_ref, 0), (5, 1, attn_ref, 3), (6, 1, whole_ref, 2), (7, 3, attn_ref, 4),
    ):
        mine[rows_of(first, rows)] = ref[rows_of(start, rows)]
    for k in range(1, line):
        across(k).start()
    send_pieces((0, 1, 2))
    for c in range(2):

        @pl.when(core == c)
        def _():
            for i, (first, second, dst) in enumerate(pairs):
                side(i, first if c == 1 else second, dst).start()
                side_keep(i, second if c == 1 else first, dst).start()

    total = mine[:, lanes(me)].astype(F32)
    for k in range(1, line):
        incoming(k).wait_recv()
        total = total + z_in[lax.rem(me + k, line)].astype(F32)
    quarter[...] = total.astype(BF)
    send_pieces((3, 4))

    def arrived(s, i):
        src, dst = pieces(s)[i]
        return remote(src, dst, dp_send.at[0, i], dp_recv.at[s, i], section=0)

    def along(s, o, side):
        place = out.at[s, pl.ds(0, 8 * r), lanes(o)]
        return remote(
            place, place, (t_right if side > 0 else t_left).at[s, o], t_recv.at[s, o], tensor=me + side
        )

    @pl.when(core == 0)
    def _():
        def own_rows(n, carry):
            s = lax.rem(seq + n, seqs)

            @pl.when(n == 0)
            def _():
                stay(3).wait()

            @pl.when(n > 0)
            def _():
                arrived(s, 3).wait_recv()

            @pl.when(has_right)
            def _():
                along(s, me, 1).start()

            @pl.when(has_left)
            def _():
                along(s, me, -1).start()

            return carry

        lax.fori_loop(0, seqs, own_rows, 0)
        for d in range(1, line):

            def others(n, carry):
                s = lax.rem(seq + n, seqs)

                @pl.when(me >= d)
                def _():
                    along(s, me - d, 1).wait_recv()

                    @pl.when(has_right)
                    def _():
                        along(s, me - d, 1).start()

                @pl.when(me + d < line)
                def _():
                    along(s, me + d, -1).wait_recv()

                    @pl.when(has_left)
                    def _():
                        along(s, me + d, -1).start()

                return carry

            lax.fori_loop(0, seqs, others, 0)

        def finish(n, carry):
            s = lax.rem(seq + n, seqs)

            @pl.when(n > 0)
            def _():
                for i in (0, 1, 2, 4):
                    arrived(s, i).wait_recv()

            for o in range(line):

                @pl.when(jnp.logical_and(has_right, me >= o))
                def _():
                    along(s, o, 1).wait_send()

                @pl.when(jnp.logical_and(has_left, me <= o))
                def _():
                    along(s, o, -1).wait_send()

            return carry

        lax.fori_loop(0, seqs, finish, 0)
        for i in (0, 1, 2, 4):
            stay(i).wait()

    for k in range(1, line):
        across(k).wait_send()
    for i in range(5):
        for k in range(1, peers):
            to_peer(k, i).wait_send()

        @pl.when(core != 0)
        def _():
            to_peer(0, i).wait_send()
    for i, (first, _, dst) in enumerate(pairs):
        side(i, first, dst).wait()
        side_keep(i, first, dst).wait()


def reduce_first(attn_part, whole, parts, extra, outs, grads):
    line, peers = lax.axis_size("tensor"), lax.axis_size("dp")
    width = parts.shape[1]
    seqs = 2 * peers
    dma = pltpu.SemaphoreType.DMA
    return pl.pallas_call(
        partial(reduce_kernel, line, peers, extra),
        in_specs=[vspec()] * 7,
        out_specs=[hspec()] * 3,
        out_shape=[
            jax.ShapeDtypeStruct((seqs, 14 * RANK, width), BF),
            jax.ShapeDtypeStruct((2,) + outs[0].shape, outs[0].dtype),
            jax.ShapeDtypeStruct((2,) + grads[0].shape, grads[0].dtype),
        ],
        scratch_shapes=[
            pltpu.VMEM((10 * RANK, width), BF),
            pltpu.VMEM((line, 10 * RANK, width // line), BF),
            pltpu.VMEM((10 * RANK, width // line), BF),
            dma((line,)),
            dma((line,)),
            dma((seqs, 5)),
            dma((peers, 5)),
            dma((5,)),
            dma((seqs, line)),
            dma((seqs, line)),
            dma((seqs, line)),
            dma((2,)),
            dma((2,)),
            dma((2,)),
        ],
        compiler_params=pltpu.CompilerParams(
            collective_id=6, has_side_effects=True, vmem_limit_bytes=VMEM_LIMIT
        ),
    )(attn_part, whole, parts, *outs, *grads)


def total_kernel(
    scale, hidden, q_cols,
    first, attn_in, whole_in, parts_in,
    input_ref, query_ref, kv_ref, expand_ref, attend_ref, shrink_ref, res_ref,
    block, ids, sem,
):
    r = RANK
    a = pl.program_id(0)
    core = lax.axis_index("section")
    width = block.shape[2]
    extra = hidden - width
    pad = extra + -hidden % (2 * LANES)

    @pl.when(jnp.logical_and(a == 0, core == 0))
    def _():
        load = pltpu.make_async_copy(first, block, sem.at[0])
        load.start()
        load.wait()

    @pl.when(jnp.logical_and(a == 0, core != 0))
    def _():
        def load(src, start, first, count, at):
            return pltpu.make_async_copy(src.at[:, rows_of(start, count)], block.at[:, rows_of(first, count)], sem.at[at])

        loads = [
            load(attn_in, 0, 0, 3, 1), load(whole_in, 0, 3, 2, 2), load(attn_in, 3, 5, 1, 3),
            load(whole_in, 2, 6, 1, 4), load(attn_in, 4, 7, 1, 5), load(parts_in, 0, 8, 6, 6),
        ]
        for one in loads:
            one.start()
        for one in loads:
            one.wait()
        mine = pl.ds(pl.multiple_of(lax.axis_index("tensor") * q_cols, LANES), q_cols)
        last = pltpu.make_async_copy(
            attn_in.at[:, rows_of(5, 2), mine], block.at[:, rows_of(11, 2), pl.ds(pad, q_cols)], sem.at[7]
        )
        last.start()
        last.wait()

    @pl.when(a == 0)
    def _():
        lane = lax.broadcasted_iota(jnp.int32, (1, LANES), 1).astype(F32)
        for i in range(block.shape[0]):
            names = block[i, 13 * r : 14 * r, pad : pad + LANES][:1].astype(F32)
            ids[i] = jnp.sum(lane * names).astype(jnp.int32)

    for ref in (input_ref, query_ref, kv_ref, expand_ref, attend_ref, shrink_ref, res_ref):
        ref[...] = jnp.zeros_like(ref)

    for i in range(block.shape[0]):

        @pl.when(ids[i] == a)
        def _():
            def part(row, rows, col, cols):
                return block[i, row : row + rows, col : col + cols].astype(F32) * scale

            input_ref[0] += part(0, 5 * r, 0, width)
            res_ref[0, 0] += part(5 * r, r, 0, width)
            res_ref[0, 1] += part(6 * r, r, 0, width)
            kv = part(7 * r, r, 0, 2 * kv_ref.shape[3])
            kv_ref[0, 0] += kv[:, : kv_ref.shape[3]]
            kv_ref[0, 1] += kv[:, kv_ref.shape[3] :]
            for j in range(2):
                expand_ref[0, j, :, :width] += part((8 + j) * r, r, 0, width)
                expand_ref[0, j, :, width:] += part((11 + j) * r, r, 0, pad)[:, :extra]
            shrink_ref[0, :, :width] += part(10 * r, r, 0, width)
            shrink_ref[0, :, width:] += part(13 * r, r, 0, pad)[:, :extra]
            query_ref[0] += part(11 * r, r, pad, q_cols)
            attend_ref[0] += part(12 * r, r, pad, q_cols)


def total_by_adapter(first, attn_in, whole_in, parts_in, count, scale, hidden, q_cols, kv_half):
    width = first.shape[2]
    r = RANK
    shapes = [
        (5 * r, width), (r, q_cols), (2, r, kv_half), (2, r, hidden), (r, q_cols), (r, hidden), (2, r, width),
    ]
    return pl.pallas_call(
        partial(total_kernel, scale, hidden, q_cols),
        grid=(count,),
        in_specs=[hspec()] * 4,
        out_specs=[pl.BlockSpec((1,) + s, lambda a, n=len(s): (a,) + (0,) * n) for s in shapes],
        out_shape=[jax.ShapeDtypeStruct((count,) + s, F32) for s in shapes],
        scratch_shapes=[
            pltpu.VMEM(first.shape, BF),
            pltpu.SMEM((first.shape[0],), jnp.int32),
            pltpu.SemaphoreType.DMA((8,)),
        ],
        compiler_params=pltpu.CompilerParams(vmem_limit_bytes=VMEM_LIMIT),
    )(first, attn_in, whole_in, parts_in)


def swap(pair):
    return lax.all_to_all(pair, "section", split_axis=0, concat_axis=0, tiled=True)


def local(
    inputs,
    lengths,
    adapter_ids,
    cotangent,
    norm_gain,
    query_weight,
    query_bias,
    keyvalue_weight,
    keyvalue_bias,
    output_weight,
    expand_weight,
    shrink_weight,
    adapter_input,
    adapter_query,
    adapter_keyvalue,
    adapter_expand,
    adapter_attend,
    adapter_shrink,
    adapter_residual,
):
    layers = lax.axis_size("section")
    tensor = lax.axis_size("tensor")
    core = lax.axis_index("section")
    place = lax.axis_index("tensor")
    rows, width = inputs.shape[1:]
    tokens = layers * rows * tensor * lax.axis_size("dp")
    kv_half = KV_HEADS * HEAD_DIM
    hidden = expand_weight.shape[3]
    r = RANK

    def turned(stack):
        return jnp.swapaxes(stack[0], 1, 2)

    def lined(stack):
        return stack[0].reshape(stack.shape[1], -1, stack.shape[-1])

    bundles, heads = pick_adapters(
        adapter_ids,
        (
            turned(adapter_input), lined(adapter_residual), lined(adapter_keyvalue), lined(adapter_expand),
            turned(adapter_shrink), adapter_query[0], turned(adapter_attend),
        ),
        (norm_gain[0], keyvalue_bias.reshape(1, -1), query_bias),
    )

    ff = weight_halves(turned(expand_weight), shrink_weight[0])
    kv = jnp.concatenate([keyvalue_weight[0, 0], keyvalue_weight[0, 1]], axis=1)
    kv_cols = kv.shape[1] // tensor
    kv = lax.dynamic_slice_in_dim(kv, place * kv_cols, kv_cols, 1)
    attn = jnp.concatenate([query_weight[0], output_weight[0].T, kv], axis=1)
    q_cols = query_weight.shape[2]
    attn = swap(attn.reshape(layers, attn.shape[0] // layers, attn.shape[1]))
    first_attn, line_attn, bundle = gather_first(attn, bundles, heads)

    def weights(layer):
        packed = first_attn if layer == 0 else lax.all_gather(line_attn, ("dp", "section"), axis=0)
        mlp = lax.all_gather(ff[layer], ("section", "dp"), axis=0)
        mlp = mlp.reshape(layers, -1, *mlp.shape[1:])
        if mlp.shape[4] % LANES:
            mlp = jnp.moveaxis(mlp, 1, 3)
            mlp = mlp.reshape(layers, 1, *mlp.shape[1:3], width)
        return dict(packed=packed, mlp=mlp, bundle=bundle[layer])

    x = lax.dynamic_index_in_dim(inputs, core, 0, keepdims=False)
    cot = lax.dynamic_index_in_dim(cotangent, core, 0, keepdims=False)
    length = lax.dynamic_index_in_dim(lengths, core, 0, keepdims=False)
    own_id = lax.dynamic_index_in_dim(adapter_ids, core, 0, keepdims=False)
    first_slot = place * rows
    info = jnp.stack([first_slot, length]).astype(jnp.int32)
    tables = rotary_tables(first_slot, rows)
    slot_ids = first_slot + jnp.arange(rows, dtype=jnp.int32)

    w = [weights(layer) for layer in range(layers)]
    outs, kept = [], []
    for layer in range(layers):
        middle, normed_two, attn_kept = attend_forward(x, w[layer], info, tables)
        shrunk, mlp_kept = mlp_forward(normed_two, w[layer])
        outs.append((middle + shrunk).astype(BF))
        kept.append((x, middle, attn_kept, mlp_kept))
        x = outs[-1]
    count = adapter_input.shape[1]
    extra = hidden + -hidden % (2 * LANES) - width
    names = jnp.broadcast_to((jnp.arange(LANES, dtype=jnp.int32) == own_id).astype(BF)[None], (r, LANES))

    def gather_all(*arrays):
        return [lax.all_gather(a, ("section", "dp"), axis=0) for a in arrays]

    grad = low_grad = jnp.where((slot_ids < length)[:, None], cot, jnp.zeros_like(cot))
    grads, gathered = [None] * layers, [None] * layers
    for layer in reversed(range(layers)):
        x, middle, attn_kept, mlp_kept = kept[layer]
        if layer < layers - 1:
            low_grad, here, last_parts = lax.optimization_barrier((low_grad, here, last_parts))
        dn2, whole, parts = mlp_backward(low_grad, w[layer], mlp_kept, names)
        if layer < layers - 1:
            total, dn2 = lax.optimization_barrier((total, dn2))
            gathered[layer + 1] = gather_all(*total) + last_parts
        grad, low_grad, attn_part = attend_backward(x, middle, grad, dn2, w[layer], attn_kept, info, tables)
        grads[layer] = grad
        here = (attn_part, whole)
        if layer > 0:
            total = lax.psum(here, "tensor")
            last_parts = gather_all(parts)
    gathered[0], layer_output, input_grad = reduce_first(*here, parts, extra, outs, grads)
    totals = total_by_adapter(
        gathered[0], *gathered[1], count, 1.0 / math.sqrt(tokens), hidden, q_cols, kv_half
    )
    turned = (0, 4, 5)
    totals = [jnp.swapaxes(total, 1, 2) if i in turned else total for i, total in enumerate(totals)]
    return (layer_output[None], input_grad[None]) + tuple(total[None] for total in totals)


def solution(mesh):
    placed = (
        P("dp", "tensor", None),
        P("dp"),
        P("dp"),
        P("dp", "tensor", None),
        P("section", None, None),
        P("section", "dp", "tensor"),
        P("section", "tensor"),
        P("section", None, "dp", None),
        P("section", None, None),
        P("section", "tensor", "dp"),
        P("section", None, "dp", "tensor"),
        P("section", "tensor", "dp"),
        P("section", None, None, None),
        P("section", None, None, "tensor"),
        P("section", None, None, None, None),
        P("section", None, None, None, "tensor"),
        P("section", None, "tensor", None),
        P("section", None, "tensor", None),
        P("section", None, None, None, None),
    )
    return jax.shard_map(
        local,
        mesh=mesh,
        in_specs=placed,
        out_specs=(
            P("section", "dp", "tensor", None),
            P("section", "dp", "tensor", None),
            P("section", None, None, None),
            P("section", None, None, "tensor"),
            P("section", None, None, None, None),
            P("section", None, None, None, "tensor"),
            P("section", None, "tensor", None),
            P("section", None, "tensor", None),
            P("section", None, None, None, None),
        ),
        check_vma=False,
    )
```

```python
from functools import partial
import math

import jax
import jax.numpy as jnp
from jax import lax
from jax.experimental import pallas as pl
from jax.experimental.pallas import tpu as pltpu
from jax.sharding import PartitionSpec as P

KV_HEADS = 2
HEAD_DIM = 128
RANK = 16
EPSILON = 1e-06
ROPE_BASE = 1000000.0
MASKED_SCORE = -1e30
LOG2_E = math.log2(math.e)
CHUNKS = 8
LANES = 128
VMEM_LIMIT = 60 * 2**20
MESH = pl.DeviceIdType.MESH
BF = jnp.bfloat16
F32 = jnp.float32


def dot(a, b):
    return jnp.dot(a, b, preferred_element_type=F32)


def dot_t(a, b):
    return lax.dot_general(a, b, (((1,), (1,)), ((), ())), preferred_element_type=F32)


def t_dot(a, b):
    return lax.dot_general(a, b, (((0,), (0,)), ((), ())), preferred_element_type=F32)


def rotary_tables(first_slot, rows):
    half = HEAD_DIM // 2
    frequency = jnp.exp(-math.log(ROPE_BASE) * (2.0 * jnp.arange(half, dtype=F32) / HEAD_DIM))
    slots = (first_slot + jnp.arange(rows, dtype=jnp.int32)).astype(F32)
    angles = slots[:, None] * frequency[None, :]
    cos, sin = jnp.cos(angles), jnp.sin(angles)
    return jnp.concatenate([cos, cos], axis=1), jnp.concatenate([-sin, sin], axis=1)


B_INPUT, B_RES_ONE, B_RES_TWO, B_KV, B_MISC, B_FF, B_FF_TAIL, B_HEADS, B_ROWS = 0, 5, 6, 7, 8, 9, 12, 15, 18


def rows_of(first, count=1):
    return slice(first * RANK, (first + count) * RANK)


def pick_kernel(
    ids_ref, input_ref, res_ref, kv_ref, expand_ref, shrink_ref, query_ref, attend_ref, gain_ref, kvb_ref, qb_ref,
    out_ref, heads_ref,
):
    width = out_ref.shape[2]
    out_ref[0] = jnp.zeros(out_ref.shape[1:], BF)
    out_ref[0, rows_of(B_INPUT, 5)] = input_ref[0]
    out_ref[0, rows_of(B_RES_ONE, 2)] = res_ref[0]
    kv_half = kv_ref.shape[2]
    for i in range(2):
        out_ref[0, rows_of(B_KV), i * kv_half : (i + 1) * kv_half] = kv_ref[0, rows_of(i)]
    misc = rows_of(B_MISC).start
    out_ref[0, misc : misc + 2] = gain_ref[...]
    out_ref[0, misc + 2 : misc + 3, : 2 * kv_half] = kvb_ref[...]
    tail = expand_ref.shape[2] - width
    for i in range(3):
        part = expand_ref[0, rows_of(i)] if i < 2 else shrink_ref[0]
        out_ref[0, rows_of(B_FF + i)] = part[:, :width]
        out_ref[0, rows_of(B_FF_TAIL + i), :tail] = part[:, width:]
    heads_ref[0] = jnp.zeros(heads_ref.shape[1:], BF)
    heads_ref[0, rows_of(0)] = query_ref[0]
    heads_ref[0, rows_of(1)] = attend_ref[0]
    heads_ref[0, 2 * RANK : 2 * RANK + 1] = qb_ref[...]


def pick_adapters(ids, stacks, shared):
    count = ids.shape[0]
    width = stacks[0].shape[2]
    q_cols = stacks[5].shape[2]
    shapes = [(B_ROWS * RANK, width), (3 * RANK, q_cols)]
    return pl.pallas_call(
        pick_kernel,
        grid_spec=pltpu.PrefetchScalarGridSpec(
            num_scalar_prefetch=1,
            grid=(count,),
            in_specs=[pl.BlockSpec((1,) + a.shape[1:], lambda i, ids: (ids[i], 0, 0)) for a in stacks]
            + [pl.BlockSpec(a.shape, lambda i, ids: (0, 0)) for a in shared],
            out_specs=[pl.BlockSpec((1,) + a, lambda i, ids: (i, 0, 0)) for a in shapes],
        ),
        out_shape=[jax.ShapeDtypeStruct((count,) + a, BF) for a in shapes],
    )(ids, *stacks, *shared)


def spread_factors(bundle_ref, expand_ref, ash_ref):
    width = bundle_ref.shape[1]
    tail = ash_ref.shape[1] - width
    expand_ref[...] = jnp.zeros_like(expand_ref)
    for i in range(2):
        expand_ref[i, rows_of(i), :width] = bundle_ref[rows_of(B_FF + i)]
        expand_ref[i, rows_of(i), width:] = bundle_ref[rows_of(B_FF_TAIL + i), :tail]
    ash_ref[:, :width] = bundle_ref[rows_of(B_FF + 2)]
    ash_ref[:, width:] = bundle_ref[rows_of(B_FF_TAIL + 2), :tail]


def vspec():
    return pl.BlockSpec(memory_space=pltpu.VMEM)


def hspec():
    return pl.BlockSpec(memory_space=pl.ANY)


def line_barrier(me, line):
    barrier = pltpu.get_barrier_semaphore()

    @pl.when(me > 0)
    def _():
        pl.semaphore_signal(barrier, inc=1, device_id={"tensor": me - 1}, device_id_type=MESH)

    @pl.when(me < line - 1)
    def _():
        pl.semaphore_signal(barrier, inc=1, device_id={"tensor": me + 1}, device_id_type=MESH)

    pl.semaphore_wait(barrier, jnp.where(me > 0, 1, 0) + jnp.where(me < line - 1, 1, 0))


def within(c, chunks):
    return jnp.logical_and(c >= 0, c < chunks)


def line_exchange(line, chunks, gathered, partial_ref, from_left, from_right, own_out, sems, begin, work):
    ag_recv, ag_right, ag_left, r_recv, r_send, l_recv, l_send = sems
    me = lax.axis_index("tensor")

    def copy(ref, src, c, o, send, recv, side):
        return pltpu.make_async_remote_copy(
            src_ref=src.at[c, o],
            dst_ref=ref.at[c, o],
            send_sem=send.at[c, o],
            recv_sem=recv.at[c, o],
            device_id={"tensor": me + side},
            device_id_type=MESH,
        )

    def ag(c, o, side):
        return copy(gathered, gathered, c, o, ag_right if side > 0 else ag_left, ag_recv, side)

    def rs(c, o, side):
        if side > 0:
            return copy(from_left, partial_ref, c, o, r_send, r_recv, 1)
        return copy(from_right, partial_ref, c, o, l_send, l_recv, -1)

    has_left, has_right = me > 0, me < line - 1

    def step(s, carry):
        first = s + line - 1

        @pl.when(jnp.logical_and(within(first, chunks), has_right))
        def _():
            ag(first, me, 1).start()

        @pl.when(jnp.logical_and(within(first, chunks), has_left))
        def _():
            ag(first, me, -1).start()

        for d in range(1, line):
            c = s + line - 1 - d

            @pl.when(jnp.logical_and(within(c, chunks), me - d >= 0))
            def _():
                ag(c, me - d, 1).wait_recv()

                @pl.when(has_right)
                def _():
                    ag(c, me - d, 1).start()

            @pl.when(jnp.logical_and(within(c, chunks), me + d < line))
            def _():
                ag(c, me + d, -1).wait_recv()

                @pl.when(has_left)
                def _():
                    ag(c, me + d, -1).start()

        @pl.when(within(s, chunks))
        def _():
            work(s)

        for h in range(line):
            c = s - h

            @pl.when(jnp.logical_and(within(c, chunks), me == h))
            def _():
                for j in range(line - 1, h, -1):
                    if h > 0:
                        rs(c, j, 1).wait_recv()
                        partial_ref[c, j] = (
                            partial_ref[c, j].astype(F32) + from_left[c, j].astype(F32)
                        ).astype(BF)
                    if h < line - 1:
                        rs(c, j, 1).start()

            @pl.when(jnp.logical_and(within(c, chunks), me == line - 1 - h))
            def _():
                for j in range(line - 1 - h):
                    if h > 0:
                        rs(c, j, -1).wait_recv()
                        partial_ref[c, j] = (
                            partial_ref[c, j].astype(F32) + from_right[c, j].astype(F32)
                        ).astype(BF)
                    if h < line - 1:
                        rs(c, j, -1).start()

        last = s - (line - 1)

        @pl.when(within(last, chunks))
        def _():
            own_out[last] = partial_ref[last, me].astype(F32)

            @pl.when(has_left)
            def _():
                rs(last, me, 1).wait_recv()
                own_out[last] += from_left[last, me].astype(F32)

            @pl.when(has_right)
            def _():
                rs(last, me, -1).wait_recv()
                own_out[last] += from_right[last, me].astype(F32)

        return carry

    line_barrier(me, line)
    begin()
    lax.fori_loop(-(line - 1), chunks + line - 1, step, 0)

    def drain(c, carry):
        for o in range(line):

            @pl.when(jnp.logical_and(has_right, me >= o))
            def _():
                ag(c, o, 1).wait_send()

            @pl.when(jnp.logical_and(has_left, me <= o))
            def _():
                ag(c, o, -1).wait_send()

            @pl.when(me < o)
            def _():
                rs(c, o, 1).wait_send()

            @pl.when(me > o)
            def _():
                rs(c, o, -1).wait_send()

        return carry

    lax.fori_loop(0, chunks, drain, 0)


def exchange_scratch(line, chunks, rows, width):
    slots = (chunks, line, rows, width)
    return [pltpu.VMEM(slots, BF)] * 4 + [pltpu.SemaphoreType.DMA((chunks, line))] * 7


def ff_loads(packed, refs, wsem):
    halves, parts, _, rows, cols = packed.shape
    return [
        pltpu.make_async_copy(
            packed.at[h, p, i],
            ref.at[pl.ds(h * rows, rows), pl.ds(p * cols, cols)],
            wsem.at[i, h, p],
        )
        for i, ref in enumerate(refs)
        for h in range(halves)
        for p in range(parts)
    ]


def clear_tail(packed, refs):
    hidden = packed.shape[0] * packed.shape[3]
    for ref in refs:
        if ref.shape[0] > hidden:
            ref[hidden:] = jnp.zeros((ref.shape[0] - hidden, ref.shape[1]), BF)


def mlp_kernel(
    line, chunks, tile,
    n2_ref, packed, bundle_ref,
    out_ref, n2_out, gate_out, up_out,
    gathered, partial_ref, from_left, from_right, s0, s1, s2, s3, s4, s5, s6,
    wg, wu, ws, gate_st, up_st, acc, expand_ref, ash_ref, wsem, osem, nsem,
):
    rows, width = n2_ref.shape[1:]
    every = line * rows
    tiles = wg.shape[0] // tile
    high = bundle_ref[rows_of(B_INPUT + 3, 2)]
    res = bundle_ref[rows_of(B_RES_TWO)]
    me = lax.axis_index("tensor")
    loads = ff_loads(packed, (wg, wu, ws), wsem)

    def begin():
        for load in loads:
            load.start()
        clear_tail(packed, (wg, wu, ws))
        spread_factors(bundle_ref, expand_ref, ash_ref)
        for c in range(chunks):
            gathered[c, me] = n2_ref[c]

    def saves(c, slot):
        return (
            pltpu.make_async_copy(gate_st.at[slot], gate_out.at[c], osem.at[0, slot]),
            pltpu.make_async_copy(up_st.at[slot], up_out.at[c], osem.at[1, slot]),
        )

    def keep(c):
        return pltpu.make_async_copy(gathered.at[c], n2_out.at[c], nsem.at[c])

    def work(c):
        slot = c % 2

        @pl.when(c == 0)
        def _():
            for load in loads:
                load.wait()

        @pl.when(c >= 2)
        def _():
            for save in saves(c - 2, slot):
                save.wait()

        keep(c).start()
        x = gathered[c].reshape(every, width)
        er = dot_t(x, high).astype(BF)

        def one(f, rank):
            cols = pl.ds(pl.multiple_of(f * tile, tile), tile)
            gate = dot_t(x, wg[cols]) + dot(er, expand_ref[0, :, cols])
            up = dot_t(x, wu[cols]) + dot(er, expand_ref[1, :, cols])
            gate_st[slot, :, cols] = gate.astype(BF)
            up_st[slot, :, cols] = up.astype(BF)
            act = (gate * (1.0 / (1.0 + jnp.exp(-gate))) * up).astype(BF)
            now = dot(act, ws[cols])

            @pl.when(f == 0)
            def _():
                acc[...] = now

            @pl.when(f > 0)
            def _():
                acc[...] += now

            return rank + dot_t(act, ash_ref[:, cols])

        rank = lax.fori_loop(0, tiles, one, jnp.zeros((every, ash_ref.shape[0]), F32))
        total = acc[...] + dot(rank.astype(BF), res)
        partial_ref[c] = total.astype(BF).reshape(line, rows, width)
        for save in saves(c, slot):
            save.start()

    line_exchange(
        line, chunks, gathered, partial_ref, from_left, from_right, out_ref,
        (s0, s1, s2, s3, s4, s5, s6), begin, work,
    )
    for c in range(chunks):
        keep(c).wait()
    for c in range(max(chunks - 2, 0), chunks):
        for save in saves(c, c % 2):
            save.wait()


def ff_tile(hidden):
    return hidden


def mlp_forward(n2, w):
    line = lax.axis_size("tensor")
    rows, width = n2.shape
    halves, groups, _, low_rows, _ = w["mlp"].shape
    hidden = halves * low_rows + -(halves * low_rows) % (2 * LANES)
    part = rows // CHUNKS
    every = line * part
    out, n2_all, gate, up = pl.pallas_call(
        partial(mlp_kernel, line, CHUNKS, ff_tile(hidden)),
        in_specs=[vspec(), hspec(), vspec()],
        out_specs=[vspec()] + [hspec()] * 3,
        out_shape=[
            jax.ShapeDtypeStruct((CHUNKS, part, width), F32),
            jax.ShapeDtypeStruct((CHUNKS, line, part, width), BF),
            jax.ShapeDtypeStruct((CHUNKS, every, hidden), BF),
            jax.ShapeDtypeStruct((CHUNKS, every, hidden), BF),
        ],
        scratch_shapes=exchange_scratch(line, CHUNKS, part, width)
        + [pltpu.VMEM((hidden, width), BF)] * 3
        + [pltpu.VMEM((2, every, hidden), BF)] * 2
        + [
            pltpu.VMEM((every, width), F32),
            pltpu.VMEM((2, 2 * RANK, hidden), BF),
            pltpu.VMEM((RANK, hidden), BF),
            pltpu.SemaphoreType.DMA((3, halves, groups)),
            pltpu.SemaphoreType.DMA((2, 2)),
            pltpu.SemaphoreType.DMA((CHUNKS,)),
        ],
        compiler_params=pltpu.CompilerParams(
            collective_id=0, has_side_effects=True, vmem_limit_bytes=VMEM_LIMIT
        ),
        cost_estimate=pl.CostEstimate(
            flops=6 * line * rows * width * hidden,
            bytes_accessed=6 * width * hidden + 4 * line * rows * hidden,
            transcendentals=line * rows * hidden,
        ),
    )(
        n2.reshape(CHUNKS, part, width), w["mlp"], w["bundle"],
    )
    return out.reshape(rows, width), (n2_all.reshape(CHUNKS, every, width), gate, up)


def mlp_back_kernel(
    line, chunks, tile,
    ds_ref, packed, n2_hbm, gate_in, up_in, bundle_ref, names_ref,
    out_ref, whole_ref, parts_ref,
    gathered, partial_ref, from_left, from_right, s0, s1, s2, s3, s4, s5, s6,
    wg, wu, ws, gate_st, up_st, n2_st, acc, ghigh_ref, gexp_ref, gsh_ref, gres_ref, expand_ref, ash_ref, wsem, isem,
):
    rows, width = ds_ref.shape[1:]
    every = line * rows
    tiles = wg.shape[0] // tile
    high = bundle_ref[rows_of(B_INPUT + 3, 2)]
    res = bundle_ref[rows_of(B_RES_TWO)]
    me = lax.axis_index("tensor")
    loads = ff_loads(packed, (wg, wu, ws), wsem)

    def fetch(c):
        slot = c % 2
        return (
            pltpu.make_async_copy(gate_in.at[c], gate_st.at[slot], isem.at[0, slot]),
            pltpu.make_async_copy(up_in.at[c], up_st.at[slot], isem.at[1, slot]),
            pltpu.make_async_copy(n2_hbm.at[c], n2_st.at[slot], isem.at[2, slot]),
        )

    def begin():
        for load in loads:
            load.start()
        clear_tail(packed, (wg, wu, ws))
        spread_factors(bundle_ref, expand_ref, ash_ref)
        for one in fetch(0):
            one.start()
        for c in range(chunks):
            gathered[c, me] = ds_ref[c]
        for ref in (ghigh_ref, gexp_ref, gsh_ref, gres_ref):
            ref[...] = jnp.zeros_like(ref)

    def work(c):
        slot = c % 2

        @pl.when(c == 0)
        def _():
            for load in loads:
                load.wait()

        for one in fetch(c):
            one.wait()

        @pl.when(c + 1 < chunks)
        def _():
            for one in fetch(c + 1):
                one.start()

        ds = gathered[c].reshape(every, width)
        n2 = n2_st[slot]
        er = dot_t(n2, high).astype(BF)
        rank_in = dot_t(ds, res).astype(BF)

        def one(f, carry):
            rank_out, srank = carry
            cols = pl.ds(pl.multiple_of(f * tile, tile), tile)
            act_grad = dot_t(ds, ws[cols]) + dot(rank_in, ash_ref[:, cols])
            gate = gate_st[slot, :, cols].astype(F32)
            up = up_st[slot, :, cols].astype(F32)
            sig = 1.0 / (1.0 + jnp.exp(-gate))
            silu = gate * sig
            act = (silu * up).astype(BF)
            gate_grad = (act_grad * up * (sig + silu * (1.0 - sig))).astype(BF)
            up_grad = (act_grad * silu).astype(BF)
            now = dot(gate_grad, wg[cols]) + dot(up_grad, wu[cols])

            @pl.when(f == 0)
            def _():
                acc[...] = now

            @pl.when(f > 0)
            def _():
                acc[...] += now

            gexp_ref[0, :, cols] += t_dot(er, gate_grad)
            gexp_ref[1, :, cols] += t_dot(er, up_grad)
            gsh_ref[:, cols] += t_dot(rank_in, act)
            rank_out = rank_out + dot_t(gate_grad, expand_ref[0, :, cols])
            rank_out = rank_out + dot_t(up_grad, expand_ref[1, :, cols])
            return rank_out, srank + dot_t(act, ash_ref[:, cols])

        rank_out, srank = lax.fori_loop(
            0,
            tiles,
            one,
            (
                jnp.zeros((every, expand_ref.shape[1]), F32),
                jnp.zeros((every, ash_ref.shape[0]), F32),
            ),
        )
        rank_out = rank_out.astype(BF)
        total = acc[...] + dot(rank_out, high)
        partial_ref[c] = total.astype(BF).reshape(line, rows, width)
        ghigh_ref[...] += t_dot(rank_out, n2)
        gres_ref[...] += t_dot(srank.astype(BF), ds)

    line_exchange(
        line, chunks, gathered, partial_ref, from_left, from_right, out_ref,
        (s0, s1, s2, s3, s4, s5, s6), begin, work,
    )
    whole_ref[: 2 * RANK] = ghigh_ref[...].astype(BF)
    whole_ref[2 * RANK :] = gres_ref[...].astype(BF)
    extra = gsh_ref.shape[1] - width
    parts_ref[3 * RANK :, extra:] = jnp.zeros((3 * RANK, width - extra), BF)
    for i, part in enumerate((gexp_ref[0, :RANK], gexp_ref[1, RANK:], gsh_ref[...])):
        part = part.astype(BF)
        parts_ref[i * RANK : (i + 1) * RANK] = part[:, :width]
        parts_ref[(3 + i) * RANK : (4 + i) * RANK, :extra] = part[:, width:]
    parts_ref[rows_of(5), extra : extra + LANES] = names_ref[...]


def mlp_backward(ds, w, saved, names):
    n2_all, gate, up = saved
    line = lax.axis_size("tensor")
    rows, width = ds.shape
    halves, groups, _, low_rows, _ = w["mlp"].shape
    hidden = halves * low_rows + -(halves * low_rows) % (2 * LANES)
    part = rows // CHUNKS
    every = line * part
    out, whole, parts = pl.pallas_call(
        partial(mlp_back_kernel, line, CHUNKS, ff_tile(hidden)),
        in_specs=[vspec()] + [hspec()] * 4 + [vspec()] * 2,
        out_specs=[vspec()] * 3,
        out_shape=[
            jax.ShapeDtypeStruct((CHUNKS, part, width), F32),
            jax.ShapeDtypeStruct((3 * RANK, width), BF),
            jax.ShapeDtypeStruct((6 * RANK, width), BF),
        ],
        scratch_shapes=exchange_scratch(line, CHUNKS, part, width)
        + [pltpu.VMEM((hidden, width), BF)] * 3
        + [pltpu.VMEM((2, every, hidden), BF)] * 2
        + [
            pltpu.VMEM((2, every, width), BF),
            pltpu.VMEM((every, width), F32),
            pltpu.VMEM((2 * RANK, width), F32),
            pltpu.VMEM((2, 2 * RANK, hidden), F32),
            pltpu.VMEM((RANK, hidden), F32),
            pltpu.VMEM((RANK, width), F32),
            pltpu.VMEM((2, 2 * RANK, hidden), BF),
            pltpu.VMEM((RANK, hidden), BF),
            pltpu.SemaphoreType.DMA((3, halves, groups)),
            pltpu.SemaphoreType.DMA((3, 2)),
        ],
        compiler_params=pltpu.CompilerParams(
            collective_id=1, has_side_effects=True, vmem_limit_bytes=VMEM_LIMIT
        ),
        cost_estimate=pl.CostEstimate(
            flops=6 * line * rows * width * hidden,
            bytes_accessed=6 * width * hidden + 4 * line * rows * hidden,
            transcendentals=line * rows * hidden,
        ),
    )(
        ds.reshape(CHUNKS, part, width), w["mlp"], n2_all, gate, up, w["bundle"], names,
    )
    return out.reshape(rows, width), whole, parts


def halves_kernel(expand, shrink, first, second, stage, in_sem, keep_sem, send_sem, recv_sem):
    core = lax.axis_index("section")
    half = first.shape[1]
    barrier = pltpu.get_barrier_semaphore()
    pl.semaphore_signal(barrier, inc=1, device_id={"section": 1 - core}, device_id_type=MESH)
    for c in range(2):

        @pl.when(core == c)
        def _():
            own = (expand.at[:, pl.ds(c * half, half)], shrink.at[pl.ds(c * half, half)])
            for i, dst in enumerate((stage.at[pl.ds(0, 2)], stage.at[2])):
                pltpu.make_async_copy(own[i], dst, in_sem.at[i]).start()

    pl.semaphore_wait(barrier, 1)
    for c, out in enumerate((first, second)):

        @pl.when(core == c)
        def _():
            away = (expand.at[:, pl.ds((1 - c) * half, half)], shrink.at[pl.ds((1 - c) * half, half)])
            places = (out.at[pl.ds(0, 2)], out.at[2])
            sends = [
                pltpu.make_async_remote_copy(
                    src_ref=away[i],
                    dst_ref=places[i],
                    send_sem=send_sem.at[i],
                    recv_sem=recv_sem.at[i],
                    device_id={"section": 1 - c},
                    device_id_type=MESH,
                )
                for i in range(2)
            ]
            for send in sends:
                send.start()
            own = (expand.at[:, pl.ds(c * half, half)], shrink.at[pl.ds(c * half, half)])
            for i, dst in enumerate((stage.at[pl.ds(0, 2)], stage.at[2])):
                pltpu.make_async_copy(own[i], dst, in_sem.at[i]).wait()
            keep = pltpu.make_async_copy(stage, out, keep_sem)
            keep.start()
            keep.wait()
            for send in sends:
                send.wait()


def weight_halves(expand, shrink):
    _, hidden, cols = expand.shape
    shape = (3, hidden // 2, cols)
    dma = pltpu.SemaphoreType.DMA
    return pl.pallas_call(
        halves_kernel,
        in_specs=[hspec()] * 2,
        out_specs=[hspec()] * 2,
        out_shape=[jax.ShapeDtypeStruct(shape, BF)] * 2,
        scratch_shapes=[pltpu.VMEM(shape, BF), dma((2,)), dma, dma((2,)), dma((2,))],
        compiler_params=pltpu.CompilerParams(
            collective_id=7, has_side_effects=True, vmem_limit_bytes=VMEM_LIMIT
        ),
    )(expand, shrink)


def gather_kernel(
    line, peers,
    attn, bundles, heads,
    first_out, second_out, bundle_out,
    own_sem, z_recv, z_right, z_left, dp_recv, dp_send, core_recv, core_send, side_recv, side_send, side_own,
):
    me, spot, core = lax.axis_index("tensor"), lax.axis_index("dp"), lax.axis_index("section")
    other = 1 - core
    has_left, has_right = me > 0, me < line - 1
    barrier = pltpu.get_barrier_semaphore()

    def greet(**where):
        pl.semaphore_signal(barrier, inc=1, device_id=where, device_id_type=MESH)

    @pl.when(has_left)
    def _():
        greet(tensor=me - 1)

    @pl.when(has_right)
    def _():
        greet(tensor=me + 1)

    greet(section=other)
    square = peers == 4

    def partner(k):
        if square:
            return (None, spot + 1 - 2 * lax.rem(spot, 2), lax.rem(spot + 2, 4), 3 - spot)[k]
        return lax.rem(spot + k, peers)

    def origin(k):
        return partner(k) if square else lax.rem(spot + peers - k, peers)

    direct = (1, 2) if square else tuple(range(1, peers))
    for k in range(1, peers):
        greet(dp=partner(k))
    pl.semaphore_wait(barrier, jnp.where(has_left, 1, 0) + jnp.where(has_right, 1, 0) + peers)

    mine = spot * 2 + core
    plain, part = bundles.shape[1] - heads.shape[1], heads.shape[2]

    def head_place(layer, o):
        return bundle_out.at[layer, pl.ds(plain, heads.shape[1]), pl.ds(o * part, part)]

    def places(o):
        return first_out.at[mine, o], second_out.at[o], head_place(core, o), head_place(other, o)

    sides = [
        pltpu.make_async_remote_copy(
            src_ref=src,
            dst_ref=dst,
            send_sem=side_send.at[i],
            recv_sem=side_recv.at[i],
            device_id={"section": other},
            device_id_type=MESH,
        )
        for i, (src, dst) in enumerate(
            (
                (bundles.at[other, pl.ds(0, plain)], bundle_out.at[core, pl.ds(0, plain)]),
                (heads.at[other], head_place(core, me)),
            )
        )
    ]
    side_keep = pltpu.make_async_copy(
        bundles.at[core, pl.ds(0, plain)], bundle_out.at[core, pl.ds(0, plain)], side_own
    )
    sources = (attn.at[0], attn.at[1], heads.at[core], head_place(other, me))
    keeps = [
        pltpu.make_async_copy(src, dst, own_sem.at[i]) for i, (src, dst) in enumerate(zip(sources[:3], places(me)))
    ]

    def remote(src, dst, send, recv, **where):
        return pltpu.make_async_remote_copy(
            src_ref=src, dst_ref=dst, send_sem=send, recv_sem=recv, device_id=where, device_id_type=MESH
        )

    def along(i, o, side, own):
        dst = places(o)[i]
        return remote(
            sources[i] if own else dst,
            dst,
            (z_right if side > 0 else z_left).at[i, o],
            z_recv.at[i, o],
            tensor=me + side,
        )

    outs = (first_out,)

    def to_peer(lay, k, o, own):
        dst = outs[lay].at[mine, o]
        return remote(
            attn.at[lay] if own else dst, dst, dp_send.at[lay, k, o], dp_recv.at[lay, spot, o], dp=partner(k)
        )

    def from_peer(lay, k, o):
        p = origin(k)
        slot = outs[lay].at[p * 2 + core, o]
        to = partner(3 - k) if square and k < 3 else p
        return remote(slot, slot, dp_send.at[lay, peers - 1, o], dp_recv.at[lay, p, o], dp=to)

    def to_core(lay, p, o, own):
        dst = outs[lay].at[p * 2 + core, o]
        return remote(
            attn.at[lay] if own else dst, dst, core_send.at[lay, p, o], core_recv.at[lay, p, o], section=other
        )

    def spread(lay, o, own):
        for k in direct:
            to_peer(lay, k, o, own).start()
        to_core(lay, spot, o, own).start()

    for side in sides:
        side.start()
    for i in range(4):
        if i == 3:
            sides[1].wait_recv()

        @pl.when(has_right)
        def _():
            along(i, me, 1, True).start()

        @pl.when(has_left)
        def _():
            along(i, me, -1, True).start()

        if i == 0:
            spread(i, me, True)
    for keep in keeps:
        keep.start()
    side_keep.start()
    for d in range(1, line):
        for i in range(4):

            @pl.when(me >= d)
            def _():
                along(i, me - d, 1, False).wait_recv()

                @pl.when(has_right)
                def _():
                    along(i, me - d, 1, False).start()

                if i == 0:
                    spread(i, me - d, False)

            @pl.when(me + d < line)
            def _():
                along(i, me + d, -1, False).wait_recv()

                @pl.when(has_left)
                def _():
                    along(i, me + d, -1, False).start()

                if i == 0:
                    spread(i, me + d, False)

    half = line // 2

    def pass_on(n, carry):
        o = lax.rem(me + n, line)
        for lay in range(1):
            for k in direct:
                from_peer(lay, k, o).wait_recv()
                if square:

                    @pl.when(o < half if k == 1 else o >= half)
                    def _():
                        from_peer(lay, k, o).start()

                to_core(lay, origin(k), o, False).start()
        return carry

    lax.fori_loop(0, line, pass_on, 0)

    def pass_last(n, carry):
        o = lax.rem(me + n, line)
        for lay in range(1):
            from_peer(lay, 3, o).wait_recv()
            to_core(lay, origin(3), o, False).start()
        return carry

    if square:
        lax.fori_loop(0, line, pass_last, 0)

    def finish(o, carry):
        for lay in range(1):
            for k in direct:
                to_peer(lay, k, o, False).wait_send()
            if square:
                from_peer(lay, 1, o).wait_send()
            for p in range(peers):
                to_core(lay, p, o, False).wait_send()
                slot = outs[lay].at[p * 2 + other, o]
                remote(slot, slot, core_send.at[lay, p, o], core_recv.at[lay, p, o], section=other).wait_recv()
        for i in range(4):

            @pl.when(jnp.logical_and(has_right, me >= o))
            def _():
                along(i, o, 1, False).wait_send()

            @pl.when(jnp.logical_and(has_left, me <= o))
            def _():
                along(i, o, -1, False).wait_send()

        return carry

    lax.fori_loop(0, line, finish, 0)
    for keep in keeps:
        keep.wait()
    side_keep.wait()
    sides[0].wait_recv()
    for side in sides:
        side.wait_send()


def gather_first(attn, bundles, heads):
    line, peers = lax.axis_size("tensor"), lax.axis_size("dp")
    cores, part, cols = attn.shape
    dma = pltpu.SemaphoreType.DMA
    return pl.pallas_call(
        partial(gather_kernel, line, peers),
        in_specs=[vspec()] * 3,
        out_specs=[hspec()] * 3,
        out_shape=[
            jax.ShapeDtypeStruct((peers * cores, line, part, cols), BF),
            jax.ShapeDtypeStruct((line, part, cols), BF),
            jax.ShapeDtypeStruct(bundles.shape, BF),
        ],
        scratch_shapes=[dma((3,)), dma((4, line)), dma((4, line)), dma((4, line))]
        + [dma((1, peers, line))] * 4
        + [dma((2,)), dma((2,)), dma],
        compiler_params=pltpu.CompilerParams(
            collective_id=4, has_side_effects=True, vmem_limit_bytes=VMEM_LIMIT
        ),
    )(attn, bundles, heads)


def rotated(x, cos, sin):
    return x * cos + pltpu.roll(x, HEAD_DIM // 2, 1) * sin


def head_cols(h):
    return pl.ds(pl.multiple_of(h * HEAD_DIM, HEAD_DIM), HEAD_DIM)


def weight_loads(packed, wq, wo, wkv, wsem):
    cols, kv_cols = wq.shape[-1], wkv.shape[-1]
    loads = []
    for i, (ref, start, size) in enumerate(((wkv, 2 * cols, kv_cols), (wq, 0, cols), (wo, cols, cols))):
        loads.append(
            [
                pltpu.make_async_copy(packed.at[:, t, :, pl.ds(start, size)], ref.at[t], wsem.at[i, t])
                for t in range(ref.shape[0])
            ]
        )
    return loads


def flat(ref, t):
    groups, rows, cols = ref.shape[1:]
    return ref[t].reshape(groups * rows, cols)


def allowed_keys(info_ref, block, keys, rows):
    row = info_ref[0] + lax.broadcasted_iota(jnp.int32, (1, rows), 1)
    last = jnp.minimum(row, info_ref[1] - 1)
    return block * keys + lax.broadcasted_iota(jnp.int32, (keys, rows), 0) <= last


def one_way_barrier(me, line, side):
    barrier = pltpu.get_barrier_semaphore()
    first, last = (0, line - 1) if side > 0 else (line - 1, 0)

    @pl.when(me != first)
    def _():
        pl.semaphore_signal(barrier, inc=1, device_id={"tensor": me - side}, device_id_type=MESH)

    @pl.when(me != last)
    def _():
        pl.semaphore_wait(barrier, 1)


def spread_qkv(bundle_ref, bq_ref, bkv_ref):
    kv_half = bkv_ref.shape[1] // 2
    bq_ref[...] = jnp.zeros_like(bq_ref)
    bkv_ref[...] = jnp.zeros_like(bkv_ref)
    bq_ref[rows_of(0)] = bundle_ref[rows_of(B_HEADS)]
    for i in range(2):
        span = slice(i * kv_half, (i + 1) * kv_half)
        bkv_ref[rows_of(1 + i), span] = bundle_ref[rows_of(B_KV), span]


def kv_exchange(me, line, kvbuf, recv, send):
    def move(o):
        return pltpu.make_async_remote_copy(
            src_ref=kvbuf.at[o],
            dst_ref=kvbuf.at[o],
            send_sem=send.at[o],
            recv_sem=recv.at[o],
            device_id={"tensor": me + 1},
            device_id_type=MESH,
        )

    return move


def attend_kernel(
    line, group,
    info_ref, x_ref, bundle_ref, cos_ref, sin_ref, packed,
    mid_ref, n2_ref, normed_ref, lowr_ref, rank_ref, q_ref, kv_out, attended_ref, log_ref,
    wq, wo, wkv, kvbuf, acc, peak, total, bq_ref, bkv_ref, wsem, recv, send, ksem,
):
    rows, width = x_ref.shape
    heads = width // HEAD_DIM
    cols = wq.shape[-1]
    kv_cols = wkv.shape[-1]
    scale = HEAD_DIM**-0.5
    me = lax.axis_index("tensor")
    one_way_barrier(me, line, 1)
    kv_loads, q_loads, o_loads = weight_loads(packed, wq, wo, wkv, wsem)
    for load in kv_loads + q_loads + o_loads:
        load.start()
    move = kv_exchange(me, line, kvbuf, recv, send)
    spread_qkv(bundle_ref, bq_ref, bkv_ref)
    misc = bundle_ref[rows_of(B_MISC)].astype(F32)
    q_bias = bundle_ref[rows_of(B_HEADS + 2)].astype(F32)[:1]
    low_in = bundle_ref[rows_of(B_INPUT, 3)]
    x = x_ref[...].astype(F32)
    inverse = lax.rsqrt(jnp.mean(x * x, axis=-1, keepdims=True) + EPSILON)
    normed_ref[...] = (x * inverse * misc[0:1]).astype(BF)
    low = dot_t(normed_ref[...], low_in).astype(BF)
    cos, sin = cos_ref[...], sin_ref[...]
    for load in kv_loads:
        load.wait()
    for t in range(line):
        span = slice(t * kv_cols, (t + 1) * kv_cols)
        kv = dot(normed_ref[...], flat(wkv, t)) + misc[2:3, span] + dot(low, bkv_ref[:, span])
        for h in range(kv_cols // HEAD_DIM):
            at = t * kv_cols + h * HEAD_DIM
            one = kv[:, h * HEAD_DIM : (h + 1) * HEAD_DIM]
            if at < KV_HEADS * HEAD_DIM:
                one = rotated(one, cos, sin)
            kvbuf[me, :, at : at + HEAD_DIM] = one.astype(BF)

    @pl.when(me < line - 1)
    def _():
        move(me).start()

    for load in q_loads:
        load.wait()
    for t in range(line):
        span = slice(t * cols, (t + 1) * cols)
        q = dot(normed_ref[...], flat(wq, t)) + q_bias[:, span] + dot(low, bq_ref[:, span])
        for h in range(cols // HEAD_DIM):
            at = t * cols + h * HEAD_DIM
            q_ref[:, at : at + HEAD_DIM] = rotated(
                q[:, h * HEAD_DIM : (h + 1) * HEAD_DIM], cos, sin
            ).astype(BF)
    acc[...] = jnp.zeros_like(acc)
    total[...] = jnp.zeros_like(total)
    peak[...] = jnp.full_like(peak, MASKED_SCORE)

    def block(o):
        allowed = allowed_keys(info_ref, o, rows, rows)

        def one(h, carry):
            kv_head = h // group
            k = kvbuf[o, :, head_cols(kv_head)]
            v = kvbuf[o, :, head_cols(KV_HEADS + kv_head)]
            scores = jnp.where(allowed, dot_t(k, q_ref[:, head_cols(h)]) * (scale * LOG2_E), MASKED_SCORE)
            top = jnp.maximum(peak[h], jnp.max(scores, axis=0, keepdims=True))
            soft = jnp.exp2(scores - top)
            shift = jnp.exp2(peak[h] - top)
            total[h] = total[h] * shift + jnp.sum(soft, axis=0, keepdims=True)
            acc[h] = acc[h] * shift + t_dot(v, soft.astype(BF))
            peak[h] = top
            return carry

        lax.fori_loop(0, heads, one, 0, unroll=12)

    for d in range(line):

        @pl.when(me >= d)
        def _():
            if d > 0:
                move(me - d).wait_recv()

                @pl.when(me < line - 1)
                def _():
                    move(me - d).start()

            block(me - d)

    keep = pltpu.make_async_copy(kvbuf, kv_out, ksem)
    keep.start()
    for h in range(heads):
        attended_ref[:, h * HEAD_DIM : (h + 1) * HEAD_DIM] = (acc[h] * (1.0 / total[h])).T.astype(BF)
        log_ref[h] = peak[h] + jnp.log(total[h]) * LOG2_E
    rank = dot_t(attended_ref[...], bundle_ref[rows_of(B_HEADS + 1)]).astype(BF)
    lowr_ref[...] = low
    rank_ref[...] = rank
    middle = x_ref[...].astype(F32) + dot(rank, bundle_ref[rows_of(B_RES_ONE)])
    for load in o_loads:
        load.wait()
    for t in range(line):
        middle = middle + dot_t(attended_ref[:, t * cols : (t + 1) * cols], flat(wo, t))
    mid_ref[...] = middle
    inverse = lax.rsqrt(jnp.mean(middle * middle, axis=-1, keepdims=True) + EPSILON)
    n2_ref[...] = (middle * inverse * misc[1:2]).astype(BF)
    keep.wait()
    for o in range(line):

        @pl.when(jnp.logical_and(me < line - 1, me >= o))
        def _():
            move(o).wait_send()


def attend_forward(x, w, info, tables):
    line = lax.axis_size("tensor")
    rows, width = x.shape
    heads = width // HEAD_DIM
    kv_width = 2 * KV_HEADS * HEAD_DIM
    groups, low_rows = w["packed"].shape[0], w["packed"].shape[2]
    outs = pl.pallas_call(
        partial(attend_kernel, line, heads // KV_HEADS),
        in_specs=[pl.BlockSpec(memory_space=pltpu.SMEM)] + [vspec()] * 4 + [hspec()],
        out_specs=[vspec()] * 6 + [hspec()] + [vspec()] * 2,
        out_shape=[
            jax.ShapeDtypeStruct((rows, width), F32),
            jax.ShapeDtypeStruct((rows, width), BF),
            jax.ShapeDtypeStruct((rows, width), BF),
            jax.ShapeDtypeStruct((rows, 3 * RANK), BF),
            jax.ShapeDtypeStruct((rows, RANK), BF),
            jax.ShapeDtypeStruct((rows, width), BF),
            jax.ShapeDtypeStruct((line, rows, kv_width), BF),
            jax.ShapeDtypeStruct((rows, width), BF),
            jax.ShapeDtypeStruct((heads, 1, rows), F32),
        ],
        scratch_shapes=[
            pltpu.VMEM((line, groups, low_rows, width // line), BF),
            pltpu.VMEM((line, groups, low_rows, width // line), BF),
            pltpu.VMEM((line, groups, low_rows, kv_width // line), BF),
            pltpu.VMEM((line, rows, kv_width), BF),
            pltpu.VMEM((heads, HEAD_DIM, rows), F32),
            pltpu.VMEM((heads, 1, rows), F32),
            pltpu.VMEM((heads, 1, rows), F32),
            pltpu.VMEM((3 * RANK, width), BF),
            pltpu.VMEM((3 * RANK, kv_width), BF),
            pltpu.SemaphoreType.DMA((3, line)),
            pltpu.SemaphoreType.DMA((line,)),
            pltpu.SemaphoreType.DMA((line,)),
            pltpu.SemaphoreType.DMA,
        ],
        compiler_params=pltpu.CompilerParams(
            collective_id=2, has_side_effects=True, vmem_limit_bytes=VMEM_LIMIT
        ),
        cost_estimate=pl.CostEstimate(
            flops=4 * rows * width * width * 2, bytes_accessed=5 * width * width, transcendentals=0
        ),
    )(
        info, x, w["bundle"], tables[0], tables[1], w["packed"],
    )
    return outs[0], outs[1], outs[2:]


def attend_back_kernel(
    line, group,
    info_ref, x_ref, mid_ref, dy_ref, dn2_ref, bundle_ref, cos_ref, sin_ref,
    normed_ref, lowr_ref, rank_ref, q_ref, kv_ref, attended_ref, log_ref, packed,
    dx_ref, dx_low_ref, grads_ref,
    wq, wo, wkv, do_ref, dq_acc, dq_ref, dkv_acc, partial_ref, from_right, delta, bq_ref, bkv_ref, wsem, recv, send,
):
    rows, width = x_ref.shape
    heads = width // HEAD_DIM
    cols = wq.shape[-1]
    kv_cols = wkv.shape[-1]
    kv_half = KV_HEADS * HEAD_DIM
    scale = HEAD_DIM**-0.5
    me = lax.axis_index("tensor")
    one_way_barrier(me, line, -1)
    kv_loads, q_loads, o_loads = weight_loads(packed, wq, wo, wkv, wsem)
    for load in o_loads + q_loads + kv_loads:
        load.start()

    def move(o):
        return pltpu.make_async_remote_copy(
            src_ref=partial_ref.at[o],
            dst_ref=from_right.at[o],
            send_sem=send.at[o],
            recv_sem=recv.at[o],
            device_id={"tensor": me - 1},
            device_id_type=MESH,
        )

    def through_norm(values, gain, grad_out):
        inverse = lax.rsqrt(jnp.mean(values * values, axis=-1, keepdims=True) + EPSILON)
        weighted = gain * grad_out
        return inverse * weighted - inverse * inverse * inverse * values * jnp.mean(
            weighted * values, axis=-1, keepdims=True
        )

    spread_qkv(bundle_ref, bq_ref, bkv_ref)
    misc = bundle_ref[rows_of(B_MISC)].astype(F32)
    att = bundle_ref[rows_of(B_HEADS + 1)]
    middle_grad = dy_ref[...].astype(F32) + through_norm(mid_ref[...], misc[1:2], dn2_ref[...])
    dx_ref[...] = middle_grad
    branch_grad = middle_grad.astype(BF)
    low, rank = lowr_ref[...], rank_ref[...]
    rank_grad = dot_t(branch_grad, bundle_ref[rows_of(B_RES_ONE)]).astype(BF)
    grads_ref[3 * RANK : 4 * RANK] = t_dot(rank, branch_grad).astype(BF)
    grads_ref[6 * RANK :] = t_dot(rank_grad, attended_ref[...]).astype(BF)
    for load in o_loads:
        load.wait()
    for t in range(line):
        span = slice(t * cols, (t + 1) * cols)
        do_ref[:, span] = (dot(branch_grad, flat(wo, t)) + dot(rank_grad, att[:, span])).astype(BF)
    for h in range(heads):
        span = slice(h * HEAD_DIM, (h + 1) * HEAD_DIM)
        both = do_ref[:, span].astype(F32) * attended_ref[:, span].astype(F32)
        delta[h] = jnp.sum(both.T, axis=0, keepdims=True)
    dq_acc[...] = jnp.zeros_like(dq_acc)

    def block(o):
        allowed = allowed_keys(info_ref, o, rows, rows)
        dkv_acc[...] = jnp.zeros_like(dkv_acc)

        def one(h, carry):
            kv_head = h // group
            k = kv_ref[o, :, head_cols(kv_head)]
            v = kv_ref[o, :, head_cols(KV_HEADS + kv_head)]
            q = q_ref[:, head_cols(h)]
            do = do_ref[:, head_cols(h)]
            scores = dot_t(k, q) * (scale * LOG2_E) - log_ref[h]
            soft = jnp.exp2(jnp.where(allowed, scores, MASKED_SCORE))
            grad = (soft * (dot_t(v, do) - delta[h])).astype(BF)
            dq_acc[h] += t_dot(k, grad)
            dkv_acc[:, head_cols(kv_head)] += dot(grad, q) * scale
            dkv_acc[:, head_cols(KV_HEADS + kv_head)] += dot(soft.astype(BF), do)
            return carry

        lax.fori_loop(0, heads, one, 0, unroll=12)
        partial_ref[o] = dkv_acc[...].astype(BF)

    for s in range(2 * line - 1):
        if s < line:

            @pl.when(me >= s)
            def _():
                block(s)

        for h in range(line - 1):
            o = s - h
            if 0 <= o < line - 1 - h:

                @pl.when(me == line - 1 - h)
                def _():
                    if h > 0:
                        move(o).wait_recv()
                        partial_ref[o] = (partial_ref[o].astype(F32) + from_right[o].astype(F32)).astype(BF)
                    move(o).start()

    cos, sin = cos_ref[...], -sin_ref[...]
    for h in range(heads):
        dq_ref[:, h * HEAD_DIM : (h + 1) * HEAD_DIM] = rotated(dq_acc[h].T * scale, cos, sin).astype(BF)
    dq = dq_ref[...]
    grads_ref[5 * RANK : 6 * RANK] = t_dot(low, dq)[:RANK].astype(BF)
    low_grad = dot_t(dq, bq_ref[...])
    for load in q_loads:
        load.wait()
    normed_grad = dot_t(dq[:, :cols], flat(wq, 0))
    for t in range(1, line):
        normed_grad = normed_grad + dot_t(dq[:, t * cols : (t + 1) * cols], flat(wq, t))
    dkv_acc[...] = partial_ref[me].astype(F32)

    @pl.when(me < line - 1)
    def _():
        move(me).wait_recv()
        dkv_acc[...] += from_right[me].astype(F32)

    for h in range(KV_HEADS):
        span = slice(h * HEAD_DIM, (h + 1) * HEAD_DIM)
        dkv_acc[:, span] = rotated(dkv_acc[:, span], cos, sin)
    dkv = dkv_acc[...].astype(BF)
    kv_grad = t_dot(low, dkv).astype(BF)
    grads_ref[4 * RANK : 5 * RANK, :kv_half] = kv_grad[RANK : 2 * RANK, :kv_half]
    grads_ref[4 * RANK : 5 * RANK, kv_half : 2 * kv_half] = kv_grad[2 * RANK :, kv_half:]
    grads_ref[4 * RANK : 5 * RANK, 2 * kv_half :] = jnp.zeros((RANK, width - 2 * kv_half), BF)
    low_grad = (low_grad + dot_t(dkv, bkv_ref[...])).astype(BF)
    grads_ref[: 3 * RANK] = t_dot(low_grad, normed_ref[...]).astype(BF)
    for load in kv_loads:
        load.wait()
    for t in range(line):
        normed_grad = normed_grad + dot_t(dkv[:, t * kv_cols : (t + 1) * kv_cols], flat(wkv, t))
    normed_grad = normed_grad + dot(low_grad, bundle_ref[rows_of(B_INPUT, 3)])
    dx = dx_ref[...] + through_norm(x_ref[...].astype(F32), misc[0:1], normed_grad)
    dx_ref[...] = dx
    dx_low_ref[...] = dx.astype(BF)
    for o in range(line - 1):

        @pl.when(me > o)
        def _():
            move(o).wait_send()


def attend_backward(x, middle, dy, dn2, w, kept, info, tables):
    line = lax.axis_size("tensor")
    rows, width = x.shape
    heads = width // HEAD_DIM
    kv_width = 2 * KV_HEADS * HEAD_DIM
    groups, low_rows = w["packed"].shape[0], w["packed"].shape[2]
    return pl.pallas_call(
        partial(attend_back_kernel, line, heads // KV_HEADS),
        in_specs=[pl.BlockSpec(memory_space=pltpu.SMEM)] + [vspec()] * 14 + [hspec()],
        out_specs=[vspec()] * 3,
        out_shape=[
            jax.ShapeDtypeStruct((rows, width), F32),
            jax.ShapeDtypeStruct((rows, width), BF),
            jax.ShapeDtypeStruct((7 * RANK, width), BF),
        ],
        scratch_shapes=[
            pltpu.VMEM((line, groups, low_rows, width // line), BF),
            pltpu.VMEM((line, groups, low_rows, width // line), BF),
            pltpu.VMEM((line, groups, low_rows, kv_width // line), BF),
            pltpu.VMEM((rows, width), BF),
            pltpu.VMEM((heads, HEAD_DIM, rows), F32),
            pltpu.VMEM((rows, width), BF),
            pltpu.VMEM((rows, kv_width), F32),
            pltpu.VMEM((line, rows, kv_width), BF),
            pltpu.VMEM((line, rows, kv_width), BF),
            pltpu.VMEM((heads, 1, rows), F32),
            pltpu.VMEM((3 * RANK, width), BF),
            pltpu.VMEM((3 * RANK, kv_width), BF),
            pltpu.SemaphoreType.DMA((3, line)),
            pltpu.SemaphoreType.DMA((line,)),
            pltpu.SemaphoreType.DMA((line,)),
        ],
        compiler_params=pltpu.CompilerParams(
            collective_id=3 if dy.dtype == F32 else 5, has_side_effects=True, vmem_limit_bytes=VMEM_LIMIT
        ),
        cost_estimate=pl.CostEstimate(
            flops=4 * rows * width * width * 2, bytes_accessed=5 * width * width, transcendentals=0
        ),
    )(
        info, x, middle, dy, dn2, w["bundle"], tables[0], tables[1], *kept, w["packed"],
    )


def reduce_kernel(
    line, peers, extra,
    attn_ref, whole_ref, parts_ref, y_first, y_second, g_first, g_second,
    out, y_out, g_out,
    mine, z_in, quarter, z_recv, z_send, dp_recv, dp_send, own_sem, t_recv, t_right, t_left,
    side_recv, side_send, side_own,
):
    r = RANK
    me, spot, core = lax.axis_index("tensor"), lax.axis_index("dp"), lax.axis_index("section")
    width = mine.shape[1]
    cols = width // line
    seqs = out.shape[0]
    seq = spot * 2 + core
    has_left, has_right = me > 0, me < line - 1
    barrier = pltpu.get_barrier_semaphore()

    def greet(**where):
        pl.semaphore_signal(barrier, inc=1, device_id=where, device_id_type=MESH)

    for k in range(1, line):
        greet(tensor=lax.rem(me + k, line))

    greet(section=1 - core)

    @pl.when(core == 0)
    def _():
        for k in range(1, peers):
            for c in range(2):
                greet(section=c, dp=lax.rem(spot + k, peers))

    pl.semaphore_wait(barrier, line - 1 + peers)

    def remote(src, dst, send, recv, **where):
        return pltpu.make_async_remote_copy(
            src_ref=src, dst_ref=dst, send_sem=send, recv_sem=recv, device_id=where, device_id_type=MESH
        )

    def lanes(t):
        return pl.ds(pl.multiple_of(t * cols, LANES), cols)

    def pieces(s):
        return (
            (parts_ref.at[pl.ds(0, 3 * r)], out.at[s, pl.ds(8 * r, 3 * r)]),
            (parts_ref.at[pl.ds(3 * r, 3 * r), pl.ds(0, extra)], out.at[s, pl.ds(11 * r, 3 * r), pl.ds(0, extra)]),
            (
                parts_ref.at[pl.ds(5 * r, r), pl.ds(extra, LANES)],
                out.at[s, pl.ds(13 * r, r), pl.ds(extra, LANES)],
            ),
            (quarter.at[pl.ds(0, 8 * r)], out.at[s, pl.ds(0, 8 * r), lanes(me)]),
            (quarter.at[pl.ds(8 * r, 2 * r)], out.at[s, pl.ds(11 * r, 2 * r), pl.ds(extra, cols)]),
        )

    def to_peer(k, i):
        src, dst = pieces(seq)[i]
        return remote(src, dst, dp_send.at[k, i], dp_recv.at[seq, i], section=0, dp=lax.rem(spot + k, peers))

    def stay(i):
        src, dst = pieces(seq)[i]
        return pltpu.make_async_copy(src, dst, own_sem.at[i])

    def send_pieces(which):
        for i in which:
            for k in range(1, peers):
                to_peer(k, i).start()

            @pl.when(core != 0)
            def _():
                to_peer(0, i).start()

            @pl.when(core == 0)
            def _():
                stay(i).start()

    def across(k):
        to = lax.rem(me + k, line)
        return remote(mine.at[:, lanes(to)], z_in.at[me], z_send.at[k], z_recv.at[me], tensor=to)

    def incoming(k):
        o = lax.rem(me + k, line)
        return remote(mine.at[:, lanes(me)], z_in.at[o], z_send.at[k], z_recv.at[o], tensor=o)

    def side(i, src, dst):
        return remote(src, dst.at[core], side_send.at[i], side_recv.at[i], section=1 - core)

    def side_keep(i, src, dst):
        return pltpu.make_async_copy(src, dst.at[core], side_own.at[i])

    pairs = ((y_first, y_second, y_out), (g_first, g_second, g_out))

    for first, rows, ref, start in (
        (0, 3, attn_ref, 0), (3, 2, whole_ref, 0), (5, 1, attn_ref, 3), (6, 1, whole_ref, 2), (7, 3, attn_ref, 4),
    ):
        mine[rows_of(first, rows)] = ref[rows_of(start, rows)]
    for k in range(1, line):
        across(k).start()
    send_pieces((0, 1, 2))
    for c in range(2):

        @pl.when(core == c)
        def _():
            for i, (first, second, dst) in enumerate(pairs):
                side(i, first if c == 1 else second, dst).start()
                side_keep(i, second if c == 1 else first, dst).start()

    total = mine[:, lanes(me)].astype(F32)
    for k in range(1, line):
        incoming(k).wait_recv()
        total = total + z_in[lax.rem(me + k, line)].astype(F32)
    quarter[...] = total.astype(BF)
    send_pieces((3, 4))

    def arrived(s, i):
        src, dst = pieces(s)[i]
        return remote(src, dst, dp_send.at[0, i], dp_recv.at[s, i], section=0)

    def along(s, o, side):
        place = out.at[s, pl.ds(0, 8 * r), lanes(o)]
        return remote(
            place, place, (t_right if side > 0 else t_left).at[s, o], t_recv.at[s, o], tensor=me + side
        )

    @pl.when(core == 0)
    def _():
        def own_rows(n, carry):
            s = lax.rem(seq + n, seqs)

            @pl.when(n == 0)
            def _():
                stay(3).wait()

            @pl.when(n > 0)
            def _():
                arrived(s, 3).wait_recv()

            @pl.when(has_right)
            def _():
                along(s, me, 1).start()

            @pl.when(has_left)
            def _():
                along(s, me, -1).start()

            return carry

        lax.fori_loop(0, seqs, own_rows, 0)
        for d in range(1, line):

            def others(n, carry):
                s = lax.rem(seq + n, seqs)

                @pl.when(me >= d)
                def _():
                    along(s, me - d, 1).wait_recv()

                    @pl.when(has_right)
                    def _():
                        along(s, me - d, 1).start()

                @pl.when(me + d < line)
                def _():
                    along(s, me + d, -1).wait_recv()

                    @pl.when(has_left)
                    def _():
                        along(s, me + d, -1).start()

                return carry

            lax.fori_loop(0, seqs, others, 0)

        def finish(n, carry):
            s = lax.rem(seq + n, seqs)

            @pl.when(n > 0)
            def _():
                for i in (0, 1, 2, 4):
                    arrived(s, i).wait_recv()

            for o in range(line):

                @pl.when(jnp.logical_and(has_right, me >= o))
                def _():
                    along(s, o, 1).wait_send()

                @pl.when(jnp.logical_and(has_left, me <= o))
                def _():
                    along(s, o, -1).wait_send()

            return carry

        lax.fori_loop(0, seqs, finish, 0)
        for i in (0, 1, 2, 4):
            stay(i).wait()

    for k in range(1, line):
        across(k).wait_send()
    for i in range(5):
        for k in range(1, peers):
            to_peer(k, i).wait_send()

        @pl.when(core != 0)
        def _():
            to_peer(0, i).wait_send()
    for i, (first, _, dst) in enumerate(pairs):
        side(i, first, dst).wait()
        side_keep(i, first, dst).wait()


def reduce_first(attn_part, whole, parts, extra, outs, grads):
    line, peers = lax.axis_size("tensor"), lax.axis_size("dp")
    width = parts.shape[1]
    seqs = 2 * peers
    dma = pltpu.SemaphoreType.DMA
    return pl.pallas_call(
        partial(reduce_kernel, line, peers, extra),
        in_specs=[vspec()] * 7,
        out_specs=[hspec()] * 3,
        out_shape=[
            jax.ShapeDtypeStruct((seqs, 14 * RANK, width), BF),
            jax.ShapeDtypeStruct((2,) + outs[0].shape, outs[0].dtype),
            jax.ShapeDtypeStruct((2,) + grads[0].shape, grads[0].dtype),
        ],
        scratch_shapes=[
            pltpu.VMEM((10 * RANK, width), BF),
            pltpu.VMEM((line, 10 * RANK, width // line), BF),
            pltpu.VMEM((10 * RANK, width // line), BF),
            dma((line,)),
            dma((line,)),
            dma((seqs, 5)),
            dma((peers, 5)),
            dma((5,)),
            dma((seqs, line)),
            dma((seqs, line)),
            dma((seqs, line)),
            dma((2,)),
            dma((2,)),
            dma((2,)),
        ],
        compiler_params=pltpu.CompilerParams(
            collective_id=6, has_side_effects=True, vmem_limit_bytes=VMEM_LIMIT
        ),
    )(attn_part, whole, parts, *outs, *grads)


def total_kernel(
    scale, hidden, q_cols,
    first, attn_in, whole_in, parts_in,
    input_ref, query_ref, kv_ref, expand_ref, attend_ref, shrink_ref, res_ref,
    block, ids, sem,
):
    r = RANK
    a = pl.program_id(0)
    core = lax.axis_index("section")
    width = block.shape[2]
    extra = hidden - width
    pad = extra + -hidden % (2 * LANES)

    @pl.when(jnp.logical_and(a == 0, core == 0))
    def _():
        load = pltpu.make_async_copy(first, block, sem.at[0])
        load.start()
        load.wait()

    @pl.when(jnp.logical_and(a == 0, core != 0))
    def _():
        def load(src, start, first, count, at):
            return pltpu.make_async_copy(src.at[:, rows_of(start, count)], block.at[:, rows_of(first, count)], sem.at[at])

        loads = [
            load(attn_in, 0, 0, 3, 1), load(whole_in, 0, 3, 2, 2), load(attn_in, 3, 5, 1, 3),
            load(whole_in, 2, 6, 1, 4), load(attn_in, 4, 7, 1, 5), load(parts_in, 0, 8, 6, 6),
        ]
        for one in loads:
            one.start()
        for one in loads:
            one.wait()
        mine = pl.ds(pl.multiple_of(lax.axis_index("tensor") * q_cols, LANES), q_cols)
        last = pltpu.make_async_copy(
            attn_in.at[:, rows_of(5, 2), mine], block.at[:, rows_of(11, 2), pl.ds(pad, q_cols)], sem.at[7]
        )
        last.start()
        last.wait()

    @pl.when(a == 0)
    def _():
        lane = lax.broadcasted_iota(jnp.int32, (1, LANES), 1).astype(F32)
        for i in range(block.shape[0]):
            names = block[i, 13 * r : 14 * r, pad : pad + LANES][:1].astype(F32)
            ids[i] = jnp.sum(lane * names).astype(jnp.int32)

    for ref in (input_ref, query_ref, kv_ref, expand_ref, attend_ref, shrink_ref, res_ref):
        ref[...] = jnp.zeros_like(ref)

    for i in range(block.shape[0]):

        @pl.when(ids[i] == a)
        def _():
            def part(row, rows, col, cols):
                return block[i, row : row + rows, col : col + cols].astype(F32) * scale

            input_ref[0] += part(0, 5 * r, 0, width)
            res_ref[0, 0] += part(5 * r, r, 0, width)
            res_ref[0, 1] += part(6 * r, r, 0, width)
            kv = part(7 * r, r, 0, 2 * kv_ref.shape[3])
            kv_ref[0, 0] += kv[:, : kv_ref.shape[3]]
            kv_ref[0, 1] += kv[:, kv_ref.shape[3] :]
            for j in range(2):
                expand_ref[0, j, :, :width] += part((8 + j) * r, r, 0, width)
                expand_ref[0, j, :, width:] += part((11 + j) * r, r, 0, pad)[:, :extra]
            shrink_ref[0, :, :width] += part(10 * r, r, 0, width)
            shrink_ref[0, :, width:] += part(13 * r, r, 0, pad)[:, :extra]
            query_ref[0] += part(11 * r, r, pad, q_cols)
            attend_ref[0] += part(12 * r, r, pad, q_cols)


def total_by_adapter(first, attn_in, whole_in, parts_in, count, scale, hidden, q_cols, kv_half):
    width = first.shape[2]
    r = RANK
    shapes = [
        (5 * r, width), (r, q_cols), (2, r, kv_half), (2, r, hidden), (r, q_cols), (r, hidden), (2, r, width),
    ]
    return pl.pallas_call(
        partial(total_kernel, scale, hidden, q_cols),
        grid=(count,),
        in_specs=[hspec()] * 4,
        out_specs=[pl.BlockSpec((1,) + s, lambda a, n=len(s): (a,) + (0,) * n) for s in shapes],
        out_shape=[jax.ShapeDtypeStruct((count,) + s, F32) for s in shapes],
        scratch_shapes=[
            pltpu.VMEM(first.shape, BF),
            pltpu.SMEM((first.shape[0],), jnp.int32),
            pltpu.SemaphoreType.DMA((8,)),
        ],
        compiler_params=pltpu.CompilerParams(vmem_limit_bytes=VMEM_LIMIT),
    )(first, attn_in, whole_in, parts_in)


def swap(pair):
    return lax.all_to_all(pair, "section", split_axis=0, concat_axis=0, tiled=True)


def local(
    inputs,
    lengths,
    adapter_ids,
    cotangent,
    norm_gain,
    query_weight,
    query_bias,
    keyvalue_weight,
    keyvalue_bias,
    output_weight,
    expand_weight,
    shrink_weight,
    adapter_input,
    adapter_query,
    adapter_keyvalue,
    adapter_expand,
    adapter_attend,
    adapter_shrink,
    adapter_residual,
):
    layers = lax.axis_size("section")
    tensor = lax.axis_size("tensor")
    core = lax.axis_index("section")
    place = lax.axis_index("tensor")
    rows, width = inputs.shape[1:]
    tokens = layers * rows * tensor * lax.axis_size("dp")
    kv_half = KV_HEADS * HEAD_DIM
    hidden = expand_weight.shape[3]
    r = RANK

    def turned(stack):
        return jnp.swapaxes(stack[0], 1, 2)

    def lined(stack):
        return stack[0].reshape(stack.shape[1], -1, stack.shape[-1])

    bundles, heads = pick_adapters(
        adapter_ids,
        (
            turned(adapter_input), lined(adapter_residual), lined(adapter_keyvalue), lined(adapter_expand),
            turned(adapter_shrink), adapter_query[0], turned(adapter_attend),
        ),
        (norm_gain[0], keyvalue_bias.reshape(1, -1), query_bias),
    )

    ff = weight_halves(turned(expand_weight), shrink_weight[0])
    kv = jnp.concatenate([keyvalue_weight[0, 0], keyvalue_weight[0, 1]], axis=1)
    kv_cols = kv.shape[1] // tensor
    kv = lax.dynamic_slice_in_dim(kv, place * kv_cols, kv_cols, 1)
    attn = jnp.concatenate([query_weight[0], output_weight[0].T, kv], axis=1)
    q_cols = query_weight.shape[2]
    attn = swap(attn.reshape(layers, attn.shape[0] // layers, attn.shape[1]))
    first_attn, line_attn, bundle = gather_first(attn, bundles, heads)

    def weights(layer):
        packed = first_attn if layer == 0 else lax.all_gather(line_attn, ("dp", "section"), axis=0)
        mlp = lax.all_gather(ff[layer], ("section", "dp"), axis=0)
        mlp = mlp.reshape(layers, -1, *mlp.shape[1:])
        if mlp.shape[4] % LANES:
            mlp = jnp.moveaxis(mlp, 1, 3)
            mlp = mlp.reshape(layers, 1, *mlp.shape[1:3], width)
        return dict(packed=packed, mlp=mlp, bundle=bundle[layer])

    x = lax.dynamic_index_in_dim(inputs, core, 0, keepdims=False)
    cot = lax.dynamic_index_in_dim(cotangent, core, 0, keepdims=False)
    length = lax.dynamic_index_in_dim(lengths, core, 0, keepdims=False)
    own_id = lax.dynamic_index_in_dim(adapter_ids, core, 0, keepdims=False)
    first_slot = place * rows
    info = jnp.stack([first_slot, length]).astype(jnp.int32)
    tables = rotary_tables(first_slot, rows)
    slot_ids = first_slot + jnp.arange(rows, dtype=jnp.int32)

    w = [weights(layer) for layer in range(layers)]
    outs, kept = [], []
    for layer in range(layers):
        middle, normed_two, attn_kept = attend_forward(x, w[layer], info, tables)
        shrunk, mlp_kept = mlp_forward(normed_two, w[layer])
        outs.append((middle + shrunk).astype(BF))
        kept.append((x, middle, attn_kept, mlp_kept))
        x = outs[-1]
    count = adapter_input.shape[1]
    extra = hidden + -hidden % (2 * LANES) - width
    names = jnp.broadcast_to((jnp.arange(LANES, dtype=jnp.int32) == own_id).astype(BF)[None], (r, LANES))

    def gather_all(*arrays):
        return [lax.all_gather(a, ("section", "dp"), axis=0) for a in arrays]

    grad = low_grad = jnp.where((slot_ids < length)[:, None], cot, jnp.zeros_like(cot))
    grads, gathered = [None] * layers, [None] * layers
    for layer in reversed(range(layers)):
        x, middle, attn_kept, mlp_kept = kept[layer]
        if layer < layers - 1:
            low_grad, here, last_parts = lax.optimization_barrier((low_grad, here, last_parts))
        dn2, whole, parts = mlp_backward(low_grad, w[layer], mlp_kept, names)
        if layer < layers - 1:
            total, dn2 = lax.optimization_barrier((total, dn2))
            gathered[layer + 1] = gather_all(*total) + last_parts
        grad, low_grad, attn_part = attend_backward(x, middle, grad, dn2, w[layer], attn_kept, info, tables)
        grads[layer] = grad
        here = (attn_part, whole)
        if layer > 0:
            total = lax.psum(here, "tensor")
            last_parts = gather_all(parts)
    gathered[0], layer_output, input_grad = reduce_first(*here, parts, extra, outs, grads)
    totals = total_by_adapter(
        gathered[0], *gathered[1], count, 1.0 / math.sqrt(tokens), hidden, q_cols, kv_half
    )
    turned = (0, 4, 5)
    totals = [jnp.swapaxes(total, 1, 2) if i in turned else total for i, total in enumerate(totals)]
    return (layer_output[None], input_grad[None]) + tuple(total[None] for total in totals)


def solution(mesh):
    placed = (
        P("dp", "tensor", None),
        P("dp"),
        P("dp"),
        P("dp", "tensor", None),
        P("section", None, None),
        P("section", "dp", "tensor"),
        P("section", "tensor"),
        P("section", None, "dp", None),
        P("section", None, None),
        P("section", "tensor", "dp"),
        P("section", None, "dp", "tensor"),
        P("section", "tensor", "dp"),
        P("section", None, None, None),
        P("section", None, None, "tensor"),
        P("section", None, None, None, None),
        P("section", None, None, None, "tensor"),
        P("section", None, "tensor", None),
        P("section", None, "tensor", None),
        P("section", None, None, None, None),
    )
    return jax.shard_map(
        local,
        mesh=mesh,
        in_specs=placed,
        out_specs=(
            P("section", "dp", "tensor", None),
            P("section", "dp", "tensor", None),
            P("section", None, None, None),
            P("section", None, None, "tensor"),
            P("section", None, None, None, None),
            P("section", None, None, None, "tensor"),
            P("section", None, "tensor", None),
            P("section", None, "tensor", None),
            P("section", None, None, None, None),
        ),
        check_vma=False,
    )
```
